32 devices in a mesh: batch: 4 (over y, core), seq: 8 (over z, x).
Axes of the slice: x: 2, y: 2, z: 4, core: 2. Of those that a mesh axis runs over, the one named last changes fastest.
Arguments:
- inputs: bfloat16 [4, 2048, 2048], P('batch', 'seq'), may hold values from -6 to 6
- exit_layers: int32 [4, 2048], P('batch'), may hold values from 1 to 24, as said below
- lengths: int32 [4, 7], P('batch'), may hold values from 1 to 512, as said below
- layer_index: int32 [1], replicated, may hold values from 8 to 15
- out_grad: bfloat16 [4, 2048, 2048], P('batch', 'seq'), may hold values from -6 to 6
- ln1_gain: bfloat16 [2048], P(('batch', 'seq')), may hold values from 0.5 to 1.5
- ln1_bias: bfloat16 [2048], P(('batch', 'seq')), may hold values from -1.75 to 1.75
- q_weight: bfloat16 [2048, 2048], P(('batch', 'seq')), may hold values from -0.125 to 0.125
- q_bias: bfloat16 [2048], P(('batch', 'seq')), may hold values from -1.75 to 1.75
- k_weight: bfloat16 [2048, 2048], P(('batch', 'seq')), may hold values from -0.125 to 0.125
- v_weight: bfloat16 [2048, 2048], P(('batch', 'seq')), may hold values from -0.125 to 0.125
- v_bias: bfloat16 [2048], P(('batch', 'seq')), may hold values from -1.75 to 1.75
- o_weight: bfloat16 [2048, 2048], P(('batch', 'seq')), may hold values from -0.5 to 0.5
- o_bias: bfloat16 [2048], P(('batch', 'seq')), may hold values from -1.75 to 1.75
- ln2_gain: bfloat16 [2048], P(('batch', 'seq')), may hold values from 0.5 to 1.5
- ln2_bias: bfloat16 [2048], P(('batch', 'seq')), may hold values from -1.75 to 1.75
- fc1_weight: bfloat16 [2048, 8192], P(None, ('batch', 'seq')), may hold values from -0.125 to 0.125
- fc1_bias: bfloat16 [8192], P(('batch', 'seq')), may hold values from -1.75 to 1.75
- fc2_weight: bfloat16 [8192, 2048], P(('batch', 'seq')), may hold values from -0.09375 to 0.09375
- fc2_bias: bfloat16 [2048], P(('batch', 'seq')), may hold values from -1.75 to 1.75
Outputs:
- outputs: bfloat16 [4, 2048, 2048], P('batch', 'seq')
- input_grad: bfloat16 [4, 2048, 2048], P('batch', 'seq')
- ln1_gain_grad: float32 [2048], P(('batch', 'seq'))
- ln1_bias_grad: float32 [2048], P(('batch', 'seq'))
- q_weight_grad: float32 [2048, 2048], P(('batch', 'seq'))
- q_bias_grad: float32 [2048], P(('batch', 'seq'))
- k_weight_grad: float32 [2048, 2048], P(('batch', 'seq'))
- v_weight_grad: float32 [2048, 2048], P(('batch', 'seq'))
- v_bias_grad: float32 [2048], P(('batch', 'seq'))
- o_weight_grad: float32 [2048, 2048], P(('batch', 'seq'))
- o_bias_grad: float32 [2048], P(('batch', 'seq'))
- ln2_gain_grad: float32 [2048], P(('batch', 'seq'))
- ln2_bias_grad: float32 [2048], P(('batch', 'seq'))
- fc1_weight_grad: float32 [2048, 8192], P(None, ('batch', 'seq'))
- fc1_bias_grad: float32 [8192], P(('batch', 'seq'))
- fc2_weight_grad: float32 [8192, 2048], P(('batch', 'seq'))
- fc2_bias_grad: float32 [2048], P(('batch', 'seq'))
The draws below stay inside these ranges and needn't reach their ends.
Inputs may be any that keep to these rules, and one draw needn't show every extreme that they name: Each group's 7 lengths sum to 2048; in every group the largest is exactly 512. `exit_layers`: along each sequence the exit layer never rises from one position to the next; the first position of every sequence exits above every drawn layer index.
All inputs are finite; a program needn't handle non-finite values.
Results may differ from the reference program's by a relative error of at most 0.013.
Values may be sent and summed in bfloat16 or wider, within the bound.
A program may use at most 448 MiB of HBM per device.

```python
import jax
import jax.numpy as jnp
from jax import lax

D = 2048
HEADS = 32
HEAD_DIM = 64
FF = 8192
LAYERS = 24
SEQS = 7
GROUPS = 4
GROUP_TOK = 2048


def group_lengths(key):
    longest_len = GROUP_TOK // 4
    low_end = max(longest_len // 8, 1)
    pair_key = jax.random.fold_in(key, 11)
    shuffle_key = jax.random.fold_in(key, 12)
    halves = jax.random.randint(pair_key, (GROUPS, 3), low_end, longest_len - low_end + 1).astype(jnp.int32)
    all_rows = jnp.concatenate([jnp.full((GROUPS, 1), longest_len, jnp.int32), halves, longest_len - halves], axis=1)
    scores = jax.random.randint(shuffle_key, (GROUPS, SEQS), 0, 1 << 20).astype(jnp.int32) * SEQS + jnp.arange(SEQS, dtype=jnp.int32)[None, :]
    shuffle = jnp.argsort(scores, axis=1)
    return jnp.take_along_axis(all_rows, shuffle, axis=1).astype(jnp.int32)


def draw_lengths(key, part):
    return group_lengths(key)


def draw_exit_layers(key, part):
    seq_lengths = group_lengths(key)
    key = jax.random.fold_in(key, 3)
    top_key, bottom_key = jax.random.split(key)
    top_layer = jax.random.randint(top_key, (GROUPS, SEQS), LAYERS * 3 // 4, LAYERS + 1).astype(jnp.int32)
    bottoms = jax.random.randint(bottom_key, (GROUPS, SEQS), 1, LAYERS // 3 + 1).astype(jnp.int32)
    longest = (seq_lengths == GROUP_TOK // 4) & (jnp.arange(GROUPS, dtype=jnp.int32)[:, None] == 0)
    top_layer = jnp.where(longest, LAYERS, top_layer)
    bottoms = jnp.where(longest, 1, bottoms)
    seq_ends = jnp.cumsum(seq_lengths, axis=1).astype(jnp.int32)
    places = jnp.arange(GROUP_TOK, dtype=jnp.int32)
    segment = jnp.sum((places[None, :, None] >= seq_ends[:, None, :]).astype(jnp.int32), axis=2)
    starts = seq_ends - seq_lengths
    seq_first = jnp.take_along_axis(starts, segment, axis=1)
    seq_span = jnp.take_along_axis(seq_lengths, segment, axis=1)
    top_tok = jnp.take_along_axis(top_layer, segment, axis=1)
    bottom_tok = jnp.take_along_axis(bottoms, segment, axis=1)
    offset = places[None, :] - seq_first
    return (top_tok - (top_tok - bottom_tok) * offset // jnp.maximum(seq_span - 1, 1)).astype(jnp.int32)


def shard_levels(rng, shape, pieces, low, high):
    level = 1.0
    for axis_at, parts in pieces:
        heights = jax.random.uniform(jax.random.fold_in(jax.random.fold_in(rng, 6), axis_at), (parts,), jnp.float32, low / len(pieces), high / len(pieces))
        level = level * jnp.repeat(jnp.exp(heights), shape[axis_at] // parts).reshape((-1,) + (1,) * (len(shape) - 1 - axis_at))
    return level


def normal_values(key, dims, scale, most, cuts=(), kind=jnp.bfloat16):
    result = jax.random.normal(key, dims, jnp.float32) * scale
    if len(cuts) > 0:
        result = shard_levels(key, dims, cuts, -0.22, 0.18) * result
    return jnp.clip(result, min=-most, max=most).astype(kind)


def setup_inputs(seed: int = 0) -> dict:
    key_of = jax.random.split(jax.random.key(seed), 21)
    return {
        "inputs": normal_values(key_of[0], (GROUPS, GROUP_TOK, D), 1.0, 6.0, ((0, 4), (1, 8))),
        "exit_layers": draw_exit_layers(jax.random.fold_in(key_of[20], 71), 0),
        "lengths": draw_lengths(jax.random.fold_in(key_of[20], 71), 0),
        "layer_index": jax.random.randint(key_of[3], (1,), LAYERS // 3, LAYERS * 2 // 3).astype(jnp.int32),
        "out_grad": normal_values(key_of[4], (GROUPS, GROUP_TOK, D), 1.0, 6.0, ((0, 4), (1, 8))),
        "ln1_gain": jnp.clip(1.0 + 0.1 * jax.random.normal(key_of[5], (D,), jnp.float32), 0.5, 1.5).astype(jnp.bfloat16),
        "ln1_bias": normal_values(key_of[6], (D,), 0.3, 1.75, ((0, 32),)),
        "q_weight": normal_values(key_of[7], (D, D), D ** -0.5, 0.125, ((0, 32),)),
        "q_bias": normal_values(key_of[8], (D,), 0.3, 1.75, ((0, 32),)),
        "k_weight": normal_values(key_of[9], (D, D), D ** -0.5, 0.125, ((0, 32),)),
        "v_weight": normal_values(key_of[10], (D, D), D ** -0.5, 0.125, ((0, 32),)),
        "v_bias": normal_values(key_of[11], (D,), 0.3, 1.75, ((0, 32),)),
        "o_weight": normal_values(key_of[12], (D, D), (D // 16) ** -0.5, 0.5, ((0, 32),)),
        "o_bias": normal_values(key_of[13], (D,), 0.3, 1.75, ((0, 32),)),
        "ln2_gain": jnp.clip(1.0 + 0.1 * jax.random.normal(key_of[14], (D,), jnp.float32), 0.5, 1.5).astype(jnp.bfloat16),
        "ln2_bias": normal_values(key_of[15], (D,), 0.3, 1.75, ((0, 32),)),
        "fc1_weight": normal_values(key_of[16], (D, FF), D ** -0.5, 0.125, ((1, 32),)),
        "fc1_bias": normal_values(key_of[17], (FF,), 0.3, 1.75, ((0, 32),)),
        "fc2_weight": normal_values(key_of[18], (FF, D), (FF // 2) ** -0.5, 0.09375, ((0, 32),)),
        "fc2_bias": normal_values(key_of[19], (D,), 0.3, 1.75, ((0, 32),)),
    }


@jax.custom_vjp
def low(v):
    return lax.optimization_barrier(v.astype(jnp.bfloat16)).astype(jnp.float32)

@jax.custom_vjp
def low_back(v):
    return v

def low_keep(v):
    return (low(v), None)

def low_pass(kept, grad):
    return (grad,)

def back_keep(v):
    return (v, None)

def back_low(kept, grad):
    return (low(grad),)
low.defvjp(low_keep, low_pass)
low_back.defvjp(back_keep, back_low)
highest = lax.Precision.HIGHEST

def matmul(left, right):
    return jnp.dot(left, right, precision=highest, preferred_element_type=jnp.float32)

def layer_norm(values, gain_vec, shift_vec):
    center = lax.optimization_barrier(jnp.mean(values, axis=-1, keepdims=True))
    centered = values - center
    spread = lax.optimization_barrier(jnp.mean(centered * centered, axis=-1, keepdims=True))
    return centered * lax.rsqrt(spread + 1e-05) * gain_vec + shift_vec

def group_layer(tokens_in, params, active, segment):
    ln1_gain, ln1_bias, q_weight, q_bias, k_weight, v_weight, v_bias, o_weight, o_bias, ln2_gain, ln2_bias, fc1_weight, fc1_bias, fc2_weight, fc2_bias = params
    length = tokens_in.shape[0]
    normed = low(layer_norm(tokens_in, ln1_gain, ln1_bias))
    queries = low(low_back(matmul(normed, q_weight) + q_bias))
    keys_all = low(low_back(matmul(normed, k_weight)))
    values = low(low_back(matmul(normed, v_weight) + v_bias))

    def split_heads(matrix):
        return matrix.reshape(length, HEADS, HEAD_DIM).transpose(1, 0, 2)
    places = jnp.arange(length, dtype=jnp.int32)
    allowed = (segment[:, None] == segment[None, :]) & (places[None, :] <= places[:, None])

    def one_head(triple):
        head_query, head_key, head_value = triple
        scores = low_back(matmul(head_query, head_key.T) * HEAD_DIM ** (-0.5))
        scores = jnp.where(allowed, scores, -1e+30)
        row_peak = lax.optimization_barrier(jnp.max(scores, axis=-1, keepdims=True))
        weights_exp = jnp.exp(scores - row_peak)
        prob_rows = weights_exp / lax.optimization_barrier(jnp.sum(weights_exp, axis=-1, keepdims=True))
        return matmul(low(prob_rows), head_value)
    context = lax.map(jax.checkpoint(one_head), (split_heads(queries), split_heads(keys_all), split_heads(values)))
    context = context.transpose(1, 0, 2).reshape(length, HEADS * HEAD_DIM)
    context = low(low_back(context))
    attended = low_back(matmul(context, o_weight) + o_bias)
    middle = tokens_in + active[:, None] * attended
    normed_two = low(layer_norm(middle, ln2_gain, ln2_bias))
    hidden_pre = low_back(matmul(normed_two, fc1_weight) + fc1_bias)
    hidden = low(jax.nn.gelu(hidden_pre, approximate=True))
    branch = low_back(matmul(hidden, fc2_weight) + fc2_bias)
    return middle + active[:, None] * branch

def reference(inputs, exit_layers, lengths, layer_index, out_grad, ln1_gain, ln1_bias, q_weight, q_bias, k_weight, v_weight, v_bias, o_weight, o_bias, ln2_gain, ln2_bias, fc1_weight, fc1_bias, fc2_weight, fc2_bias):
    single = jnp.float32
    params = (ln1_gain.astype(single), ln1_bias.astype(single), q_weight.astype(single), q_bias.astype(single), k_weight.astype(single), v_weight.astype(single), v_bias.astype(single), o_weight.astype(single), o_bias.astype(single), ln2_gain.astype(single), ln2_bias.astype(single), fc1_weight.astype(single), fc1_bias.astype(single), fc2_weight.astype(single), fc2_bias.astype(single))
    group_tok = inputs.shape[1]
    active = (exit_layers > layer_index[0]).astype(single)
    counts = lax.optimization_barrier(jnp.sum(active, axis=1))
    seq_ends = jnp.cumsum(lengths, axis=1)
    places = jnp.arange(group_tok, dtype=jnp.int32)
    segment = lax.optimization_barrier(jnp.sum((places[None, :, None] >= seq_ends[:, None, :]).astype(jnp.int32), axis=2)).astype(jnp.int32)

    def forward(float_inputs, float_params):

        def per_group(packed):
            return group_layer(packed[0], float_params, packed[1], packed[2])
        return lax.map(jax.checkpoint(per_group), (float_inputs, active, segment))
    outputs, pullback = jax.vjp(forward, inputs.astype(single), params)
    cotangent = out_grad.astype(single) * (group_tok / counts)[:, None, None]
    input_grad, grads = pullback(cotangent)
    return (outputs.astype(jnp.bfloat16), input_grad.astype(jnp.bfloat16), grads[0], grads[1], grads[2], grads[3], grads[4], grads[5], grads[6], grads[7], grads[8], grads[9], grads[10], grads[11], grads[12], grads[13], grads[14])
```

```python
from functools import partial

import jax
import jax.numpy as jnp
from jax import lax
from jax.sharding import Mesh
from jax.sharding import PartitionSpec as P

HEAD_DIM = 64
SPANS = 4

bfloat = jnp.bfloat16
single = jnp.float32

PLANE = ("b", "x")
ALL = ("b", "z", "x")


def dot(left, right):
    return jnp.dot(left, right, preferred_element_type=single)


def dot_tn(left, right):
    return lax.dot_general(left, right, (((0,), (0,)), ((), ())), preferred_element_type=single)


def dot_nt(left, right):
    return lax.dot_general(left, right, (((1,), (1,)), ((), ())), preferred_element_type=single)


def layer_norm(values, gain_vec, shift_vec):
    center = jnp.mean(values, axis=-1, keepdims=True)
    centered = values - center
    spread = jnp.mean(centered * centered, axis=-1, keepdims=True)
    return centered * lax.rsqrt(spread + 1e-05) * gain_vec + shift_vec


def column_sums(matrix):
    return jnp.sum(matrix.astype(single), axis=0)


def attention_forward(query, key_two, value_two, allowed):
    scores = jnp.einsum("gqhd,gkhd->ghqk", query, key_two, preferred_element_type=single) * HEAD_DIM ** (-0.5)
    scores = jnp.where(allowed[:, None], scores, -1e30)
    row_peak = jnp.max(scores, axis=-1, keepdims=True)
    weights_exp = jnp.exp(scores - row_peak)
    row_total = jnp.sum(weights_exp, axis=-1, keepdims=True)
    prob_low = (weights_exp / row_total).astype(bfloat)
    context = jnp.einsum("ghqk,gkhd->gqhd", prob_low, value_two, preferred_element_type=single)
    return context.astype(bfloat), row_peak + jnp.log(row_total)


def attention_backward(query, key_two, value_two, grad, logsum, allowed):
    scores = jnp.einsum("gqhd,gkhd->ghqk", query, key_two, preferred_element_type=single) * HEAD_DIM ** (-0.5)
    probs = jnp.exp(jnp.where(allowed[:, None], scores, -1e30) - logsum)
    prob_grad = jnp.einsum("gqhd,gkhd->ghqk", grad, value_two, preferred_element_type=single)
    row_dot = jnp.sum(probs * prob_grad, axis=-1, keepdims=True)
    score_grad = (probs * (prob_grad - row_dot)).astype(bfloat)
    query_grad = jnp.einsum("ghqk,gkhd->gqhd", score_grad, key_two, preferred_element_type=single) * HEAD_DIM ** (-0.5)
    key_grad = jnp.einsum("ghqk,gqhd->gkhd", score_grad, query, preferred_element_type=single) * HEAD_DIM ** (-0.5)
    value_grad = jnp.einsum("ghqk,gqhd->gkhd", probs.astype(bfloat), grad, preferred_element_type=single)
    return query_grad, key_grad, value_grad


def norm_backward(values, out_grad, gain_vec):
    center = jnp.mean(values, axis=-1, keepdims=True)
    centered = values - center
    rs = lax.rsqrt(jnp.mean(centered * centered, axis=-1, keepdims=True) + 1e-05)
    xhat = centered * rs
    g = out_grad * gain_vec
    part = rs * (g - jnp.mean(g, axis=-1, keepdims=True) - xhat * jnp.mean(g * xhat, axis=-1, keepdims=True))
    return part, jnp.sum(out_grad * xhat, axis=0), jnp.sum(out_grad, axis=0)


def on_device(
    inputs,
    exit_layers,
    lengths,
    layer_index,
    out_grad,
    ln1_gain,
    ln1_bias,
    q_weight,
    q_bias,
    k_weight,
    v_weight,
    v_bias,
    o_weight,
    o_bias,
    ln2_gain,
    ln2_bias,
    fc1_weight,
    fc1_bias,
    fc2_weight,
    fc2_bias,
):
    B, Z, X = lax.axis_size("b"), lax.axis_size("z"), lax.axis_size("x")
    R = B * X
    local = inputs[0].astype(single)
    tok, D = local.shape
    span = X * tok
    group_tok = Z * span
    at_z, at_x = lax.axis_index("z"), lax.axis_index("x")
    rank = lax.axis_index("b") * X + at_x
    rows_dev = q_weight.shape[0]
    cols = D // R
    heads = cols // HEAD_DIM
    whole_heads = rows_dev % HEAD_DIM == 0

    group_active = (exit_layers[0] > layer_index[0]).astype(single)
    active_total = jnp.sum(group_active)
    active = lax.dynamic_slice_in_dim(group_active, at_z * span + at_x * tok, tok, 0)[:, None]

    ends = jnp.cumsum(lax.all_gather(lengths[0], "b", axis=0), axis=1)
    places = at_z * span + jnp.arange(span, dtype=jnp.int32)
    starts = jnp.max(jnp.where(ends[:, None, :] <= places[None, :, None], ends[:, None, :], 0), axis=2)
    key_places = (at_z - 1) * span + jnp.arange(2 * span, dtype=jnp.int32)
    allowed = (key_places[None, None, :] >= starts[:, :, None]) & (key_places[None, None, :] <= places[None, :, None])

    small = jnp.stack([ln1_gain, ln1_bias, q_bias, v_bias, o_bias, ln2_gain, ln2_bias, fc2_bias])
    small = lax.all_gather(small, ALL, axis=1, tiled=True).astype(single)
    gain_one, bias_one, bias_q, bias_v, bias_o, gain_two, bias_two, bias_down = [small[i] for i in range(8)]

    def to_ranks(matrix):
        lead = matrix.shape[:-1]
        if whole_heads:
            matrix = matrix.reshape(*lead, B, Z, X, rows_dev)
            k = len(lead)
            return matrix.transpose(k, k + 2, *range(k), k + 1, k + 3).reshape(R, *lead, cols)
        return jnp.moveaxis(matrix.reshape(*lead, R, cols), -2, 0)

    def from_ranks(parts):
        if whole_heads:
            parts = parts.reshape(B, X, -1, Z, rows_dev)
            return parts.transpose(2, 0, 3, 1, 4).reshape(-1, D)
        return parts.transpose(1, 0, 2).reshape(-1, D)

    def mine(vector):
        return lax.dynamic_index_in_dim(to_ranks(vector), rank, 0, keepdims=False)

    qkv_parts = jnp.concatenate([to_ranks(q_weight), to_ranks(k_weight), to_ranks(v_weight)], axis=2)
    qkv_mine = lax.all_to_all(qkv_parts, PLANE, split_axis=0, concat_axis=0, tiled=True)
    weight_qkv = lax.all_gather(qkv_mine, "z", axis=0)
    weight_qkv = weight_qkv.reshape(Z, B, X, rows_dev, 3 * cols).transpose(1, 0, 2, 3, 4).reshape(D, 3 * cols)
    bias_qkv = jnp.concatenate([mine(bias_q), jnp.zeros((cols,), single), mine(bias_v)])
    if whole_heads:
        weight_o = lax.all_gather(o_weight, "z", axis=0, tiled=True)
    else:
        weight_o = lax.dynamic_slice_in_dim(lax.all_gather(o_weight, ALL, axis=0, tiled=True), rank * cols, cols, 0)
    weight_up = lax.all_gather(fc1_weight, "z", axis=1, tiled=True)
    weight_down = lax.all_gather(fc2_weight, "z", axis=0, tiled=True)
    bias_up = lax.all_gather(fc1_bias, "z", axis=0, tiled=True).astype(single)

    normed_low = layer_norm(local, gain_one, bias_one).astype(bfloat)
    normed_all = lax.all_gather(normed_low, PLANE, axis=0, tiled=True)
    qkv = (dot(normed_all, weight_qkv) + bias_qkv).astype(bfloat)
    query = qkv[:, :cols].reshape(B, span, heads, HEAD_DIM)
    key_value = qkv[:, cols:]
    up = [(i, i + 1) for i in range(Z - 1)]
    down = [(i + 1, i) for i in range(Z - 1)]
    before = lax.ppermute(key_value, "z", up)
    both = jnp.concatenate([before.reshape(B, span, 2 * cols), key_value.reshape(B, span, 2 * cols)], axis=1)
    key_two = both[..., :cols].reshape(B, 2 * span, heads, HEAD_DIM)
    value_two = both[..., cols:].reshape(B, 2 * span, heads, HEAD_DIM)
    context, logsum = attention_forward(query, key_two, value_two, allowed)
    context = context.reshape(B * span, cols)

    def reduce_plane(partial_sums):
        return lax.psum_scatter(partial_sums.astype(bfloat), PLANE, scatter_dimension=0, tiled=True).astype(single)

    attended = reduce_plane(dot(context, weight_o)) + bias_o
    middle = local + active * attended
    normed_two = layer_norm(middle, gain_two, bias_two).astype(bfloat)
    cotangent = out_grad[0].astype(single) * (group_tok / active_total)
    branch_grad = (active * cotangent).astype(bfloat)
    down_b_grad = column_sums(branch_grad)
    branch_all = lax.all_gather(branch_grad, PLANE, axis=0, tiled=True)
    two_all = lax.all_gather(normed_two, PLANE, axis=0, tiled=True)
    hidden_pre = dot(two_all, weight_up) + bias_up
    gelu_value, gelu_pull = jax.vjp(partial(jax.nn.gelu, approximate=True), hidden_pre)
    hidden = gelu_value.astype(bfloat)
    hidden_grad = dot_nt(branch_all, weight_down)
    pre_grad = gelu_pull(hidden_grad)[0].astype(bfloat)
    normed_two_grad = reduce_plane(dot_nt(pre_grad, weight_up))
    branch = reduce_plane(dot(hidden, weight_down)) + bias_down
    outputs = middle + active * branch
    down_w_grad = dot_tn(hidden, branch_all)
    up_w_grad = dot_tn(two_all, pre_grad)
    up_b_grad = column_sums(pre_grad)
    down_w_shard = lax.psum_scatter(down_w_grad.astype(bfloat), "z", scatter_dimension=0, tiled=True).astype(single)
    up_w_shard = lax.psum_scatter(up_w_grad.astype(bfloat), "z", scatter_dimension=1, tiled=True).astype(single)
    up_b_shard = lax.psum_scatter(up_b_grad, "z", scatter_dimension=0, tiled=True)

    middle_part, gain_two_grad, bias_two_grad = norm_backward(middle, normed_two_grad, gain_two)
    middle_grad = cotangent + middle_part
    attended_grad = (active * middle_grad).astype(bfloat)
    out_b_grad = column_sums(attended_grad)
    attended_all = lax.all_gather(attended_grad, PLANE, axis=0, tiled=True)
    context_grad = dot_nt(attended_all, weight_o).astype(bfloat)
    out_w_grad = dot_tn(context, attended_all)
    query_grad, key_grad, value_grad = attention_backward(
        query, key_two, value_two, context_grad.reshape(B, span, heads, HEAD_DIM), logsum, allowed
    )
    pair = jnp.concatenate(
        [key_grad.reshape(B, 2 * span, cols), value_grad.reshape(B, 2 * span, cols)], axis=2
    )
    after = lax.ppermute(pair[:, :span].astype(bfloat), "z", down).astype(single)
    pair_grad = (pair[:, span:] + after).astype(bfloat).reshape(B * span, 2 * cols)
    qkv_grad = jnp.concatenate([query_grad.astype(bfloat).reshape(B * span, cols), pair_grad], axis=1)
    normed_grad = reduce_plane(dot_nt(qkv_grad, weight_qkv))
    qkv_w_grad = dot_tn(normed_all, qkv_grad)
    qkv_b_grad = column_sums(qkv_grad)
    input_part, gain_one_grad, bias_one_grad = norm_backward(local, normed_grad, gain_one)
    input_grad = middle_grad + input_part

    qkv_w_grad = qkv_w_grad.astype(bfloat).reshape(B, Z, X, rows_dev, 3 * cols)
    qkv_w_grad = lax.psum_scatter(qkv_w_grad.transpose(1, 0, 2, 3, 4), "z", scatter_dimension=0, tiled=True)
    qkv_w_grad = lax.all_to_all(qkv_w_grad.reshape(R, rows_dev, 3 * cols), PLANE, split_axis=0, concat_axis=0, tiled=True)
    qkv_w_grad = qkv_w_grad.astype(single)
    q_w_shard, k_w_shard, v_w_shard = [from_ranks(qkv_w_grad[..., i * cols : (i + 1) * cols]) for i in range(3)]
    if whole_heads:
        out_w_shard = lax.psum_scatter(out_w_grad.astype(bfloat), "z", scatter_dimension=0, tiled=True).astype(single)
        q_b_shard = lax.psum_scatter(qkv_b_grad[:cols], "z", scatter_dimension=0, tiled=True)
        v_b_shard = lax.psum_scatter(qkv_b_grad[2 * cols :], "z", scatter_dimension=0, tiled=True)
    else:

        def placed(rows):
            full = jnp.zeros((D,) + rows.shape[1:], rows.dtype)
            full = lax.dynamic_update_slice_in_dim(full, rows, rank * cols, 0)
            return lax.psum_scatter(full, ALL, scatter_dimension=0, tiled=True).astype(single)

        out_w_shard = placed(out_w_grad.astype(bfloat))
        q_b_shard = placed(qkv_b_grad[:cols])
        v_b_shard = placed(qkv_b_grad[2 * cols :])
    sums = jnp.stack([gain_one_grad, bias_one_grad, out_b_grad, gain_two_grad, bias_two_grad, down_b_grad])
    sums = lax.psum_scatter(sums, ALL, scatter_dimension=1, tiled=True)
    return (
        outputs.astype(bfloat)[None],
        input_grad.astype(bfloat)[None],
        sums[0],
        sums[1],
        q_w_shard,
        q_b_shard,
        k_w_shard,
        v_w_shard,
        v_b_shard,
        out_w_shard,
        sums[2],
        sums[3],
        sums[4],
        up_w_shard,
        up_b_shard,
        down_w_shard,
        sums[5],
    )


def solution(mesh):
    groups, parts = mesh.shape["batch"], mesh.shape["seq"]
    inner = Mesh(mesh.devices.reshape(groups, SPANS, parts // SPANS), ("b", "z", "x"))
    token = P("b", ("z", "x"), None)
    vector = P(ALL)
    rows = P(ALL, None)
    columns = P(None, ALL)
    return jax.shard_map(
        on_device,
        mesh=inner,
        in_specs=(
            token,
            P("b", None),
            P("b", None),
            P(),
            token,
            vector,
            vector,
            rows,
            vector,
            rows,
            rows,
            vector,
            rows,
            vector,
            vector,
            vector,
            columns,
            vector,
            rows,
            vector,
        ),
        out_specs=(
            token,
            token,
            vector,
            vector,
            rows,
            vector,
            rows,
            rows,
            vector,
            rows,
            vector,
            vector,
            vector,
            columns,
            vector,
            rows,
            vector,
        ),
        check_vma=False,
    )
```

```python
import functools
from functools import partial

import jax
import jax.numpy as jnp
from jax import lax
from jax.experimental import pallas as pl
from jax.experimental.pallas import tpu as pltpu
from jax.sharding import Mesh
from jax.sharding import PartitionSpec as P

HEAD_DIM = 64
SPANS = 4

bfloat = jnp.bfloat16
single = jnp.float32

PLANE = ("b", "x")
ALL = ("b", "z", "x")
MESH = pl.DeviceIdType.MESH
TILE = 512

def plane_place():
    b, z, x = lax.axis_index("b"), lax.axis_index("z"), lax.axis_index("x")
    sib_b = b + 1 - 2 * lax.rem(b, 2)
    far_b = lax.rem(b + 2, 4)
    far_sib_b = lax.rem(sib_b + 2, 4)
    ids = {"s": (sib_b, z, x), "x": (b, z, 1 - x), "y": (far_b, z, x)}
    ranks = {
        "o": b * 2 + x,
        "s": sib_b * 2 + x,
        "x": b * 2 + 1 - x,
        "xs": sib_b * 2 + 1 - x,
        "y": far_b * 2 + x,
        "ys": far_sib_b * 2 + x,
        "d": far_b * 2 + 1 - x,
        "ds": far_sib_b * 2 + 1 - x,
    }
    return ids, ranks

def greet(ids):
    barrier = pltpu.get_barrier_semaphore()
    for device in ids.values():
        pl.semaphore_signal(barrier, inc=1, device_id=device, device_id_type=MESH)
    pl.semaphore_wait(barrier, len(ids))

def tiles(lo, hi, body):
    def step(i, _):
        body(pl.ds(pl.multiple_of(i * TILE, TILE), TILE))
        return 0
    lax.fori_loop(lo // TILE, hi // TILE, step, 0)

def gather_kernel(body_of, n_in, n_out, x_ref, *refs):
    ins = refs[:n_in]; all_ref = refs[n_in]; outs = refs[n_in + 1 : n_in + 1 + n_out]
    held, send, recv, keep = refs[n_in + 1 + n_out :]
    ids, at = plane_place()
    half = x_ref.shape[0] // 2
    parts = (pl.ds(0, half), pl.ds(half, half))
    greet(ids)
    count = [0]
    started = []
    def ship(src, dst, to):
        n = count[0]; count[0] += 1
        c = pltpu.make_async_remote_copy(src_ref=src, dst_ref=dst, send_sem=send.at[n], recv_sem=recv.at[n], device_id=ids[to], device_id_type=MESH)
        c.start(); started.append(c)
        return c
    own = at["o"]
    x0 = ship(x_ref.at[parts[0]], held.at[own, parts[0]], "x")
    y1 = ship(x_ref.at[parts[1]], held.at[own, parts[1]], "y")
    x1 = ship(x_ref.at[parts[1]], held.at[own, parts[1]], "x")
    y0 = ship(x_ref.at[parts[0]], held.at[own, parts[0]], "y")
    s0 = ship(x_ref, held.at[own], "s")
    kept = []
    def done(rank, src):
        c = pltpu.make_async_copy(src, all_ref.at[rank], keep.at[len(kept)])
        c.start(); kept.append(c)
        if body_of is not None:
            body_of(rank, src, ins, outs)
    done(own, x_ref)
    s0.wait_recv()
    done(at["s"], held.at[at["s"]])
    x0.wait_recv()
    ry = ship(held.at[at["x"], parts[0]], held.at[at["x"], parts[0]], "y")
    y1.wait_recv()
    rx = ship(held.at[at["y"], parts[1]], held.at[at["y"], parts[1]], "x")
    x1.wait_recv()
    sx = ship(held.at[at["x"]], held.at[at["x"]], "s")
    y0.wait_recv()
    sy = ship(held.at[at["y"]], held.at[at["y"]], "s")
    done(at["x"], held.at[at["x"]])
    done(at["y"], held.at[at["y"]])
    sx.wait_recv()
    done(at["xs"], held.at[at["xs"]])
    sy.wait_recv()
    done(at["ys"], held.at[at["ys"]])
    ry.wait_recv(); rx.wait_recv()
    sd = ship(held.at[at["d"]], held.at[at["d"]], "s")
    done(at["d"], held.at[at["d"]])
    sd.wait_recv()
    done(at["ds"], held.at[at["ds"]])
    for c in started: c.wait_send()
    for c in kept: c.wait()

def vmem(n): return [pl.BlockSpec(memory_space=pltpu.VMEM)] * n

def plane_gather(x, ins, out_types, body_of, cid, name, ranks=8):
    tok, D = x.shape
    res = pl.pallas_call(
        functools.partial(gather_kernel, body_of, len(ins), len(out_types)),
        out_shape=[jax.ShapeDtypeStruct((ranks, tok, D), x.dtype), *out_types],
        in_specs=vmem(1 + len(ins)),
        out_specs=[pl.BlockSpec(memory_space=pl.ANY)] + vmem(len(out_types)),
        scratch_shapes=[pltpu.VMEM((ranks, tok, D), x.dtype), pltpu.SemaphoreType.DMA((10,)), pltpu.SemaphoreType.DMA((10,)), pltpu.SemaphoreType.DMA((8,))],
        compiler_params=pltpu.CompilerParams(collective_id=cid, has_side_effects=True, vmem_limit_bytes=60 << 20),
        name=name,
    )(x, *ins)
    return res[0].reshape(ranks * tok, D), *res[1:]

def gather_dot(x, w, bias, out_dtype, turned, cid, name):
    ranks, tok, D = 8, *x.shape
    N = w.shape[0] if turned else w.shape[1]
    tile = min(N, 512) if N % 512 == 0 else 256
    def body(rank, src, ins, outs):
        w_ref, b_ref = ins
        def step(i, _):
            cols = pl.ds(pl.multiple_of(i * tile, tile), tile)
            if turned:
                y = lax.dot_general(src[...], w_ref[cols, :], (((1,), (1,)), ((), ())), preferred_element_type=single)
            else:
                y = jnp.dot(src[...], w_ref[:, cols], preferred_element_type=single)
            outs[0][rank, :, cols] = (y + b_ref[:, cols]).astype(out_dtype)
            return 0
        lax.fori_loop(0, N // tile, step, 0)
    all_, y = plane_gather(x, (w, bias), [jax.ShapeDtypeStruct((ranks, tok, N), out_dtype)], body, cid, name)
    return all_, y.reshape(ranks * tok, N)

def reduce_kernel(turned, a_ref, w_ref, out_ref, sib_out, sib_in, stage, landed, send, recv):
    ids, at = plane_place()
    ranks, tok, _ = a_ref.shape
    D = out_ref.shape[1]
    mid = D // 2
    greet(ids)
    count = [0]; started = []
    def ship(src, dst, to):
        n = count[0]; count[0] += 1
        c = pltpu.make_async_remote_copy(src_ref=src, dst_ref=dst, send_sem=send.at[n], recv_sem=recv.at[n], device_id=ids[to], device_id_type=MESH)
        c.start(); started.append(c)
        return c
    def term(rank, cols):
        if turned:
            return lax.dot_general(a_ref[rank], w_ref[cols, :], (((1,), (1,)), ((), ())), preferred_element_type=single)
        return jnp.dot(a_ref[rank], w_ref[:, cols], preferred_element_type=single)
    order = ("d", "x", "y", "o")
    twin = {"d": "ds", "x": "xs", "y": "ys", "o": "s"}
    sib = []
    for j, d in enumerate(order):
        def fill(cols, j=j, d=d):
            sib_out[j, :, cols] = term(at[twin[d]], cols).astype(bfloat)
        tiles(0, D, fill)
        sib.append(ship(sib_out.at[j], sib_in.at[j], "s"))
    def pair(j, cols):
        return term(at[order[j]], cols) + sib_in[j, :, cols].astype(single)
    def local(h, cols):
        return pl.ds(pl.multiple_of(cols.start - h * mid, TILE), TILE)
    def put(j, h, extra=None):
        def fill(cols):
            value = pair(j, cols)
            if extra is not None:
                value = value + landed[extra, :, local(h, cols)].astype(single)
            stage[j, h, :, local(h, cols)] = value.astype(bfloat)
        tiles(h * mid, (h + 1) * mid, fill)
    sib[0].wait_recv()
    put(0, 0)
    d_a = ship(stage.at[0, 0], landed.at[0], "x")
    put(0, 1)
    d_b = ship(stage.at[0, 1], landed.at[1], "y")
    sib[1].wait_recv()
    put(1, 0)
    x_a = ship(stage.at[1, 0], landed.at[2], "x")
    sib[2].wait_recv()
    put(2, 1)
    y_b = ship(stage.at[2, 1], landed.at[3], "y")
    sib[3].wait_recv()
    def first(cols):
        out_ref[:, cols] = pair(3, cols)
    tiles(0, D, first)
    d_b.wait_recv()
    put(1, 1, extra=1)
    x_b = ship(stage.at[1, 1], landed.at[5], "x")
    d_a.wait_recv()
    put(2, 0, extra=0)
    y_a = ship(stage.at[2, 0], landed.at[4], "y")
    x_a.wait_recv(); y_b.wait_recv(); x_b.wait_recv(); y_a.wait_recv()
    for h, (n, m) in enumerate(((2, 4), (3, 5))):
        def add(cols, h=h, n=n, m=m):
            c = local(h, cols)
            out_ref[:, cols] = out_ref[:, cols] + landed[n, :, c].astype(single) + landed[m, :, c].astype(single)
        tiles(h * mid, (h + 1) * mid, add)
    for c in started: c.wait_send()

def dot_reduce(a, w, turned, cid, name):
    ranks = 8
    D = w.shape[0] if turned else w.shape[1]
    tok = a.shape[0] // ranks
    return pl.pallas_call(
        functools.partial(reduce_kernel, turned),
        out_shape=jax.ShapeDtypeStruct((tok, D), single),
        in_specs=vmem(2), out_specs=vmem(1)[0],
        scratch_shapes=[pltpu.VMEM((4, tok, D), bfloat), pltpu.VMEM((4, tok, D), bfloat), pltpu.VMEM((3, 2, tok, D // 2), bfloat), pltpu.VMEM((6, tok, D // 2), bfloat),
            pltpu.SemaphoreType.DMA((10,)), pltpu.SemaphoreType.DMA((10,))],
        compiler_params=pltpu.CompilerParams(collective_id=cid, has_side_effects=True, vmem_limit_bytes=60 << 20),
        name=name,
    )(a.reshape(ranks, tok, -1), w)


def dot(left, right):
    return jnp.dot(left, right, preferred_element_type=single)


def dot_tn(left, right):
    return lax.dot_general(left, right, (((0,), (0,)), ((), ())), preferred_element_type=single)


def dot_nt(left, right):
    return lax.dot_general(left, right, (((1,), (1,)), ((), ())), preferred_element_type=single)


def layer_norm(values, gain_vec, shift_vec):
    center = jnp.mean(values, axis=-1, keepdims=True)
    centered = values - center
    spread = jnp.mean(centered * centered, axis=-1, keepdims=True)
    return centered * lax.rsqrt(spread + 1e-05) * gain_vec + shift_vec


def column_sums(matrix):
    return jnp.sum(matrix.astype(single), axis=0)


def attention_forward(query, key_two, value_two, allowed):
    scores = jnp.einsum("gqhd,gkhd->ghqk", query, key_two, preferred_element_type=single) * HEAD_DIM ** (-0.5)
    scores = jnp.where(allowed[:, None], scores, -1e30)
    row_peak = jnp.max(scores, axis=-1, keepdims=True)
    weights_exp = jnp.exp(scores - row_peak)
    row_total = jnp.sum(weights_exp, axis=-1, keepdims=True)
    prob_low = (weights_exp / row_total).astype(bfloat)
    context = jnp.einsum("ghqk,gkhd->gqhd", prob_low, value_two, preferred_element_type=single)
    return context.astype(bfloat), row_peak + jnp.log(row_total)


def attention_backward(query, key_two, value_two, grad, logsum, allowed):
    scores = jnp.einsum("gqhd,gkhd->ghqk", query, key_two, preferred_element_type=single) * HEAD_DIM ** (-0.5)
    probs = jnp.exp(jnp.where(allowed[:, None], scores, -1e30) - logsum)
    prob_grad = jnp.einsum("gqhd,gkhd->ghqk", grad, value_two, preferred_element_type=single)
    row_dot = jnp.sum(probs * prob_grad, axis=-1, keepdims=True)
    score_grad = (probs * (prob_grad - row_dot)).astype(bfloat)
    query_grad = jnp.einsum("ghqk,gkhd->gqhd", score_grad, key_two, preferred_element_type=single) * HEAD_DIM ** (-0.5)
    key_grad = jnp.einsum("ghqk,gqhd->gkhd", score_grad, query, preferred_element_type=single) * HEAD_DIM ** (-0.5)
    value_grad = jnp.einsum("ghqk,gqhd->gkhd", probs.astype(bfloat), grad, preferred_element_type=single)
    return query_grad, key_grad, value_grad


def norm_backward(values, out_grad, gain_vec):
    center = jnp.mean(values, axis=-1, keepdims=True)
    centered = values - center
    rs = lax.rsqrt(jnp.mean(centered * centered, axis=-1, keepdims=True) + 1e-05)
    xhat = centered * rs
    g = out_grad * gain_vec
    part = rs * (g - jnp.mean(g, axis=-1, keepdims=True) - xhat * jnp.mean(g * xhat, axis=-1, keepdims=True))
    return part, jnp.sum(out_grad * xhat, axis=0), jnp.sum(out_grad, axis=0)


def on_device(
    inputs,
    exit_layers,
    lengths,
    layer_index,
    out_grad,
    ln1_gain,
    ln1_bias,
    q_weight,
    q_bias,
    k_weight,
    v_weight,
    v_bias,
    o_weight,
    o_bias,
    ln2_gain,
    ln2_bias,
    fc1_weight,
    fc1_bias,
    fc2_weight,
    fc2_bias,
):
    B, Z, X = lax.axis_size("b"), lax.axis_size("z"), lax.axis_size("x")
    R = B * X
    local = inputs[0].astype(single)
    tok, D = local.shape
    span = X * tok
    group_tok = Z * span
    at_z, at_x = lax.axis_index("z"), lax.axis_index("x")
    rank = lax.axis_index("b") * X + at_x
    rows_dev = q_weight.shape[0]
    cols = D // R
    heads = cols // HEAD_DIM
    whole_heads = rows_dev % HEAD_DIM == 0

    group_active = (exit_layers[0] > layer_index[0]).astype(single)
    active_total = jnp.sum(group_active)
    active = lax.dynamic_slice_in_dim(group_active, at_z * span + at_x * tok, tok, 0)[:, None]

    count = lengths.shape[1]
    upto = jnp.arange(count)[:, None] <= jnp.arange(count)[None, :]
    ends = jnp.sum(jnp.where(upto, lax.all_gather(lengths[0], "b", axis=0)[:, :, None], 0), axis=1)
    places = at_z * span + jnp.arange(span, dtype=jnp.int32)
    starts = jnp.max(jnp.where(ends[:, None, :] <= places[None, :, None], ends[:, None, :], 0), axis=2)
    key_places = (at_z - 1) * span + jnp.arange(2 * span, dtype=jnp.int32)
    allowed = (key_places[None, None, :] >= starts[:, :, None]) & (key_places[None, None, :] <= places[None, :, None])

    small = jnp.stack([ln1_gain, ln1_bias, q_bias, v_bias, o_bias, ln2_gain, ln2_bias, fc2_bias])
    small = lax.all_gather(small, ALL, axis=1, tiled=True).astype(single)
    gain_one, bias_one, bias_q, bias_v, bias_o, gain_two, bias_two, bias_down = [small[i] for i in range(8)]

    def to_ranks(matrix):
        lead = matrix.shape[:-1]
        if whole_heads:
            matrix = matrix.reshape(*lead, B, Z, X, rows_dev)
            k = len(lead)
            return matrix.transpose(k, k + 2, *range(k), k + 1, k + 3).reshape(R, *lead, cols)
        return jnp.moveaxis(matrix.reshape(*lead, R, cols), -2, 0)

    def from_ranks(parts):
        if whole_heads:
            parts = parts.reshape(B, X, -1, Z, rows_dev)
            return parts.transpose(2, 0, 3, 1, 4).reshape(-1, D)
        return parts.transpose(1, 0, 2).reshape(-1, D)

    def mine(vector):
        return lax.dynamic_index_in_dim(to_ranks(vector), rank, 0, keepdims=False)

    qkv_parts = jnp.concatenate([to_ranks(q_weight), to_ranks(k_weight), to_ranks(v_weight)], axis=2)
    qkv_mine = lax.all_to_all(qkv_parts, PLANE, split_axis=0, concat_axis=0, tiled=True)
    weight_qkv = lax.all_gather(qkv_mine, "z", axis=0)
    weight_qkv = weight_qkv.reshape(Z, B, X, rows_dev, 3 * cols).transpose(1, 0, 2, 3, 4).reshape(D, 3 * cols)
    bias_qkv = jnp.concatenate([mine(bias_q), jnp.zeros((cols,), single), mine(bias_v)])
    if whole_heads:
        weight_o = lax.all_gather(o_weight, "z", axis=0, tiled=True)
    else:
        weight_o = lax.dynamic_slice_in_dim(lax.all_gather(o_weight, ALL, axis=0, tiled=True), rank * cols, cols, 0)
    weight_up = lax.all_gather(fc1_weight, "z", axis=1, tiled=True)
    weight_down = lax.all_gather(fc2_weight, "z", axis=0, tiled=True)
    bias_up = lax.all_gather(fc1_bias, "z", axis=0, tiled=True).astype(single)

    normed_low = layer_norm(local, gain_one, bias_one).astype(bfloat)
    fast = (B, X) == (4, 2)

    def gather_plane(rows, cid, name):
        if fast:
            return plane_gather(rows, (), [], None, cid, name)[0]
        return lax.all_gather(rows, PLANE, axis=0, tiled=True)

    def gather_plane_dot(rows, weight, shift, out_type, turned, cid, name):
        if fast:
            return gather_dot(rows, weight, shift, out_type, turned, cid, name)
        rows = lax.all_gather(rows, PLANE, axis=0, tiled=True)
        return rows, ((dot_nt if turned else dot)(rows, weight) + shift).astype(out_type)

    def reduce_plane(left, weight, turned, cid, name):
        if fast:
            return dot_reduce(left, weight, turned, cid, name)
        terms = (dot_nt if turned else dot)(left, weight).astype(bfloat)
        return lax.psum_scatter(terms, PLANE, scatter_dimension=0, tiled=True).astype(single)

    normed_all = gather_plane(normed_low, 0, "gather_normed")
    qkv = (dot(normed_all, weight_qkv) + bias_qkv).astype(bfloat)
    query = qkv[:, :cols].reshape(B, span, heads, HEAD_DIM)
    key_value = qkv[:, cols:]
    up = [(i, i + 1) for i in range(Z - 1)]
    down = [(i + 1, i) for i in range(Z - 1)]
    before = lax.ppermute(key_value, "z", up)
    both = jnp.concatenate([before.reshape(B, span, 2 * cols), key_value.reshape(B, span, 2 * cols)], axis=1)
    key_two = both[..., :cols].reshape(B, 2 * span, heads, HEAD_DIM)
    value_two = both[..., cols:].reshape(B, 2 * span, heads, HEAD_DIM)
    context, logsum = attention_forward(query, key_two, value_two, allowed)
    context = context.reshape(B * span, cols)

    attended = reduce_plane(context, weight_o, False, 1, "attended") + bias_o
    middle = local + active * attended
    normed_two = layer_norm(middle, gain_two, bias_two).astype(bfloat)
    cotangent = out_grad[0].astype(single) * (group_tok / active_total)
    branch_grad = (active * cotangent).astype(bfloat)
    down_b_grad = column_sums(branch_grad)
    branch_all = lax.all_gather(branch_grad, PLANE, axis=0, tiled=True)
    two_all, hidden_pre = gather_plane_dot(normed_two, weight_up, bias_up[None], single, False, 2, "up")
    gelu_value, gelu_pull = jax.vjp(partial(jax.nn.gelu, approximate=True), hidden_pre)
    hidden = gelu_value.astype(bfloat)
    hidden_grad = dot_nt(branch_all, weight_down)
    pre_grad = gelu_pull(hidden_grad)[0].astype(bfloat)
    normed_two_grad = reduce_plane(pre_grad, weight_up, True, 3, "up_grad")
    branch = reduce_plane(hidden, weight_down, False, 4, "down") + bias_down
    outputs = middle + active * branch
    down_w_grad = dot_tn(hidden, branch_all)
    up_w_grad = dot_tn(two_all, pre_grad)
    up_b_grad = column_sums(pre_grad)
    down_w_shard = lax.psum_scatter(down_w_grad.astype(bfloat), "z", scatter_dimension=0, tiled=True).astype(single)
    up_w_shard = lax.psum_scatter(up_w_grad.astype(bfloat), "z", scatter_dimension=1, tiled=True).astype(single)

    middle_part, gain_two_grad, bias_two_grad = norm_backward(middle, normed_two_grad, gain_two)
    middle_grad = cotangent + middle_part
    attended_grad = (active * middle_grad).astype(bfloat)
    out_b_grad = column_sums(attended_grad)
    attended_all, context_grad = gather_plane_dot(
        attended_grad, weight_o, jnp.zeros((1, cols), single), bfloat, True, 5, "attended_grad"
    )
    out_w_grad = dot_tn(context, attended_all)
    query_grad, key_grad, value_grad = attention_backward(
        query, key_two, value_two, context_grad.reshape(B, span, heads, HEAD_DIM), logsum, allowed
    )
    pair = jnp.concatenate(
        [key_grad.reshape(B, 2 * span, cols), value_grad.reshape(B, 2 * span, cols)], axis=2
    )
    after = lax.ppermute(pair[:, :span].astype(bfloat), "z", down).astype(single)
    pair_grad = (pair[:, span:] + after).astype(bfloat).reshape(B * span, 2 * cols)
    qkv_grad = jnp.concatenate([query_grad.astype(bfloat).reshape(B * span, cols), pair_grad], axis=1)
    normed_grad = reduce_plane(qkv_grad, weight_qkv, True, 6, "qkv_grad")
    qkv_w_grad = dot_tn(normed_all, qkv_grad)
    qkv_b_grad = column_sums(qkv_grad)
    input_part, gain_one_grad, bias_one_grad = norm_backward(local, normed_grad, gain_one)
    input_grad = middle_grad + input_part

    def sum_to_owners(vectors, axes, parts):
        split = jnp.concatenate([v.reshape(parts, -1) for v in vectors], axis=1)
        summed = jnp.sum(lax.all_to_all(split, axes, split_axis=0, concat_axis=0, tiled=True), axis=0)
        widths = [v.shape[0] // parts for v in vectors]
        return [summed[sum(widths[:i]) : sum(widths[: i + 1])] for i in range(len(widths))]

    qkv_w_grad = qkv_w_grad.astype(bfloat).reshape(B, Z, X, rows_dev, 3 * cols)
    qkv_w_grad = qkv_w_grad.transpose(1, 0, 2, 3, 4).reshape(D, 3 * cols)
    qkv_w_grad = lax.psum_scatter(qkv_w_grad, "z", scatter_dimension=0, tiled=True)
    qkv_w_grad = lax.all_to_all(qkv_w_grad.reshape(R, rows_dev, 3 * cols), PLANE, split_axis=0, concat_axis=0, tiled=True)
    qkv_w_grad = qkv_w_grad.astype(single)
    q_w_shard, k_w_shard, v_w_shard = [from_ranks(qkv_w_grad[..., i * cols : (i + 1) * cols]) for i in range(3)]
    if whole_heads:
        out_w_shard = lax.psum_scatter(out_w_grad.astype(bfloat), "z", scatter_dimension=0, tiled=True).astype(single)
        q_b_shard, v_b_shard, up_b_shard = sum_to_owners([qkv_b_grad[:cols], qkv_b_grad[2 * cols :], up_b_grad], "z", Z)
    else:

        def placed(rows):
            full = jnp.zeros((D,) + rows.shape[1:], rows.dtype)
            full = lax.dynamic_update_slice_in_dim(full, rows, rank * cols, 0)
            return lax.psum_scatter(full, ALL, scatter_dimension=0, tiled=True).astype(single)

        out_w_shard = placed(out_w_grad.astype(bfloat))
        q_b_shard = placed(qkv_b_grad[:cols])
        v_b_shard = placed(qkv_b_grad[2 * cols :])
        [up_b_shard] = sum_to_owners([up_b_grad], "z", Z)
    sums = sum_to_owners(
        [gain_one_grad, bias_one_grad, out_b_grad, gain_two_grad, bias_two_grad, down_b_grad], ALL, R * Z
    )
    return (
        outputs.astype(bfloat)[None],
        input_grad.astype(bfloat)[None],
        sums[0],
        sums[1],
        q_w_shard,
        q_b_shard,
        k_w_shard,
        v_w_shard,
        v_b_shard,
        out_w_shard,
        sums[2],
        sums[3],
        sums[4],
        up_w_shard,
        up_b_shard,
        down_w_shard,
        sums[5],
    )


def solution(mesh):
    groups, parts = mesh.shape["batch"], mesh.shape["seq"]
    inner = Mesh(mesh.devices.reshape(groups, SPANS, parts // SPANS), ("b", "z", "x"))
    token = P("b", ("z", "x"), None)
    vector = P(ALL)
    rows = P(ALL, None)
    columns = P(None, ALL)
    return jax.shard_map(
        on_device,
        mesh=inner,
        in_specs=(
            token,
            P("b", None),
            P("b", None),
            P(),
            token,
            vector,
            vector,
            rows,
            vector,
            rows,
            rows,
            vector,
            rows,
            vector,
            vector,
            vector,
            columns,
            vector,
            rows,
            vector,
        ),
        out_specs=(
            token,
            token,
            vector,
            vector,
            rows,
            vector,
            rows,
            rows,
            vector,
            rows,
            vector,
            vector,
            vector,
            columns,
            vector,
            rows,
            vector,
        ),
        check_vma=False,
    )
```

```python
import functools
from functools import partial

import jax
import jax.numpy as jnp
from jax import lax
from jax.experimental import pallas as pl
from jax.experimental.pallas import tpu as pltpu
from jax.sharding import Mesh
from jax.sharding import PartitionSpec as P

HEAD_DIM = 64
SPANS = 4

bfloat = jnp.bfloat16
single = jnp.float32

PLANE = ("b", "x")
ALL = ("b", "z", "x")
MESH = pl.DeviceIdType.MESH
TILE = 512

def plane_place():
    b, z, x = lax.axis_index("b"), lax.axis_index("z"), lax.axis_index("x")
    sib_b = b + 1 - 2 * lax.rem(b, 2)
    far_b = lax.rem(b + 2, 4)
    far_sib_b = lax.rem(sib_b + 2, 4)
    ids = {"s": (sib_b, z, x), "x": (b, z, 1 - x), "y": (far_b, z, x)}
    ranks = {
        "o": b * 2 + x,
        "s": sib_b * 2 + x,
        "x": b * 2 + 1 - x,
        "xs": sib_b * 2 + 1 - x,
        "y": far_b * 2 + x,
        "ys": far_sib_b * 2 + x,
        "d": far_b * 2 + 1 - x,
        "ds": far_sib_b * 2 + 1 - x,
    }
    return ids, ranks

def greet(ids):
    barrier = pltpu.get_barrier_semaphore()
    for device in ids.values():
        pl.semaphore_signal(barrier, inc=1, device_id=device, device_id_type=MESH)
    pl.semaphore_wait(barrier, len(ids))

def tiles(lo, hi, body):
    def step(i, _):
        body(pl.ds(pl.multiple_of(i * TILE, TILE), TILE))
        return 0
    lax.fori_loop(lo // TILE, hi // TILE, step, 0)

def gather_kernel(body_of, n_in, n_out, x_ref, *refs):
    ins = refs[:n_in]; all_ref = refs[n_in]; outs = refs[n_in + 1 : n_in + 1 + n_out]
    held, send, recv, keep = refs[n_in + 1 + n_out :]
    ids, at = plane_place()
    half = x_ref.shape[0] // 2
    parts = (pl.ds(0, half), pl.ds(half, half))
    greet(ids)
    count = [0]
    started = []
    def ship(src, dst, to):
        n = count[0]; count[0] += 1
        c = pltpu.make_async_remote_copy(src_ref=src, dst_ref=dst, send_sem=send.at[n], recv_sem=recv.at[n], device_id=ids[to], device_id_type=MESH)
        c.start(); started.append(c)
        return c
    own = at["o"]
    x0 = ship(x_ref.at[parts[0]], held.at[own, parts[0]], "x")
    y1 = ship(x_ref.at[parts[1]], held.at[own, parts[1]], "y")
    x1 = ship(x_ref.at[parts[1]], held.at[own, parts[1]], "x")
    y0 = ship(x_ref.at[parts[0]], held.at[own, parts[0]], "y")
    s0 = ship(x_ref, held.at[own], "s")
    kept = []
    def done(rank, src):
        c = pltpu.make_async_copy(src, all_ref.at[rank], keep.at[len(kept)])
        c.start(); kept.append(c)
        if body_of is not None:
            body_of(rank, src, ins, outs)
    done(own, x_ref)
    s0.wait_recv()
    done(at["s"], held.at[at["s"]])
    x0.wait_recv()
    ry = ship(held.at[at["x"], parts[0]], held.at[at["x"], parts[0]], "y")
    y1.wait_recv()
    rx = ship(held.at[at["y"], parts[1]], held.at[at["y"], parts[1]], "x")
    x1.wait_recv()
    sx = ship(held.at[at["x"]], held.at[at["x"]], "s")
    y0.wait_recv()
    sy = ship(held.at[at["y"]], held.at[at["y"]], "s")
    done(at["x"], held.at[at["x"]])
    done(at["y"], held.at[at["y"]])
    sx.wait_recv()
    done(at["xs"], held.at[at["xs"]])
    sy.wait_recv()
    done(at["ys"], held.at[at["ys"]])
    ry.wait_recv(); rx.wait_recv()
    sd = ship(held.at[at["d"]], held.at[at["d"]], "s")
    done(at["d"], held.at[at["d"]])
    sd.wait_recv()
    done(at["ds"], held.at[at["ds"]])
    for c in started: c.wait_send()
    for c in kept: c.wait()

def vmem(n): return [pl.BlockSpec(memory_space=pltpu.VMEM)] * n

def plane_gather(x, ins, out_types, body_of, cid, name, ranks=8):
    tok, D = x.shape
    res = pl.pallas_call(
        functools.partial(gather_kernel, body_of, len(ins), len(out_types)),
        out_shape=[jax.ShapeDtypeStruct((ranks, tok, D), x.dtype), *out_types],
        in_specs=vmem(1 + len(ins)),
        out_specs=[pl.BlockSpec(memory_space=pl.ANY)] + vmem(len(out_types)),
        scratch_shapes=[pltpu.VMEM((ranks, tok, D), x.dtype), pltpu.SemaphoreType.DMA((10,)), pltpu.SemaphoreType.DMA((10,)), pltpu.SemaphoreType.DMA((8,))],
        compiler_params=pltpu.CompilerParams(collective_id=cid, has_side_effects=True, vmem_limit_bytes=60 << 20),
        cost_estimate=pl.CostEstimate(flops=1 << 30, bytes_accessed=128 << 20, transcendentals=0),
        name=name,
    )(x, *ins)
    return res[0].reshape(ranks * tok, D), *res[1:]

def gather_dot(x, w, bias, out_dtype, turned, cid, name):
    ranks, tok, D = 8, *x.shape
    N = w.shape[0] if turned else w.shape[1]
    tile = min(N, 512) if N % 512 == 0 else 256
    def body(rank, src, ins, outs):
        w_ref, b_ref = ins
        def step(i, _):
            cols = pl.ds(pl.multiple_of(i * tile, tile), tile)
            if turned:
                y = lax.dot_general(src[...], w_ref[cols, :], (((1,), (1,)), ((), ())), preferred_element_type=single)
            else:
                y = jnp.dot(src[...], w_ref[:, cols], preferred_element_type=single)
            outs[0][rank, :, cols] = (y + b_ref[:, cols]).astype(out_dtype)
            return 0
        lax.fori_loop(0, N // tile, step, 0)
    all_, y = plane_gather(x, (w, bias), [jax.ShapeDtypeStruct((ranks, tok, N), out_dtype)], body, cid, name)
    return all_, y.reshape(ranks * tok, N)

def reduce_kernel(turned, a_ref, w_ref, out_ref, sib_out, sib_in, stage, landed, send, recv):
    ids, at = plane_place()
    ranks, tok, _ = a_ref.shape
    D = out_ref.shape[1]
    mid = D // 2
    greet(ids)
    count = [0]; started = []
    def ship(src, dst, to):
        n = count[0]; count[0] += 1
        c = pltpu.make_async_remote_copy(src_ref=src, dst_ref=dst, send_sem=send.at[n], recv_sem=recv.at[n], device_id=ids[to], device_id_type=MESH)
        c.start(); started.append(c)
        return c
    def term(rank, cols):
        if turned:
            return lax.dot_general(a_ref[rank], w_ref[cols, :], (((1,), (1,)), ((), ())), preferred_element_type=single)
        return jnp.dot(a_ref[rank], w_ref[:, cols], preferred_element_type=single)
    order = ("d", "x", "y", "o")
    twin = {"d": "ds", "x": "xs", "y": "ys", "o": "s"}
    sib = []
    for j, d in enumerate(order):
        def fill(cols, j=j, d=d):
            sib_out[j, :, cols] = term(at[twin[d]], cols).astype(bfloat)
        tiles(0, D, fill)
        sib.append(ship(sib_out.at[j], sib_in.at[j], "s"))
    def pair(j, cols):
        return term(at[order[j]], cols) + sib_in[j, :, cols].astype(single)
    def local(h, cols):
        return pl.ds(pl.multiple_of(cols.start - h * mid, TILE), TILE)
    def put(j, h, extra=None):
        def fill(cols):
            value = pair(j, cols)
            if extra is not None:
                value = value + landed[extra, :, local(h, cols)].astype(single)
            stage[j, h, :, local(h, cols)] = value.astype(bfloat)
        tiles(h * mid, (h + 1) * mid, fill)
    sib[0].wait_recv()
    put(0, 0)
    d_a = ship(stage.at[0, 0], landed.at[0], "x")
    put(0, 1)
    d_b = ship(stage.at[0, 1], landed.at[1], "y")
    sib[1].wait_recv()
    put(1, 0)
    x_a = ship(stage.at[1, 0], landed.at[2], "x")
    sib[2].wait_recv()
    put(2, 1)
    y_b = ship(stage.at[2, 1], landed.at[3], "y")
    sib[3].wait_recv()
    def first(cols):
        out_ref[:, cols] = pair(3, cols)
    tiles(0, D, first)
    d_b.wait_recv()
    put(1, 1, extra=1)
    x_b = ship(stage.at[1, 1], landed.at[5], "x")
    d_a.wait_recv()
    put(2, 0, extra=0)
    y_a = ship(stage.at[2, 0], landed.at[4], "y")
    x_a.wait_recv(); y_b.wait_recv(); x_b.wait_recv(); y_a.wait_recv()
    for h, (n, m) in enumerate(((2, 4), (3, 5))):
        def add(cols, h=h, n=n, m=m):
            c = local(h, cols)
            out_ref[:, cols] = out_ref[:, cols] + landed[n, :, c].astype(single) + landed[m, :, c].astype(single)
        tiles(h * mid, (h + 1) * mid, add)
    for c in started: c.wait_send()

def dot_reduce(a, w, turned, cid, name):
    ranks = 8
    D = w.shape[0] if turned else w.shape[1]
    tok = a.shape[0] // ranks
    return pl.pallas_call(
        functools.partial(reduce_kernel, turned),
        out_shape=jax.ShapeDtypeStruct((tok, D), single),
        in_specs=vmem(2), out_specs=vmem(1)[0],
        scratch_shapes=[pltpu.VMEM((4, tok, D), bfloat), pltpu.VMEM((4, tok, D), bfloat), pltpu.VMEM((3, 2, tok, D // 2), bfloat), pltpu.VMEM((6, tok, D // 2), bfloat),
            pltpu.SemaphoreType.DMA((10,)), pltpu.SemaphoreType.DMA((10,))],
        compiler_params=pltpu.CompilerParams(collective_id=cid, has_side_effects=True, vmem_limit_bytes=60 << 20),
        cost_estimate=pl.CostEstimate(flops=1 << 30, bytes_accessed=128 << 20, transcendentals=0),
        name=name,
    )(a.reshape(ranks, tok, -1), w)


def dot(left, right):
    return jnp.dot(left, right, preferred_element_type=single)


def dot_tn(left, right):
    return lax.dot_general(left, right, (((0,), (0,)), ((), ())), preferred_element_type=single)


def dot_nt(left, right):
    return lax.dot_general(left, right, (((1,), (1,)), ((), ())), preferred_element_type=single)


def layer_norm(values, gain_vec, shift_vec):
    center = jnp.mean(values, axis=-1, keepdims=True)
    centered = values - center
    spread = jnp.mean(centered * centered, axis=-1, keepdims=True)
    return centered * lax.rsqrt(spread + 1e-05) * gain_vec + shift_vec


def column_sums(matrix):
    return jnp.sum(matrix.astype(single), axis=0)


def windows(span):
    block = span // 2
    return [(i * block, i * block + block + span) for i in range(2)]

def key_window(before, own, lo, hi, span):
    return jnp.concatenate([before[lo:span], own[0 : hi - span]], axis=0)

def hidden_bias(start_ref, i, block, lo, hi, span):
    rows = span + i * block + lax.broadcasted_iota(jnp.int32, (block, hi - lo), 0)
    keys = lo + lax.broadcasted_iota(jnp.int32, (block, hi - lo), 1)
    start = start_ref[i * block : (i + 1) * block, :]
    return jnp.where((keys >= start) & (keys <= rows), 0.0, -1e30).astype(single)

def attend_kernel(start_ref, q_ref, k_ref, v_ref, kb_ref, vb_ref, out_ref):
    span, cols = q_ref.shape
    block = span // 2
    lane = lax.broadcasted_iota(jnp.int32, (block, cols), 1) // HEAD_DIM
    for i, (lo, hi) in enumerate(windows(span)):
        rows = pl.ds(i * block, block)
        bias = hidden_bias(start_ref, i, block, lo, hi, span)
        keys = key_window(kb_ref, k_ref, lo, hi, span)
        vals = key_window(vb_ref, v_ref, lo, hi, span)
        query = q_ref[rows, :] * jnp.asarray(HEAD_DIM ** (-0.5), bfloat)
        def head(h, total):
            mine = lane == h
            scores = dot_nt(jnp.where(mine, query, 0), keys) + bias
            weights = jnp.exp(scores - jnp.max(scores, axis=1, keepdims=True))
            part = jnp.dot(weights.astype(bfloat), vals, preferred_element_type=single)
            part = part * (1.0 / jnp.sum(weights, axis=1, keepdims=True))
            return jnp.where(mine, part, total)
        total = lax.fori_loop(0, cols // HEAD_DIM, head, jnp.zeros((block, cols), single), unroll=True)
        out_ref[rows, :] = total.astype(bfloat)

def attend_back_kernel(start_ref, q_ref, k_ref, v_ref, kb_ref, vb_ref, do_ref, dq_ref, edge_ref, pair_ref, dk, dv):
    span, cols = q_ref.shape
    block = span // 2
    scale = HEAD_DIM ** (-0.5)
    dk[...] = jnp.zeros_like(dk)
    dv[...] = jnp.zeros_like(dv)
    lane = lax.broadcasted_iota(jnp.int32, (block, cols), 1) // HEAD_DIM
    for i, (lo, hi) in enumerate(windows(span)):
        rows = pl.ds(i * block, block)
        bias = hidden_bias(start_ref, i, block, lo, hi, span)
        keys = key_window(kb_ref, k_ref, lo, hi, span)
        vals = key_window(vb_ref, v_ref, lo, hi, span)
        query = q_ref[rows, :] * jnp.asarray(scale, bfloat)
        grad = do_ref[rows, :]
        def head(h, total):
            mine = lane == h
            query_h = jnp.where(mine, query, 0)
            grad_h = jnp.where(mine, grad, 0)
            scores = dot_nt(query_h, keys) + bias
            weights = jnp.exp(scores - jnp.max(scores, axis=1, keepdims=True))
            probs = weights * (1.0 / jnp.sum(weights, axis=1, keepdims=True))
            prob_grad = dot_nt(grad_h, vals)
            row_dot = jnp.sum(probs * prob_grad, axis=1, keepdims=True)
            score_grad = (probs * (prob_grad - row_dot)).astype(bfloat)
            dv[lo:hi, :] += dot_tn(probs.astype(bfloat), grad_h)
            dk[lo:hi, :] += dot_tn(score_grad, query_h)
            part = jnp.dot(score_grad, keys, preferred_element_type=single)
            return jnp.where(mine, part, total)
        total = lax.fori_loop(0, cols // HEAD_DIM, head, jnp.zeros((block, cols), single), unroll=True)
        dq_ref[rows, :] = (total * scale).astype(bfloat)
    edge_ref[:, :cols] = dk[:span, :].astype(bfloat)
    edge_ref[:, cols:] = dv[:span, :].astype(bfloat)
    pair_ref[:, :cols] = dk[span:, :]
    pair_ref[:, cols:] = dv[span:, :]

def attention_specs(span, cols):
    def at(j):
        return pl.BlockSpec((span, cols), lambda g: (g, j))
    return [pl.BlockSpec((span, 1), lambda g: (g, 0)), at(0), at(1), at(2), at(0), at(1)]

def attend(starts, qkv, before, groups):
    span, cols = qkv.shape[0] // groups, qkv.shape[1] // 3
    return pl.pallas_call(
        attend_kernel,
        grid=(groups,),
        out_shape=jax.ShapeDtypeStruct((groups * span, cols), bfloat),
        in_specs=attention_specs(span, cols),
        out_specs=pl.BlockSpec((span, cols), lambda g: (g, 0)),
        compiler_params=pltpu.CompilerParams(vmem_limit_bytes=60 << 20),
        name="attend",
    )(starts, qkv, qkv, qkv, before, before)

def attend_back(starts, qkv, before, grad, groups):
    span, cols = qkv.shape[0] // groups, qkv.shape[1] // 3
    rows = groups * span
    return pl.pallas_call(
        attend_back_kernel,
        grid=(groups,),
        out_shape=[jax.ShapeDtypeStruct((rows, cols), bfloat), jax.ShapeDtypeStruct((rows, 2 * cols), bfloat), jax.ShapeDtypeStruct((rows, 2 * cols), single)],
        in_specs=attention_specs(span, cols) + [pl.BlockSpec((span, cols), lambda g: (g, 0))],
        out_specs=[pl.BlockSpec((span, cols), lambda g: (g, 0))] + [pl.BlockSpec((span, 2 * cols), lambda g: (g, 0))] * 2,
        scratch_shapes=[pltpu.VMEM((2 * span, cols), single)] * 2,
        compiler_params=pltpu.CompilerParams(vmem_limit_bytes=60 << 20),
        name="attend_back",
    )(starts, qkv, qkv, qkv, before, before, grad)


def attention_heads(starts, qkv, before, groups):
    span, cols = qkv.shape[0] // groups, qkv.shape[1] // 3
    both = jnp.concatenate([before.reshape(groups, span, -1), qkv[:, cols:].reshape(groups, span, -1)], axis=1)
    key_two, value_two = [both[..., i * cols : (i + 1) * cols].reshape(groups, 2 * span, -1, HEAD_DIM) for i in (0, 1)]
    query = qkv[:, :cols].reshape(groups, span, -1, HEAD_DIM)
    keys = jnp.arange(2 * span)[None, None, :]
    rows = span + jnp.arange(span)[None, :, None]
    allowed = (keys >= starts.reshape(groups, span, 1)) & (keys <= rows)
    scores = jnp.einsum("gqhd,gkhd->ghqk", query, key_two, preferred_element_type=single) * HEAD_DIM ** (-0.5)
    scores = jnp.where(allowed[:, None], scores, -1e30)
    weights = jnp.exp(scores - jnp.max(scores, axis=-1, keepdims=True))
    return query, key_two, value_two, weights / jnp.sum(weights, axis=-1, keepdims=True)


def attention_forward(starts, qkv, before, groups):
    if qkv.shape[1] // 3 % 128 == 0:
        return attend(starts, qkv, before, groups)
    _, _, value_two, probs = attention_heads(starts, qkv, before, groups)
    context = jnp.einsum("ghqk,gkhd->gqhd", probs.astype(bfloat), value_two, preferred_element_type=single)
    return context.astype(bfloat).reshape(qkv.shape[0], -1)


def attention_backward(starts, qkv, before, grad, groups):
    if qkv.shape[1] // 3 % 128 == 0:
        return attend_back(starts, qkv, before, grad, groups)
    query, key_two, value_two, probs = attention_heads(starts, qkv, before, groups)
    span = query.shape[1]
    grad = grad.reshape(query.shape)
    prob_grad = jnp.einsum("gqhd,gkhd->ghqk", grad, value_two, preferred_element_type=single)
    row_dot = jnp.sum(probs * prob_grad, axis=-1, keepdims=True)
    score_grad = (probs * (prob_grad - row_dot)).astype(bfloat)
    query_grad = jnp.einsum("ghqk,gkhd->gqhd", score_grad, key_two, preferred_element_type=single) * HEAD_DIM ** (-0.5)
    key_grad = jnp.einsum("ghqk,gqhd->gkhd", score_grad, query, preferred_element_type=single) * HEAD_DIM ** (-0.5)
    value_grad = jnp.einsum("ghqk,gqhd->gkhd", probs.astype(bfloat), grad, preferred_element_type=single)
    pair = jnp.concatenate([t.reshape(groups, 2 * span, -1) for t in (key_grad, value_grad)], axis=2)
    rows = qkv.shape[0]
    edge, pair = [t.reshape(rows, -1) for t in (pair[:, :span].astype(bfloat), pair[:, span:])]
    return query_grad.astype(bfloat).reshape(rows, -1), edge, pair


def norm_backward(values, out_grad, gain_vec):
    center = jnp.mean(values, axis=-1, keepdims=True)
    centered = values - center
    rs = lax.rsqrt(jnp.mean(centered * centered, axis=-1, keepdims=True) + 1e-05)
    xhat = centered * rs
    g = out_grad * gain_vec
    part = rs * (g - jnp.mean(g, axis=-1, keepdims=True) - xhat * jnp.mean(g * xhat, axis=-1, keepdims=True))
    return part, jnp.sum(out_grad * xhat, axis=0), jnp.sum(out_grad, axis=0)


def on_device(
    inputs,
    exit_layers,
    lengths,
    layer_index,
    out_grad,
    ln1_gain,
    ln1_bias,
    q_weight,
    q_bias,
    k_weight,
    v_weight,
    v_bias,
    o_weight,
    o_bias,
    ln2_gain,
    ln2_bias,
    fc1_weight,
    fc1_bias,
    fc2_weight,
    fc2_bias,
):
    B, Z, X = lax.axis_size("b"), lax.axis_size("z"), lax.axis_size("x")
    R = B * X
    local = inputs[0].astype(single)
    tok, D = local.shape
    span = X * tok
    group_tok = Z * span
    at_z, at_x = lax.axis_index("z"), lax.axis_index("x")
    rank = lax.axis_index("b") * X + at_x
    rows_dev = q_weight.shape[0]
    cols = D // R
    heads = cols // HEAD_DIM
    whole_heads = rows_dev % HEAD_DIM == 0

    group_active = (exit_layers[0] > layer_index[0]).astype(single)
    active_total = jnp.sum(group_active)
    active = lax.dynamic_slice_in_dim(group_active, at_z * span + at_x * tok, tok, 0)[:, None]

    count = lengths.shape[1]
    upto = jnp.arange(count)[:, None] <= jnp.arange(count)[None, :]
    small = [ln1_gain, ln1_bias, q_bias, v_bias, o_bias, ln2_gain, ln2_bias, fc2_bias]
    pack = jnp.concatenate([v.astype(single) for v in (*small, fc1_bias, lengths[0])])
    pad = -pack.shape[0] % 128
    pack = lax.all_gather(jnp.concatenate([pack, jnp.zeros((pad,), single)]), ALL, axis=0)
    vectors = [pack[:, i * rows_dev : (i + 1) * rows_dev].reshape(-1) for i in range(len(small))]
    gain_one, bias_one, bias_q, bias_v, bias_o, gain_two, bias_two, bias_down = vectors
    pack = pack.reshape(B, Z, X, -1)[..., len(small) * rows_dev :]
    up_dev = fc1_bias.shape[0]
    bias_up = lax.dynamic_index_in_dim(
        pack[..., :up_dev].transpose(0, 2, 1, 3).reshape(R, Z * up_dev), rank, 0, keepdims=False
    )
    group_lengths = pack[:, 0, 0, up_dev : up_dev + count].astype(jnp.int32)
    ends = jnp.sum(jnp.where(upto, group_lengths[:, :, None], 0), axis=1)
    places = at_z * span + jnp.arange(span, dtype=jnp.int32)
    starts = jnp.max(jnp.where(ends[:, None, :] <= places[None, :, None], ends[:, None, :], 0), axis=2)
    starts = starts - (at_z - 1) * span

    def to_ranks(matrix):
        lead = matrix.shape[:-1]
        if whole_heads:
            matrix = matrix.reshape(*lead, B, Z, X, rows_dev)
            k = len(lead)
            return matrix.transpose(k, k + 2, *range(k), k + 1, k + 3).reshape(R, *lead, cols)
        return jnp.moveaxis(matrix.reshape(*lead, R, cols), -2, 0)

    def from_ranks(parts):
        if whole_heads:
            parts = parts.reshape(B, X, -1, Z, rows_dev)
            return parts.transpose(2, 0, 3, 1, 4).reshape(-1, D)
        return parts.transpose(1, 0, 2).reshape(-1, D)

    def mine(vector):
        return lax.dynamic_index_in_dim(to_ranks(vector), rank, 0, keepdims=False)

    qkv_parts = jnp.concatenate([to_ranks(q_weight), to_ranks(k_weight), to_ranks(v_weight)], axis=2)
    qkv_mine = lax.all_to_all(qkv_parts, PLANE, split_axis=0, concat_axis=0, tiled=True)
    weight_qkv = lax.all_gather(qkv_mine.reshape(D // Z, 3 * cols), "z", axis=0, tiled=True)
    weight_qkv = weight_qkv.reshape(Z, B, X, rows_dev, 3 * cols).transpose(1, 0, 2, 3, 4).reshape(D, 3 * cols)
    bias_qkv = jnp.concatenate([mine(bias_q), jnp.zeros((cols,), single), mine(bias_v)])
    if whole_heads:
        weight_o = lax.all_gather(o_weight, "z", axis=0, tiled=True)
    else:
        weight_o = lax.dynamic_slice_in_dim(lax.all_gather(o_weight, ALL, axis=0, tiled=True), rank * cols, cols, 0)
    weight_up = lax.all_gather(fc1_weight, "z", axis=1, tiled=True)
    weight_down = lax.all_gather(fc2_weight, "z", axis=0, tiled=True)

    normed_low = layer_norm(local, gain_one, bias_one).astype(bfloat)
    fast = (B, X) == (4, 2)

    def gather_plane(rows, cid, name):
        if fast:
            return plane_gather(rows, (), [], None, cid, name)[0]
        return lax.all_gather(rows, PLANE, axis=0, tiled=True)

    def gather_plane_dot(rows, weight, shift, out_type, turned, cid, name):
        if fast:
            return gather_dot(rows, weight, shift, out_type, turned, cid, name)
        rows = lax.all_gather(rows, PLANE, axis=0, tiled=True)
        return rows, ((dot_nt if turned else dot)(rows, weight) + shift).astype(out_type)

    def reduce_plane(left, weight, turned, cid, name):
        if fast:
            return dot_reduce(left, weight, turned, cid, name)
        terms = (dot_nt if turned else dot)(left, weight).astype(bfloat)
        return lax.psum_scatter(terms, PLANE, scatter_dimension=0, tiled=True).astype(single)

    normed_all = gather_plane(normed_low, 0, "gather_normed")
    qkv = (dot(normed_all, weight_qkv) + bias_qkv).astype(bfloat)
    up = [(i, i + 1) for i in range(Z - 1)]
    down = [(i + 1, i) for i in range(Z - 1)]
    cotangent = out_grad[0].astype(single) * (group_tok / active_total)
    branch_grad = (active * cotangent).astype(bfloat)
    down_b_grad = column_sums(branch_grad)
    qkv, branch_grad = lax.optimization_barrier((qkv, branch_grad))
    before = lax.ppermute(qkv[:, cols:], "z", up)
    branch_all = gather_plane(branch_grad, 7, "gather_branch")
    before, branch_all = lax.optimization_barrier((before, branch_all))
    starts = starts.reshape(B * span, 1)
    context = attention_forward(starts, qkv, before, B)

    attended = reduce_plane(context, weight_o, False, 1, "attended") + bias_o
    middle = local + active * attended
    normed_two = layer_norm(middle, gain_two, bias_two).astype(bfloat)
    two_all, hidden_pre = gather_plane_dot(normed_two, weight_up, bias_up[None], single, False, 2, "up")
    gelu_value, gelu_pull = jax.vjp(partial(jax.nn.gelu, approximate=True), hidden_pre)
    hidden = gelu_value.astype(bfloat)
    hidden_grad = dot_nt(branch_all, weight_down)
    pre_grad = gelu_pull(hidden_grad)[0].astype(bfloat)
    down_w_grad = dot_tn(hidden, branch_all).astype(bfloat)
    up_w_grad = dot_tn(two_all, pre_grad).astype(bfloat)
    up_b_grad = column_sums(pre_grad)
    hidden, pre_grad, down_w_grad, up_w_grad = lax.optimization_barrier((hidden, pre_grad, down_w_grad, up_w_grad))
    normed_two_grad = reduce_plane(pre_grad, weight_up, True, 3, "up_grad")
    down_w_shard = lax.psum_scatter(down_w_grad, "z", scatter_dimension=0, tiled=True).astype(single)
    up_w_shard = lax.psum_scatter(up_w_grad, "z", scatter_dimension=1, tiled=True).astype(single)

    middle_part, gain_two_grad, bias_two_grad = norm_backward(middle, normed_two_grad, gain_two)
    middle_grad = cotangent + middle_part
    attended_grad = (active * middle_grad).astype(bfloat)
    out_b_grad = column_sums(attended_grad)
    attended_all, context_grad = gather_plane_dot(
        attended_grad, weight_o, jnp.zeros((1, cols), single), bfloat, True, 5, "attended_grad"
    )
    out_w_grad = dot_tn(context, attended_all)
    query_grad, edge, pair = attention_backward(starts, qkv, before, context_grad, B)
    hidden, edge, pair = lax.optimization_barrier((hidden, edge, pair))
    after = lax.ppermute(edge, "z", down)
    branch = reduce_plane(hidden, weight_down, False, 4, "down")
    branch, after = lax.optimization_barrier((branch, after))
    outputs = middle + active * (branch + bias_down)
    pair_grad = (pair + after.astype(single)).astype(bfloat)
    qkv_grad = jnp.concatenate([query_grad, pair_grad], axis=1)
    normed_grad = reduce_plane(qkv_grad, weight_qkv, True, 6, "qkv_grad")
    qkv_w_grad = dot_tn(normed_all, qkv_grad)
    qkv_b_grad = column_sums(qkv_grad)
    input_part, gain_one_grad, bias_one_grad = norm_backward(local, normed_grad, gain_one)
    input_grad = middle_grad + input_part

    def sum_to_owners(vectors, axes, parts):
        split = jnp.concatenate([v.reshape(parts, -1) for v in vectors], axis=1)
        summed = jnp.sum(lax.all_to_all(split, axes, split_axis=0, concat_axis=0, tiled=True), axis=0)
        widths = [v.shape[0] // parts for v in vectors]
        return [summed[sum(widths[:i]) : sum(widths[: i + 1])] for i in range(len(widths))]

    qkv_w_grad = qkv_w_grad.astype(bfloat).reshape(B, Z, X, rows_dev, 3 * cols)
    qkv_w_grad = qkv_w_grad.transpose(1, 0, 2, 3, 4).reshape(D, 3 * cols)
    qkv_w_grad = lax.psum_scatter(qkv_w_grad, "z", scatter_dimension=0, tiled=True)
    qkv_w_grad = lax.all_to_all(qkv_w_grad.reshape(R, rows_dev, 3 * cols), PLANE, split_axis=0, concat_axis=0, tiled=True)
    qkv_w_grad = qkv_w_grad.astype(single)
    q_w_shard, k_w_shard, v_w_shard = [from_ranks(qkv_w_grad[..., i * cols : (i + 1) * cols]) for i in range(3)]
    if whole_heads:
        out_w_shard = lax.psum_scatter(out_w_grad.astype(bfloat), "z", scatter_dimension=0, tiled=True).astype(single)
        q_b_shard, v_b_shard, up_b_shard = sum_to_owners([qkv_b_grad[:cols], qkv_b_grad[2 * cols :], up_b_grad], "z", Z)
    else:

        def placed(rows):
            full = jnp.zeros((D,) + rows.shape[1:], rows.dtype)
            full = lax.dynamic_update_slice_in_dim(full, rows, rank * cols, 0)
            return lax.psum_scatter(full, ALL, scatter_dimension=0, tiled=True).astype(single)

        out_w_shard = placed(out_w_grad.astype(bfloat))
        q_b_shard = placed(qkv_b_grad[:cols])
        v_b_shard = placed(qkv_b_grad[2 * cols :])
        [up_b_shard] = sum_to_owners([up_b_grad], "z", Z)
    sums = sum_to_owners(
        [gain_one_grad, bias_one_grad, out_b_grad, gain_two_grad, bias_two_grad, down_b_grad], ALL, R * Z
    )
    return (
        outputs.astype(bfloat)[None],
        input_grad.astype(bfloat)[None],
        sums[0],
        sums[1],
        q_w_shard,
        q_b_shard,
        k_w_shard,
        v_w_shard,
        v_b_shard,
        out_w_shard,
        sums[2],
        sums[3],
        sums[4],
        up_w_shard,
        up_b_shard,
        down_w_shard,
        sums[5],
    )


def solution(mesh):
    groups, parts = mesh.shape["batch"], mesh.shape["seq"]
    inner = Mesh(mesh.devices.reshape(groups, SPANS, parts // SPANS), ("b", "z", "x"))
    token = P("b", ("z", "x"), None)
    vector = P(ALL)
    rows = P(ALL, None)
    columns = P(None, ALL)
    return jax.shard_map(
        on_device,
        mesh=inner,
        in_specs=(
            token,
            P("b", None),
            P("b", None),
            P(),
            token,
            vector,
            vector,
            rows,
            vector,
            rows,
            rows,
            vector,
            rows,
            vector,
            vector,
            vector,
            columns,
            vector,
            rows,
            vector,
        ),
        out_specs=(
            token,
            token,
            vector,
            vector,
            rows,
            vector,
            rows,
            rows,
            vector,
            rows,
            vector,
            vector,
            vector,
            columns,
            vector,
            rows,
            vector,
        ),
        check_vma=False,
    )
```

```python
import functools
from functools import partial

import jax
import jax.numpy as jnp
from jax import lax
from jax.experimental import pallas as pl
from jax.experimental.pallas import tpu as pltpu
from jax.sharding import Mesh
from jax.sharding import PartitionSpec as P

HEAD_DIM = 64
SPANS = 4

bfloat = jnp.bfloat16
single = jnp.float32

PLANE = ("b", "x")
ALL = ("b", "z", "x")
MESH = pl.DeviceIdType.MESH
TILE = 512

def plane_place():
    b, z, x = lax.axis_index("b"), lax.axis_index("z"), lax.axis_index("x")
    sib_b = b + 1 - 2 * lax.rem(b, 2)
    far_b = lax.rem(b + 2, 4)
    far_sib_b = lax.rem(sib_b + 2, 4)
    ids = {"s": (sib_b, z, x), "x": (b, z, 1 - x), "y": (far_b, z, x)}
    ranks = {
        "o": b * 2 + x,
        "s": sib_b * 2 + x,
        "x": b * 2 + 1 - x,
        "xs": sib_b * 2 + 1 - x,
        "y": far_b * 2 + x,
        "ys": far_sib_b * 2 + x,
        "d": far_b * 2 + 1 - x,
        "ds": far_sib_b * 2 + 1 - x,
    }
    return ids, ranks

def greet(ids):
    barrier = pltpu.get_barrier_semaphore()
    for device in ids.values():
        pl.semaphore_signal(barrier, inc=1, device_id=device, device_id_type=MESH)
    pl.semaphore_wait(barrier, len(ids))

def tiles(lo, hi, body):
    def step(i, _):
        body(pl.ds(pl.multiple_of(i * TILE, TILE), TILE))
        return 0
    lax.fori_loop(lo // TILE, hi // TILE, step, 0)

def gather_kernel(body_of, n_in, n_out, x_ref, *refs):
    ins = refs[:n_in]; all_ref = refs[n_in]; outs = refs[n_in + 1 : n_in + 1 + n_out]
    held, send, recv, keep = refs[n_in + 1 + n_out :]
    ids, at = plane_place()
    half = x_ref.shape[0] // 2
    parts = (pl.ds(0, half), pl.ds(half, half))
    greet(ids)
    count = [0]
    started = []
    def ship(src, dst, to):
        n = count[0]; count[0] += 1
        c = pltpu.make_async_remote_copy(src_ref=src, dst_ref=dst, send_sem=send.at[n], recv_sem=recv.at[n], device_id=ids[to], device_id_type=MESH)
        c.start(); started.append(c)
        return c
    own = at["o"]
    x0 = ship(x_ref.at[parts[0]], held.at[own, parts[0]], "x")
    y1 = ship(x_ref.at[parts[1]], held.at[own, parts[1]], "y")
    x1 = ship(x_ref.at[parts[1]], held.at[own, parts[1]], "x")
    y0 = ship(x_ref.at[parts[0]], held.at[own, parts[0]], "y")
    s0 = ship(x_ref, held.at[own], "s")
    kept = []
    def done(rank, src):
        c = pltpu.make_async_copy(src, all_ref.at[rank], keep.at[len(kept)])
        c.start(); kept.append(c)
        if body_of is not None:
            body_of(rank, src, ins, outs)
    done(own, x_ref)
    s0.wait_recv()
    done(at["s"], held.at[at["s"]])
    x0.wait_recv()
    ry = ship(held.at[at["x"], parts[0]], held.at[at["x"], parts[0]], "y")
    y1.wait_recv()
    rx = ship(held.at[at["y"], parts[1]], held.at[at["y"], parts[1]], "x")
    x1.wait_recv()
    sx = ship(held.at[at["x"]], held.at[at["x"]], "s")
    y0.wait_recv()
    sy = ship(held.at[at["y"]], held.at[at["y"]], "s")
    done(at["x"], held.at[at["x"]])
    done(at["y"], held.at[at["y"]])
    sx.wait_recv()
    done(at["xs"], held.at[at["xs"]])
    sy.wait_recv()
    done(at["ys"], held.at[at["ys"]])
    ry.wait_recv(); rx.wait_recv()
    sd = ship(held.at[at["d"]], held.at[at["d"]], "s")
    done(at["d"], held.at[at["d"]])
    sd.wait_recv()
    done(at["ds"], held.at[at["ds"]])
    for c in started: c.wait_send()
    for c in kept: c.wait()

def vmem(n): return [pl.BlockSpec(memory_space=pltpu.VMEM)] * n

def plane_gather(x, ins, out_types, body_of, cid, name, ranks=8):
    tok, D = x.shape
    res = pl.pallas_call(
        functools.partial(gather_kernel, body_of, len(ins), len(out_types)),
        out_shape=[jax.ShapeDtypeStruct((ranks, tok, D), x.dtype), *out_types],
        in_specs=vmem(1 + len(ins)),
        out_specs=[pl.BlockSpec(memory_space=pl.ANY)] + vmem(len(out_types)),
        scratch_shapes=[pltpu.VMEM((ranks, tok, D), x.dtype), pltpu.SemaphoreType.DMA((10,)), pltpu.SemaphoreType.DMA((10,)), pltpu.SemaphoreType.DMA((8,))],
        compiler_params=pltpu.CompilerParams(collective_id=cid, has_side_effects=True, vmem_limit_bytes=60 << 20),
        cost_estimate=pl.CostEstimate(flops=1 << 30, bytes_accessed=128 << 20, transcendentals=0),
        name=name,
    )(x, *ins)
    return res[0].reshape(ranks * tok, D), *res[1:]

def gather_dot(x, w, bias, out_dtype, turned, cid, name):
    ranks, tok, D = 8, *x.shape
    N = w.shape[0] if turned else w.shape[1]
    tile = min(N, 512) if N % 512 == 0 else 256
    def body(rank, src, ins, outs):
        w_ref, b_ref = ins
        def step(i, _):
            cols = pl.ds(pl.multiple_of(i * tile, tile), tile)
            if turned:
                y = lax.dot_general(src[...], w_ref[cols, :], (((1,), (1,)), ((), ())), preferred_element_type=single)
            else:
                y = jnp.dot(src[...], w_ref[:, cols], preferred_element_type=single)
            outs[0][rank, :, cols] = (y + b_ref[:, cols]).astype(out_dtype)
            return 0
        lax.fori_loop(0, N // tile, step, 0)
    all_, y = plane_gather(x, (w, bias), [jax.ShapeDtypeStruct((ranks, tok, N), out_dtype)], body, cid, name)
    return all_, y.reshape(ranks * tok, N)

def reduce_kernel(turned, a_ref, w_ref, out_ref, sib_out, sib_in, stage, landed, send, recv):
    ids, at = plane_place()
    ranks, tok, _ = a_ref.shape
    D = out_ref.shape[1]
    mid = D // 2
    greet(ids)
    count = [0]; started = []
    def ship(src, dst, to):
        n = count[0]; count[0] += 1
        c = pltpu.make_async_remote_copy(src_ref=src, dst_ref=dst, send_sem=send.at[n], recv_sem=recv.at[n], device_id=ids[to], device_id_type=MESH)
        c.start(); started.append(c)
        return c
    def term(rank, cols):
        if turned:
            return lax.dot_general(a_ref[rank], w_ref[cols, :], (((1,), (1,)), ((), ())), preferred_element_type=single)
        return jnp.dot(a_ref[rank], w_ref[:, cols], preferred_element_type=single)
    order = ("d", "x", "y", "o")
    twin = {"d": "ds", "x": "xs", "y": "ys", "o": "s"}
    sib = []
    for j, d in enumerate(order):
        def fill(cols, j=j, d=d):
            sib_out[j, :, cols] = term(at[twin[d]], cols).astype(bfloat)
        tiles(0, D, fill)
        sib.append(ship(sib_out.at[j], sib_in.at[j], "s"))
    def pair(j, cols):
        return term(at[order[j]], cols) + sib_in[j, :, cols].astype(single)
    def local(h, cols):
        return pl.ds(pl.multiple_of(cols.start - h * mid, TILE), TILE)
    def put(j, h, extra=None):
        def fill(cols):
            value = pair(j, cols)
            if extra is not None:
                value = value + landed[extra, :, local(h, cols)].astype(single)
            stage[j, h, :, local(h, cols)] = value.astype(bfloat)
        tiles(h * mid, (h + 1) * mid, fill)
    sib[0].wait_recv()
    put(0, 0)
    d_a = ship(stage.at[0, 0], landed.at[0], "x")
    put(0, 1)
    d_b = ship(stage.at[0, 1], landed.at[1], "y")
    sib[1].wait_recv()
    put(1, 0)
    x_a = ship(stage.at[1, 0], landed.at[2], "x")
    sib[2].wait_recv()
    put(2, 1)
    y_b = ship(stage.at[2, 1], landed.at[3], "y")
    sib[3].wait_recv()
    def first(cols):
        out_ref[:, cols] = pair(3, cols)
    tiles(0, D, first)
    d_b.wait_recv()
    put(1, 1, extra=1)
    x_b = ship(stage.at[1, 1], landed.at[5], "x")
    d_a.wait_recv()
    put(2, 0, extra=0)
    y_a = ship(stage.at[2, 0], landed.at[4], "y")
    x_a.wait_recv(); y_b.wait_recv(); x_b.wait_recv(); y_a.wait_recv()
    for h, (n, m) in enumerate(((2, 4), (3, 5))):
        def add(cols, h=h, n=n, m=m):
            c = local(h, cols)
            out_ref[:, cols] = out_ref[:, cols] + landed[n, :, c].astype(single) + landed[m, :, c].astype(single)
        tiles(h * mid, (h + 1) * mid, add)
    for c in started: c.wait_send()

def dot_reduce(a, w, turned, cid, name):
    ranks = 8
    D = w.shape[0] if turned else w.shape[1]
    tok = a.shape[0] // ranks
    return pl.pallas_call(
        functools.partial(reduce_kernel, turned),
        out_shape=jax.ShapeDtypeStruct((tok, D), single),
        in_specs=vmem(2), out_specs=vmem(1)[0],
        scratch_shapes=[pltpu.VMEM((4, tok, D), bfloat), pltpu.VMEM((4, tok, D), bfloat), pltpu.VMEM((3, 2, tok, D // 2), bfloat), pltpu.VMEM((6, tok, D // 2), bfloat),
            pltpu.SemaphoreType.DMA((10,)), pltpu.SemaphoreType.DMA((10,))],
        compiler_params=pltpu.CompilerParams(collective_id=cid, has_side_effects=True, vmem_limit_bytes=60 << 20),
        cost_estimate=pl.CostEstimate(flops=1 << 30, bytes_accessed=128 << 20, transcendentals=0),
        name=name,
    )(a.reshape(ranks, tok, -1), w)


def dot(left, right):
    return jnp.dot(left, right, preferred_element_type=single)


def dot_tn(left, right):
    return lax.dot_general(left, right, (((0,), (0,)), ((), ())), preferred_element_type=single)


def dot_nt(left, right):
    return lax.dot_general(left, right, (((1,), (1,)), ((), ())), preferred_element_type=single)


def layer_norm(values, gain_vec, shift_vec):
    center = jnp.mean(values, axis=-1, keepdims=True)
    centered = values - center
    spread = jnp.mean(centered * centered, axis=-1, keepdims=True)
    return centered * lax.rsqrt(spread + 1e-05) * gain_vec + shift_vec


def column_sums(matrix):
    return jnp.sum(matrix.astype(single), axis=0)


def windows(span):
    block = span // 2
    return [(i * block, i * block + block + span) for i in range(2)]

def key_window(before, own, lo, hi, span):
    return jnp.concatenate([before[lo:span], own[0 : hi - span]], axis=0)

def hidden_bias(start_ref, i, block, lo, hi, span):
    rows = span + i * block + lax.broadcasted_iota(jnp.int32, (block, hi - lo), 0)
    keys = lo + lax.broadcasted_iota(jnp.int32, (block, hi - lo), 1)
    start = start_ref[i * block : (i + 1) * block, :]
    return jnp.where((keys >= start) & (keys <= rows), 0.0, -1e30).astype(single)

def attend_kernel(start_ref, q_ref, k_ref, v_ref, kb_ref, vb_ref, out_ref):
    span, cols = q_ref.shape
    block = span // 2
    lane = lax.broadcasted_iota(jnp.int32, (block, cols), 1) // HEAD_DIM
    for i, (lo, hi) in enumerate(windows(span)):
        rows = pl.ds(i * block, block)
        bias = hidden_bias(start_ref, i, block, lo, hi, span)
        keys = key_window(kb_ref, k_ref, lo, hi, span)
        vals = key_window(vb_ref, v_ref, lo, hi, span)
        query = q_ref[rows, :] * jnp.asarray(HEAD_DIM ** (-0.5), bfloat)
        def head(h, total):
            mine = lane == h
            scores = dot_nt(jnp.where(mine, query, 0), keys) + bias
            weights = jnp.exp(scores - jnp.max(scores, axis=1, keepdims=True))
            part = jnp.dot(weights.astype(bfloat), vals, preferred_element_type=single)
            part = part * (1.0 / jnp.sum(weights, axis=1, keepdims=True))
            return jnp.where(mine, part, total)
        total = lax.fori_loop(0, cols // HEAD_DIM, head, jnp.zeros((block, cols), single), unroll=True)
        out_ref[rows, :] = total.astype(bfloat)

def attend_back_kernel(start_ref, q_ref, k_ref, v_ref, kb_ref, vb_ref, do_ref, dq_ref, edge_ref, pair_ref, dk, dv):
    span, cols = q_ref.shape
    block = span // 2
    scale = HEAD_DIM ** (-0.5)
    dk[...] = jnp.zeros_like(dk)
    dv[...] = jnp.zeros_like(dv)
    lane = lax.broadcasted_iota(jnp.int32, (block, cols), 1) // HEAD_DIM
    for i, (lo, hi) in enumerate(windows(span)):
        rows = pl.ds(i * block, block)
        bias = hidden_bias(start_ref, i, block, lo, hi, span)
        keys = key_window(kb_ref, k_ref, lo, hi, span)
        vals = key_window(vb_ref, v_ref, lo, hi, span)
        query = q_ref[rows, :] * jnp.asarray(scale, bfloat)
        grad = do_ref[rows, :]
        def head(h, total):
            mine = lane == h
            query_h = jnp.where(mine, query, 0)
            grad_h = jnp.where(mine, grad, 0)
            scores = dot_nt(query_h, keys) + bias
            weights = jnp.exp(scores - jnp.max(scores, axis=1, keepdims=True))
            probs = weights * (1.0 / jnp.sum(weights, axis=1, keepdims=True))
            prob_grad = dot_nt(grad_h, vals)
            row_dot = jnp.sum(probs * prob_grad, axis=1, keepdims=True)
            score_grad = (probs * (prob_grad - row_dot)).astype(bfloat)
            dv[lo:hi, :] += dot_tn(probs.astype(bfloat), grad_h)
            dk[lo:hi, :] += dot_tn(score_grad, query_h)
            part = jnp.dot(score_grad, keys, preferred_element_type=single)
            return jnp.where(mine, part, total)
        total = lax.fori_loop(0, cols // HEAD_DIM, head, jnp.zeros((block, cols), single), unroll=True)
        dq_ref[rows, :] = (total * scale).astype(bfloat)
    edge_ref[:, :cols] = dk[:span, :].astype(bfloat)
    edge_ref[:, cols:] = dv[:span, :].astype(bfloat)
    pair_ref[:, :cols] = dk[span:, :]
    pair_ref[:, cols:] = dv[span:, :]

def attention_specs(span, cols):
    def at(j):
        return pl.BlockSpec((span, cols), lambda g: (g, j))
    return [pl.BlockSpec((span, 1), lambda g: (g, 0)), at(0), at(0), at(1), at(0), at(1)]

def attend(starts, query, key_value, before, groups):
    span, cols = query.shape[0] // groups, query.shape[1]
    return pl.pallas_call(
        attend_kernel,
        grid=(groups,),
        out_shape=jax.ShapeDtypeStruct((groups * span, cols), bfloat),
        in_specs=attention_specs(span, cols),
        out_specs=pl.BlockSpec((span, cols), lambda g: (g, 0)),
        compiler_params=pltpu.CompilerParams(vmem_limit_bytes=60 << 20),
        name="attend",
    )(starts, query, key_value, key_value, before, before)

def attend_back(starts, query, key_value, before, grad, groups):
    span, cols = query.shape[0] // groups, query.shape[1]
    rows = groups * span
    return pl.pallas_call(
        attend_back_kernel,
        grid=(groups,),
        out_shape=[jax.ShapeDtypeStruct((rows, cols), bfloat), jax.ShapeDtypeStruct((rows, 2 * cols), bfloat), jax.ShapeDtypeStruct((rows, 2 * cols), single)],
        in_specs=attention_specs(span, cols) + [pl.BlockSpec((span, cols), lambda g: (g, 0))],
        out_specs=[pl.BlockSpec((span, cols), lambda g: (g, 0))] + [pl.BlockSpec((span, 2 * cols), lambda g: (g, 0))] * 2,
        scratch_shapes=[pltpu.VMEM((2 * span, cols), single)] * 2,
        compiler_params=pltpu.CompilerParams(vmem_limit_bytes=60 << 20),
        name="attend_back",
    )(starts, query, key_value, key_value, before, before, grad)


def attention_heads(starts, query, key_value, before, groups):
    span, cols = query.shape[0] // groups, query.shape[1]
    both = jnp.concatenate([before.reshape(groups, span, -1), key_value.reshape(groups, span, -1)], axis=1)
    key_two, value_two = [both[..., i * cols : (i + 1) * cols].reshape(groups, 2 * span, -1, HEAD_DIM) for i in (0, 1)]
    query = query.reshape(groups, span, -1, HEAD_DIM)
    keys = jnp.arange(2 * span)[None, None, :]
    rows = span + jnp.arange(span)[None, :, None]
    allowed = (keys >= starts.reshape(groups, span, 1)) & (keys <= rows)
    scores = jnp.einsum("gqhd,gkhd->ghqk", query, key_two, preferred_element_type=single) * HEAD_DIM ** (-0.5)
    scores = jnp.where(allowed[:, None], scores, -1e30)
    weights = jnp.exp(scores - jnp.max(scores, axis=-1, keepdims=True))
    return query, key_two, value_two, weights / jnp.sum(weights, axis=-1, keepdims=True)


def attention_forward(starts, query, key_value, before, groups):
    if query.shape[1] % 128 == 0:
        return attend(starts, query, key_value, before, groups)
    _, _, value_two, probs = attention_heads(starts, query, key_value, before, groups)
    context = jnp.einsum("ghqk,gkhd->gqhd", probs.astype(bfloat), value_two, preferred_element_type=single)
    return context.astype(bfloat).reshape(query.shape)


def attention_backward(starts, query, key_value, before, grad, groups):
    if query.shape[1] % 128 == 0:
        return attend_back(starts, query, key_value, before, grad, groups)
    rows = query.shape[0]
    query, key_two, value_two, probs = attention_heads(starts, query, key_value, before, groups)
    span = query.shape[1]
    grad = grad.reshape(query.shape)
    prob_grad = jnp.einsum("gqhd,gkhd->ghqk", grad, value_two, preferred_element_type=single)
    row_dot = jnp.sum(probs * prob_grad, axis=-1, keepdims=True)
    score_grad = (probs * (prob_grad - row_dot)).astype(bfloat)
    query_grad = jnp.einsum("ghqk,gkhd->gqhd", score_grad, key_two, preferred_element_type=single) * HEAD_DIM ** (-0.5)
    key_grad = jnp.einsum("ghqk,gqhd->gkhd", score_grad, query, preferred_element_type=single) * HEAD_DIM ** (-0.5)
    value_grad = jnp.einsum("ghqk,gqhd->gkhd", probs.astype(bfloat), grad, preferred_element_type=single)
    pair = jnp.concatenate([t.reshape(groups, 2 * span, -1) for t in (key_grad, value_grad)], axis=2)
    edge, pair = [t.reshape(rows, -1) for t in (pair[:, :span].astype(bfloat), pair[:, span:])]
    return query_grad.astype(bfloat).reshape(rows, -1), edge, pair


def norm_backward(values, out_grad, gain_vec):
    center = jnp.mean(values, axis=-1, keepdims=True)
    centered = values - center
    rs = lax.rsqrt(jnp.mean(centered * centered, axis=-1, keepdims=True) + 1e-05)
    xhat = centered * rs
    g = out_grad * gain_vec
    part = rs * (g - jnp.mean(g, axis=-1, keepdims=True) - xhat * jnp.mean(g * xhat, axis=-1, keepdims=True))
    return part, jnp.sum(out_grad * xhat, axis=0), jnp.sum(out_grad, axis=0)


def on_device(
    inputs,
    exit_layers,
    lengths,
    layer_index,
    out_grad,
    ln1_gain,
    ln1_bias,
    q_weight,
    q_bias,
    k_weight,
    v_weight,
    v_bias,
    o_weight,
    o_bias,
    ln2_gain,
    ln2_bias,
    fc1_weight,
    fc1_bias,
    fc2_weight,
    fc2_bias,
):
    B, Z, X = lax.axis_size("b"), lax.axis_size("z"), lax.axis_size("x")
    R = B * X
    local = inputs[0].astype(single)
    tok, D = local.shape
    span = X * tok
    group_tok = Z * span
    at_z, at_x = lax.axis_index("z"), lax.axis_index("x")
    rank = lax.axis_index("b") * X + at_x
    rows_dev = q_weight.shape[0]
    cols = D // R
    heads = cols // HEAD_DIM
    whole_heads = rows_dev % HEAD_DIM == 0

    group_active = (exit_layers[0] > layer_index[0]).astype(single)
    active_total = jnp.sum(group_active)
    active = lax.dynamic_slice_in_dim(group_active, at_z * span + at_x * tok, tok, 0)[:, None]

    count = lengths.shape[1]
    upto = jnp.arange(count)[:, None] <= jnp.arange(count)[None, :]
    small = [ln1_gain, ln1_bias, q_bias, v_bias, o_bias, ln2_gain, ln2_bias, fc2_bias]
    pack = jnp.concatenate([v.astype(single) for v in (*small, fc1_bias, lengths[0])])
    pad = -pack.shape[0] % 128
    pack = lax.all_gather(jnp.concatenate([pack, jnp.zeros((pad,), single)]), ALL, axis=0)
    vectors = [pack[:, i * rows_dev : (i + 1) * rows_dev].reshape(-1) for i in range(len(small))]
    gain_one, bias_one, bias_q, bias_v, bias_o, gain_two, bias_two, bias_down = vectors
    pack = pack.reshape(B, Z, X, -1)[..., len(small) * rows_dev :]
    up_dev = fc1_bias.shape[0]
    bias_up = lax.dynamic_index_in_dim(
        pack[..., :up_dev].transpose(0, 2, 1, 3).reshape(R, Z * up_dev), rank, 0, keepdims=False
    )
    group_lengths = pack[:, 0, 0, up_dev : up_dev + count].astype(jnp.int32)
    ends = jnp.sum(jnp.where(upto, group_lengths[:, :, None], 0), axis=1)
    places = at_z * span + jnp.arange(span, dtype=jnp.int32)
    starts = jnp.max(jnp.where(ends[:, None, :] <= places[None, :, None], ends[:, None, :], 0), axis=2)
    starts = starts - (at_z - 1) * span

    def to_ranks(matrix):
        lead = matrix.shape[:-1]
        if whole_heads:
            matrix = matrix.reshape(*lead, B, Z, X, rows_dev)
            k = len(lead)
            return matrix.transpose(k, k + 2, *range(k), k + 1, k + 3).reshape(R, *lead, cols)
        return jnp.moveaxis(matrix.reshape(*lead, R, cols), -2, 0)

    def from_ranks(parts):
        if whole_heads:
            parts = parts.reshape(B, X, -1, Z, rows_dev)
            return parts.transpose(2, 0, 3, 1, 4).reshape(-1, D)
        return parts.transpose(1, 0, 2).reshape(-1, D)

    def mine(vector):
        return lax.dynamic_index_in_dim(to_ranks(vector), rank, 0, keepdims=False)

    gain_one, q_weight, k_weight, v_weight = lax.optimization_barrier((gain_one, q_weight, k_weight, v_weight))
    qkv_parts = jnp.concatenate([to_ranks(q_weight), to_ranks(k_weight), to_ranks(v_weight)], axis=2)
    qkv_mine = lax.all_to_all(qkv_parts, PLANE, split_axis=0, concat_axis=0, tiled=True)
    qkv_mine = qkv_mine.reshape(D // Z, 3 * cols)

    def feature_rows(mine):
        full = lax.all_gather(mine, "z", axis=0, tiled=True)
        return full.reshape(Z, B, X, rows_dev, -1).transpose(1, 0, 2, 3, 4).reshape(D, -1)

    weight_kv = feature_rows(qkv_mine[:, cols:])
    bias_kv = jnp.concatenate([jnp.zeros((cols,), single), mine(bias_v)])
    normed_low = layer_norm(local, gain_one, bias_one).astype(bfloat)
    fast = (B, X) == (4, 2)

    def gather_plane(rows, cid, name):
        if fast:
            return plane_gather(rows, (), [], None, cid, name)[0]
        return lax.all_gather(rows, PLANE, axis=0, tiled=True)

    def gather_plane_dot(rows, weight, shift, out_type, turned, cid, name):
        if fast:
            return gather_dot(rows, weight, shift, out_type, turned, cid, name)
        rows = lax.all_gather(rows, PLANE, axis=0, tiled=True)
        return rows, ((dot_nt if turned else dot)(rows, weight) + shift).astype(out_type)

    def reduce_plane(left, weight, turned, cid, name):
        if fast:
            return dot_reduce(left, weight, turned, cid, name)
        terms = (dot_nt if turned else dot)(left, weight).astype(bfloat)
        return lax.psum_scatter(terms, PLANE, scatter_dimension=0, tiled=True).astype(single)

    normed_all = gather_plane(normed_low, 0, "gather_normed")
    normed_all, weight_kv, query_mine, o_weight, fc1_weight, fc2_weight = lax.optimization_barrier(
        (normed_all, weight_kv, qkv_mine[:, :cols], o_weight, fc1_weight, fc2_weight)
    )
    weight_q = feature_rows(query_mine)
    if whole_heads:
        weight_o = lax.all_gather(o_weight, "z", axis=0, tiled=True)
    else:
        weight_o = lax.dynamic_slice_in_dim(lax.all_gather(o_weight, ALL, axis=0, tiled=True), rank * cols, cols, 0)
    weight_up = lax.all_gather(fc1_weight, "z", axis=1, tiled=True)
    weight_down = lax.all_gather(fc2_weight, "z", axis=0, tiled=True)
    key_value = (dot(normed_all, weight_kv) + bias_kv).astype(bfloat)
    up = [(i, i + 1) for i in range(Z - 1)]
    down = [(i + 1, i) for i in range(Z - 1)]
    cotangent = out_grad[0].astype(single) * (group_tok / active_total)
    branch_grad = (active * cotangent).astype(bfloat)
    down_b_grad = column_sums(branch_grad)
    key_value, branch_grad = lax.optimization_barrier((key_value, branch_grad))
    before = lax.ppermute(key_value, "z", up)
    branch_all = gather_plane(branch_grad, 7, "gather_branch")
    branch_all, late_normed = lax.optimization_barrier((branch_all, normed_all))
    query = (dot(late_normed, weight_q) + mine(bias_q)).astype(bfloat)
    before, query = lax.optimization_barrier((before, query))
    starts = starts.reshape(B * span, 1)
    context = attention_forward(starts, query, key_value, before, B)

    attended = reduce_plane(context, weight_o, False, 1, "attended") + bias_o
    middle = local + active * attended
    normed_two = layer_norm(middle, gain_two, bias_two).astype(bfloat)
    two_all, hidden_pre = gather_plane_dot(normed_two, weight_up, bias_up[None], single, False, 2, "up")
    gelu_value, gelu_pull = jax.vjp(partial(jax.nn.gelu, approximate=True), hidden_pre)
    hidden = gelu_value.astype(bfloat)
    hidden_grad = dot_nt(branch_all, weight_down)
    pre_grad = gelu_pull(hidden_grad)[0].astype(bfloat)
    down_w_grad = dot_tn(hidden, branch_all).astype(bfloat)
    up_w_grad = dot_tn(two_all, pre_grad).astype(bfloat)
    up_b_grad = column_sums(pre_grad)
    hidden, pre_grad, down_w_grad, up_w_grad = lax.optimization_barrier((hidden, pre_grad, down_w_grad, up_w_grad))
    normed_two_grad = reduce_plane(pre_grad, weight_up, True, 3, "up_grad")
    down_w_shard = lax.psum_scatter(down_w_grad, "z", scatter_dimension=0, tiled=True)
    up_w_shard = lax.psum_scatter(up_w_grad, "z", scatter_dimension=1, tiled=True)

    middle_part, gain_two_grad, bias_two_grad = norm_backward(middle, normed_two_grad, gain_two)
    middle_grad = cotangent + middle_part
    attended_grad = (active * middle_grad).astype(bfloat)
    out_b_grad = column_sums(attended_grad)
    attended_all, context_grad = gather_plane_dot(
        attended_grad, weight_o, jnp.zeros((1, cols), single), bfloat, True, 5, "attended_grad"
    )
    context_grad, down_w_shard = lax.optimization_barrier((context_grad, down_w_shard))
    out_w_grad = dot_tn(context, attended_all)
    query_grad, edge, pair = attention_backward(starts, query, key_value, before, context_grad, B)
    hidden, edge, pair = lax.optimization_barrier((hidden, edge, pair))
    after = lax.ppermute(edge, "z", down)
    branch = reduce_plane(hidden, weight_down, False, 4, "down")
    branch, after, up_w_shard = lax.optimization_barrier((branch, after, up_w_shard))
    outputs = middle + active * (branch + bias_down)
    pair_grad = (pair + after.astype(single)).astype(bfloat)
    qkv_grad = jnp.concatenate([query_grad, pair_grad], axis=1)
    weight_qkv = jnp.concatenate([weight_q, weight_kv], axis=1)
    normed_grad = reduce_plane(qkv_grad, weight_qkv, True, 6, "qkv_grad")
    qkv_w_grad = dot_tn(normed_all, qkv_grad)
    qkv_b_grad = column_sums(qkv_grad)
    input_part, gain_one_grad, bias_one_grad = norm_backward(local, normed_grad, gain_one)
    input_grad = middle_grad + input_part

    def sum_to_owners(vectors, axes, parts):
        split = jnp.concatenate([v.reshape(parts, -1) for v in vectors], axis=1)
        summed = jnp.sum(lax.all_to_all(split, axes, split_axis=0, concat_axis=0, tiled=True), axis=0)
        widths = [v.shape[0] // parts for v in vectors]
        return [summed[sum(widths[:i]) : sum(widths[: i + 1])] for i in range(len(widths))]

    qkv_w_grad = qkv_w_grad.astype(bfloat).reshape(B, Z, X, rows_dev, 3 * cols)
    qkv_w_grad = qkv_w_grad.transpose(1, 0, 2, 3, 4).reshape(D, 3 * cols)
    qkv_w_grad = lax.psum_scatter(qkv_w_grad, "z", scatter_dimension=0, tiled=True)
    qkv_w_grad = lax.all_to_all(qkv_w_grad.reshape(R, rows_dev, 3 * cols), PLANE, split_axis=0, concat_axis=0, tiled=True)
    qkv_w_grad = qkv_w_grad.astype(single)
    q_w_shard, k_w_shard, v_w_shard = [from_ranks(qkv_w_grad[..., i * cols : (i + 1) * cols]) for i in range(3)]
    if whole_heads:
        out_w_shard = lax.psum_scatter(out_w_grad.astype(bfloat), "z", scatter_dimension=0, tiled=True).astype(single)
        q_b_shard, v_b_shard, up_b_shard = sum_to_owners([qkv_b_grad[:cols], qkv_b_grad[2 * cols :], up_b_grad], "z", Z)
    else:

        def placed(rows):
            full = jnp.zeros((D,) + rows.shape[1:], rows.dtype)
            full = lax.dynamic_update_slice_in_dim(full, rows, rank * cols, 0)
            return lax.psum_scatter(full, ALL, scatter_dimension=0, tiled=True).astype(single)

        out_w_shard = placed(out_w_grad.astype(bfloat))
        q_b_shard = placed(qkv_b_grad[:cols])
        v_b_shard = placed(qkv_b_grad[2 * cols :])
        [up_b_shard] = sum_to_owners([up_b_grad], "z", Z)
    sums = sum_to_owners(
        [gain_one_grad, bias_one_grad, out_b_grad, gain_two_grad, bias_two_grad, down_b_grad], ALL, R * Z
    )
    return (
        outputs.astype(bfloat)[None],
        input_grad.astype(bfloat)[None],
        sums[0],
        sums[1],
        q_w_shard,
        q_b_shard,
        k_w_shard,
        v_w_shard,
        v_b_shard,
        out_w_shard,
        sums[2],
        sums[3],
        sums[4],
        up_w_shard.astype(single),
        up_b_shard,
        down_w_shard.astype(single),
        sums[5],
    )


def solution(mesh):
    groups, parts = mesh.shape["batch"], mesh.shape["seq"]
    inner = Mesh(mesh.devices.reshape(groups, SPANS, parts // SPANS), ("b", "z", "x"))
    token = P("b", ("z", "x"), None)
    vector = P(ALL)
    rows = P(ALL, None)
    columns = P(None, ALL)
    return jax.shard_map(
        on_device,
        mesh=inner,
        in_specs=(
            token,
            P("b", None),
            P("b", None),
            P(),
            token,
            vector,
            vector,
            rows,
            vector,
            rows,
            rows,
            vector,
            rows,
            vector,
            vector,
            vector,
            columns,
            vector,
            rows,
            vector,
        ),
        out_specs=(
            token,
            token,
            vector,
            vector,
            rows,
            vector,
            rows,
            rows,
            vector,
            rows,
            vector,
            vector,
            vector,
            columns,
            vector,
            rows,
            vector,
        ),
        check_vma=False,
    )
```

```python
import functools
from functools import partial

import jax
import jax.numpy as jnp
from jax import lax
from jax.experimental import pallas as pl
from jax.experimental.pallas import tpu as pltpu
from jax.sharding import Mesh
from jax.sharding import PartitionSpec as P

HEAD_DIM = 64
SPANS = 4

bfloat = jnp.bfloat16
single = jnp.float32

PLANE = ("b", "x")
ALL = ("b", "z", "x")
MESH = pl.DeviceIdType.MESH
TILE = 512

def plane_place():
    b, z, x = lax.axis_index("b"), lax.axis_index("z"), lax.axis_index("x")
    sib_b = b + 1 - 2 * lax.rem(b, 2)
    far_b = lax.rem(b + 2, 4)
    far_sib_b = lax.rem(sib_b + 2, 4)
    ids = {"s": (sib_b, z, x), "x": (b, z, 1 - x), "y": (far_b, z, x)}
    ranks = {
        "o": b * 2 + x,
        "s": sib_b * 2 + x,
        "x": b * 2 + 1 - x,
        "xs": sib_b * 2 + 1 - x,
        "y": far_b * 2 + x,
        "ys": far_sib_b * 2 + x,
        "d": far_b * 2 + 1 - x,
        "ds": far_sib_b * 2 + 1 - x,
    }
    return ids, ranks

def greet(ids):
    barrier = pltpu.get_barrier_semaphore()
    for device in ids.values():
        pl.semaphore_signal(barrier, inc=1, device_id=device, device_id_type=MESH)
    pl.semaphore_wait(barrier, len(ids))

def tiles(lo, hi, body):
    def step(i, _):
        body(pl.ds(pl.multiple_of(i * TILE, TILE), TILE))
        return 0
    lax.fori_loop(lo // TILE, hi // TILE, step, 0)

def gather_kernel(body_of, n_in, n_out, x_ref, *refs):
    ins = refs[:n_in]; all_ref = refs[n_in]; outs = refs[n_in + 1 : n_in + 1 + n_out]
    held, send, recv, keep = refs[n_in + 1 + n_out :]
    ids, at = plane_place()
    half = x_ref.shape[0] // 2
    parts = (pl.ds(0, half), pl.ds(half, half))
    greet(ids)
    count = [0]
    started = []
    def ship(src, dst, to):
        n = count[0]; count[0] += 1
        c = pltpu.make_async_remote_copy(src_ref=src, dst_ref=dst, send_sem=send.at[n], recv_sem=recv.at[n], device_id=ids[to], device_id_type=MESH)
        c.start(); started.append(c)
        return c
    own = at["o"]
    x0 = ship(x_ref.at[parts[0]], held.at[own, parts[0]], "x")
    y1 = ship(x_ref.at[parts[1]], held.at[own, parts[1]], "y")
    x1 = ship(x_ref.at[parts[1]], held.at[own, parts[1]], "x")
    y0 = ship(x_ref.at[parts[0]], held.at[own, parts[0]], "y")
    s0 = ship(x_ref, held.at[own], "s")
    kept = []
    def done(rank, src):
        c = pltpu.make_async_copy(src, all_ref.at[rank], keep.at[len(kept)])
        c.start(); kept.append(c)
        if body_of is not None:
            body_of(rank, src, ins, outs)
    done(own, x_ref)
    s0.wait_recv()
    done(at["s"], held.at[at["s"]])
    x0.wait_recv()
    ry = ship(held.at[at["x"], parts[0]], held.at[at["x"], parts[0]], "y")
    y1.wait_recv()
    rx = ship(held.at[at["y"], parts[1]], held.at[at["y"], parts[1]], "x")
    x1.wait_recv()
    sx = ship(held.at[at["x"]], held.at[at["x"]], "s")
    y0.wait_recv()
    sy = ship(held.at[at["y"]], held.at[at["y"]], "s")
    done(at["x"], held.at[at["x"]])
    done(at["y"], held.at[at["y"]])
    sx.wait_recv()
    done(at["xs"], held.at[at["xs"]])
    sy.wait_recv()
    done(at["ys"], held.at[at["ys"]])
    ry.wait_recv(); rx.wait_recv()
    sd = ship(held.at[at["d"]], held.at[at["d"]], "s")
    done(at["d"], held.at[at["d"]])
    sd.wait_recv()
    done(at["ds"], held.at[at["ds"]])
    for c in started: c.wait_send()
    for c in kept: c.wait()

def vmem(n): return [pl.BlockSpec(memory_space=pltpu.VMEM)] * n

def plane_gather(x, ins, out_types, body_of, cid, name, ranks=8):
    tok, D = x.shape
    res = pl.pallas_call(
        functools.partial(gather_kernel, body_of, len(ins), len(out_types)),
        out_shape=[jax.ShapeDtypeStruct((ranks, tok, D), x.dtype), *out_types],
        in_specs=vmem(1 + len(ins)),
        out_specs=[pl.BlockSpec(memory_space=pl.ANY)] + vmem(len(out_types)),
        scratch_shapes=[pltpu.VMEM((ranks, tok, D), x.dtype), pltpu.SemaphoreType.DMA((10,)), pltpu.SemaphoreType.DMA((10,)), pltpu.SemaphoreType.DMA((8,))],
        compiler_params=pltpu.CompilerParams(collective_id=cid, has_side_effects=True, vmem_limit_bytes=60 << 20),
        cost_estimate=pl.CostEstimate(flops=1 << 30, bytes_accessed=128 << 20, transcendentals=0),
        name=name,
    )(x, *ins)
    return res[0].reshape(ranks * tok, D), *res[1:]

def gather_dot(x, w, bias, out_dtype, turned, cid, name):
    ranks, tok, D = 8, *x.shape
    N = w.shape[0] if turned else w.shape[1]
    tile = min(N, 512) if N % 512 == 0 else 256
    def body(rank, src, ins, outs):
        w_ref, b_ref = ins
        def step(i, _):
            cols = pl.ds(pl.multiple_of(i * tile, tile), tile)
            if turned:
                y = lax.dot_general(src[...], w_ref[cols, :], (((1,), (1,)), ((), ())), preferred_element_type=single)
            else:
                y = jnp.dot(src[...], w_ref[:, cols], preferred_element_type=single)
            outs[0][rank, :, cols] = (y + b_ref[:, cols]).astype(out_dtype)
            return 0
        lax.fori_loop(0, N // tile, step, 0)
    all_, y = plane_gather(x, (w, bias), [jax.ShapeDtypeStruct((ranks, tok, N), out_dtype)], body, cid, name)
    return all_, y.reshape(ranks * tok, N)

def reduce_kernel(turned, a_ref, w_ref, out_ref, sib_out, sib_in, stage, landed, send, recv):
    ids, at = plane_place()
    ranks, tok, _ = a_ref.shape
    D = out_ref.shape[1]
    mid = D // 2
    greet(ids)
    count = [0]; started = []
    def ship(src, dst, to):
        n = count[0]; count[0] += 1
        c = pltpu.make_async_remote_copy(src_ref=src, dst_ref=dst, send_sem=send.at[n], recv_sem=recv.at[n], device_id=ids[to], device_id_type=MESH)
        c.start(); started.append(c)
        return c
    def term(rank, cols):
        if turned:
            return lax.dot_general(a_ref[rank], w_ref[cols, :], (((1,), (1,)), ((), ())), preferred_element_type=single)
        return jnp.dot(a_ref[rank], w_ref[:, cols], preferred_element_type=single)
    order = ("d", "x", "y", "o")
    twin = {"d": "ds", "x": "xs", "y": "ys", "o": "s"}
    sib = []
    for j, d in enumerate(order):
        def fill(cols, j=j, d=d):
            sib_out[j, :, cols] = term(at[twin[d]], cols).astype(bfloat)
        tiles(0, D, fill)
        sib.append(ship(sib_out.at[j], sib_in.at[j], "s"))
    def pair(j, cols):
        return term(at[order[j]], cols) + sib_in[j, :, cols].astype(single)
    def local(h, cols):
        return pl.ds(pl.multiple_of(cols.start - h * mid, TILE), TILE)
    def put(j, h, extra=None):
        def fill(cols):
            value = pair(j, cols)
            if extra is not None:
                value = value + landed[extra, :, local(h, cols)].astype(single)
            stage[j, h, :, local(h, cols)] = value.astype(bfloat)
        tiles(h * mid, (h + 1) * mid, fill)
    sib[0].wait_recv()
    put(0, 0)
    d_a = ship(stage.at[0, 0], landed.at[0], "x")
    put(0, 1)
    d_b = ship(stage.at[0, 1], landed.at[1], "y")
    sib[1].wait_recv()
    put(1, 0)
    x_a = ship(stage.at[1, 0], landed.at[2], "x")
    sib[2].wait_recv()
    put(2, 1)
    y_b = ship(stage.at[2, 1], landed.at[3], "y")
    sib[3].wait_recv()
    def first(cols):
        out_ref[:, cols] = pair(3, cols)
    tiles(0, D, first)
    d_b.wait_recv()
    put(1, 1, extra=1)
    x_b = ship(stage.at[1, 1], landed.at[5], "x")
    d_a.wait_recv()
    put(2, 0, extra=0)
    y_a = ship(stage.at[2, 0], landed.at[4], "y")
    x_a.wait_recv(); y_b.wait_recv(); x_b.wait_recv(); y_a.wait_recv()
    for h, (n, m) in enumerate(((2, 4), (3, 5))):
        def add(cols, h=h, n=n, m=m):
            c = local(h, cols)
            out_ref[:, cols] = out_ref[:, cols] + landed[n, :, c].astype(single) + landed[m, :, c].astype(single)
        tiles(h * mid, (h + 1) * mid, add)
    for c in started: c.wait_send()

def dot_reduce(a, w, turned, cid, name):
    ranks = 8
    D = w.shape[0] if turned else w.shape[1]
    tok = a.shape[0] // ranks
    return pl.pallas_call(
        functools.partial(reduce_kernel, turned),
        out_shape=jax.ShapeDtypeStruct((tok, D), single),
        in_specs=vmem(2), out_specs=vmem(1)[0],
        scratch_shapes=[pltpu.VMEM((4, tok, D), bfloat), pltpu.VMEM((4, tok, D), bfloat), pltpu.VMEM((3, 2, tok, D // 2), bfloat), pltpu.VMEM((6, tok, D // 2), bfloat),
            pltpu.SemaphoreType.DMA((10,)), pltpu.SemaphoreType.DMA((10,))],
        compiler_params=pltpu.CompilerParams(collective_id=cid, has_side_effects=True, vmem_limit_bytes=60 << 20),
        cost_estimate=pl.CostEstimate(flops=1 << 30, bytes_accessed=128 << 20, transcendentals=0),
        name=name,
    )(a.reshape(ranks, tok, -1), w)


def dot(left, right):
    return jnp.dot(left, right, preferred_element_type=single)


def dot_tn(left, right):
    return lax.dot_general(left, right, (((0,), (0,)), ((), ())), preferred_element_type=single)


def dot_nt(left, right):
    return lax.dot_general(left, right, (((1,), (1,)), ((), ())), preferred_element_type=single)


def layer_norm(values, gain_vec, shift_vec):
    center = jnp.mean(values, axis=-1, keepdims=True)
    centered = values - center
    spread = jnp.mean(centered * centered, axis=-1, keepdims=True)
    return centered * lax.rsqrt(spread + 1e-05) * gain_vec + shift_vec


def column_sums(matrix):
    return jnp.sum(matrix.astype(single), axis=0)


def shipper(send, recv, ids):
    started = []
    def ship(src, dst, to):
        n = len(started)
        copy = pltpu.make_async_remote_copy(
            src_ref=src, dst_ref=dst, send_sem=send.at[n], recv_sem=recv.at[n], device_id=ids[to], device_id_type=MESH
        )
        copy.start()
        started.append(copy)
        return copy
    return ship, started

def ffn_kernel(x_ref, bg_ref, w1_ref, w2_ref, b_ref, hid_ref, pb_ref, r_ref, down_ref, up_ref,
               held, bg, pg_ref, sib_out, sib_in, stage, landed, rows_out, send, recv, keep, load, store):
    ids, at = plane_place()
    tok, D = x_ref.shape
    F = w1_ref.shape[1]
    mid = D // 2
    half = tok // 2
    parts = (pl.ds(0, half), pl.ds(half, half))
    own = at["o"]
    loads = {}
    for n, name in enumerate(at):
        loads[name] = pltpu.make_async_copy(bg_ref.at[at[name]], bg.at[at[name]], load.at[n])
        loads[name].start()
    kept = pltpu.make_async_copy(x_ref, held.at[own], keep)
    kept.start()
    pb_ref[...] = jnp.zeros_like(pb_ref)
    greet(ids)
    ship, started = shipper(send, recv, ids)
    x0 = ship(x_ref.at[parts[0]], held.at[own, parts[0]], "x")
    y1 = ship(x_ref.at[parts[1]], held.at[own, parts[1]], "y")
    x1 = ship(x_ref.at[parts[1]], held.at[own, parts[1]], "x")
    y0 = ship(x_ref.at[parts[0]], held.at[own, parts[0]], "y")
    s0 = ship(x_ref, held.at[own], "s")

    def units(name):
        rank = at[name]
        src = x_ref if name == "o" else held.at[rank]
        loads[name].wait()
        def body(cols):
            pre = jnp.dot(src[...], w1_ref[:, cols], preferred_element_type=single) + b_ref[:, cols]
            square = pre * pre
            bend = jnp.tanh(0.7978845608028654 * (pre + 0.044715 * (pre * square)))
            rise = 0.5 * (1.0 + bend)
            hid_ref[rank, :, cols] = (pre * rise).astype(bfloat)
            slope = rise + (0.5 * 0.7978845608028654) * pre * (1.0 - bend * bend) * (1.0 + 3 * 0.044715 * square)
            grad = (dot_nt(bg[rank], w2_ref[cols, :]) * slope).astype(bfloat)
            pg_ref[rank, :, cols] = grad
            pb_ref[:, cols] += jnp.sum(grad.astype(single), axis=0, keepdims=True)
        tiles(0, F, body)

    def term(name, cols):
        return dot_nt(pg_ref[at[name]], w1_ref[cols, :])
    order = ("d", "x", "y", "o")
    twin = {"d": "ds", "x": "xs", "y": "ys", "o": "s"}
    def to_sibling(j):
        def fill(cols):
            sib_out[j, :, cols] = term(twin[order[j]], cols).astype(bfloat)
        tiles(0, D, fill)
        return ship(sib_out.at[j], sib_in.at[j], "s")
    def pair(j, cols):
        return term(order[j], cols) + sib_in[j, :, cols].astype(single)
    def local(h, cols):
        return pl.ds(pl.multiple_of(cols.start - h * mid, TILE), TILE)
    def put(j, h, extra=None):
        def fill(cols):
            value = pair(j, cols)
            if extra is not None:
                value = value + landed[extra, :, local(h, cols)].astype(single)
            stage[j, h, :, local(h, cols)] = value.astype(bfloat)
        tiles(h * mid, (h + 1) * mid, fill)

    units("o")
    s0.wait_recv()
    units("s")
    x0.wait_recv()
    ry = ship(held.at[at["x"], parts[0]], held.at[at["x"], parts[0]], "y")
    y1.wait_recv()
    rx = ship(held.at[at["y"], parts[1]], held.at[at["y"], parts[1]], "x")
    own_sib = to_sibling(3)
    x1.wait_recv()
    sx = ship(held.at[at["x"]], held.at[at["x"]], "s")
    y0.wait_recv()
    sy = ship(held.at[at["y"]], held.at[at["y"]], "s")
    units("x")
    sx.wait_recv()
    units("xs")
    x_sib = to_sibling(1)
    units("y")
    sy.wait_recv()
    units("ys")
    y_sib = to_sibling(2)
    ry.wait_recv()
    rx.wait_recv()
    sd = ship(held.at[at["d"]], held.at[at["d"]], "s")
    x_sib.wait_recv()
    put(1, 0)
    x_a = ship(stage.at[1, 0], landed.at[2], "x")
    y_sib.wait_recv()
    put(2, 1)
    y_b = ship(stage.at[2, 1], landed.at[3], "y")
    sd.wait_recv()
    units("ds")
    d_sib = to_sibling(0)
    units("d")
    d_sib.wait_recv()
    put(0, 0)
    d_a = ship(stage.at[0, 0], landed.at[0], "x")
    put(0, 1)
    d_b = ship(stage.at[0, 1], landed.at[1], "y")
    own_sib.wait_recv()
    def first(cols):
        r_ref[:, cols] = pair(3, cols)
    tiles(0, D, first)

    kept.wait()
    wide = rows_out.shape[1]
    def grads(out_ref, count, value):
        def step(i, _):
            slot = lax.rem(i, 2)
            here = pl.ds(pl.multiple_of(i * wide, wide), wide)
            copy = pltpu.make_async_copy(rows_out.at[slot, :, pl.ds(0, out_ref.shape[1])], out_ref.at[here], store.at[slot])
            @pl.when(i >= 2)
            def _():
                copy.wait()
            rows_out[slot, :, : out_ref.shape[1]] = value(here).astype(bfloat)
            copy.start()
            return 0
        lax.fori_loop(0, count, step, 0)
        for slot in range(2):
            pltpu.make_async_copy(rows_out.at[slot, :, pl.ds(0, out_ref.shape[1])], out_ref.at[pl.ds(0, wide)], store.at[slot]).wait()
    ranks = held.shape[0]
    grads(down_ref, F // wide, lambda cols: dot_tn(hid_ref[:, :, cols].reshape(ranks * tok, wide), bg[...].reshape(ranks * tok, D)))
    d_b.wait_recv()
    put(1, 1, extra=1)
    x_b = ship(stage.at[1, 1], landed.at[5], "x")
    d_a.wait_recv()
    put(2, 0, extra=0)
    y_a = ship(stage.at[2, 0], landed.at[4], "y")
    grads(up_ref, D // wide, lambda cols: dot_tn(held[:, :, cols].reshape(ranks * tok, wide), pg_ref[...].reshape(ranks * tok, F)))
    for copy in (x_a, y_b, x_b, y_a):
        copy.wait_recv()
    for h, (n, m) in enumerate(((2, 4), (3, 5))):
        def add(cols, h=h, n=n, m=m):
            c = local(h, cols)
            r_ref[:, cols] = r_ref[:, cols] + landed[n, :, c].astype(single) + landed[m, :, c].astype(single)
        tiles(h * mid, (h + 1) * mid, add)
    for copy in started:
        copy.wait_send()

def feed_forward(x, bg, w1, w2, bias, cid):
    ranks = 8
    tok, D = x.shape
    F = w1.shape[1]
    anywhere = pl.BlockSpec(memory_space=pl.ANY)
    inside = pl.BlockSpec(memory_space=pltpu.VMEM)
    hid, pb, r, down, up = pl.pallas_call(
        ffn_kernel,
        out_shape=[
            jax.ShapeDtypeStruct((ranks, tok, F), bfloat),
            jax.ShapeDtypeStruct((1, F), single),
            jax.ShapeDtypeStruct((tok, D), single),
            jax.ShapeDtypeStruct((F, D), bfloat),
            jax.ShapeDtypeStruct((D, F), bfloat),
        ],
        in_specs=[inside, anywhere, inside, inside, inside],
        out_specs=[inside, inside, inside, anywhere, anywhere],
        scratch_shapes=[
            pltpu.VMEM((ranks, tok, D), bfloat),
            pltpu.VMEM((ranks, tok, D), bfloat),
            pltpu.VMEM((ranks, tok, F), bfloat),
            pltpu.VMEM((4, tok, D), bfloat),
            pltpu.VMEM((4, tok, D), bfloat),
            pltpu.VMEM((3, 2, tok, D // 2), bfloat),
            pltpu.VMEM((6, tok, D // 2), bfloat),
            pltpu.VMEM((2, 128, D), bfloat),
            pltpu.SemaphoreType.DMA((20,)),
            pltpu.SemaphoreType.DMA((20,)),
            pltpu.SemaphoreType.DMA,
            pltpu.SemaphoreType.DMA((8,)),
            pltpu.SemaphoreType.DMA((2,)),
        ],
        compiler_params=pltpu.CompilerParams(collective_id=cid, has_side_effects=True, vmem_limit_bytes=63 << 20),
        cost_estimate=pl.CostEstimate(flops=1 << 30, bytes_accessed=256 << 20, transcendentals=0),
        name="feed_forward",
    )(x, bg.reshape(ranks, tok, D), w1, w2, bias)
    return hid.reshape(ranks * tok, F), pb[0], r, down, up


def windows(span):
    block = span // 2
    return [(i * block, i * block + block + span) for i in range(2)]

def key_window(before, own, lo, hi, span):
    return jnp.concatenate([before[lo:span], own[0 : hi - span]], axis=0)

def hidden_bias(start_ref, i, block, lo, hi, span):
    rows = span + i * block + lax.broadcasted_iota(jnp.int32, (block, hi - lo), 0)
    keys = lo + lax.broadcasted_iota(jnp.int32, (block, hi - lo), 1)
    start = start_ref[i * block : (i + 1) * block, :]
    return jnp.where((keys >= start) & (keys <= rows), 0.0, -1e30).astype(single)

def attend_kernel(start_ref, q_ref, k_ref, v_ref, kb_ref, vb_ref, out_ref):
    span, cols = q_ref.shape
    block = span // 2
    lane = lax.broadcasted_iota(jnp.int32, (block, cols), 1) // HEAD_DIM
    for i, (lo, hi) in enumerate(windows(span)):
        rows = pl.ds(i * block, block)
        bias = hidden_bias(start_ref, i, block, lo, hi, span)
        keys = key_window(kb_ref, k_ref, lo, hi, span)
        vals = key_window(vb_ref, v_ref, lo, hi, span)
        query = q_ref[rows, :] * jnp.asarray(HEAD_DIM ** (-0.5), bfloat)
        def head(h, total):
            mine = lane == h
            scores = dot_nt(jnp.where(mine, query, 0), keys) + bias
            weights = jnp.exp(scores - jnp.max(scores, axis=1, keepdims=True))
            part = jnp.dot(weights.astype(bfloat), vals, preferred_element_type=single)
            part = part * (1.0 / jnp.sum(weights, axis=1, keepdims=True))
            return jnp.where(mine, part, total)
        total = lax.fori_loop(0, cols // HEAD_DIM, head, jnp.zeros((block, cols), single), unroll=True)
        out_ref[rows, :] = total.astype(bfloat)

def attend_back_kernel(start_ref, q_ref, k_ref, v_ref, kb_ref, vb_ref, do_ref, dq_ref, edge_ref, pair_ref, dk, dv):
    span, cols = q_ref.shape
    block = span // 2
    scale = HEAD_DIM ** (-0.5)
    dk[...] = jnp.zeros_like(dk)
    dv[...] = jnp.zeros_like(dv)
    lane = lax.broadcasted_iota(jnp.int32, (block, cols), 1) // HEAD_DIM
    for i, (lo, hi) in enumerate(windows(span)):
        rows = pl.ds(i * block, block)
        bias = hidden_bias(start_ref, i, block, lo, hi, span)
        keys = key_window(kb_ref, k_ref, lo, hi, span)
        vals = key_window(vb_ref, v_ref, lo, hi, span)
        query = q_ref[rows, :] * jnp.asarray(scale, bfloat)
        grad = do_ref[rows, :]
        def head(h, total):
            mine = lane == h
            query_h = jnp.where(mine, query, 0)
            grad_h = jnp.where(mine, grad, 0)
            scores = dot_nt(query_h, keys) + bias
            weights = jnp.exp(scores - jnp.max(scores, axis=1, keepdims=True))
            probs = weights * (1.0 / jnp.sum(weights, axis=1, keepdims=True))
            prob_grad = dot_nt(grad_h, vals)
            row_dot = jnp.sum(probs * prob_grad, axis=1, keepdims=True)
            score_grad = (probs * (prob_grad - row_dot)).astype(bfloat)
            dv[lo:hi, :] += dot_tn(probs.astype(bfloat), grad_h)
            dk[lo:hi, :] += dot_tn(score_grad, query_h)
            part = jnp.dot(score_grad, keys, preferred_element_type=single)
            return jnp.where(mine, part, total)
        total = lax.fori_loop(0, cols // HEAD_DIM, head, jnp.zeros((block, cols), single), unroll=True)
        dq_ref[rows, :] = (total * scale).astype(bfloat)
    edge_ref[:, :cols] = dk[:span, :].astype(bfloat)
    edge_ref[:, cols:] = dv[:span, :].astype(bfloat)
    pair_ref[:, :cols] = dk[span:, :]
    pair_ref[:, cols:] = dv[span:, :]

def attention_specs(span, cols):
    def at(j):
        return pl.BlockSpec((span, cols), lambda g: (g, j))
    return [pl.BlockSpec((span, 1), lambda g: (g, 0)), at(0), at(0), at(1), at(0), at(1)]

def attend(starts, query, key_value, before, groups):
    span, cols = query.shape[0] // groups, query.shape[1]
    return pl.pallas_call(
        attend_kernel,
        grid=(groups,),
        out_shape=jax.ShapeDtypeStruct((groups * span, cols), bfloat),
        in_specs=attention_specs(span, cols),
        out_specs=pl.BlockSpec((span, cols), lambda g: (g, 0)),
        compiler_params=pltpu.CompilerParams(vmem_limit_bytes=60 << 20),
        name="attend",
    )(starts, query, key_value, key_value, before, before)

def attend_back(starts, query, key_value, before, grad, groups):
    span, cols = query.shape[0] // groups, query.shape[1]
    rows = groups * span
    return pl.pallas_call(
        attend_back_kernel,
        grid=(groups,),
        out_shape=[jax.ShapeDtypeStruct((rows, cols), bfloat), jax.ShapeDtypeStruct((rows, 2 * cols), bfloat), jax.ShapeDtypeStruct((rows, 2 * cols), single)],
        in_specs=attention_specs(span, cols) + [pl.BlockSpec((span, cols), lambda g: (g, 0))],
        out_specs=[pl.BlockSpec((span, cols), lambda g: (g, 0))] + [pl.BlockSpec((span, 2 * cols), lambda g: (g, 0))] * 2,
        scratch_shapes=[pltpu.VMEM((2 * span, cols), single)] * 2,
        compiler_params=pltpu.CompilerParams(vmem_limit_bytes=60 << 20),
        name="attend_back",
    )(starts, query, key_value, key_value, before, before, grad)


def attention_heads(starts, query, key_value, before, groups):
    span, cols = query.shape[0] // groups, query.shape[1]
    both = jnp.concatenate([before.reshape(groups, span, -1), key_value.reshape(groups, span, -1)], axis=1)
    key_two, value_two = [both[..., i * cols : (i + 1) * cols].reshape(groups, 2 * span, -1, HEAD_DIM) for i in (0, 1)]
    query = query.reshape(groups, span, -1, HEAD_DIM)
    keys = jnp.arange(2 * span)[None, None, :]
    rows = span + jnp.arange(span)[None, :, None]
    allowed = (keys >= starts.reshape(groups, span, 1)) & (keys <= rows)
    scores = jnp.einsum("gqhd,gkhd->ghqk", query, key_two, preferred_element_type=single) * HEAD_DIM ** (-0.5)
    scores = jnp.where(allowed[:, None], scores, -1e30)
    weights = jnp.exp(scores - jnp.max(scores, axis=-1, keepdims=True))
    return query, key_two, value_two, weights / jnp.sum(weights, axis=-1, keepdims=True)


def attention_forward(starts, query, key_value, before, groups):
    if query.shape[1] % 128 == 0:
        return attend(starts, query, key_value, before, groups)
    _, _, value_two, probs = attention_heads(starts, query, key_value, before, groups)
    context = jnp.einsum("ghqk,gkhd->gqhd", probs.astype(bfloat), value_two, preferred_element_type=single)
    return context.astype(bfloat).reshape(query.shape)


def attention_backward(starts, query, key_value, before, grad, groups):
    if query.shape[1] % 128 == 0:
        return attend_back(starts, query, key_value, before, grad, groups)
    rows = query.shape[0]
    query, key_two, value_two, probs = attention_heads(starts, query, key_value, before, groups)
    span = query.shape[1]
    grad = grad.reshape(query.shape)
    prob_grad = jnp.einsum("gqhd,gkhd->ghqk", grad, value_two, preferred_element_type=single)
    row_dot = jnp.sum(probs * prob_grad, axis=-1, keepdims=True)
    score_grad = (probs * (prob_grad - row_dot)).astype(bfloat)
    query_grad = jnp.einsum("ghqk,gkhd->gqhd", score_grad, key_two, preferred_element_type=single) * HEAD_DIM ** (-0.5)
    key_grad = jnp.einsum("ghqk,gqhd->gkhd", score_grad, query, preferred_element_type=single) * HEAD_DIM ** (-0.5)
    value_grad = jnp.einsum("ghqk,gqhd->gkhd", probs.astype(bfloat), grad, preferred_element_type=single)
    pair = jnp.concatenate([t.reshape(groups, 2 * span, -1) for t in (key_grad, value_grad)], axis=2)
    edge, pair = [t.reshape(rows, -1) for t in (pair[:, :span].astype(bfloat), pair[:, span:])]
    return query_grad.astype(bfloat).reshape(rows, -1), edge, pair


def norm_backward(values, out_grad, gain_vec):
    center = jnp.mean(values, axis=-1, keepdims=True)
    centered = values - center
    rs = lax.rsqrt(jnp.mean(centered * centered, axis=-1, keepdims=True) + 1e-05)
    xhat = centered * rs
    g = out_grad * gain_vec
    part = rs * (g - jnp.mean(g, axis=-1, keepdims=True) - xhat * jnp.mean(g * xhat, axis=-1, keepdims=True))
    return part, jnp.sum(out_grad * xhat, axis=0), jnp.sum(out_grad, axis=0)


def on_device(
    inputs,
    exit_layers,
    lengths,
    layer_index,
    out_grad,
    ln1_gain,
    ln1_bias,
    q_weight,
    q_bias,
    k_weight,
    v_weight,
    v_bias,
    o_weight,
    o_bias,
    ln2_gain,
    ln2_bias,
    fc1_weight,
    fc1_bias,
    fc2_weight,
    fc2_bias,
):
    B, Z, X = lax.axis_size("b"), lax.axis_size("z"), lax.axis_size("x")
    R = B * X
    local = inputs[0].astype(single)
    tok, D = local.shape
    span = X * tok
    group_tok = Z * span
    at_z, at_x = lax.axis_index("z"), lax.axis_index("x")
    rank = lax.axis_index("b") * X + at_x
    rows_dev = q_weight.shape[0]
    cols = D // R
    heads = cols // HEAD_DIM
    whole_heads = rows_dev % HEAD_DIM == 0

    group_active = (exit_layers[0] > layer_index[0]).astype(single)
    active_total = jnp.sum(group_active)
    active = lax.dynamic_slice_in_dim(group_active, at_z * span + at_x * tok, tok, 0)[:, None]

    count = lengths.shape[1]
    upto = jnp.arange(count)[:, None] <= jnp.arange(count)[None, :]
    small = [ln1_gain, ln1_bias, q_bias, v_bias, o_bias, ln2_gain, ln2_bias, fc2_bias]
    pack = jnp.concatenate([v.astype(single) for v in (*small, fc1_bias, lengths[0])])
    pad = -pack.shape[0] % 128
    pack = jnp.concatenate([pack, jnp.zeros((pad,), single)])
    pack = lax.all_to_all(jnp.broadcast_to(pack, (R * Z, pack.shape[0])), ALL, split_axis=0, concat_axis=0, tiled=True)
    vectors = [pack[:, i * rows_dev : (i + 1) * rows_dev].reshape(-1) for i in range(len(small))]
    gain_one, bias_one, bias_q, bias_v, bias_o, gain_two, bias_two, bias_down = vectors
    pack = pack.reshape(B, Z, X, -1)[..., len(small) * rows_dev :]
    up_dev = fc1_bias.shape[0]
    bias_up = lax.dynamic_index_in_dim(
        pack[..., :up_dev].transpose(0, 2, 1, 3).reshape(R, Z * up_dev), rank, 0, keepdims=False
    )
    group_lengths = pack[:, 0, 0, up_dev : up_dev + count].astype(jnp.int32)
    ends = jnp.sum(jnp.where(upto, group_lengths[:, :, None], 0), axis=1)
    places = at_z * span + jnp.arange(span, dtype=jnp.int32)
    starts = jnp.max(jnp.where(ends[:, None, :] <= places[None, :, None], ends[:, None, :], 0), axis=2)
    starts = starts - (at_z - 1) * span

    def to_ranks(matrix):
        lead = matrix.shape[:-1]
        if whole_heads:
            matrix = matrix.reshape(*lead, B, Z, X, rows_dev)
            k = len(lead)
            return matrix.transpose(k, k + 2, *range(k), k + 1, k + 3).reshape(R, *lead, cols)
        return jnp.moveaxis(matrix.reshape(*lead, R, cols), -2, 0)

    def from_ranks(parts):
        if whole_heads:
            parts = parts.reshape(B, X, -1, Z, rows_dev)
            return parts.transpose(2, 0, 3, 1, 4).reshape(-1, D)
        return parts.transpose(1, 0, 2).reshape(-1, D)

    def mine(vector):
        return lax.dynamic_index_in_dim(to_ranks(vector), rank, 0, keepdims=False)

    gain_one, q_weight, k_weight, v_weight = lax.optimization_barrier((gain_one, q_weight, k_weight, v_weight))
    if whole_heads:
        weight_o = lax.all_gather(o_weight, "z", axis=0, tiled=True)
    else:
        weight_o = lax.dynamic_slice_in_dim(lax.all_gather(o_weight, ALL, axis=0, tiled=True), rank * cols, cols, 0)
    qkv_parts = jnp.concatenate([to_ranks(q_weight), to_ranks(k_weight), to_ranks(v_weight)], axis=2)
    qkv_mine = lax.all_to_all(qkv_parts, PLANE, split_axis=0, concat_axis=0, tiled=True)
    qkv_mine = qkv_mine.reshape(D // Z, 3 * cols)

    def feature_rows(mine):
        full = lax.all_gather(mine, "z", axis=0, tiled=True)
        return full.reshape(Z, B, X, rows_dev, -1).transpose(1, 0, 2, 3, 4).reshape(D, -1)

    weight_kv = feature_rows(qkv_mine[:, cols:])
    bias_kv = jnp.concatenate([jnp.zeros((cols,), single), mine(bias_v)])
    normed_low = layer_norm(local, gain_one, bias_one).astype(bfloat)
    normed_low, weight_o = lax.optimization_barrier((normed_low, weight_o))
    fast = (B, X) == (4, 2)

    def gather_plane(rows, cid, name):
        if fast:
            return plane_gather(rows, (), [], None, cid, name)[0]
        return lax.all_gather(rows, PLANE, axis=0, tiled=True)

    def gather_plane_dot(rows, weight, shift, out_type, turned, cid, name):
        if fast:
            return gather_dot(rows, weight, shift, out_type, turned, cid, name)
        rows = lax.all_gather(rows, PLANE, axis=0, tiled=True)
        return rows, ((dot_nt if turned else dot)(rows, weight) + shift).astype(out_type)

    def reduce_plane(left, weight, turned, cid, name):
        if fast:
            return dot_reduce(left, weight, turned, cid, name)
        terms = (dot_nt if turned else dot)(left, weight).astype(bfloat)
        return lax.psum_scatter(terms, PLANE, scatter_dimension=0, tiled=True).astype(single)

    normed_all = gather_plane(normed_low, 0, "gather_normed")
    normed_all, weight_kv, query_mine, fc1_weight, fc2_weight = lax.optimization_barrier(
        (normed_all, weight_kv, qkv_mine[:, :cols], fc1_weight, fc2_weight)
    )
    weight_q = feature_rows(query_mine)
    weight_up = lax.all_gather(fc1_weight, "z", axis=1, tiled=True)
    weight_down = lax.all_gather(fc2_weight, "z", axis=0, tiled=True)
    key_value = (dot(normed_all, weight_kv) + bias_kv).astype(bfloat)
    up = [(i, i + 1) for i in range(Z - 1)]
    down = [(i + 1, i) for i in range(Z - 1)]
    cotangent = out_grad[0].astype(single) * (group_tok / active_total)
    branch_grad = (active * cotangent).astype(bfloat)
    down_b_grad = column_sums(branch_grad)
    key_value, branch_grad = lax.optimization_barrier((key_value, branch_grad))
    before = lax.ppermute(key_value, "z", up)
    branch_all = gather_plane(branch_grad, 7, "gather_branch")
    branch_all, late_normed = lax.optimization_barrier((branch_all, normed_all))
    query = (dot(late_normed, weight_q) + mine(bias_q)).astype(bfloat)
    before, query = lax.optimization_barrier((before, query))
    starts = starts.reshape(B * span, 1)
    context = attention_forward(starts, query, key_value, before, B)

    attended = reduce_plane(context, weight_o, False, 1, "attended") + bias_o
    middle = local + active * attended
    normed_two = layer_norm(middle, gain_two, bias_two).astype(bfloat)
    if fast:
        hidden, up_b_grad, normed_two_grad, down_w_grad, up_w_grad = feed_forward(
            normed_two, branch_all, weight_up, weight_down, bias_up[None], 2
        )
    else:
        two_all = gather_plane(normed_two, 2, "gather_two")
        hidden_pre = dot(two_all, weight_up) + bias_up
        gelu_value, gelu_pull = jax.vjp(partial(jax.nn.gelu, approximate=True), hidden_pre)
        hidden = gelu_value.astype(bfloat)
        pre_grad = gelu_pull(dot_nt(branch_all, weight_down))[0].astype(bfloat)
        down_w_grad = dot_tn(hidden, branch_all).astype(bfloat)
        up_w_grad = dot_tn(two_all, pre_grad).astype(bfloat)
        up_b_grad = column_sums(pre_grad)
        normed_two_grad = reduce_plane(pre_grad, weight_up, True, 3, "up_grad")
    down_w_shard = lax.psum_scatter(down_w_grad, "z", scatter_dimension=0, tiled=True)
    up_w_shard = lax.psum_scatter(up_w_grad, "z", scatter_dimension=1, tiled=True)

    middle_part, gain_two_grad, bias_two_grad = norm_backward(middle, normed_two_grad, gain_two)
    middle_grad = cotangent + middle_part
    attended_grad = (active * middle_grad).astype(bfloat)
    out_b_grad = column_sums(attended_grad)
    attended_all, context_grad = gather_plane_dot(
        attended_grad, weight_o, jnp.zeros((1, cols), single), bfloat, True, 5, "attended_grad"
    )
    context_grad, down_w_shard = lax.optimization_barrier((context_grad, down_w_shard))
    out_w_grad = dot_tn(context, attended_all)
    query_grad, edge, pair = attention_backward(starts, query, key_value, before, context_grad, B)
    hidden, edge, pair = lax.optimization_barrier((hidden, edge, pair))
    after = lax.ppermute(edge, "z", down)
    branch = reduce_plane(hidden, weight_down, False, 4, "down")
    branch, after, up_w_shard = lax.optimization_barrier((branch, after, up_w_shard))
    outputs = middle + active * (branch + bias_down)
    pair_grad = (pair + after.astype(single)).astype(bfloat)
    qkv_grad = jnp.concatenate([query_grad, pair_grad], axis=1)
    weight_qkv = jnp.concatenate([weight_q, weight_kv], axis=1)
    normed_grad = reduce_plane(qkv_grad, weight_qkv, True, 6, "qkv_grad")
    qkv_w_grad = dot_tn(normed_all, qkv_grad)
    qkv_b_grad = column_sums(qkv_grad)
    input_part, gain_one_grad, bias_one_grad = norm_backward(local, normed_grad, gain_one)
    input_grad = middle_grad + input_part

    def sum_to_owners(vectors, axes, parts):
        split = jnp.concatenate([v.reshape(parts, -1) for v in vectors], axis=1)
        summed = jnp.sum(lax.all_to_all(split, axes, split_axis=0, concat_axis=0, tiled=True), axis=0)
        widths = [v.shape[0] // parts for v in vectors]
        return [summed[sum(widths[:i]) : sum(widths[: i + 1])] for i in range(len(widths))]

    qkv_w_grad = qkv_w_grad.astype(bfloat).reshape(B, Z, X, rows_dev, 3 * cols)
    qkv_w_grad = qkv_w_grad.transpose(1, 0, 2, 3, 4).reshape(D, 3 * cols)
    qkv_w_grad = lax.psum_scatter(qkv_w_grad, "z", scatter_dimension=0, tiled=True)
    qkv_w_grad = lax.all_to_all(qkv_w_grad.reshape(R, rows_dev, 3 * cols), PLANE, split_axis=0, concat_axis=0, tiled=True)
    qkv_w_grad = qkv_w_grad.astype(single)
    q_w_shard, k_w_shard, v_w_shard = [from_ranks(qkv_w_grad[..., i * cols : (i + 1) * cols]) for i in range(3)]
    if whole_heads:
        out_w_shard = lax.psum_scatter(out_w_grad.astype(bfloat), "z", scatter_dimension=0, tiled=True).astype(single)
        q_b_shard, v_b_shard, up_b_shard = sum_to_owners([qkv_b_grad[:cols], qkv_b_grad[2 * cols :], up_b_grad], "z", Z)
    else:

        def placed(rows):
            full = jnp.zeros((D,) + rows.shape[1:], rows.dtype)
            full = lax.dynamic_update_slice_in_dim(full, rows, rank * cols, 0)
            return lax.psum_scatter(full, ALL, scatter_dimension=0, tiled=True).astype(single)

        out_w_shard = placed(out_w_grad.astype(bfloat))
        q_b_shard = placed(qkv_b_grad[:cols])
        v_b_shard = placed(qkv_b_grad[2 * cols :])
        [up_b_shard] = sum_to_owners([up_b_grad], "z", Z)
    sums = sum_to_owners(
        [gain_one_grad, bias_one_grad, out_b_grad, gain_two_grad, bias_two_grad, down_b_grad], ALL, R * Z
    )
    return (
        outputs.astype(bfloat)[None],
        input_grad.astype(bfloat)[None],
        sums[0],
        sums[1],
        q_w_shard,
        q_b_shard,
        k_w_shard,
        v_w_shard,
        v_b_shard,
        out_w_shard,
        sums[2],
        sums[3],
        sums[4],
        up_w_shard.astype(single),
        up_b_shard,
        down_w_shard.astype(single),
        sums[5],
    )


def solution(mesh):
    groups, parts = mesh.shape["batch"], mesh.shape["seq"]
    inner = Mesh(mesh.devices.reshape(groups, SPANS, parts // SPANS), ("b", "z", "x"))
    token = P("b", ("z", "x"), None)
    vector = P(ALL)
    rows = P(ALL, None)
    columns = P(None, ALL)
    return jax.shard_map(
        on_device,
        mesh=inner,
        in_specs=(
            token,
            P("b", None),
            P("b", None),
            P(),
            token,
            vector,
            vector,
            rows,
            vector,
            rows,
            rows,
            vector,
            rows,
            vector,
            vector,
            vector,
            columns,
            vector,
            rows,
            vector,
        ),
        out_specs=(
            token,
            token,
            vector,
            vector,
            rows,
            vector,
            rows,
            rows,
            vector,
            rows,
            vector,
            vector,
            vector,
            columns,
            vector,
            rows,
            vector,
        ),
        check_vma=False,
    )
```

```python
import functools
from functools import partial

import jax
import jax.numpy as jnp
from jax import lax
from jax.experimental import pallas as pl
from jax.experimental.pallas import tpu as pltpu
from jax.sharding import Mesh
from jax.sharding import PartitionSpec as P

HEAD_DIM = 64
SPANS = 4

bfloat = jnp.bfloat16
single = jnp.float32

PLANE = ("b", "x")
ALL = ("b", "z", "x")
MESH = pl.DeviceIdType.MESH
TILE = 512

def plane_place():
    b, z, x = lax.axis_index("b"), lax.axis_index("z"), lax.axis_index("x")
    sib_b = b + 1 - 2 * lax.rem(b, 2)
    far_b = lax.rem(b + 2, 4)
    far_sib_b = lax.rem(sib_b + 2, 4)
    ids = {"s": (sib_b, z, x), "x": (b, z, 1 - x), "y": (far_b, z, x)}
    ranks = {
        "o": b * 2 + x,
        "s": sib_b * 2 + x,
        "x": b * 2 + 1 - x,
        "xs": sib_b * 2 + 1 - x,
        "y": far_b * 2 + x,
        "ys": far_sib_b * 2 + x,
        "d": far_b * 2 + 1 - x,
        "ds": far_sib_b * 2 + 1 - x,
    }
    return ids, ranks

def greet(ids):
    barrier = pltpu.get_barrier_semaphore()
    for device in ids.values():
        pl.semaphore_signal(barrier, inc=1, device_id=device, device_id_type=MESH)
    pl.semaphore_wait(barrier, len(ids))

def tiles(lo, hi, body):
    def step(i, _):
        body(pl.ds(pl.multiple_of(i * TILE, TILE), TILE))
        return 0
    lax.fori_loop(lo // TILE, hi // TILE, step, 0)

def gather_kernel(body_of, n_in, n_out, x_ref, *refs):
    ins = refs[:n_in]; all_ref = refs[n_in]; outs = refs[n_in + 1 : n_in + 1 + n_out]
    held, send, recv, keep = refs[n_in + 1 + n_out :]
    ids, at = plane_place()
    half = x_ref.shape[0] // 2
    parts = (pl.ds(0, half), pl.ds(half, half))
    greet(ids)
    count = [0]
    started = []
    def ship(src, dst, to):
        n = count[0]; count[0] += 1
        c = pltpu.make_async_remote_copy(src_ref=src, dst_ref=dst, send_sem=send.at[n], recv_sem=recv.at[n], device_id=ids[to], device_id_type=MESH)
        c.start(); started.append(c)
        return c
    own = at["o"]
    x0 = ship(x_ref.at[parts[0]], held.at[own, parts[0]], "x")
    y1 = ship(x_ref.at[parts[1]], held.at[own, parts[1]], "y")
    x1 = ship(x_ref.at[parts[1]], held.at[own, parts[1]], "x")
    y0 = ship(x_ref.at[parts[0]], held.at[own, parts[0]], "y")
    s0 = ship(x_ref, held.at[own], "s")
    kept = []
    def done(rank, src):
        c = pltpu.make_async_copy(src, all_ref.at[rank], keep.at[len(kept)])
        c.start(); kept.append(c)
        if body_of is not None:
            body_of(rank, src, ins, outs)
    done(own, x_ref)
    s0.wait_recv()
    done(at["s"], held.at[at["s"]])
    x0.wait_recv()
    ry = ship(held.at[at["x"], parts[0]], held.at[at["x"], parts[0]], "y")
    y1.wait_recv()
    rx = ship(held.at[at["y"], parts[1]], held.at[at["y"], parts[1]], "x")
    x1.wait_recv()
    sx = ship(held.at[at["x"]], held.at[at["x"]], "s")
    y0.wait_recv()
    sy = ship(held.at[at["y"]], held.at[at["y"]], "s")
    done(at["x"], held.at[at["x"]])
    done(at["y"], held.at[at["y"]])
    sx.wait_recv()
    done(at["xs"], held.at[at["xs"]])
    sy.wait_recv()
    done(at["ys"], held.at[at["ys"]])
    ry.wait_recv(); rx.wait_recv()
    sd = ship(held.at[at["d"]], held.at[at["d"]], "s")
    done(at["d"], held.at[at["d"]])
    sd.wait_recv()
    done(at["ds"], held.at[at["ds"]])
    for c in started: c.wait_send()
    for c in kept: c.wait()

def vmem(n): return [pl.BlockSpec(memory_space=pltpu.VMEM)] * n

def plane_gather(x, ins, out_types, body_of, cid, name, ranks=8):
    tok, D = x.shape
    res = pl.pallas_call(
        functools.partial(gather_kernel, body_of, len(ins), len(out_types)),
        out_shape=[jax.ShapeDtypeStruct((ranks, tok, D), x.dtype), *out_types],
        in_specs=vmem(1 + len(ins)),
        out_specs=[pl.BlockSpec(memory_space=pl.ANY)] + vmem(len(out_types)),
        scratch_shapes=[pltpu.VMEM((ranks, tok, D), x.dtype), pltpu.SemaphoreType.DMA((10,)), pltpu.SemaphoreType.DMA((10,)), pltpu.SemaphoreType.DMA((8,))],
        compiler_params=pltpu.CompilerParams(collective_id=cid, has_side_effects=True, vmem_limit_bytes=60 << 20),
        cost_estimate=pl.CostEstimate(flops=1 << 30, bytes_accessed=128 << 20, transcendentals=0),
        name=name,
    )(x, *ins)
    return res[0].reshape(ranks * tok, D), *res[1:]

def gather_dot(x, w, bias, out_dtype, turned, cid, name):
    ranks, tok, D = 8, *x.shape
    N = w.shape[0] if turned else w.shape[1]
    tile = min(N, 512) if N % 512 == 0 else 256
    def body(rank, src, ins, outs):
        w_ref, b_ref = ins
        def step(i, _):
            cols = pl.ds(pl.multiple_of(i * tile, tile), tile)
            if turned:
                y = lax.dot_general(src[...], w_ref[cols, :], (((1,), (1,)), ((), ())), preferred_element_type=single)
            else:
                y = jnp.dot(src[...], w_ref[:, cols], preferred_element_type=single)
            outs[0][rank, :, cols] = (y + b_ref[:, cols]).astype(out_dtype)
            return 0
        lax.fori_loop(0, N // tile, step, 0)
    all_, y = plane_gather(x, (w, bias), [jax.ShapeDtypeStruct((ranks, tok, N), out_dtype)], body, cid, name)
    return all_, y.reshape(ranks * tok, N)

def reduce_kernel(turned, pairs, *refs):
    left, right = refs[:pairs], refs[pairs : 2 * pairs]
    out_ref, sib_out, sib_in, stage, landed, send, recv = refs[2 * pairs :]
    ids, at = plane_place()
    D = out_ref.shape[1]
    mid = D // 2
    greet(ids)
    count = [0]; started = []
    def ship(src, dst, to):
        n = count[0]; count[0] += 1
        c = pltpu.make_async_remote_copy(src_ref=src, dst_ref=dst, send_sem=send.at[n], recv_sem=recv.at[n], device_id=ids[to], device_id_type=MESH)
        c.start(); started.append(c)
        return c
    def term(rank, cols):
        if turned:
            return sum(dot_nt(a[rank], w[cols, :]) for a, w in zip(left, right))
        return sum(dot(a[rank], w[:, cols]) for a, w in zip(left, right))
    order = ("d", "x", "y", "o")
    twin = {"d": "ds", "x": "xs", "y": "ys", "o": "s"}
    sib = []
    for j, d in enumerate(order):
        def fill(cols, j=j, d=d):
            sib_out[j, :, cols] = term(at[twin[d]], cols).astype(bfloat)
        tiles(0, D, fill)
        sib.append(ship(sib_out.at[j], sib_in.at[j], "s"))
    def pair(j, cols):
        return term(at[order[j]], cols) + sib_in[j, :, cols].astype(single)
    def local(h, cols):
        return pl.ds(pl.multiple_of(cols.start - h * mid, TILE), TILE)
    def put(j, h, extra=None):
        def fill(cols):
            value = pair(j, cols)
            if extra is not None:
                value = value + landed[extra, :, local(h, cols)].astype(single)
            stage[j, h, :, local(h, cols)] = value.astype(bfloat)
        tiles(h * mid, (h + 1) * mid, fill)
    sib[0].wait_recv()
    put(0, 0)
    d_a = ship(stage.at[0, 0], landed.at[0], "x")
    put(0, 1)
    d_b = ship(stage.at[0, 1], landed.at[1], "y")
    sib[1].wait_recv()
    put(1, 0)
    x_a = ship(stage.at[1, 0], landed.at[2], "x")
    sib[2].wait_recv()
    put(2, 1)
    y_b = ship(stage.at[2, 1], landed.at[3], "y")
    sib[3].wait_recv()
    def first(cols):
        out_ref[:, cols] = pair(3, cols)
    tiles(0, D, first)
    d_b.wait_recv()
    put(1, 1, extra=1)
    x_b = ship(stage.at[1, 1], landed.at[5], "x")
    d_a.wait_recv()
    put(2, 0, extra=0)
    y_a = ship(stage.at[2, 0], landed.at[4], "y")
    x_a.wait_recv(); y_b.wait_recv(); x_b.wait_recv(); y_a.wait_recv()
    for h, (n, m) in enumerate(((2, 4), (3, 5))):
        def add(cols, h=h, n=n, m=m):
            c = local(h, cols)
            out_ref[:, cols] = out_ref[:, cols] + landed[n, :, c].astype(single) + landed[m, :, c].astype(single)
        tiles(h * mid, (h + 1) * mid, add)
    for c in started: c.wait_send()

def dot_reduce(left, right, turned, cid, name):
    ranks = 8
    D = right[0].shape[0] if turned else right[0].shape[1]
    tok = left[0].size // left[0].shape[-1] // ranks
    return pl.pallas_call(
        functools.partial(reduce_kernel, turned, len(left)),
        out_shape=jax.ShapeDtypeStruct((tok, D), single),
        in_specs=vmem(2 * len(left)), out_specs=vmem(1)[0],
        scratch_shapes=[pltpu.VMEM((4, tok, D), bfloat), pltpu.VMEM((4, tok, D), bfloat), pltpu.VMEM((3, 2, tok, D // 2), bfloat), pltpu.VMEM((6, tok, D // 2), bfloat),
            pltpu.SemaphoreType.DMA((10,)), pltpu.SemaphoreType.DMA((10,))],
        compiler_params=pltpu.CompilerParams(collective_id=cid, has_side_effects=True, vmem_limit_bytes=60 << 20),
        cost_estimate=pl.CostEstimate(flops=1 << 30, bytes_accessed=128 << 20, transcendentals=0),
        name=name,
    )(*[a.reshape(ranks, tok, -1) for a in left], *right)


def dot(left, right):
    return jnp.dot(left, right, preferred_element_type=single)


def dot_tn(left, right):
    return lax.dot_general(left, right, (((0,), (0,)), ((), ())), preferred_element_type=single)


def dot_nt(left, right):
    return lax.dot_general(left, right, (((1,), (1,)), ((), ())), preferred_element_type=single)


def layer_norm(values, gain_vec, shift_vec):
    center = jnp.mean(values, axis=-1, keepdims=True)
    centered = values - center
    spread = jnp.mean(centered * centered, axis=-1, keepdims=True)
    return centered * lax.rsqrt(spread + 1e-05) * gain_vec + shift_vec


def column_sums(matrix):
    return jnp.sum(matrix.astype(single), axis=0)


def shipper(send, recv, ids):
    started = []

    def ship(src, dst, to):
        n = len(started)
        copy = pltpu.make_async_remote_copy(
            src_ref=src, dst_ref=dst, send_sem=send.at[n], recv_sem=recv.at[n], device_id=ids[to], device_id_type=MESH
        )
        copy.start()
        started.append(copy)
        return copy

    return ship, started


TWIN = {"o": "s", "x": "xs", "y": "ys", "d": "ds"}


def hidden_units(src, branch, w1_ref, w2_ref, b_ref, hid_ref, pg_ref, pb_ref, rank):
    pre = jnp.dot(src[...], w1_ref[...], preferred_element_type=single) + b_ref[...]
    square = pre * pre
    bend = jnp.tanh(0.7978845608028654 * (pre + 0.044715 * (pre * square)))
    rise = 0.5 * (1.0 + bend)
    hid_ref[rank] = (pre * rise).astype(bfloat)
    slope = rise + (0.5 * 0.7978845608028654) * pre * (1.0 - bend * bend) * (1.0 + 3 * 0.044715 * square)
    grad = (dot_nt(branch[...], w2_ref[...]) * slope).astype(bfloat)
    pg_ref[rank] = grad
    pb_ref[...] += jnp.sum(grad.astype(single), axis=0, keepdims=True)


def first_units_kernel(
    x_ref, bg_ref, w1_ref, w2_ref, b_ref, all_ref, hid_ref, pg_ref, pb_ref, down_ref, up_ref,
    held, bg, down_sum, up_sum, send, recv, keep, load,
):
    ids, at = plane_place()
    tok = x_ref.shape[0]
    half = tok // 2
    parts = (pl.ds(0, half), pl.ds(half, half))
    own = at["o"]
    loads = {}
    for n, name in enumerate(at):
        loads[name] = pltpu.make_async_copy(bg_ref.at[at[name]], bg.at[at[name]], load.at[n])
        loads[name].start()
    greet(ids)
    ship, started = shipper(send, recv, ids)
    x0 = ship(x_ref.at[parts[0]], held.at[own, parts[0]], "x")
    y1 = ship(x_ref.at[parts[1]], held.at[own, parts[1]], "y")
    x1 = ship(x_ref.at[parts[1]], held.at[own, parts[1]], "x")
    y0 = ship(x_ref.at[parts[0]], held.at[own, parts[0]], "y")
    s0 = ship(x_ref, held.at[own], "s")
    pb_ref[...] = jnp.zeros_like(pb_ref)
    kept = []

    def units(name):
        rank = at[name]
        src = x_ref if name == "o" else held.at[rank]
        copy = pltpu.make_async_copy(src, all_ref.at[rank], keep.at[len(kept)])
        copy.start()
        kept.append(copy)
        loads[name].wait()
        hidden_units(src, bg.at[rank], w1_ref, w2_ref, b_ref, hid_ref, pg_ref, pb_ref, rank)

    def weigh(name, last=False):
        wide = 256

        def add(total, out, here, pairs):
            term = sum(dot_tn(left, right) for left, right in pairs)
            if name == "o":
                total[here, :] = term
            elif last:
                out[here, :] = (total[here, :] + term).astype(bfloat)
            else:
                total[here, :] += term

        both = [(n, at[n]) for n in (name, TWIN[name])]

        def down(i, _):
            here = pl.ds(pl.multiple_of(i * wide, wide), wide)
            add(down_sum, down_ref, here, [(hid_ref[r, :, here], bg[r]) for n, r in both])
            return 0

        def up(i, _):
            here = pl.ds(pl.multiple_of(i * wide, wide), wide)
            tokens = [(x_ref[:, here] if n == "o" else held[r, :, here], pg_ref[r]) for n, r in both]
            add(up_sum, up_ref, here, tokens)
            return 0

        lax.fori_loop(0, hid_ref.shape[2] // wide, down, 0)
        lax.fori_loop(0, x_ref.shape[1] // wide, up, 0)

    units("o")
    s0.wait_recv()
    units("s")
    x0.wait_recv()
    ry = ship(held.at[at["x"], parts[0]], held.at[at["x"], parts[0]], "y")
    y1.wait_recv()
    rx = ship(held.at[at["y"], parts[1]], held.at[at["y"], parts[1]], "x")
    weigh("o")
    x1.wait_recv()
    sx = ship(held.at[at["x"]], held.at[at["x"]], "s")
    y0.wait_recv()
    sy = ship(held.at[at["y"]], held.at[at["y"]], "s")
    units("x")
    sx.wait_recv()
    units("xs")
    units("y")
    sy.wait_recv()
    units("ys")
    weigh("x")
    ry.wait_recv()
    rx.wait_recv()
    sd = ship(held.at[at["d"]], held.at[at["d"]], "s")
    weigh("y")
    units("d")
    sd.wait_recv()
    units("ds")
    weigh("d", last=True)
    for copy in started:
        copy.wait_send()
    for copy in kept:
        copy.wait()


def last_units_kernel(
    all_ref, bg_ref, pg1_ref, w1a_ref, w1_ref, w2_ref, b_ref, hid_ref, pb_ref, r_ref, down_ref, up_ref,
    held, bg, pg_ref, sib_out, sib_in, stage, landed, send, recv, load, load_b,
):
    ids, at = plane_place()
    ranks, tok, D = held.shape
    F = w1_ref.shape[1]
    mid = D // 2
    names = ("ds", "d", "xs", "x", "ys", "y", "s", "o")
    loads = {}
    for n, name in enumerate(names):
        loads[name] = [
            pltpu.make_async_copy(all_ref.at[at[name]], held.at[at[name]], load.at[n]),
            pltpu.make_async_copy(bg_ref.at[at[name]], bg.at[at[name]], load_b.at[n]),
        ]
        for copy in loads[name]:
            copy.start()
    greet(ids)
    ship, started = shipper(send, recv, ids)
    pb_ref[...] = jnp.zeros_like(pb_ref)

    def units(name):
        for copy in loads[name]:
            copy.wait()
        rank = at[name]
        hidden_units(held.at[rank], bg.at[rank], w1_ref, w2_ref, b_ref, hid_ref, pg_ref, pb_ref, rank)

    def term(name, cols):
        rank = at[name]
        return dot_nt(pg1_ref[rank], w1a_ref[cols, :]) + dot_nt(pg_ref[rank], w1_ref[cols, :])

    order = ("d", "x", "y", "o")

    def to_sibling(j):
        def fill(cols):
            sib_out[j, :, cols] = term(TWIN[order[j]], cols).astype(bfloat)

        tiles(0, D, fill)
        return ship(sib_out.at[j], sib_in.at[j], "s")

    def pair(j, cols):
        return term(order[j], cols) + sib_in[j, :, cols].astype(single)

    def local(h, cols):
        return pl.ds(pl.multiple_of(cols.start - h * mid, TILE), TILE)

    def put(j, h, extra=None):
        def fill(cols):
            value = pair(j, cols)
            if extra is not None:
                value = value + landed[extra, :, local(h, cols)].astype(single)
            stage[j, h, :, local(h, cols)] = value.astype(bfloat)

        tiles(h * mid, (h + 1) * mid, fill)

    units("ds")
    d_sib = to_sibling(0)
    units("d")
    d_sib.wait_recv()
    put(0, 0)
    d_a = ship(stage.at[0, 0], landed.at[0], "x")
    put(0, 1)
    d_b = ship(stage.at[0, 1], landed.at[1], "y")
    units("xs")
    x_sib = to_sibling(1)
    units("x")
    x_sib.wait_recv()
    put(1, 0)
    x_a = ship(stage.at[1, 0], landed.at[2], "x")
    units("ys")
    y_sib = to_sibling(2)
    units("y")
    y_sib.wait_recv()
    put(2, 1)
    y_b = ship(stage.at[2, 1], landed.at[3], "y")
    d_b.wait_recv()
    put(1, 1, extra=1)
    x_b = ship(stage.at[1, 1], landed.at[5], "x")
    d_a.wait_recv()
    put(2, 0, extra=0)
    y_a = ship(stage.at[2, 0], landed.at[4], "y")
    units("s")
    own_sib = to_sibling(3)
    units("o")
    own_sib.wait_recv()

    def first(cols):
        r_ref[:, cols] = pair(3, cols)

    tiles(0, D, first)

    wide = 256

    def grads(out_ref, count, value):
        def step(i, _):
            here = pl.ds(pl.multiple_of(i * wide, wide), wide)
            out_ref[here, :] = value(here).astype(bfloat)
            return 0

        lax.fori_loop(0, count, step, 0)

    rows = ranks * tok
    grads(down_ref, F // wide, lambda c: dot_tn(hid_ref[:, :, c].reshape(rows, wide), bg[...].reshape(rows, D)))
    grads(up_ref, D // wide, lambda c: dot_tn(held[:, :, c].reshape(rows, wide), pg_ref[...].reshape(rows, F)))
    for copy in (x_a, y_b, x_b, y_a):
        copy.wait_recv()
    for h, (n, m) in enumerate(((2, 4), (3, 5))):

        def add(cols, h=h, n=n, m=m):
            c = local(h, cols)
            r_ref[:, cols] = r_ref[:, cols] + landed[n, :, c].astype(single) + landed[m, :, c].astype(single)

        tiles(h * mid, (h + 1) * mid, add)
    for copy in started:
        copy.wait_send()


def first_units(x, bg, w1, w2, bias, cid):
    ranks = 8
    tok, D = x.shape
    F = w1.shape[1]
    anywhere = pl.BlockSpec(memory_space=pl.ANY)
    inside = pl.BlockSpec(memory_space=pltpu.VMEM)
    return pl.pallas_call(
        first_units_kernel,
        out_shape=[
            jax.ShapeDtypeStruct((ranks, tok, D), bfloat),
            jax.ShapeDtypeStruct((ranks, tok, F), bfloat),
            jax.ShapeDtypeStruct((ranks, tok, F), bfloat),
            jax.ShapeDtypeStruct((1, F), single),
            jax.ShapeDtypeStruct((F, D), bfloat),
            jax.ShapeDtypeStruct((D, F), bfloat),
        ],
        in_specs=[inside, anywhere, inside, inside, inside],
        out_specs=[anywhere, inside, inside, inside, inside, inside],
        scratch_shapes=[
            pltpu.VMEM((ranks, tok, D), bfloat),
            pltpu.VMEM((ranks, tok, D), bfloat),
            pltpu.VMEM((F, D), single),
            pltpu.VMEM((D, F), single),
            pltpu.SemaphoreType.DMA((10,)),
            pltpu.SemaphoreType.DMA((10,)),
            pltpu.SemaphoreType.DMA((8,)),
            pltpu.SemaphoreType.DMA((8,)),
        ],
        compiler_params=pltpu.CompilerParams(collective_id=cid, has_side_effects=True, vmem_limit_bytes=62 << 20),
        cost_estimate=pl.CostEstimate(flops=1 << 30, bytes_accessed=160 << 20, transcendentals=0),
        name="first_units",
    )(x, bg, w1, w2, bias)


def last_units(rows, bg, pg, w1a, w1, w2, bias, cid):
    ranks, tok, D = rows.shape
    F = w1.shape[1]
    anywhere = pl.BlockSpec(memory_space=pl.ANY)
    inside = pl.BlockSpec(memory_space=pltpu.VMEM)
    return pl.pallas_call(
        last_units_kernel,
        out_shape=[
            jax.ShapeDtypeStruct((ranks, tok, F), bfloat),
            jax.ShapeDtypeStruct((1, F), single),
            jax.ShapeDtypeStruct((tok, D), single),
            jax.ShapeDtypeStruct((F, D), bfloat),
            jax.ShapeDtypeStruct((D, F), bfloat),
        ],
        in_specs=[anywhere, anywhere, inside, inside, inside, inside, inside],
        out_specs=[inside] * 5,
        scratch_shapes=[
            pltpu.VMEM((ranks, tok, D), bfloat),
            pltpu.VMEM((ranks, tok, D), bfloat),
            pltpu.VMEM((ranks, tok, F), bfloat),
            pltpu.VMEM((4, tok, D), bfloat),
            pltpu.VMEM((4, tok, D), bfloat),
            pltpu.VMEM((3, 2, tok, D // 2), bfloat),
            pltpu.VMEM((6, tok, D // 2), bfloat),
            pltpu.SemaphoreType.DMA((10,)),
            pltpu.SemaphoreType.DMA((10,)),
            pltpu.SemaphoreType.DMA((8,)),
            pltpu.SemaphoreType.DMA((8,)),
        ],
        compiler_params=pltpu.CompilerParams(collective_id=cid, has_side_effects=True, vmem_limit_bytes=62 << 20),
        cost_estimate=pl.CostEstimate(flops=1 << 30, bytes_accessed=160 << 20, transcendentals=0),
        name="last_units",
    )(rows, bg, pg, w1a, w1, w2, bias)


def windows(span):
    block = span // 2
    return [(i * block, i * block + block + span) for i in range(2)]

def key_window(before, own, lo, hi, span):
    return jnp.concatenate([before[lo:span], own[0 : hi - span]], axis=0)

def hidden_bias(start_ref, i, block, lo, hi, span):
    rows = span + i * block + lax.broadcasted_iota(jnp.int32, (block, hi - lo), 0)
    keys = lo + lax.broadcasted_iota(jnp.int32, (block, hi - lo), 1)
    start = start_ref[i * block : (i + 1) * block, :]
    return jnp.where((keys >= start) & (keys <= rows), 0.0, -1e30).astype(single)

def attend_kernel(start_ref, q_ref, k_ref, v_ref, kb_ref, vb_ref, out_ref):
    span, cols = q_ref.shape
    block = span // 2
    lane = lax.broadcasted_iota(jnp.int32, (block, cols), 1) // HEAD_DIM
    for i, (lo, hi) in enumerate(windows(span)):
        rows = pl.ds(i * block, block)
        bias = hidden_bias(start_ref, i, block, lo, hi, span)
        keys = key_window(kb_ref, k_ref, lo, hi, span)
        vals = key_window(vb_ref, v_ref, lo, hi, span)
        query = q_ref[rows, :] * jnp.asarray(HEAD_DIM ** (-0.5), bfloat)
        def head(h, total):
            mine = lane == h
            scores = dot_nt(jnp.where(mine, query, 0), keys) + bias
            weights = jnp.exp(scores - jnp.max(scores, axis=1, keepdims=True))
            part = jnp.dot(weights.astype(bfloat), vals, preferred_element_type=single)
            part = part * (1.0 / jnp.sum(weights, axis=1, keepdims=True))
            return jnp.where(mine, part, total)
        total = lax.fori_loop(0, cols // HEAD_DIM, head, jnp.zeros((block, cols), single), unroll=True)
        out_ref[rows, :] = total.astype(bfloat)

def attend_back_kernel(start_ref, q_ref, k_ref, v_ref, kb_ref, vb_ref, do_ref, dq_ref, edge_ref, pair_ref, dk, dv):
    span, cols = q_ref.shape
    block = span // 2
    scale = HEAD_DIM ** (-0.5)
    dk[...] = jnp.zeros_like(dk)
    dv[...] = jnp.zeros_like(dv)
    lane = lax.broadcasted_iota(jnp.int32, (block, cols), 1) // HEAD_DIM
    for i, (lo, hi) in enumerate(windows(span)):
        rows = pl.ds(i * block, block)
        bias = hidden_bias(start_ref, i, block, lo, hi, span)
        keys = key_window(kb_ref, k_ref, lo, hi, span)
        vals = key_window(vb_ref, v_ref, lo, hi, span)
        query = q_ref[rows, :] * jnp.asarray(scale, bfloat)
        grad = do_ref[rows, :]
        def head(h, total):
            mine = lane == h
            query_h = jnp.where(mine, query, 0)
            grad_h = jnp.where(mine, grad, 0)
            scores = dot_nt(query_h, keys) + bias
            weights = jnp.exp(scores - jnp.max(scores, axis=1, keepdims=True))
            probs = weights * (1.0 / jnp.sum(weights, axis=1, keepdims=True))
            prob_grad = dot_nt(grad_h, vals)
            row_dot = jnp.sum(probs * prob_grad, axis=1, keepdims=True)
            score_grad = (probs * (prob_grad - row_dot)).astype(bfloat)
            dv[lo:hi, :] += dot_tn(probs.astype(bfloat), grad_h)
            dk[lo:hi, :] += dot_tn(score_grad, query_h)
            part = jnp.dot(score_grad, keys, preferred_element_type=single)
            return jnp.where(mine, part, total)
        total = lax.fori_loop(0, cols // HEAD_DIM, head, jnp.zeros((block, cols), single), unroll=True)
        dq_ref[rows, :] = (total * scale).astype(bfloat)
    edge_ref[:, :cols] = dk[:span, :].astype(bfloat)
    edge_ref[:, cols:] = dv[:span, :].astype(bfloat)
    pair_ref[:, :cols] = dk[span:, :]
    pair_ref[:, cols:] = dv[span:, :]

def attention_specs(span, cols):
    def at(j):
        return pl.BlockSpec((span, cols), lambda g: (g, j))
    return [pl.BlockSpec((span, 1), lambda g: (g, 0)), at(0), at(0), at(1), at(0), at(1)]

def attend(starts, query, key_value, before, groups):
    span, cols = query.shape[0] // groups, query.shape[1]
    return pl.pallas_call(
        attend_kernel,
        grid=(groups,),
        out_shape=jax.ShapeDtypeStruct((groups * span, cols), bfloat),
        in_specs=attention_specs(span, cols),
        out_specs=pl.BlockSpec((span, cols), lambda g: (g, 0)),
        compiler_params=pltpu.CompilerParams(vmem_limit_bytes=60 << 20),
        name="attend",
    )(starts, query, key_value, key_value, before, before)

def attend_back(starts, query, key_value, before, grad, groups):
    span, cols = query.shape[0] // groups, query.shape[1]
    rows = groups * span
    return pl.pallas_call(
        attend_back_kernel,
        grid=(groups,),
        out_shape=[jax.ShapeDtypeStruct((rows, cols), bfloat), jax.ShapeDtypeStruct((rows, 2 * cols), bfloat), jax.ShapeDtypeStruct((rows, 2 * cols), single)],
        in_specs=attention_specs(span, cols) + [pl.BlockSpec((span, cols), lambda g: (g, 0))],
        out_specs=[pl.BlockSpec((span, cols), lambda g: (g, 0))] + [pl.BlockSpec((span, 2 * cols), lambda g: (g, 0))] * 2,
        scratch_shapes=[pltpu.VMEM((2 * span, cols), single)] * 2,
        compiler_params=pltpu.CompilerParams(vmem_limit_bytes=60 << 20),
        name="attend_back",
    )(starts, query, key_value, key_value, before, before, grad)


def attention_heads(starts, query, key_value, before, groups):
    span, cols = query.shape[0] // groups, query.shape[1]
    both = jnp.concatenate([before.reshape(groups, span, -1), key_value.reshape(groups, span, -1)], axis=1)
    key_two, value_two = [both[..., i * cols : (i + 1) * cols].reshape(groups, 2 * span, -1, HEAD_DIM) for i in (0, 1)]
    query = query.reshape(groups, span, -1, HEAD_DIM)
    keys = jnp.arange(2 * span)[None, None, :]
    rows = span + jnp.arange(span)[None, :, None]
    allowed = (keys >= starts.reshape(groups, span, 1)) & (keys <= rows)
    scores = jnp.einsum("gqhd,gkhd->ghqk", query, key_two, preferred_element_type=single) * HEAD_DIM ** (-0.5)
    scores = jnp.where(allowed[:, None], scores, -1e30)
    weights = jnp.exp(scores - jnp.max(scores, axis=-1, keepdims=True))
    return query, key_two, value_two, weights / jnp.sum(weights, axis=-1, keepdims=True)


def attention_forward(starts, query, key_value, before, groups):
    if query.shape[1] % 128 == 0:
        return attend(starts, query, key_value, before, groups)
    _, _, value_two, probs = attention_heads(starts, query, key_value, before, groups)
    context = jnp.einsum("ghqk,gkhd->gqhd", probs.astype(bfloat), value_two, preferred_element_type=single)
    return context.astype(bfloat).reshape(query.shape)


def attention_backward(starts, query, key_value, before, grad, groups):
    if query.shape[1] % 128 == 0:
        return attend_back(starts, query, key_value, before, grad, groups)
    rows = query.shape[0]
    query, key_two, value_two, probs = attention_heads(starts, query, key_value, before, groups)
    span = query.shape[1]
    grad = grad.reshape(query.shape)
    prob_grad = jnp.einsum("gqhd,gkhd->ghqk", grad, value_two, preferred_element_type=single)
    row_dot = jnp.sum(probs * prob_grad, axis=-1, keepdims=True)
    score_grad = (probs * (prob_grad - row_dot)).astype(bfloat)
    query_grad = jnp.einsum("ghqk,gkhd->gqhd", score_grad, key_two, preferred_element_type=single) * HEAD_DIM ** (-0.5)
    key_grad = jnp.einsum("ghqk,gqhd->gkhd", score_grad, query, preferred_element_type=single) * HEAD_DIM ** (-0.5)
    value_grad = jnp.einsum("ghqk,gqhd->gkhd", probs.astype(bfloat), grad, preferred_element_type=single)
    pair = jnp.concatenate([t.reshape(groups, 2 * span, -1) for t in (key_grad, value_grad)], axis=2)
    edge, pair = [t.reshape(rows, -1) for t in (pair[:, :span].astype(bfloat), pair[:, span:])]
    return query_grad.astype(bfloat).reshape(rows, -1), edge, pair


def norm_backward(values, out_grad, gain_vec):
    center = jnp.mean(values, axis=-1, keepdims=True)
    centered = values - center
    rs = lax.rsqrt(jnp.mean(centered * centered, axis=-1, keepdims=True) + 1e-05)
    xhat = centered * rs
    g = out_grad * gain_vec
    part = rs * (g - jnp.mean(g, axis=-1, keepdims=True) - xhat * jnp.mean(g * xhat, axis=-1, keepdims=True))
    return part, jnp.sum(out_grad * xhat, axis=0), jnp.sum(out_grad, axis=0)


def on_device(
    inputs,
    exit_layers,
    lengths,
    layer_index,
    out_grad,
    ln1_gain,
    ln1_bias,
    q_weight,
    q_bias,
    k_weight,
    v_weight,
    v_bias,
    o_weight,
    o_bias,
    ln2_gain,
    ln2_bias,
    fc1_weight,
    fc1_bias,
    fc2_weight,
    fc2_bias,
):
    B, Z, X = lax.axis_size("b"), lax.axis_size("z"), lax.axis_size("x")
    R = B * X
    local = inputs[0].astype(single)
    tok, D = local.shape
    span = X * tok
    group_tok = Z * span
    at_z, at_x = lax.axis_index("z"), lax.axis_index("x")
    rank = lax.axis_index("b") * X + at_x
    rows_dev = q_weight.shape[0]
    cols = D // R
    heads = cols // HEAD_DIM
    whole_heads = rows_dev % HEAD_DIM == 0

    group_active = (exit_layers[0] > layer_index[0]).astype(single)
    active_total = jnp.sum(group_active)
    active = lax.dynamic_slice_in_dim(group_active, at_z * span + at_x * tok, tok, 0)[:, None]

    count = lengths.shape[1]
    upto = jnp.arange(count)[:, None] <= jnp.arange(count)[None, :]
    def to_ranks(matrix):
        lead = matrix.shape[:-1]
        if whole_heads:
            matrix = matrix.reshape(*lead, B, Z, X, rows_dev)
            k = len(lead)
            return matrix.transpose(k, k + 2, *range(k), k + 1, k + 3).reshape(R, *lead, cols)
        return jnp.moveaxis(matrix.reshape(*lead, R, cols), -2, 0)

    def from_ranks(parts):
        if whole_heads:
            parts = parts.reshape(B, X, -1, Z, rows_dev)
            return parts.transpose(2, 0, 3, 1, 4).reshape(-1, D)
        return parts.transpose(1, 0, 2).reshape(-1, D)

    def mine(vector):
        return lax.dynamic_index_in_dim(to_ranks(vector), rank, 0, keepdims=False)

    qkv_parts = jnp.concatenate([to_ranks(q_weight), to_ranks(k_weight), to_ranks(v_weight)], axis=2)
    qkv_mine = lax.all_to_all(qkv_parts, PLANE, split_axis=0, concat_axis=0, tiled=True)
    qkv_mine = qkv_mine.reshape(D // Z, 3 * cols)
    qkv_mine, fc2_bias = lax.optimization_barrier((qkv_mine, fc2_bias))
    small = [ln1_gain, ln1_bias, q_bias, v_bias, o_bias, ln2_gain, ln2_bias, fc2_bias]
    pack = jnp.concatenate([v.astype(single) for v in (*small, fc1_bias, lengths[0])])
    pad = -pack.shape[0] % 128
    pack = jnp.concatenate([pack, jnp.zeros((pad,), single)])
    pack = lax.all_to_all(jnp.broadcast_to(pack, (R * Z, pack.shape[0])), ALL, split_axis=0, concat_axis=0, tiled=True)
    vectors = [pack[:, i * rows_dev : (i + 1) * rows_dev].reshape(-1) for i in range(len(small))]
    gain_one, bias_one, bias_q, bias_v, bias_o, gain_two, bias_two, bias_down = vectors
    pack = pack.reshape(B, Z, X, -1)[..., len(small) * rows_dev :]
    up_dev = fc1_bias.shape[0]
    bias_up = lax.dynamic_index_in_dim(
        pack[..., :up_dev].transpose(0, 2, 1, 3).reshape(R, Z * up_dev), rank, 0, keepdims=False
    )
    group_lengths = pack[:, 0, 0, up_dev : up_dev + count].astype(jnp.int32)
    ends = jnp.sum(jnp.where(upto, group_lengths[:, :, None], 0), axis=1)
    places = at_z * span + jnp.arange(span, dtype=jnp.int32)
    starts = jnp.max(jnp.where(ends[:, None, :] <= places[None, :, None], ends[:, None, :], 0), axis=2)
    starts = starts - (at_z - 1) * span

    def feature_rows(mine):
        full = lax.all_gather(mine, "z", axis=0, tiled=True)
        return full.reshape(Z, B, X, rows_dev, -1).transpose(1, 0, 2, 3, 4).reshape(D, -1)

    weight_kv = feature_rows(qkv_mine[:, cols:])
    bias_kv = jnp.concatenate([jnp.zeros((cols,), single), mine(bias_v)])
    bias_one, query_mine, o_weight = lax.optimization_barrier((bias_one, qkv_mine[:, :cols], o_weight))
    normed_low = layer_norm(local, gain_one, bias_one).astype(bfloat)
    fast = (B, X) == (4, 2)

    def gather_plane(rows, cid, name):
        if fast:
            return plane_gather(rows, (), [], None, cid, name)[0]
        return lax.all_gather(rows, PLANE, axis=0, tiled=True)

    def gather_plane_dot(rows, weight, shift, out_type, turned, cid, name):
        if fast:
            return gather_dot(rows, weight, shift, out_type, turned, cid, name)
        rows = lax.all_gather(rows, PLANE, axis=0, tiled=True)
        return rows, ((dot_nt if turned else dot)(rows, weight) + shift).astype(out_type)

    def reduce_plane(left, weight, turned, cid, name):
        if fast:
            return dot_reduce([left], [weight], turned, cid, name)
        terms = (dot_nt if turned else dot)(left, weight).astype(bfloat)
        return lax.psum_scatter(terms, PLANE, scatter_dimension=0, tiled=True).astype(single)

    normed_all = gather_plane(normed_low, 0, "gather_normed")
    units = fc1_bias.shape[0] // 2
    up_one, down_one = fc1_weight[:, :units], fc2_weight[:units]
    normed_all, weight_kv, up_one, down_one = lax.optimization_barrier((normed_all, weight_kv, up_one, down_one))
    weight_q = feature_rows(query_mine)
    if whole_heads:
        weight_o = lax.all_gather(o_weight, "z", axis=0, tiled=True)
    else:
        weight_o = lax.dynamic_slice_in_dim(lax.all_gather(o_weight, ALL, axis=0, tiled=True), rank * cols, cols, 0)
    up_one = lax.all_gather(up_one, "z", axis=1, tiled=True)
    down_one = lax.all_gather(down_one, "z", axis=0, tiled=True)
    key_value = (dot(normed_all, weight_kv) + bias_kv).astype(bfloat)
    up = [(i, i + 1) for i in range(Z - 1)]
    down = [(i + 1, i) for i in range(Z - 1)]
    cotangent = out_grad[0].astype(single) * (group_tok / active_total)
    branch_grad = (active * cotangent).astype(bfloat)
    down_b_grad = column_sums(branch_grad)
    key_value, branch_grad = lax.optimization_barrier((key_value, branch_grad))
    before = lax.ppermute(key_value, "z", up)
    branch_all = gather_plane(branch_grad, 7, "gather_branch")
    branch_all, late_normed = lax.optimization_barrier((branch_all, normed_all))
    query = (dot(late_normed, weight_q) + mine(bias_q)).astype(bfloat)
    before, query = lax.optimization_barrier((before, query))
    starts = starts.reshape(B * span, 1)
    context = attention_forward(starts, query, key_value, before, B)
    context, up_two, down_two = lax.optimization_barrier((context, fc1_weight[:, units:], fc2_weight[units:]))
    up_two = lax.all_gather(up_two, "z", axis=1, tiled=True)
    down_two = lax.all_gather(down_two, "z", axis=0, tiled=True)

    attended = reduce_plane(context, weight_o, False, 1, "attended") + bias_o
    middle = local + active * attended
    normed_two = layer_norm(middle, gain_two, bias_two).astype(bfloat)
    bias_up = bias_up.reshape(Z, 2, units)
    bias_up = [bias_up[:, i].reshape(1, Z * units) for i in range(2)]

    def sum_halves(left, right, turned, cid, name):
        if fast:
            return dot_reduce(left, right, turned, cid, name)
        terms = sum((dot_nt if turned else dot)(a, w) for a, w in zip(left, right)).astype(bfloat)
        return lax.psum_scatter(terms, PLANE, scatter_dimension=0, tiled=True).astype(single)

    def sum_z(down_grad, up_grad):
        down_grad = lax.psum_scatter(down_grad, "z", scatter_dimension=0, tiled=True)
        return down_grad, lax.psum_scatter(up_grad, "z", scatter_dimension=1, tiled=True)

    if fast:
        branch_rows = branch_all.reshape(R, tok, D)
        two_all, hidden_one, pre_one, bias_one_up, down_grad, up_grad = first_units(
            normed_two, branch_rows, up_one, down_one, bias_up[0], 2
        )
        shards_one = sum_z(down_grad, up_grad)
        hidden_two, bias_two_up, normed_two_grad, down_grad, up_grad = last_units(
            two_all, branch_rows, pre_one, up_one, up_two, down_two, bias_up[1], 3
        )
        shards_two = sum_z(down_grad, up_grad)
        up_b_halves = [bias_one_up[0], bias_two_up[0]]
    else:
        two_all = gather_plane(normed_two, 2, "gather_two")

        def half_units(weight_up, weight_down, bias):
            hidden, gelu_pull = jax.vjp(partial(jax.nn.gelu, approximate=True), dot(two_all, weight_up) + bias)
            hidden = hidden.astype(bfloat)
            pre_grad = gelu_pull(dot_nt(branch_all, weight_down))[0].astype(bfloat)
            grads = dot_tn(hidden, branch_all).astype(bfloat), dot_tn(two_all, pre_grad).astype(bfloat)
            return hidden, pre_grad, sum_z(*grads)

        hidden_one, pre_one, shards_one = half_units(up_one, down_one, bias_up[0])
        hidden_two, pre_two, shards_two = half_units(up_two, down_two, bias_up[1])
        up_b_halves = [column_sums(pre_one), column_sums(pre_two)]
        normed_two_grad = sum_halves([pre_one, pre_two], [up_one, up_two], True, 3, "up_grad")
    up_b_grad = jnp.stack([half.reshape(Z, units) for half in up_b_halves], axis=1).reshape(-1)

    middle_part, gain_two_grad, bias_two_grad = norm_backward(middle, normed_two_grad, gain_two)
    middle_grad = cotangent + middle_part
    attended_grad = (active * middle_grad).astype(bfloat)
    out_b_grad = column_sums(attended_grad)
    attended_all, context_grad = gather_plane_dot(
        attended_grad, weight_o, jnp.zeros((1, cols), single), bfloat, True, 5, "attended_grad"
    )
    context_grad, shards_one = lax.optimization_barrier((context_grad, shards_one))
    out_w_grad = dot_tn(context, attended_all)
    query_grad, edge, pair = attention_backward(starts, query, key_value, before, context_grad, B)
    hidden_one, edge, pair = lax.optimization_barrier((hidden_one, edge, pair))
    after = lax.ppermute(edge, "z", down)
    branch = sum_halves([hidden_one, hidden_two], [down_one, down_two], False, 4, "down")
    branch, after, shards_two = lax.optimization_barrier((branch, after, shards_two))
    outputs = middle + active * (branch + bias_down)
    pair_grad = (pair + after.astype(single)).astype(bfloat)
    qkv_grad = jnp.concatenate([query_grad, pair_grad], axis=1)
    weight_qkv = jnp.concatenate([weight_q, weight_kv], axis=1)
    normed_grad = reduce_plane(qkv_grad, weight_qkv, True, 6, "qkv_grad")
    qkv_w_grad = dot_tn(normed_all, qkv_grad)
    qkv_b_grad = column_sums(qkv_grad)
    input_part, gain_one_grad, bias_one_grad = norm_backward(local, normed_grad, gain_one)
    input_grad = middle_grad + input_part

    def sum_to_owners(vectors, axes, parts):
        split = jnp.concatenate([v.reshape(parts, -1) for v in vectors], axis=1)
        summed = jnp.sum(lax.all_to_all(split, axes, split_axis=0, concat_axis=0, tiled=True), axis=0)
        widths = [v.shape[0] // parts for v in vectors]
        return [summed[sum(widths[:i]) : sum(widths[: i + 1])] for i in range(len(widths))]

    qkv_w_grad = qkv_w_grad.astype(bfloat).reshape(B, Z, X, rows_dev, 3 * cols)
    qkv_w_grad = qkv_w_grad.transpose(1, 0, 2, 3, 4).reshape(D, 3 * cols)
    qkv_w_grad = lax.psum_scatter(qkv_w_grad, "z", scatter_dimension=0, tiled=True)
    qkv_w_grad = lax.all_to_all(qkv_w_grad.reshape(R, rows_dev, 3 * cols), PLANE, split_axis=0, concat_axis=0, tiled=True)
    qkv_w_grad = qkv_w_grad.astype(single)
    q_w_shard, k_w_shard, v_w_shard = [from_ranks(qkv_w_grad[..., i * cols : (i + 1) * cols]) for i in range(3)]
    if whole_heads:
        out_w_shard = lax.psum_scatter(out_w_grad.astype(bfloat), "z", scatter_dimension=0, tiled=True).astype(single)
        q_b_shard, v_b_shard, up_b_shard = sum_to_owners([qkv_b_grad[:cols], qkv_b_grad[2 * cols :], up_b_grad], "z", Z)
    else:

        def placed(rows):
            full = jnp.zeros((D,) + rows.shape[1:], rows.dtype)
            full = lax.dynamic_update_slice_in_dim(full, rows, rank * cols, 0)
            return lax.psum_scatter(full, ALL, scatter_dimension=0, tiled=True).astype(single)

        out_w_shard = placed(out_w_grad.astype(bfloat))
        q_b_shard = placed(qkv_b_grad[:cols])
        v_b_shard = placed(qkv_b_grad[2 * cols :])
        [up_b_shard] = sum_to_owners([up_b_grad], "z", Z)
    sums = sum_to_owners(
        [gain_one_grad, bias_one_grad, out_b_grad, gain_two_grad, bias_two_grad, down_b_grad], ALL, R * Z
    )
    return (
        outputs.astype(bfloat)[None],
        input_grad.astype(bfloat)[None],
        sums[0],
        sums[1],
        q_w_shard,
        q_b_shard,
        k_w_shard,
        v_w_shard,
        v_b_shard,
        out_w_shard,
        sums[2],
        sums[3],
        sums[4],
        jnp.concatenate([shards_one[1], shards_two[1]], axis=1).astype(single),
        up_b_shard,
        jnp.concatenate([shards_one[0], shards_two[0]], axis=0).astype(single),
        sums[5],
    )


def solution(mesh):
    groups, parts = mesh.shape["batch"], mesh.shape["seq"]
    inner = Mesh(mesh.devices.reshape(groups, SPANS, parts // SPANS), ("b", "z", "x"))
    token = P("b", ("z", "x"), None)
    vector = P(ALL)
    rows = P(ALL, None)
    columns = P(None, ALL)
    return jax.shard_map(
        on_device,
        mesh=inner,
        in_specs=(
            token,
            P("b", None),
            P("b", None),
            P(),
            token,
            vector,
            vector,
            rows,
            vector,
            rows,
            rows,
            vector,
            rows,
            vector,
            vector,
            vector,
            columns,
            vector,
            rows,
            vector,
        ),
        out_specs=(
            token,
            token,
            vector,
            vector,
            rows,
            vector,
            rows,
            rows,
            vector,
            rows,
            vector,
            vector,
            vector,
            columns,
            vector,
            rows,
            vector,
        ),
        check_vma=False,
    )
```

```python
import functools
from functools import partial

import jax
import jax.numpy as jnp
from jax import lax
from jax.experimental import pallas as pl
from jax.experimental.pallas import tpu as pltpu
from jax.sharding import Mesh
from jax.sharding import PartitionSpec as P

HEAD_DIM = 64
SPANS = 4

bfloat = jnp.bfloat16
single = jnp.float32

PLANE = ("b", "x")
ALL = ("b", "z", "x")
MESH = pl.DeviceIdType.MESH
TILE = 512

def plane_place():
    b, z, x = lax.axis_index("b"), lax.axis_index("z"), lax.axis_index("x")
    sib_b = b + 1 - 2 * lax.rem(b, 2)
    far_b = lax.rem(b + 2, 4)
    far_sib_b = lax.rem(sib_b + 2, 4)
    ids = {"s": (sib_b, z, x), "x": (b, z, 1 - x), "y": (far_b, z, x)}
    ranks = {
        "o": b * 2 + x,
        "s": sib_b * 2 + x,
        "x": b * 2 + 1 - x,
        "xs": sib_b * 2 + 1 - x,
        "y": far_b * 2 + x,
        "ys": far_sib_b * 2 + x,
        "d": far_b * 2 + 1 - x,
        "ds": far_sib_b * 2 + 1 - x,
    }
    return ids, ranks

def greet(ids):
    barrier = pltpu.get_barrier_semaphore()
    for device in ids.values():
        pl.semaphore_signal(barrier, inc=1, device_id=device, device_id_type=MESH)
    pl.semaphore_wait(barrier, len(ids))

def tiles(lo, hi, body):
    def step(i, _):
        body(pl.ds(pl.multiple_of(i * TILE, TILE), TILE))
        return 0
    lax.fori_loop(lo // TILE, hi // TILE, step, 0)

def gather_kernel(body_of, n_in, n_out, x_ref, *refs):
    ins = refs[:n_in]; all_ref = refs[n_in]; outs = refs[n_in + 1 : n_in + 1 + n_out]
    held, send, recv, keep = refs[n_in + 1 + n_out :]
    ids, at = plane_place()
    half = x_ref.shape[0] // 2
    parts = (pl.ds(0, half), pl.ds(half, half))
    greet(ids)
    count = [0]
    started = []
    def ship(src, dst, to):
        n = count[0]; count[0] += 1
        c = pltpu.make_async_remote_copy(src_ref=src, dst_ref=dst, send_sem=send.at[n], recv_sem=recv.at[n], device_id=ids[to], device_id_type=MESH)
        c.start(); started.append(c)
        return c
    own = at["o"]
    x0 = ship(x_ref.at[parts[0]], held.at[own, parts[0]], "x")
    y1 = ship(x_ref.at[parts[1]], held.at[own, parts[1]], "y")
    x1 = ship(x_ref.at[parts[1]], held.at[own, parts[1]], "x")
    y0 = ship(x_ref.at[parts[0]], held.at[own, parts[0]], "y")
    s0 = ship(x_ref, held.at[own], "s")
    kept = []
    def done(rank, src):
        c = pltpu.make_async_copy(src, all_ref.at[rank], keep.at[len(kept)])
        c.start(); kept.append(c)
        if body_of is not None:
            body_of(rank, src, ins, outs)
    done(own, x_ref)
    s0.wait_recv()
    done(at["s"], held.at[at["s"]])
    x0.wait_recv()
    ry = ship(held.at[at["x"], parts[0]], held.at[at["x"], parts[0]], "y")
    y1.wait_recv()
    rx = ship(held.at[at["y"], parts[1]], held.at[at["y"], parts[1]], "x")
    x1.wait_recv()
    sx = ship(held.at[at["x"]], held.at[at["x"]], "s")
    y0.wait_recv()
    sy = ship(held.at[at["y"]], held.at[at["y"]], "s")
    done(at["x"], held.at[at["x"]])
    done(at["y"], held.at[at["y"]])
    sx.wait_recv()
    done(at["xs"], held.at[at["xs"]])
    sy.wait_recv()
    done(at["ys"], held.at[at["ys"]])
    ry.wait_recv(); rx.wait_recv()
    sd = ship(held.at[at["d"]], held.at[at["d"]], "s")
    done(at["d"], held.at[at["d"]])
    sd.wait_recv()
    done(at["ds"], held.at[at["ds"]])
    for c in started: c.wait_send()
    for c in kept: c.wait()

def vmem(n): return [pl.BlockSpec(memory_space=pltpu.VMEM)] * n

def plane_gather(x, ins, out_types, body_of, cid, name, ranks=8):
    tok, D = x.shape
    res = pl.pallas_call(
        functools.partial(gather_kernel, body_of, len(ins), len(out_types)),
        out_shape=[jax.ShapeDtypeStruct((ranks, tok, D), x.dtype), *out_types],
        in_specs=vmem(1 + len(ins)),
        out_specs=[pl.BlockSpec(memory_space=pl.ANY)] + vmem(len(out_types)),
        scratch_shapes=[pltpu.VMEM((ranks, tok, D), x.dtype), pltpu.SemaphoreType.DMA((10,)), pltpu.SemaphoreType.DMA((10,)), pltpu.SemaphoreType.DMA((8,))],
        compiler_params=pltpu.CompilerParams(collective_id=cid, has_side_effects=True, vmem_limit_bytes=60 << 20),
        cost_estimate=pl.CostEstimate(flops=1 << 30, bytes_accessed=128 << 20, transcendentals=0),
        name=name,
    )(x, *ins)
    return res[0].reshape(ranks * tok, D), *res[1:]

def gather_dot(x, w, bias, out_dtype, turned, cid, name):
    ranks, tok, D = 8, *x.shape
    N = w.shape[0] if turned else w.shape[1]
    tile = min(N, 512) if N % 512 == 0 else 256
    def body(rank, src, ins, outs):
        w_ref, b_ref = ins
        def step(i, _):
            cols = pl.ds(pl.multiple_of(i * tile, tile), tile)
            if turned:
                y = lax.dot_general(src[...], w_ref[cols, :], (((1,), (1,)), ((), ())), preferred_element_type=single)
            else:
                y = jnp.dot(src[...], w_ref[:, cols], preferred_element_type=single)
            outs[0][rank, :, cols] = (y + b_ref[:, cols]).astype(out_dtype)
            return 0
        lax.fori_loop(0, N // tile, step, 0)
    all_, y = plane_gather(x, (w, bias), [jax.ShapeDtypeStruct((ranks, tok, N), out_dtype)], body, cid, name)
    return all_, y.reshape(ranks * tok, N)

def reduce_kernel(turned, pairs, *refs):
    left, right = refs[:pairs], refs[pairs : 2 * pairs]
    out_ref, sib_out, sib_in, stage, landed, send, recv = refs[2 * pairs :]
    ids, at = plane_place()
    D = out_ref.shape[1]
    mid = D // 2
    greet(ids)
    count = [0]; started = []
    def ship(src, dst, to):
        n = count[0]; count[0] += 1
        c = pltpu.make_async_remote_copy(src_ref=src, dst_ref=dst, send_sem=send.at[n], recv_sem=recv.at[n], device_id=ids[to], device_id_type=MESH)
        c.start(); started.append(c)
        return c
    def term(rank, cols):
        if turned:
            return sum(dot_nt(a[rank], w[cols, :]) for a, w in zip(left, right))
        rows = [w[:, 1, :, cols].reshape(-1, TILE) if len(w.shape) == 4 else w[:, cols] for w in right]
        return sum(dot(a[rank], w) for a, w in zip(left, rows))
    order = ("d", "x", "y", "o")
    twin = {"d": "ds", "x": "xs", "y": "ys", "o": "s"}
    sib = []
    def to_sibling():
        j = len(sib)
        def fill(cols):
            sib_out[j, :, cols] = term(at[twin[order[j]]], cols).astype(bfloat)
        tiles(0, D, fill)
        sib.append(ship(sib_out.at[j], sib_in.at[j], "s"))
    def pair(j, cols):
        return term(at[order[j]], cols) + sib_in[j, :, cols].astype(single)
    def local(h, cols):
        return pl.ds(pl.multiple_of(cols.start - h * mid, TILE), TILE)
    def put(j, h, extra=None):
        def fill(cols):
            value = pair(j, cols)
            if extra is not None:
                value = value + landed[extra, :, local(h, cols)].astype(single)
            stage[j, h, :, local(h, cols)] = value.astype(bfloat)
        tiles(h * mid, (h + 1) * mid, fill)
    to_sibling()
    to_sibling()
    sib[0].wait_recv()
    put(0, 0)
    d_a = ship(stage.at[0, 0], landed.at[0], "x")
    put(0, 1)
    d_b = ship(stage.at[0, 1], landed.at[1], "y")
    to_sibling()
    sib[1].wait_recv()
    put(1, 0)
    x_a = ship(stage.at[1, 0], landed.at[2], "x")
    sib[2].wait_recv()
    put(2, 1)
    y_b = ship(stage.at[2, 1], landed.at[3], "y")
    to_sibling()
    sib[3].wait_recv()
    def first(cols):
        out_ref[:, cols] = pair(3, cols)
    tiles(0, D, first)
    d_b.wait_recv()
    put(1, 1, extra=1)
    x_b = ship(stage.at[1, 1], landed.at[5], "x")
    d_a.wait_recv()
    put(2, 0, extra=0)
    y_a = ship(stage.at[2, 0], landed.at[4], "y")
    x_a.wait_recv(); y_b.wait_recv(); x_b.wait_recv(); y_a.wait_recv()
    for h, (n, m) in enumerate(((2, 4), (3, 5))):
        def add(cols, h=h, n=n, m=m):
            c = local(h, cols)
            out_ref[:, cols] = out_ref[:, cols] + landed[n, :, c].astype(single) + landed[m, :, c].astype(single)
        tiles(h * mid, (h + 1) * mid, add)
    for c in started: c.wait_send()

def dot_reduce(left, right, turned, cid, name):
    ranks = 8
    D = right[0].shape[0] if turned else right[0].shape[-1]
    tok = left[0].size // left[0].shape[-1] // ranks
    return pl.pallas_call(
        functools.partial(reduce_kernel, turned, len(left)),
        out_shape=jax.ShapeDtypeStruct((tok, D), single),
        in_specs=vmem(2 * len(left)), out_specs=vmem(1)[0],
        scratch_shapes=[pltpu.VMEM((4, tok, D), bfloat), pltpu.VMEM((4, tok, D), bfloat), pltpu.VMEM((3, 2, tok, D // 2), bfloat), pltpu.VMEM((6, tok, D // 2), bfloat),
            pltpu.SemaphoreType.DMA((10,)), pltpu.SemaphoreType.DMA((10,))],
        compiler_params=pltpu.CompilerParams(collective_id=cid, has_side_effects=True, vmem_limit_bytes=60 << 20),
        cost_estimate=pl.CostEstimate(flops=1 << 30, bytes_accessed=128 << 20, transcendentals=0),
        name=name,
    )(*[a.reshape(ranks, tok, -1) for a in left], *right)


def dot(left, right):
    return jnp.dot(left, right, preferred_element_type=single)


def dot_tn(left, right):
    return lax.dot_general(left, right, (((0,), (0,)), ((), ())), preferred_element_type=single)


def dot_nt(left, right):
    return lax.dot_general(left, right, (((1,), (1,)), ((), ())), preferred_element_type=single)


def layer_norm(values, gain_vec, shift_vec):
    center = jnp.mean(values, axis=-1, keepdims=True)
    centered = values - center
    spread = jnp.mean(centered * centered, axis=-1, keepdims=True)
    return centered * lax.rsqrt(spread + 1e-05) * gain_vec + shift_vec


def column_sums(matrix):
    return jnp.sum(matrix.astype(single), axis=0)


def shipper(send, recv, ids):
    started = []

    def ship(src, dst, to):
        n = len(started)
        copy = pltpu.make_async_remote_copy(
            src_ref=src, dst_ref=dst, send_sem=send.at[n], recv_sem=recv.at[n], device_id=ids[to], device_id_type=MESH
        )
        copy.start()
        started.append(copy)
        return copy

    return ship, started


TWIN = {"o": "s", "x": "xs", "y": "ys", "d": "ds"}


def unit_rows(w_ref, i):
    parts, _, units, D = w_ref.shape
    return w_ref[:, i].reshape(parts * units, D)


def hidden_units(src, branch, w_ref, b_ref, hid_ref, pg_ref, pb_ref, rank):
    pre = dot_nt(src[...], unit_rows(w_ref, 0)) + b_ref[...]
    square = pre * pre
    bend = jnp.tanh(0.7978845608028654 * (pre + 0.044715 * (pre * square)))
    rise = 0.5 * (1.0 + bend)
    hid_ref[rank] = (pre * rise).astype(bfloat)
    slope = rise + (0.5 * 0.7978845608028654) * pre * (1.0 - bend * bend) * (1.0 + 3 * 0.044715 * square)
    grad = (dot_nt(branch[...], unit_rows(w_ref, 1)) * slope).astype(bfloat)
    pg_ref[rank] = grad
    pb_ref[...] += jnp.sum(grad.astype(single), axis=0, keepdims=True)


def first_units_kernel(
    x_ref, bg_ref, w_ref, b_ref, all_ref, hid_ref, pg_ref, pb_ref, grad_ref,
    held, bg, total, send, recv, keep, load,
):
    ids, at = plane_place()
    tok = x_ref.shape[0]
    half = tok // 2
    parts = (pl.ds(0, half), pl.ds(half, half))
    own = at["o"]
    loads = {}
    for n, name in enumerate(at):
        loads[name] = pltpu.make_async_copy(bg_ref.at[at[name]], bg.at[at[name]], load.at[n])
        loads[name].start()
    greet(ids)
    ship, started = shipper(send, recv, ids)
    x0 = ship(x_ref.at[parts[0]], held.at[own, parts[0]], "x")
    y1 = ship(x_ref.at[parts[1]], held.at[own, parts[1]], "y")
    x1 = ship(x_ref.at[parts[1]], held.at[own, parts[1]], "x")
    y0 = ship(x_ref.at[parts[0]], held.at[own, parts[0]], "y")
    s0 = ship(x_ref, held.at[own], "s")
    pb_ref[...] = jnp.zeros_like(pb_ref)
    kept = []

    def units(name):
        rank = at[name]
        src = x_ref if name == "o" else held.at[rank]
        copy = pltpu.make_async_copy(src, all_ref.at[rank], keep.at[len(kept)])
        copy.start()
        kept.append(copy)
        loads[name].wait()
        hidden_units(src, bg.at[rank], w_ref, b_ref, hid_ref, pg_ref, pb_ref, rank)

    def weigh(name, last=False):
        units_at = grad_ref.shape[2]
        per = 256 // units_at

        def rows(i, _):
            here = pl.ds(pl.multiple_of(i * 256, 256), 256)
            owners = pl.ds(i * per, per)
            for j, left in enumerate((pg_ref, hid_ref)):
                term = 0
                for n in (name, TWIN[name]):
                    right = bg[at[n]] if j else (x_ref[...] if n == "o" else held[at[n]])
                    term = term + dot_tn(left[at[n], :, here], right)
                term = term.reshape(per, units_at, -1)
                if name == "o":
                    total[owners, j] = term
                elif last:
                    grad_ref[owners, j] = (total[owners, j] + term).astype(bfloat)
                else:
                    total[owners, j] += term
            return 0

        lax.fori_loop(0, hid_ref.shape[2] // 256, rows, 0)

    units("o")
    s0.wait_recv()
    units("s")
    x0.wait_recv()
    ry = ship(held.at[at["x"], parts[0]], held.at[at["x"], parts[0]], "y")
    y1.wait_recv()
    rx = ship(held.at[at["y"], parts[1]], held.at[at["y"], parts[1]], "x")
    weigh("o")
    x1.wait_recv()
    sx = ship(held.at[at["x"]], held.at[at["x"]], "s")
    y0.wait_recv()
    sy = ship(held.at[at["y"]], held.at[at["y"]], "s")
    units("x")
    sx.wait_recv()
    units("xs")
    units("y")
    sy.wait_recv()
    units("ys")
    weigh("x")
    ry.wait_recv()
    rx.wait_recv()
    sd = ship(held.at[at["d"]], held.at[at["d"]], "s")
    weigh("y")
    units("d")
    sd.wait_recv()
    units("ds")
    weigh("d", last=True)
    for copy in started:
        copy.wait_send()
    for copy in kept:
        copy.wait()


def last_units_kernel(
    all_ref, bg_ref, pg1_ref, w1_ref, w_ref, b_ref, hid_ref, pb_ref, r_ref, grad_ref,
    held, bg, pg_ref, sib_out, sib_in, stage, landed, send, recv, load, load_b,
):
    ids, at = plane_place()
    ranks, tok, D = held.shape
    mid = D // 2
    names = ("ds", "d", "xs", "x", "ys", "y", "s", "o")
    loads = {}
    for n, name in enumerate(names):
        loads[name] = [
            pltpu.make_async_copy(all_ref.at[at[name]], held.at[at[name]], load.at[n]),
            pltpu.make_async_copy(bg_ref.at[at[name]], bg.at[at[name]], load_b.at[n]),
        ]
        for copy in loads[name]:
            copy.start()
    greet(ids)
    ship, started = shipper(send, recv, ids)
    pb_ref[...] = jnp.zeros_like(pb_ref)

    def units(name):
        for copy in loads[name]:
            copy.wait()
        rank = at[name]
        hidden_units(held.at[rank], bg.at[rank], w_ref, b_ref, hid_ref, pg_ref, pb_ref, rank)

    def term(name, cols):
        rank = at[name]
        first, second = [w[:, 0, :, cols].reshape(-1, TILE) for w in (w1_ref, w_ref)]
        return dot(pg1_ref[rank], first) + dot(pg_ref[rank], second)

    order = ("d", "x", "y", "o")

    def to_sibling(j):
        def fill(cols):
            sib_out[j, :, cols] = term(TWIN[order[j]], cols).astype(bfloat)

        tiles(0, D, fill)
        return ship(sib_out.at[j], sib_in.at[j], "s")

    def pair(j, cols):
        return term(order[j], cols) + sib_in[j, :, cols].astype(single)

    def local(h, cols):
        return pl.ds(pl.multiple_of(cols.start - h * mid, TILE), TILE)

    def put(j, h, extra=None):
        def fill(cols):
            value = pair(j, cols)
            if extra is not None:
                value = value + landed[extra, :, local(h, cols)].astype(single)
            stage[j, h, :, local(h, cols)] = value.astype(bfloat)

        tiles(h * mid, (h + 1) * mid, fill)

    units("ds")
    d_sib = to_sibling(0)
    units("d")
    d_sib.wait_recv()
    put(0, 0)
    d_a = ship(stage.at[0, 0], landed.at[0], "x")
    put(0, 1)
    d_b = ship(stage.at[0, 1], landed.at[1], "y")
    units("xs")
    x_sib = to_sibling(1)
    units("x")
    x_sib.wait_recv()
    put(1, 0)
    x_a = ship(stage.at[1, 0], landed.at[2], "x")
    units("ys")
    y_sib = to_sibling(2)
    units("y")
    y_sib.wait_recv()
    put(2, 1)
    y_b = ship(stage.at[2, 1], landed.at[3], "y")
    d_b.wait_recv()
    put(1, 1, extra=1)
    x_b = ship(stage.at[1, 1], landed.at[5], "x")
    d_a.wait_recv()
    put(2, 0, extra=0)
    y_a = ship(stage.at[2, 0], landed.at[4], "y")
    units("s")
    own_sib = to_sibling(3)
    units("o")
    own_sib.wait_recv()

    def first(cols):
        r_ref[:, cols] = pair(3, cols)

    tiles(0, D, first)

    units_at = grad_ref.shape[2]
    per = 256 // units_at
    tokens = ranks * tok

    def grads(i, _):
        here = pl.ds(pl.multiple_of(i * 256, 256), 256)
        owners = pl.ds(i * per, per)
        for j, (left, right) in enumerate(((pg_ref, held), (hid_ref, bg))):
            value = dot_tn(left[:, :, here].reshape(tokens, 256), right[...].reshape(tokens, D))
            grad_ref[owners, j] = value.astype(bfloat).reshape(per, units_at, D)
        return 0

    lax.fori_loop(0, hid_ref.shape[2] // 256, grads, 0)
    for copy in (x_a, y_b, x_b, y_a):
        copy.wait_recv()
    for h, (n, m) in enumerate(((2, 4), (3, 5))):

        def add(cols, h=h, n=n, m=m):
            c = local(h, cols)
            r_ref[:, cols] = r_ref[:, cols] + landed[n, :, c].astype(single) + landed[m, :, c].astype(single)

        tiles(h * mid, (h + 1) * mid, add)
    for copy in started:
        copy.wait_send()


def first_units(x, bg, w, bias, cid):
    ranks = 8
    tok, D = x.shape
    F = bias.shape[1]
    anywhere = pl.BlockSpec(memory_space=pl.ANY)
    inside = pl.BlockSpec(memory_space=pltpu.VMEM)
    return pl.pallas_call(
        first_units_kernel,
        out_shape=[
            jax.ShapeDtypeStruct((ranks, tok, D), bfloat),
            jax.ShapeDtypeStruct((ranks, tok, F), bfloat),
            jax.ShapeDtypeStruct((ranks, tok, F), bfloat),
            jax.ShapeDtypeStruct((1, F), single),
            jax.ShapeDtypeStruct(w.shape, bfloat),
        ],
        in_specs=[inside, anywhere, inside, inside],
        out_specs=[anywhere, inside, inside, inside, inside],
        scratch_shapes=[
            pltpu.VMEM((ranks, tok, D), bfloat),
            pltpu.VMEM((ranks, tok, D), bfloat),
            pltpu.VMEM(w.shape, single),
            pltpu.SemaphoreType.DMA((10,)),
            pltpu.SemaphoreType.DMA((10,)),
            pltpu.SemaphoreType.DMA((8,)),
            pltpu.SemaphoreType.DMA((8,)),
        ],
        compiler_params=pltpu.CompilerParams(collective_id=cid, has_side_effects=True, vmem_limit_bytes=62 << 20),
        cost_estimate=pl.CostEstimate(flops=1 << 30, bytes_accessed=160 << 20, transcendentals=0),
        name="first_units",
    )(x, bg, w, bias)


def last_units(rows, bg, pg, w1, w, bias, cid):
    ranks, tok, D = rows.shape
    F = bias.shape[1]
    anywhere = pl.BlockSpec(memory_space=pl.ANY)
    inside = pl.BlockSpec(memory_space=pltpu.VMEM)
    return pl.pallas_call(
        last_units_kernel,
        out_shape=[
            jax.ShapeDtypeStruct((ranks, tok, F), bfloat),
            jax.ShapeDtypeStruct((1, F), single),
            jax.ShapeDtypeStruct((tok, D), single),
            jax.ShapeDtypeStruct(w.shape, bfloat),
        ],
        in_specs=[anywhere, anywhere, inside, inside, inside, inside],
        out_specs=[inside] * 4,
        scratch_shapes=[
            pltpu.VMEM((ranks, tok, D), bfloat),
            pltpu.VMEM((ranks, tok, D), bfloat),
            pltpu.VMEM((ranks, tok, F), bfloat),
            pltpu.VMEM((4, tok, D), bfloat),
            pltpu.VMEM((4, tok, D), bfloat),
            pltpu.VMEM((3, 2, tok, D // 2), bfloat),
            pltpu.VMEM((6, tok, D // 2), bfloat),
            pltpu.SemaphoreType.DMA((10,)),
            pltpu.SemaphoreType.DMA((10,)),
            pltpu.SemaphoreType.DMA((8,)),
            pltpu.SemaphoreType.DMA((8,)),
        ],
        compiler_params=pltpu.CompilerParams(collective_id=cid, has_side_effects=True, vmem_limit_bytes=62 << 20),
        cost_estimate=pl.CostEstimate(flops=1 << 30, bytes_accessed=160 << 20, transcendentals=0),
        name="last_units",
    )(rows, bg, pg, w1, w, bias)


def windows(span):
    block = span // 2
    return [(i * block, i * block + block + span) for i in range(2)]

def key_window(before, own, lo, hi, span):
    return jnp.concatenate([before[lo:span], own[0 : hi - span]], axis=0)

def hidden_bias(start_ref, i, block, lo, hi, span):
    rows = span + i * block + lax.broadcasted_iota(jnp.int32, (block, hi - lo), 0)
    keys = lo + lax.broadcasted_iota(jnp.int32, (block, hi - lo), 1)
    start = start_ref[i * block : (i + 1) * block, :]
    return jnp.where((keys >= start) & (keys <= rows), 0.0, -1e30).astype(single)

def attend_kernel(start_ref, q_ref, k_ref, v_ref, kb_ref, vb_ref, out_ref):
    span, cols = q_ref.shape
    block = span // 2
    lane = lax.broadcasted_iota(jnp.int32, (block, cols), 1) // HEAD_DIM
    for i, (lo, hi) in enumerate(windows(span)):
        rows = pl.ds(i * block, block)
        bias = hidden_bias(start_ref, i, block, lo, hi, span)
        keys = key_window(kb_ref, k_ref, lo, hi, span)
        vals = key_window(vb_ref, v_ref, lo, hi, span)
        query = q_ref[rows, :] * jnp.asarray(HEAD_DIM ** (-0.5), bfloat)
        def head(h, total):
            mine = lane == h
            scores = dot_nt(jnp.where(mine, query, 0), keys) + bias
            weights = jnp.exp(scores - jnp.max(scores, axis=1, keepdims=True))
            part = jnp.dot(weights.astype(bfloat), vals, preferred_element_type=single)
            part = part * (1.0 / jnp.sum(weights, axis=1, keepdims=True))
            return jnp.where(mine, part, total)
        total = lax.fori_loop(0, cols // HEAD_DIM, head, jnp.zeros((block, cols), single), unroll=True)
        out_ref[rows, :] = total.astype(bfloat)

def attend_back_kernel(start_ref, q_ref, k_ref, v_ref, kb_ref, vb_ref, do_ref, dq_ref, edge_ref, pair_ref, dk, dv):
    span, cols = q_ref.shape
    block = span // 2
    scale = HEAD_DIM ** (-0.5)
    dk[...] = jnp.zeros_like(dk)
    dv[...] = jnp.zeros_like(dv)
    lane = lax.broadcasted_iota(jnp.int32, (block, cols), 1) // HEAD_DIM
    for i, (lo, hi) in enumerate(windows(span)):
        rows = pl.ds(i * block, block)
        bias = hidden_bias(start_ref, i, block, lo, hi, span)
        keys = key_window(kb_ref, k_ref, lo, hi, span)
        vals = key_window(vb_ref, v_ref, lo, hi, span)
        query = q_ref[rows, :] * jnp.asarray(scale, bfloat)
        grad = do_ref[rows, :]
        def head(h, total):
            mine = lane == h
            query_h = jnp.where(mine, query, 0)
            grad_h = jnp.where(mine, grad, 0)
            scores = dot_nt(query_h, keys) + bias
            weights = jnp.exp(scores - jnp.max(scores, axis=1, keepdims=True))
            probs = weights * (1.0 / jnp.sum(weights, axis=1, keepdims=True))
            prob_grad = dot_nt(grad_h, vals)
            row_dot = jnp.sum(probs * prob_grad, axis=1, keepdims=True)
            score_grad = (probs * (prob_grad - row_dot)).astype(bfloat)
            dv[lo:hi, :] += dot_tn(probs.astype(bfloat), grad_h)
            dk[lo:hi, :] += dot_tn(score_grad, query_h)
            part = jnp.dot(score_grad, keys, preferred_element_type=single)
            return jnp.where(mine, part, total)
        total = lax.fori_loop(0, cols // HEAD_DIM, head, jnp.zeros((block, cols), single), unroll=True)
        dq_ref[rows, :] = (total * scale).astype(bfloat)
    edge_ref[:, :cols] = dk[:span, :].astype(bfloat)
    edge_ref[:, cols:] = dv[:span, :].astype(bfloat)
    pair_ref[:, :cols] = dk[span:, :]
    pair_ref[:, cols:] = dv[span:, :]

def attention_specs(span, cols):
    def at(j):
        return pl.BlockSpec((span, cols), lambda g: (g, j))
    return [pl.BlockSpec((span, 1), lambda g: (g, 0)), at(0), at(0), at(1), at(0), at(1)]

def attend(starts, query, key_value, before, groups):
    span, cols = query.shape[0] // groups, query.shape[1]
    return pl.pallas_call(
        attend_kernel,
        grid=(groups,),
        out_shape=jax.ShapeDtypeStruct((groups * span, cols), bfloat),
        in_specs=attention_specs(span, cols),
        out_specs=pl.BlockSpec((span, cols), lambda g: (g, 0)),
        compiler_params=pltpu.CompilerParams(vmem_limit_bytes=60 << 20),
        name="attend",
    )(starts, query, key_value, key_value, before, before)

def attend_back(starts, query, key_value, before, grad, groups):
    span, cols = query.shape[0] // groups, query.shape[1]
    rows = groups * span
    return pl.pallas_call(
        attend_back_kernel,
        grid=(groups,),
        out_shape=[jax.ShapeDtypeStruct((rows, cols), bfloat), jax.ShapeDtypeStruct((rows, 2 * cols), bfloat), jax.ShapeDtypeStruct((rows, 2 * cols), single)],
        in_specs=attention_specs(span, cols) + [pl.BlockSpec((span, cols), lambda g: (g, 0))],
        out_specs=[pl.BlockSpec((span, cols), lambda g: (g, 0))] + [pl.BlockSpec((span, 2 * cols), lambda g: (g, 0))] * 2,
        scratch_shapes=[pltpu.VMEM((2 * span, cols), single)] * 2,
        compiler_params=pltpu.CompilerParams(vmem_limit_bytes=60 << 20),
        name="attend_back",
    )(starts, query, key_value, key_value, before, before, grad)


def attention_heads(starts, query, key_value, before, groups):
    span, cols = query.shape[0] // groups, query.shape[1]
    both = jnp.concatenate([before.reshape(groups, span, -1), key_value.reshape(groups, span, -1)], axis=1)
    key_two, value_two = [both[..., i * cols : (i + 1) * cols].reshape(groups, 2 * span, -1, HEAD_DIM) for i in (0, 1)]
    query = query.reshape(groups, span, -1, HEAD_DIM)
    keys = jnp.arange(2 * span)[None, None, :]
    rows = span + jnp.arange(span)[None, :, None]
    allowed = (keys >= starts.reshape(groups, span, 1)) & (keys <= rows)
    scores = jnp.einsum("gqhd,gkhd->ghqk", query, key_two, preferred_element_type=single) * HEAD_DIM ** (-0.5)
    scores = jnp.where(allowed[:, None], scores, -1e30)
    weights = jnp.exp(scores - jnp.max(scores, axis=-1, keepdims=True))
    return query, key_two, value_two, weights / jnp.sum(weights, axis=-1, keepdims=True)


def attention_forward(starts, query, key_value, before, groups):
    if query.shape[1] % 128 == 0:
        return attend(starts, query, key_value, before, groups)
    _, _, value_two, probs = attention_heads(starts, query, key_value, before, groups)
    context = jnp.einsum("ghqk,gkhd->gqhd", probs.astype(bfloat), value_two, preferred_element_type=single)
    return context.astype(bfloat).reshape(query.shape)


def attention_backward(starts, query, key_value, before, grad, groups):
    if query.shape[1] % 128 == 0:
        return attend_back(starts, query, key_value, before, grad, groups)
    rows = query.shape[0]
    query, key_two, value_two, probs = attention_heads(starts, query, key_value, before, groups)
    span = query.shape[1]
    grad = grad.reshape(query.shape)
    prob_grad = jnp.einsum("gqhd,gkhd->ghqk", grad, value_two, preferred_element_type=single)
    row_dot = jnp.sum(probs * prob_grad, axis=-1, keepdims=True)
    score_grad = (probs * (prob_grad - row_dot)).astype(bfloat)
    query_grad = jnp.einsum("ghqk,gkhd->gqhd", score_grad, key_two, preferred_element_type=single) * HEAD_DIM ** (-0.5)
    key_grad = jnp.einsum("ghqk,gqhd->gkhd", score_grad, query, preferred_element_type=single) * HEAD_DIM ** (-0.5)
    value_grad = jnp.einsum("ghqk,gqhd->gkhd", probs.astype(bfloat), grad, preferred_element_type=single)
    pair = jnp.concatenate([t.reshape(groups, 2 * span, -1) for t in (key_grad, value_grad)], axis=2)
    edge, pair = [t.reshape(rows, -1) for t in (pair[:, :span].astype(bfloat), pair[:, span:])]
    return query_grad.astype(bfloat).reshape(rows, -1), edge, pair


def norm_backward(values, out_grad, gain_vec):
    center = jnp.mean(values, axis=-1, keepdims=True)
    centered = values - center
    rs = lax.rsqrt(jnp.mean(centered * centered, axis=-1, keepdims=True) + 1e-05)
    xhat = centered * rs
    g = out_grad * gain_vec
    part = rs * (g - jnp.mean(g, axis=-1, keepdims=True) - xhat * jnp.mean(g * xhat, axis=-1, keepdims=True))
    return part, jnp.sum(out_grad * xhat, axis=0), jnp.sum(out_grad, axis=0)


def on_device(
    inputs,
    exit_layers,
    lengths,
    layer_index,
    out_grad,
    ln1_gain,
    ln1_bias,
    q_weight,
    q_bias,
    k_weight,
    v_weight,
    v_bias,
    o_weight,
    o_bias,
    ln2_gain,
    ln2_bias,
    fc1_weight,
    fc1_bias,
    fc2_weight,
    fc2_bias,
):
    B, Z, X = lax.axis_size("b"), lax.axis_size("z"), lax.axis_size("x")
    R = B * X
    local = inputs[0].astype(single)
    tok, D = local.shape
    span = X * tok
    group_tok = Z * span
    at_z, at_x = lax.axis_index("z"), lax.axis_index("x")
    rank = lax.axis_index("b") * X + at_x
    rows_dev = q_weight.shape[0]
    cols = D // R
    heads = cols // HEAD_DIM
    whole_heads = rows_dev % HEAD_DIM == 0

    group_active = (exit_layers[0] > layer_index[0]).astype(single)
    active_total = jnp.sum(group_active)
    active = lax.dynamic_slice_in_dim(group_active, at_z * span + at_x * tok, tok, 0)[:, None]

    count = lengths.shape[1]
    upto = jnp.arange(count)[:, None] <= jnp.arange(count)[None, :]
    def to_ranks(matrix):
        lead = matrix.shape[:-1]
        if whole_heads:
            matrix = matrix.reshape(*lead, B, Z, X, rows_dev)
            k = len(lead)
            return matrix.transpose(k, k + 2, *range(k), k + 1, k + 3).reshape(R, *lead, cols)
        return jnp.moveaxis(matrix.reshape(*lead, R, cols), -2, 0)

    def from_ranks(parts):
        if whole_heads:
            parts = parts.reshape(B, X, -1, Z, rows_dev)
            return parts.transpose(2, 0, 3, 1, 4).reshape(-1, D)
        return parts.transpose(1, 0, 2).reshape(-1, D)

    def mine(vector):
        return lax.dynamic_index_in_dim(to_ranks(vector), rank, 0, keepdims=False)

    if whole_heads:
        weight_o = lax.all_gather(o_weight, "z", axis=0, tiled=True)
    else:
        weight_o = lax.dynamic_slice_in_dim(lax.all_gather(o_weight, ALL, axis=0, tiled=True), rank * cols, cols, 0)
    qkv_parts = jnp.concatenate([to_ranks(q_weight), to_ranks(k_weight), to_ranks(v_weight)], axis=2)
    qkv_mine = lax.all_to_all(qkv_parts, PLANE, split_axis=0, concat_axis=0, tiled=True)
    qkv_mine = qkv_mine.reshape(D // Z, 3 * cols)
    qkv_mine, fc2_bias = lax.optimization_barrier((qkv_mine, fc2_bias))
    small = [ln1_gain, ln1_bias, q_bias, v_bias, o_bias, ln2_gain, ln2_bias, fc2_bias]
    pack = jnp.concatenate([v.astype(single) for v in (*small, fc1_bias, lengths[0])])
    pad = -pack.shape[0] % 128
    pack = jnp.concatenate([pack, jnp.zeros((pad,), single)])
    pack = lax.all_to_all(jnp.broadcast_to(pack, (R * Z, pack.shape[0])), ALL, split_axis=0, concat_axis=0, tiled=True)
    vectors = [pack[:, i * rows_dev : (i + 1) * rows_dev].reshape(-1) for i in range(len(small))]
    gain_one, bias_one, bias_q, bias_v, bias_o, gain_two, bias_two, bias_down = vectors
    pack = pack.reshape(B, Z, X, -1)[..., len(small) * rows_dev :]
    up_dev = fc1_bias.shape[0]
    bias_up = lax.dynamic_index_in_dim(
        pack[..., :up_dev].transpose(0, 2, 1, 3).reshape(R, Z * up_dev), rank, 0, keepdims=False
    )
    group_lengths = pack[:, 0, 0, up_dev : up_dev + count].astype(jnp.int32)
    ends = jnp.sum(jnp.where(upto, group_lengths[:, :, None], 0), axis=1)
    places = at_z * span + jnp.arange(span, dtype=jnp.int32)
    starts = jnp.max(jnp.where(ends[:, None, :] <= places[None, :, None], ends[:, None, :], 0), axis=2)
    starts = starts - (at_z - 1) * span

    def feature_rows(mine):
        full = lax.all_gather(mine, "z", axis=0, tiled=True)
        return full.reshape(Z, B, X, rows_dev, -1).transpose(1, 0, 2, 3, 4).reshape(D, -1)

    weight_kv = feature_rows(qkv_mine[:, cols:])
    bias_kv = jnp.concatenate([jnp.zeros((cols,), single), mine(bias_v)])
    bias_one, query_mine, weight_o = lax.optimization_barrier((bias_one, qkv_mine[:, :cols], weight_o))
    normed_low = layer_norm(local, gain_one, bias_one).astype(bfloat)
    fast = (B, X) == (4, 2)

    def gather_plane(rows, cid, name):
        if fast:
            return plane_gather(rows, (), [], None, cid, name)[0]
        return lax.all_gather(rows, PLANE, axis=0, tiled=True)

    def gather_plane_dot(rows, weight, shift, out_type, turned, cid, name):
        if fast:
            return gather_dot(rows, weight, shift, out_type, turned, cid, name)
        rows = lax.all_gather(rows, PLANE, axis=0, tiled=True)
        return rows, ((dot_nt if turned else dot)(rows, weight) + shift).astype(out_type)

    def reduce_plane(left, weight, turned, cid, name):
        if fast:
            return dot_reduce([left], [weight], turned, cid, name)
        terms = (dot_nt if turned else dot)(left, weight).astype(bfloat)
        return lax.psum_scatter(terms, PLANE, scatter_dimension=0, tiled=True).astype(single)

    normed_all = gather_plane(normed_low, 0, "gather_normed")
    units = fc1_bias.shape[0] // 2
    halves = [jnp.concatenate([fc1_weight.T[i : i + units], fc2_weight[i : i + units]]) for i in (0, units)]

    def gather_units(mine):
        return lax.all_gather(mine, "z", axis=0, tiled=True).reshape(Z, 2, units, D)

    normed_all, weight_kv, unit_one = lax.optimization_barrier((normed_all, weight_kv, halves[0]))
    weight_q = feature_rows(query_mine)
    unit_one = gather_units(unit_one)
    key_value = (dot(normed_all, weight_kv) + bias_kv).astype(bfloat)
    up = [(i, i + 1) for i in range(Z - 1)]
    down = [(i + 1, i) for i in range(Z - 1)]
    cotangent = out_grad[0].astype(single) * (group_tok / active_total)
    branch_grad = (active * cotangent).astype(bfloat)
    down_b_grad = column_sums(branch_grad)
    key_value, branch_grad = lax.optimization_barrier((key_value, branch_grad))
    before = lax.ppermute(key_value, "z", up)
    branch_all = gather_plane(branch_grad, 7, "gather_branch")
    branch_all, late_normed = lax.optimization_barrier((branch_all, normed_all))
    query = (dot(late_normed, weight_q) + mine(bias_q)).astype(bfloat)
    before, query = lax.optimization_barrier((before, query))
    starts = starts.reshape(B * span, 1)
    context = attention_forward(starts, query, key_value, before, B)
    context, unit_two = lax.optimization_barrier((context, halves[1]))
    unit_two = gather_units(unit_two)

    attended = reduce_plane(context, weight_o, False, 1, "attended") + bias_o
    middle = local + active * attended
    normed_two = layer_norm(middle, gain_two, bias_two).astype(bfloat)
    bias_up = bias_up.reshape(Z, 2, units)
    bias_up = [bias_up[:, i].reshape(1, Z * units) for i in range(2)]

    def sum_halves(left, right, turned, cid, name):
        if fast:
            return dot_reduce(left, right, turned, cid, name)
        terms = sum((dot_nt if turned else dot)(a, w) for a, w in zip(left, right)).astype(bfloat)
        return lax.psum_scatter(terms, PLANE, scatter_dimension=0, tiled=True).astype(single)

    def sum_z(grads):
        return lax.psum_scatter(grads.reshape(Z * 2 * units, D), "z", scatter_dimension=0, tiled=True)

    if fast:
        branch_rows = branch_all.reshape(R, tok, D)
        two_all, hidden_one, pre_one, bias_one_up, grads = first_units(normed_two, branch_rows, unit_one, bias_up[0], 2)
        shard_one = sum_z(grads)
        hidden_two, bias_two_up, normed_two_grad, grads = last_units(
            two_all, branch_rows, pre_one, unit_one, unit_two, bias_up[1], 3
        )
        shard_two = sum_z(grads)
        up_b_halves = [bias_one_up[0], bias_two_up[0]]
    else:
        two_all = gather_plane(normed_two, 2, "gather_two")

        def half_units(weights, bias):
            weight_up, weight_down = [weights[:, i].reshape(Z * units, D) for i in (0, 1)]
            hidden, gelu_pull = jax.vjp(partial(jax.nn.gelu, approximate=True), dot_nt(two_all, weight_up) + bias)
            hidden = hidden.astype(bfloat)
            pre_grad = gelu_pull(dot_nt(branch_all, weight_down))[0].astype(bfloat)
            grads = dot_tn(pre_grad, two_all), dot_tn(hidden, branch_all)
            grads = jnp.stack([g.astype(bfloat).reshape(Z, units, D) for g in grads], axis=1)
            return hidden, pre_grad, sum_z(grads), weight_up, weight_down

        hidden_one, pre_one, shard_one, up_one, down_one = half_units(unit_one, bias_up[0])
        hidden_two, pre_two, shard_two, up_two, down_two = half_units(unit_two, bias_up[1])
        up_b_halves = [column_sums(pre_one), column_sums(pre_two)]
        normed_two_grad = sum_halves([pre_one, pre_two], [up_one, up_two], False, 3, "up_grad")
    up_b_grad = jnp.stack([half.reshape(Z, units) for half in up_b_halves], axis=1).reshape(-1)

    middle_part, gain_two_grad, bias_two_grad = norm_backward(middle, normed_two_grad, gain_two)
    middle_grad = cotangent + middle_part
    attended_grad = (active * middle_grad).astype(bfloat)
    out_b_grad = column_sums(attended_grad)
    attended_all, context_grad = gather_plane_dot(
        attended_grad, weight_o, jnp.zeros((1, cols), single), bfloat, True, 5, "attended_grad"
    )
    context_grad, shard_one = lax.optimization_barrier((context_grad, shard_one))
    out_w_grad = dot_tn(context, attended_all)
    query_grad, edge, pair = attention_backward(starts, query, key_value, before, context_grad, B)
    hidden_one, edge, pair, query_grad = lax.optimization_barrier((hidden_one, edge, pair, query_grad))
    after = lax.ppermute(edge, "z", down)
    query_w_grad = dot_tn(normed_all, query_grad).astype(bfloat)
    hidden_one, query_w_grad, out_w_grad = lax.optimization_barrier((hidden_one, query_w_grad, out_w_grad))
    downs = [unit_one, unit_two] if fast else [down_one, down_two]
    branch = sum_halves([hidden_one, hidden_two], downs, False, 4, "down")
    branch, after, shard_two = lax.optimization_barrier((branch, after, shard_two))
    outputs = middle + active * (branch + bias_down)
    pair_grad = (pair + after.astype(single)).astype(bfloat)
    pair_w_grad = dot_tn(normed_all, pair_grad).astype(bfloat)
    pair_grad, pair_w_grad = lax.optimization_barrier((pair_grad, pair_w_grad))
    normed_grad = sum_halves([query_grad, pair_grad], [weight_q, weight_kv], True, 6, "qkv_grad")
    query_b_grad = column_sums(query_grad)
    value_b_grad = column_sums(pair_grad[:, cols:])
    input_part, gain_one_grad, bias_one_grad = norm_backward(local, normed_grad, gain_one)
    input_grad = middle_grad + input_part

    def sum_to_owners(vectors, axes, parts):
        split = jnp.concatenate([v.reshape(parts, -1) for v in vectors], axis=1)
        summed = jnp.sum(lax.all_to_all(split, axes, split_axis=0, concat_axis=0, tiled=True), axis=0)
        widths = [v.shape[0] // parts for v in vectors]
        return [summed[sum(widths[:i]) : sum(widths[: i + 1])] for i in range(len(widths))]

    def feature_shard(grads):
        width = grads.shape[1]
        grads = grads.reshape(B, Z, X, rows_dev, width).transpose(1, 0, 2, 3, 4).reshape(D, width)
        grads = lax.psum_scatter(grads, "z", scatter_dimension=0, tiled=True)
        grads = lax.all_to_all(grads.reshape(R, rows_dev, width), PLANE, split_axis=0, concat_axis=0, tiled=True)
        return [from_ranks(grads[..., i : i + cols]).astype(single) for i in range(0, width, cols)]

    [q_w_shard] = feature_shard(query_w_grad)
    k_w_shard, v_w_shard = feature_shard(pair_w_grad)
    if whole_heads:
        out_w_shard = lax.psum_scatter(out_w_grad.astype(bfloat), "z", scatter_dimension=0, tiled=True).astype(single)
        q_b_shard, v_b_shard, up_b_shard = sum_to_owners([query_b_grad, value_b_grad, up_b_grad], "z", Z)
    else:

        def placed(rows):
            full = jnp.zeros((D,) + rows.shape[1:], rows.dtype)
            full = lax.dynamic_update_slice_in_dim(full, rows, rank * cols, 0)
            return lax.psum_scatter(full, ALL, scatter_dimension=0, tiled=True).astype(single)

        out_w_shard = placed(out_w_grad.astype(bfloat))
        q_b_shard = placed(query_b_grad)
        v_b_shard = placed(value_b_grad)
        [up_b_shard] = sum_to_owners([up_b_grad], "z", Z)
    sums = sum_to_owners(
        [gain_one_grad, bias_one_grad, out_b_grad, gain_two_grad, bias_two_grad, down_b_grad], ALL, R * Z
    )
    return (
        outputs.astype(bfloat)[None],
        input_grad.astype(bfloat)[None],
        sums[0],
        sums[1],
        q_w_shard,
        q_b_shard,
        k_w_shard,
        v_w_shard,
        v_b_shard,
        out_w_shard,
        sums[2],
        sums[3],
        sums[4],
        jnp.concatenate([shard_one[:units], shard_two[:units]]).T.astype(single),
        up_b_shard,
        jnp.concatenate([shard_one[units:], shard_two[units:]]).astype(single),
        sums[5],
    )


def solution(mesh):
    groups, parts = mesh.shape["batch"], mesh.shape["seq"]
    inner = Mesh(mesh.devices.reshape(groups, SPANS, parts // SPANS), ("b", "z", "x"))
    token = P("b", ("z", "x"), None)
    vector = P(ALL)
    rows = P(ALL, None)
    columns = P(None, ALL)
    return jax.shard_map(
        on_device,
        mesh=inner,
        in_specs=(
            token,
            P("b", None),
            P("b", None),
            P(),
            token,
            vector,
            vector,
            rows,
            vector,
            rows,
            rows,
            vector,
            rows,
            vector,
            vector,
            vector,
            columns,
            vector,
            rows,
            vector,
        ),
        out_specs=(
            token,
            token,
            vector,
            vector,
            rows,
            vector,
            rows,
            rows,
            vector,
            rows,
            vector,
            vector,
            vector,
            columns,
            vector,
            rows,
            vector,
        ),
        check_vma=False,
    )
```

```python
import functools
from functools import partial

import jax
import jax.numpy as jnp
from jax import lax
from jax.experimental import pallas as pl
from jax.experimental.pallas import tpu as pltpu
from jax.sharding import Mesh
from jax.sharding import PartitionSpec as P

HEAD_DIM = 64
SPANS = 4

bfloat = jnp.bfloat16
single = jnp.float32

PLANE = ("b", "x")
ALL = ("b", "z", "x")
MESH = pl.DeviceIdType.MESH
TILE = 512

def plane_place():
    b, z, x = lax.axis_index("b"), lax.axis_index("z"), lax.axis_index("x")
    sib_b = b + 1 - 2 * lax.rem(b, 2)
    far_b = lax.rem(b + 2, 4)
    far_sib_b = lax.rem(sib_b + 2, 4)
    ids = {"s": (sib_b, z, x), "x": (b, z, 1 - x), "y": (far_b, z, x)}
    ranks = {
        "o": b * 2 + x,
        "s": sib_b * 2 + x,
        "x": b * 2 + 1 - x,
        "xs": sib_b * 2 + 1 - x,
        "y": far_b * 2 + x,
        "ys": far_sib_b * 2 + x,
        "d": far_b * 2 + 1 - x,
        "ds": far_sib_b * 2 + 1 - x,
    }
    return ids, ranks

def greet(ids):
    barrier = pltpu.get_barrier_semaphore()
    for device in ids.values():
        pl.semaphore_signal(barrier, inc=1, device_id=device, device_id_type=MESH)
    pl.semaphore_wait(barrier, len(ids))

def tiles(lo, hi, body):
    def step(i, _):
        body(pl.ds(pl.multiple_of(i * TILE, TILE), TILE))
        return 0
    lax.fori_loop(lo // TILE, hi // TILE, step, 0)

def gather_kernel(body_of, n_in, n_out, x_ref, *refs):
    ins = refs[:n_in]; all_ref = refs[n_in]; outs = refs[n_in + 1 : n_in + 1 + n_out]
    held, send, recv, keep = refs[n_in + 1 + n_out :]
    ids, at = plane_place()
    half = x_ref.shape[0] // 2
    parts = (pl.ds(0, half), pl.ds(half, half))
    greet(ids)
    count = [0]
    started = []
    def ship(src, dst, to):
        n = count[0]; count[0] += 1
        c = pltpu.make_async_remote_copy(src_ref=src, dst_ref=dst, send_sem=send.at[n], recv_sem=recv.at[n], device_id=ids[to], device_id_type=MESH)
        c.start(); started.append(c)
        return c
    own = at["o"]
    x0 = ship(x_ref.at[parts[0]], held.at[own, parts[0]], "x")
    y1 = ship(x_ref.at[parts[1]], held.at[own, parts[1]], "y")
    x1 = ship(x_ref.at[parts[1]], held.at[own, parts[1]], "x")
    y0 = ship(x_ref.at[parts[0]], held.at[own, parts[0]], "y")
    s0 = ship(x_ref, held.at[own], "s")
    kept = []
    def done(rank, src):
        c = pltpu.make_async_copy(src, all_ref.at[rank], keep.at[len(kept)])
        c.start(); kept.append(c)
        if body_of is not None:
            body_of(rank, src, ins, outs)
    done(own, x_ref)
    s0.wait_recv()
    done(at["s"], held.at[at["s"]])
    x0.wait_recv()
    ry = ship(held.at[at["x"], parts[0]], held.at[at["x"], parts[0]], "y")
    y1.wait_recv()
    rx = ship(held.at[at["y"], parts[1]], held.at[at["y"], parts[1]], "x")
    x1.wait_recv()
    sx = ship(held.at[at["x"]], held.at[at["x"]], "s")
    y0.wait_recv()
    sy = ship(held.at[at["y"]], held.at[at["y"]], "s")
    done(at["x"], held.at[at["x"]])
    done(at["y"], held.at[at["y"]])
    sx.wait_recv()
    done(at["xs"], held.at[at["xs"]])
    sy.wait_recv()
    done(at["ys"], held.at[at["ys"]])
    ry.wait_recv(); rx.wait_recv()
    sd = ship(held.at[at["d"]], held.at[at["d"]], "s")
    done(at["d"], held.at[at["d"]])
    sd.wait_recv()
    done(at["ds"], held.at[at["ds"]])
    for c in started: c.wait_send()
    for c in kept: c.wait()

def vmem(n): return [pl.BlockSpec(memory_space=pltpu.VMEM)] * n

def plane_gather(x, ins, out_types, body_of, cid, name, ranks=8):
    tok, D = x.shape
    res = pl.pallas_call(
        functools.partial(gather_kernel, body_of, len(ins), len(out_types)),
        out_shape=[jax.ShapeDtypeStruct((ranks, tok, D), x.dtype), *out_types],
        in_specs=vmem(1 + len(ins)),
        out_specs=[pl.BlockSpec(memory_space=pl.ANY)] + vmem(len(out_types)),
        scratch_shapes=[pltpu.VMEM((ranks, tok, D), x.dtype), pltpu.SemaphoreType.DMA((10,)), pltpu.SemaphoreType.DMA((10,)), pltpu.SemaphoreType.DMA((8,))],
        compiler_params=pltpu.CompilerParams(collective_id=cid, has_side_effects=True, vmem_limit_bytes=60 << 20),
        cost_estimate=pl.CostEstimate(flops=1 << 30, bytes_accessed=128 << 20, transcendentals=0),
        name=name,
    )(x, *ins)
    return res[0].reshape(ranks * tok, D), *res[1:]

def gather_dot(x, w, bias, out_dtype, turned, cid, name):
    ranks, tok, D = 8, *x.shape
    N = w.shape[0] if turned else w.shape[1]
    tile = min(N, 512) if N % 512 == 0 else 256
    def body(rank, src, ins, outs):
        w_ref, b_ref = ins
        def step(i, _):
            cols = pl.ds(pl.multiple_of(i * tile, tile), tile)
            if turned:
                y = lax.dot_general(src[...], w_ref[cols, :], (((1,), (1,)), ((), ())), preferred_element_type=single)
            else:
                y = jnp.dot(src[...], w_ref[:, cols], preferred_element_type=single)
            outs[0][rank, :, cols] = (y + b_ref[:, cols]).astype(out_dtype)
            return 0
        lax.fori_loop(0, N // tile, step, 0)
    all_, y = plane_gather(x, (w, bias), [jax.ShapeDtypeStruct((ranks, tok, N), out_dtype)], body, cid, name)
    return all_, y.reshape(ranks * tok, N)

def reduce_kernel(turned, pairs, *refs):
    left, right = refs[:pairs], refs[pairs : 2 * pairs]
    out_ref, sib_out, sib_in, stage, landed, send, recv = refs[2 * pairs :]
    ids, at = plane_place()
    D = out_ref.shape[1]
    mid = D // 2
    greet(ids)
    count = [0]; started = []
    def ship(src, dst, to):
        n = count[0]; count[0] += 1
        c = pltpu.make_async_remote_copy(src_ref=src, dst_ref=dst, send_sem=send.at[n], recv_sem=recv.at[n], device_id=ids[to], device_id_type=MESH)
        c.start(); started.append(c)
        return c
    def term(rank, cols):
        if turned:
            return sum(dot_nt(a[rank], w[cols, :]) for a, w in zip(left, right))
        rows = [w[:, 1, :, cols].reshape(-1, TILE) if len(w.shape) == 4 else w[:, cols] for w in right]
        return sum(dot(a[rank], w) for a, w in zip(left, rows))
    order = ("d", "x", "y", "o")
    twin = {"d": "ds", "x": "xs", "y": "ys", "o": "s"}
    sib = []
    def to_sibling():
        j = len(sib)
        def fill(cols):
            sib_out[j, :, cols] = term(at[twin[order[j]]], cols).astype(bfloat)
        tiles(0, D, fill)
        sib.append(ship(sib_out.at[j], sib_in.at[j], "s"))
    def pair(j, cols):
        return term(at[order[j]], cols) + sib_in[j, :, cols].astype(single)
    def local(h, cols):
        return pl.ds(pl.multiple_of(cols.start - h * mid, TILE), TILE)
    def put(j, h, extra=None):
        def fill(cols):
            value = pair(j, cols)
            if extra is not None:
                value = value + landed[extra, :, local(h, cols)].astype(single)
            stage[j, h, :, local(h, cols)] = value.astype(bfloat)
        tiles(h * mid, (h + 1) * mid, fill)
    to_sibling()
    to_sibling()
    sib[0].wait_recv()
    put(0, 0)
    d_a = ship(stage.at[0, 0], landed.at[0], "x")
    put(0, 1)
    d_b = ship(stage.at[0, 1], landed.at[1], "y")
    to_sibling()
    sib[1].wait_recv()
    put(1, 0)
    x_a = ship(stage.at[1, 0], landed.at[2], "x")
    sib[2].wait_recv()
    put(2, 1)
    y_b = ship(stage.at[2, 1], landed.at[3], "y")
    to_sibling()
    sib[3].wait_recv()
    def first(cols):
        out_ref[:, cols] = pair(3, cols)
    tiles(0, D, first)
    d_b.wait_recv()
    put(1, 1, extra=1)
    x_b = ship(stage.at[1, 1], landed.at[5], "x")
    d_a.wait_recv()
    put(2, 0, extra=0)
    y_a = ship(stage.at[2, 0], landed.at[4], "y")
    x_a.wait_recv(); y_b.wait_recv(); x_b.wait_recv(); y_a.wait_recv()
    for h, (n, m) in enumerate(((2, 4), (3, 5))):
        def add(cols, h=h, n=n, m=m):
            c = local(h, cols)
            out_ref[:, cols] = out_ref[:, cols] + landed[n, :, c].astype(single) + landed[m, :, c].astype(single)
        tiles(h * mid, (h + 1) * mid, add)
    for c in started: c.wait_send()

def dot_reduce(left, right, turned, cid, name):
    ranks = 8
    D = right[0].shape[0] if turned else right[0].shape[-1]
    tok = left[0].size // left[0].shape[-1] // ranks
    return pl.pallas_call(
        functools.partial(reduce_kernel, turned, len(left)),
        out_shape=jax.ShapeDtypeStruct((tok, D), single),
        in_specs=vmem(2 * len(left)), out_specs=vmem(1)[0],
        scratch_shapes=[pltpu.VMEM((4, tok, D), bfloat), pltpu.VMEM((4, tok, D), bfloat), pltpu.VMEM((3, 2, tok, D // 2), bfloat), pltpu.VMEM((6, tok, D // 2), bfloat),
            pltpu.SemaphoreType.DMA((10,)), pltpu.SemaphoreType.DMA((10,))],
        compiler_params=pltpu.CompilerParams(collective_id=cid, has_side_effects=True, vmem_limit_bytes=60 << 20),
        cost_estimate=pl.CostEstimate(flops=1 << 30, bytes_accessed=128 << 20, transcendentals=0),
        name=name,
    )(*[a.reshape(ranks, tok, -1) for a in left], *right)


def dot(left, right):
    return jnp.dot(left, right, preferred_element_type=single)


def dot_tn(left, right):
    return lax.dot_general(left, right, (((0,), (0,)), ((), ())), preferred_element_type=single)


def dot_nt(left, right):
    return lax.dot_general(left, right, (((1,), (1,)), ((), ())), preferred_element_type=single)


def layer_norm(values, gain_vec, shift_vec):
    center = jnp.mean(values, axis=-1, keepdims=True)
    centered = values - center
    spread = jnp.mean(centered * centered, axis=-1, keepdims=True)
    return centered * lax.rsqrt(spread + 1e-05) * gain_vec + shift_vec


def column_sums(matrix):
    return jnp.sum(matrix.astype(single), axis=0)


def shipper(send, recv, ids):
    started = []

    def ship(src, dst, to):
        n = len(started)
        copy = pltpu.make_async_remote_copy(
            src_ref=src, dst_ref=dst, send_sem=send.at[n], recv_sem=recv.at[n], device_id=ids[to], device_id_type=MESH
        )
        copy.start()
        started.append(copy)
        return copy

    return ship, started


TWIN = {"o": "s", "x": "xs", "y": "ys", "d": "ds"}


def unit_rows(w_ref, i):
    parts, _, units, D = w_ref.shape
    return w_ref[:, i].reshape(parts * units, D)


def hidden_units(src, branch, w_ref, b_ref, hid_ref, pg_ref, pb_ref, rank):
    pre = dot_nt(src[...], unit_rows(w_ref, 0)) + b_ref[...]
    square = pre * pre
    bend = jnp.tanh(0.7978845608028654 * (pre + 0.044715 * (pre * square)))
    rise = 0.5 * (1.0 + bend)
    hid_ref[rank] = (pre * rise).astype(bfloat)
    slope = rise + (0.5 * 0.7978845608028654) * pre * (1.0 - bend * bend) * (1.0 + 3 * 0.044715 * square)
    grad = (dot_nt(branch[...], unit_rows(w_ref, 1)) * slope).astype(bfloat)
    pg_ref[rank] = grad
    pb_ref[...] += jnp.sum(grad.astype(single), axis=0, keepdims=True)


def first_units_kernel(
    x_ref, bg_ref, w_ref, b_ref, all_ref, hid_ref, pg_ref, pb_ref, grad_ref,
    held, bg, total, send, recv, keep, load,
):
    ids, at = plane_place()
    tok = x_ref.shape[0]
    half = tok // 2
    parts = (pl.ds(0, half), pl.ds(half, half))
    own = at["o"]
    loads = {}
    for n, name in enumerate(at):
        loads[name] = pltpu.make_async_copy(bg_ref.at[at[name]], bg.at[at[name]], load.at[n])
        loads[name].start()
    greet(ids)
    ship, started = shipper(send, recv, ids)
    x0 = ship(x_ref.at[parts[0]], held.at[own, parts[0]], "x")
    y1 = ship(x_ref.at[parts[1]], held.at[own, parts[1]], "y")
    x1 = ship(x_ref.at[parts[1]], held.at[own, parts[1]], "x")
    y0 = ship(x_ref.at[parts[0]], held.at[own, parts[0]], "y")
    s0 = ship(x_ref, held.at[own], "s")
    pb_ref[...] = jnp.zeros_like(pb_ref)
    kept = []

    def units(name):
        rank = at[name]
        src = x_ref if name == "o" else held.at[rank]
        copy = pltpu.make_async_copy(src, all_ref.at[rank], keep.at[len(kept)])
        copy.start()
        kept.append(copy)
        loads[name].wait()
        hidden_units(src, bg.at[rank], w_ref, b_ref, hid_ref, pg_ref, pb_ref, rank)

    def weigh(name, last=False):
        units_at = grad_ref.shape[2]
        per = 256 // units_at

        def rows(i, _):
            here = pl.ds(pl.multiple_of(i * 256, 256), 256)
            owners = pl.ds(i * per, per)
            for j, left in enumerate((pg_ref, hid_ref)):
                term = 0
                for n in (name, TWIN[name]):
                    right = bg[at[n]] if j else (x_ref[...] if n == "o" else held[at[n]])
                    term = term + dot_tn(left[at[n], :, here], right)
                term = term.reshape(per, units_at, -1)
                if name == "o":
                    total[owners, j] = term
                elif last:
                    grad_ref[owners, j] = (total[owners, j] + term).astype(bfloat)
                else:
                    total[owners, j] += term
            return 0

        lax.fori_loop(0, hid_ref.shape[2] // 256, rows, 0)

    units("o")
    s0.wait_recv()
    units("s")
    x0.wait_recv()
    ry = ship(held.at[at["x"], parts[0]], held.at[at["x"], parts[0]], "y")
    y1.wait_recv()
    rx = ship(held.at[at["y"], parts[1]], held.at[at["y"], parts[1]], "x")
    weigh("o")
    x1.wait_recv()
    sx = ship(held.at[at["x"]], held.at[at["x"]], "s")
    y0.wait_recv()
    sy = ship(held.at[at["y"]], held.at[at["y"]], "s")
    units("x")
    sx.wait_recv()
    units("xs")
    units("y")
    sy.wait_recv()
    units("ys")
    weigh("x")
    ry.wait_recv()
    rx.wait_recv()
    sd = ship(held.at[at["d"]], held.at[at["d"]], "s")
    weigh("y")
    units("d")
    sd.wait_recv()
    units("ds")
    weigh("d", last=True)
    for copy in started:
        copy.wait_send()
    for copy in kept:
        copy.wait()


def last_units_kernel(
    all_ref, bg_ref, pg1_ref, w1_ref, w_ref, b_ref, hid_ref, pb_ref, r_ref, grad_ref,
    held, bg, pg_ref, sib_out, sib_in, stage, landed, send, recv, load, load_b,
):
    ids, at = plane_place()
    ranks, tok, D = held.shape
    mid = D // 2
    names = ("ds", "d", "xs", "x", "ys", "y", "s", "o")
    loads = {}
    for n, name in enumerate(names):
        loads[name] = [
            pltpu.make_async_copy(all_ref.at[at[name]], held.at[at[name]], load.at[n]),
            pltpu.make_async_copy(bg_ref.at[at[name]], bg.at[at[name]], load_b.at[n]),
        ]
        for copy in loads[name]:
            copy.start()
    greet(ids)
    ship, started = shipper(send, recv, ids)
    pb_ref[...] = jnp.zeros_like(pb_ref)

    def units(name):
        for copy in loads[name]:
            copy.wait()
        rank = at[name]
        hidden_units(held.at[rank], bg.at[rank], w_ref, b_ref, hid_ref, pg_ref, pb_ref, rank)

    def term(name, cols):
        rank = at[name]
        first, second = [w[:, 0, :, cols].reshape(-1, TILE) for w in (w1_ref, w_ref)]
        return dot(pg1_ref[rank], first) + dot(pg_ref[rank], second)

    order = ("d", "x", "y", "o")

    def to_sibling(j):
        def fill(cols):
            sib_out[j, :, cols] = term(TWIN[order[j]], cols).astype(bfloat)

        tiles(0, D, fill)
        return ship(sib_out.at[j], sib_in.at[j], "s")

    def pair(j, cols):
        return term(order[j], cols) + sib_in[j, :, cols].astype(single)

    def local(h, cols):
        return pl.ds(pl.multiple_of(cols.start - h * mid, TILE), TILE)

    def put(j, h, extra=None):
        def fill(cols):
            value = pair(j, cols)
            if extra is not None:
                value = value + landed[extra, :, local(h, cols)].astype(single)
            stage[j, h, :, local(h, cols)] = value.astype(bfloat)

        tiles(h * mid, (h + 1) * mid, fill)

    units("ds")
    d_sib = to_sibling(0)
    units("d")
    d_sib.wait_recv()
    put(0, 0)
    d_a = ship(stage.at[0, 0], landed.at[0], "x")
    put(0, 1)
    d_b = ship(stage.at[0, 1], landed.at[1], "y")
    units("xs")
    x_sib = to_sibling(1)
    units("x")
    x_sib.wait_recv()
    put(1, 0)
    x_a = ship(stage.at[1, 0], landed.at[2], "x")
    units("ys")
    y_sib = to_sibling(2)
    units("y")
    y_sib.wait_recv()
    put(2, 1)
    y_b = ship(stage.at[2, 1], landed.at[3], "y")
    d_b.wait_recv()
    put(1, 1, extra=1)
    x_b = ship(stage.at[1, 1], landed.at[5], "x")
    d_a.wait_recv()
    put(2, 0, extra=0)
    y_a = ship(stage.at[2, 0], landed.at[4], "y")
    units("s")
    own_sib = to_sibling(3)
    units("o")
    own_sib.wait_recv()

    def first(cols):
        r_ref[:, cols] = pair(3, cols)

    tiles(0, D, first)

    units_at = grad_ref.shape[2]
    per = 256 // units_at
    tokens = ranks * tok

    def grads(i, _):
        here = pl.ds(pl.multiple_of(i * 256, 256), 256)
        owners = pl.ds(i * per, per)
        for j, (left, right) in enumerate(((pg_ref, held), (hid_ref, bg))):
            value = dot_tn(left[:, :, here].reshape(tokens, 256), right[...].reshape(tokens, D))
            grad_ref[owners, j] = value.astype(bfloat).reshape(per, units_at, D)
        return 0

    lax.fori_loop(0, hid_ref.shape[2] // 256, grads, 0)
    for copy in (x_a, y_b, x_b, y_a):
        copy.wait_recv()
    for h, (n, m) in enumerate(((2, 4), (3, 5))):

        def add(cols, h=h, n=n, m=m):
            c = local(h, cols)
            r_ref[:, cols] = r_ref[:, cols] + landed[n, :, c].astype(single) + landed[m, :, c].astype(single)

        tiles(h * mid, (h + 1) * mid, add)
    for copy in started:
        copy.wait_send()


def first_units(x, bg, w, bias, cid):
    ranks = 8
    tok, D = x.shape
    F = bias.shape[1]
    anywhere = pl.BlockSpec(memory_space=pl.ANY)
    inside = pl.BlockSpec(memory_space=pltpu.VMEM)
    return pl.pallas_call(
        first_units_kernel,
        out_shape=[
            jax.ShapeDtypeStruct((ranks, tok, D), bfloat),
            jax.ShapeDtypeStruct((ranks, tok, F), bfloat),
            jax.ShapeDtypeStruct((ranks, tok, F), bfloat),
            jax.ShapeDtypeStruct((1, F), single),
            jax.ShapeDtypeStruct(w.shape, bfloat),
        ],
        in_specs=[inside, anywhere, inside, inside],
        out_specs=[anywhere, inside, inside, inside, inside],
        scratch_shapes=[
            pltpu.VMEM((ranks, tok, D), bfloat),
            pltpu.VMEM((ranks, tok, D), bfloat),
            pltpu.VMEM(w.shape, single),
            pltpu.SemaphoreType.DMA((10,)),
            pltpu.SemaphoreType.DMA((10,)),
            pltpu.SemaphoreType.DMA((8,)),
            pltpu.SemaphoreType.DMA((8,)),
        ],
        compiler_params=pltpu.CompilerParams(collective_id=cid, has_side_effects=True, vmem_limit_bytes=62 << 20),
        cost_estimate=pl.CostEstimate(flops=1 << 30, bytes_accessed=160 << 20, transcendentals=0),
        name="first_units",
    )(x, bg, w, bias)


def last_units(rows, bg, pg, w1, w, bias, cid):
    ranks, tok, D = rows.shape
    F = bias.shape[1]
    anywhere = pl.BlockSpec(memory_space=pl.ANY)
    inside = pl.BlockSpec(memory_space=pltpu.VMEM)
    return pl.pallas_call(
        last_units_kernel,
        out_shape=[
            jax.ShapeDtypeStruct((ranks, tok, F), bfloat),
            jax.ShapeDtypeStruct((1, F), single),
            jax.ShapeDtypeStruct((tok, D), single),
            jax.ShapeDtypeStruct(w.shape, bfloat),
        ],
        in_specs=[anywhere, anywhere, inside, inside, inside, inside],
        out_specs=[inside] * 4,
        scratch_shapes=[
            pltpu.VMEM((ranks, tok, D), bfloat),
            pltpu.VMEM((ranks, tok, D), bfloat),
            pltpu.VMEM((ranks, tok, F), bfloat),
            pltpu.VMEM((4, tok, D), bfloat),
            pltpu.VMEM((4, tok, D), bfloat),
            pltpu.VMEM((3, 2, tok, D // 2), bfloat),
            pltpu.VMEM((6, tok, D // 2), bfloat),
            pltpu.SemaphoreType.DMA((10,)),
            pltpu.SemaphoreType.DMA((10,)),
            pltpu.SemaphoreType.DMA((8,)),
            pltpu.SemaphoreType.DMA((8,)),
        ],
        compiler_params=pltpu.CompilerParams(collective_id=cid, has_side_effects=True, vmem_limit_bytes=62 << 20),
        cost_estimate=pl.CostEstimate(flops=1 << 30, bytes_accessed=160 << 20, transcendentals=0),
        name="last_units",
    )(rows, bg, pg, w1, w, bias)


def everyone(width):
    b, z, x = lax.axis_index("b"), lax.axis_index("z"), lax.axis_index("x")
    rank, me = b * 2 + x, (b * 4 + z) * 2 + x

    def in_plane(i):
        other = lax.rem(rank + i, 8)
        return other, (other // 2, z, lax.rem(other, 2))

    def anywhere(i):
        other = lax.rem(me + i, width)
        return other, (other // 8, lax.rem(other // 2, 4), lax.rem(other, 2))

    return rank, me, in_plane, anywhere


def exchange(blocks, landed, rows, gathered, same_row, sems):
    plane_send, plane_recv, all_send, all_recv = sems
    width = gathered.shape[0]
    rank, me, in_plane, anywhere = everyone(width)
    barrier = pltpu.get_barrier_semaphore()

    def each(count, body):
        def step(i, _):
            body(i)
            return 0

        lax.fori_loop(1, count, step, 0)

    each(width, lambda i: pl.semaphore_signal(barrier, inc=1, device_id=anywhere(i)[1], device_id_type=MESH))
    pl.semaphore_wait(barrier, width - 1)

    def block(i):
        other, device = in_plane(i)
        return pltpu.make_async_remote_copy(
            src_ref=blocks.at[other], dst_ref=landed.at[rank], send_sem=plane_send.at[i], recv_sem=plane_recv.at[i],
            device_id=device, device_id_type=MESH,
        )

    def row(i):
        other, device = anywhere(i)
        return pltpu.make_async_remote_copy(
            src_ref=rows.at[0] if same_row else rows.at[other], dst_ref=gathered.at[me],
            send_sem=all_send.at[i], recv_sem=all_recv.at[i], device_id=device, device_id_type=MESH,
        )

    each(8, lambda i: block(i).start())
    each(width, lambda i: row(i).start())
    landed[rank] = blocks[rank]
    gathered[me] = rows[0] if same_row else rows[me]
    each(width, lambda i: row(i).wait())
    each(8, lambda i: block(i).wait())


def head_at(rank, i):
    return (rank // 2 * 4 + i) * 2 + rank % 2


def spread_kernel(q_ref, k_ref, v_ref, pack_ref, q_out, kv_out, pack_out, blocks, landed, gathered, *sems):
    cols = q_out.shape[2]
    for rank in range(8):
        for part, ref in enumerate((q_ref, k_ref, v_ref)):
            heads = [ref[:, head_at(rank, i) * HEAD_DIM : (head_at(rank, i) + 1) * HEAD_DIM] for i in range(4)]
            blocks[rank, :, part * cols : (part + 1) * cols] = jnp.concatenate(heads, axis=1)
    exchange(blocks, landed, pack_ref, gathered, True, sems)
    q_out[...] = landed[:, :, :cols]
    kv_out[...] = landed[:, :, cols:]
    pack_out[...] = gathered[...]


def settle_kernel(w_ref, rows_ref, q_out, k_out, v_out, sums_ref, landed, gathered, *sems):
    cols = w_ref.shape[2] // 3
    exchange(w_ref, landed, rows_ref, gathered, False, sems)
    for part, out in enumerate((q_out, k_out, v_out)):
        for pair in range(out.shape[1] // 128):
            sides = []
            for head in (2 * pair, 2 * pair + 1):
                rank, i = head // 8 * 2 + head % 2, head // 2 % 4
                at = part * cols + i * HEAD_DIM
                sides.append(landed[rank, :, at : at + HEAD_DIM])
            out[:, pair * 128 : (pair + 1) * 128] = jnp.concatenate(sides, axis=1).astype(single)
    sums_ref[...] = jnp.sum(gathered[...], axis=0)


def exchange_call(kernel, out_shape, args, blocks, landed, gathered, cid, name):
    inside = pl.BlockSpec(memory_space=pltpu.VMEM)
    width = gathered[0]
    return pl.pallas_call(
        kernel,
        out_shape=out_shape,
        in_specs=[inside] * len(args),
        out_specs=[inside] * len(out_shape),
        scratch_shapes=blocks
        + [
            pltpu.VMEM(landed, bfloat),
            pltpu.VMEM(gathered, single),
            pltpu.SemaphoreType.DMA((8,)),
            pltpu.SemaphoreType.DMA((8,)),
            pltpu.SemaphoreType.DMA((width,)),
            pltpu.SemaphoreType.DMA((width,)),
        ],
        compiler_params=pltpu.CompilerParams(collective_id=cid, has_side_effects=True, vmem_limit_bytes=32 << 20),
        cost_estimate=pl.CostEstimate(flops=1 << 20, bytes_accessed=32 << 20, transcendentals=0),
        name=name,
    )(*args)


def spread(q, k, v, pack, devices, cid):
    rows, D = q.shape
    cols = D // 8
    return exchange_call(
        spread_kernel,
        [
            jax.ShapeDtypeStruct((8, rows, cols), bfloat),
            jax.ShapeDtypeStruct((8, rows, 2 * cols), bfloat),
            jax.ShapeDtypeStruct((devices, 1, pack.shape[0]), single),
        ],
        (q, k, v, pack[None, None]),
        [pltpu.VMEM((8, rows, 3 * cols), bfloat)],
        (8, rows, 3 * cols),
        (devices, 1, pack.shape[0]),
        cid,
        "spread",
    )


def settle(weights, rows, cid):
    _, tall, wide = weights.shape
    D = wide // 3 * 8
    return exchange_call(
        settle_kernel,
        [jax.ShapeDtypeStruct((tall, D), single)] * 3 + [jax.ShapeDtypeStruct((1, rows.shape[1]), single)],
        (weights, rows[:, None]),
        [],
        weights.shape,
        (rows.shape[0], 1, rows.shape[1]),
        cid,
        "settle",
    )


def windows(span):
    block = span // 2
    return [(i * block, i * block + block + span) for i in range(2)]

def key_window(before, own, lo, hi, span):
    return jnp.concatenate([before[lo:span], own[0 : hi - span]], axis=0)

def hidden_bias(start_ref, i, block, lo, hi, span):
    rows = span + i * block + lax.broadcasted_iota(jnp.int32, (block, hi - lo), 0)
    keys = lo + lax.broadcasted_iota(jnp.int32, (block, hi - lo), 1)
    start = start_ref[i * block : (i + 1) * block, :]
    return jnp.where((keys >= start) & (keys <= rows), 0.0, -1e30).astype(single)

def attend_kernel(start_ref, q_ref, k_ref, v_ref, kb_ref, vb_ref, out_ref):
    span, cols = q_ref.shape
    block = span // 2
    lane = lax.broadcasted_iota(jnp.int32, (block, cols), 1) // HEAD_DIM
    for i, (lo, hi) in enumerate(windows(span)):
        rows = pl.ds(i * block, block)
        bias = hidden_bias(start_ref, i, block, lo, hi, span)
        keys = key_window(kb_ref, k_ref, lo, hi, span)
        vals = key_window(vb_ref, v_ref, lo, hi, span)
        query = q_ref[rows, :] * jnp.asarray(HEAD_DIM ** (-0.5), bfloat)
        def head(h, total):
            mine = lane == h
            scores = dot_nt(jnp.where(mine, query, 0), keys) + bias
            weights = jnp.exp(scores - jnp.max(scores, axis=1, keepdims=True))
            part = jnp.dot(weights.astype(bfloat), vals, preferred_element_type=single)
            part = part * (1.0 / jnp.sum(weights, axis=1, keepdims=True))
            return jnp.where(mine, part, total)
        total = lax.fori_loop(0, cols // HEAD_DIM, head, jnp.zeros((block, cols), single), unroll=True)
        out_ref[rows, :] = total.astype(bfloat)

def attend_back_kernel(start_ref, q_ref, k_ref, v_ref, kb_ref, vb_ref, do_ref, dq_ref, edge_ref, pair_ref, dk, dv):
    span, cols = q_ref.shape
    block = span // 2
    scale = HEAD_DIM ** (-0.5)
    dk[...] = jnp.zeros_like(dk)
    dv[...] = jnp.zeros_like(dv)
    lane = lax.broadcasted_iota(jnp.int32, (block, cols), 1) // HEAD_DIM
    for i, (lo, hi) in enumerate(windows(span)):
        rows = pl.ds(i * block, block)
        bias = hidden_bias(start_ref, i, block, lo, hi, span)
        keys = key_window(kb_ref, k_ref, lo, hi, span)
        vals = key_window(vb_ref, v_ref, lo, hi, span)
        query = q_ref[rows, :] * jnp.asarray(scale, bfloat)
        grad = do_ref[rows, :]
        def head(h, total):
            mine = lane == h
            query_h = jnp.where(mine, query, 0)
            grad_h = jnp.where(mine, grad, 0)
            scores = dot_nt(query_h, keys) + bias
            weights = jnp.exp(scores - jnp.max(scores, axis=1, keepdims=True))
            probs = weights * (1.0 / jnp.sum(weights, axis=1, keepdims=True))
            prob_grad = dot_nt(grad_h, vals)
            row_dot = jnp.sum(probs * prob_grad, axis=1, keepdims=True)
            score_grad = (probs * (prob_grad - row_dot)).astype(bfloat)
            dv[lo:hi, :] += dot_tn(probs.astype(bfloat), grad_h)
            dk[lo:hi, :] += dot_tn(score_grad, query_h)
            part = jnp.dot(score_grad, keys, preferred_element_type=single)
            return jnp.where(mine, part, total)
        total = lax.fori_loop(0, cols // HEAD_DIM, head, jnp.zeros((block, cols), single), unroll=True)
        dq_ref[rows, :] = (total * scale).astype(bfloat)
    edge_ref[:, :cols] = dk[:span, :].astype(bfloat)
    edge_ref[:, cols:] = dv[:span, :].astype(bfloat)
    pair_ref[:, :cols] = dk[span:, :]
    pair_ref[:, cols:] = dv[span:, :]

def attention_specs(span, cols):
    def at(j):
        return pl.BlockSpec((span, cols), lambda g: (g, j))
    return [pl.BlockSpec((span, 1), lambda g: (g, 0)), at(0), at(0), at(1), at(0), at(1)]

def attend(starts, query, key_value, before, groups):
    span, cols = query.shape[0] // groups, query.shape[1]
    return pl.pallas_call(
        attend_kernel,
        grid=(groups,),
        out_shape=jax.ShapeDtypeStruct((groups * span, cols), bfloat),
        in_specs=attention_specs(span, cols),
        out_specs=pl.BlockSpec((span, cols), lambda g: (g, 0)),
        compiler_params=pltpu.CompilerParams(vmem_limit_bytes=60 << 20),
        name="attend",
    )(starts, query, key_value, key_value, before, before)

def attend_back(starts, query, key_value, before, grad, groups):
    span, cols = query.shape[0] // groups, query.shape[1]
    rows = groups * span
    return pl.pallas_call(
        attend_back_kernel,
        grid=(groups,),
        out_shape=[jax.ShapeDtypeStruct((rows, cols), bfloat), jax.ShapeDtypeStruct((rows, 2 * cols), bfloat), jax.ShapeDtypeStruct((rows, 2 * cols), single)],
        in_specs=attention_specs(span, cols) + [pl.BlockSpec((span, cols), lambda g: (g, 0))],
        out_specs=[pl.BlockSpec((span, cols), lambda g: (g, 0))] + [pl.BlockSpec((span, 2 * cols), lambda g: (g, 0))] * 2,
        scratch_shapes=[pltpu.VMEM((2 * span, cols), single)] * 2,
        compiler_params=pltpu.CompilerParams(vmem_limit_bytes=60 << 20),
        name="attend_back",
    )(starts, query, key_value, key_value, before, before, grad)


def attention_heads(starts, query, key_value, before, groups):
    span, cols = query.shape[0] // groups, query.shape[1]
    both = jnp.concatenate([before.reshape(groups, span, -1), key_value.reshape(groups, span, -1)], axis=1)
    key_two, value_two = [both[..., i * cols : (i + 1) * cols].reshape(groups, 2 * span, -1, HEAD_DIM) for i in (0, 1)]
    query = query.reshape(groups, span, -1, HEAD_DIM)
    keys = jnp.arange(2 * span)[None, None, :]
    rows = span + jnp.arange(span)[None, :, None]
    allowed = (keys >= starts.reshape(groups, span, 1)) & (keys <= rows)
    scores = jnp.einsum("gqhd,gkhd->ghqk", query, key_two, preferred_element_type=single) * HEAD_DIM ** (-0.5)
    scores = jnp.where(allowed[:, None], scores, -1e30)
    weights = jnp.exp(scores - jnp.max(scores, axis=-1, keepdims=True))
    return query, key_two, value_two, weights / jnp.sum(weights, axis=-1, keepdims=True)


def attention_forward(starts, query, key_value, before, groups):
    if query.shape[1] % 128 == 0:
        return attend(starts, query, key_value, before, groups)
    _, _, value_two, probs = attention_heads(starts, query, key_value, before, groups)
    context = jnp.einsum("ghqk,gkhd->gqhd", probs.astype(bfloat), value_two, preferred_element_type=single)
    return context.astype(bfloat).reshape(query.shape)


def attention_backward(starts, query, key_value, before, grad, groups):
    if query.shape[1] % 128 == 0:
        return attend_back(starts, query, key_value, before, grad, groups)
    rows = query.shape[0]
    query, key_two, value_two, probs = attention_heads(starts, query, key_value, before, groups)
    span = query.shape[1]
    grad = grad.reshape(query.shape)
    prob_grad = jnp.einsum("gqhd,gkhd->ghqk", grad, value_two, preferred_element_type=single)
    row_dot = jnp.sum(probs * prob_grad, axis=-1, keepdims=True)
    score_grad = (probs * (prob_grad - row_dot)).astype(bfloat)
    query_grad = jnp.einsum("ghqk,gkhd->gqhd", score_grad, key_two, preferred_element_type=single) * HEAD_DIM ** (-0.5)
    key_grad = jnp.einsum("ghqk,gqhd->gkhd", score_grad, query, preferred_element_type=single) * HEAD_DIM ** (-0.5)
    value_grad = jnp.einsum("ghqk,gqhd->gkhd", probs.astype(bfloat), grad, preferred_element_type=single)
    pair = jnp.concatenate([t.reshape(groups, 2 * span, -1) for t in (key_grad, value_grad)], axis=2)
    edge, pair = [t.reshape(rows, -1) for t in (pair[:, :span].astype(bfloat), pair[:, span:])]
    return query_grad.astype(bfloat).reshape(rows, -1), edge, pair


def norm_backward(values, out_grad, gain_vec):
    center = jnp.mean(values, axis=-1, keepdims=True)
    centered = values - center
    rs = lax.rsqrt(jnp.mean(centered * centered, axis=-1, keepdims=True) + 1e-05)
    xhat = centered * rs
    g = out_grad * gain_vec
    part = rs * (g - jnp.mean(g, axis=-1, keepdims=True) - xhat * jnp.mean(g * xhat, axis=-1, keepdims=True))
    return part, jnp.sum(out_grad * xhat, axis=0), jnp.sum(out_grad, axis=0)


def on_device(
    inputs,
    exit_layers,
    lengths,
    layer_index,
    out_grad,
    ln1_gain,
    ln1_bias,
    q_weight,
    q_bias,
    k_weight,
    v_weight,
    v_bias,
    o_weight,
    o_bias,
    ln2_gain,
    ln2_bias,
    fc1_weight,
    fc1_bias,
    fc2_weight,
    fc2_bias,
):
    B, Z, X = lax.axis_size("b"), lax.axis_size("z"), lax.axis_size("x")
    R = B * X
    local = inputs[0].astype(single)
    tok, D = local.shape
    span = X * tok
    group_tok = Z * span
    at_z, at_x = lax.axis_index("z"), lax.axis_index("x")
    rank = lax.axis_index("b") * X + at_x
    rows_dev = q_weight.shape[0]
    cols = D // R
    heads = cols // HEAD_DIM
    whole_heads = rows_dev % HEAD_DIM == 0
    fast = (B, Z, X, rows_dev) == (4, 4, 2, HEAD_DIM)

    group_active = (exit_layers[0] > layer_index[0]).astype(single)
    active_total = jnp.sum(group_active)
    active = lax.dynamic_slice_in_dim(group_active, at_z * span + at_x * tok, tok, 0)[:, None]

    count = lengths.shape[1]
    upto = jnp.arange(count)[:, None] <= jnp.arange(count)[None, :]
    def to_ranks(matrix):
        lead = matrix.shape[:-1]
        if whole_heads:
            matrix = matrix.reshape(*lead, B, Z, X, rows_dev)
            k = len(lead)
            return matrix.transpose(k, k + 2, *range(k), k + 1, k + 3).reshape(R, *lead, cols)
        return jnp.moveaxis(matrix.reshape(*lead, R, cols), -2, 0)

    def from_ranks(parts):
        if whole_heads:
            parts = parts.reshape(B, X, -1, Z, rows_dev)
            return parts.transpose(2, 0, 3, 1, 4).reshape(-1, D)
        return parts.transpose(1, 0, 2).reshape(-1, D)

    def mine(vector):
        return lax.dynamic_index_in_dim(to_ranks(vector), rank, 0, keepdims=False)

    if whole_heads:
        weight_o = lax.all_gather(o_weight, "z", axis=0, tiled=True)
    else:
        weight_o = lax.dynamic_slice_in_dim(lax.all_gather(o_weight, ALL, axis=0, tiled=True), rank * cols, cols, 0)
    small = [ln1_gain, ln1_bias, q_bias, v_bias, o_bias, ln2_gain, ln2_bias, fc2_bias]
    pack = jnp.concatenate([v.astype(single) for v in (*small, fc1_bias, lengths[0])])
    pack = jnp.concatenate([pack, jnp.zeros((-pack.shape[0] % 128,), single)])
    if fast:
        query_mine, pair_mine, pack = spread(q_weight, k_weight, v_weight, pack, R * Z, 8)
        query_mine, pair_mine, pack = query_mine.reshape(-1, cols), pair_mine.reshape(-1, 2 * cols), pack[:, 0]
    else:
        qkv_parts = jnp.concatenate([to_ranks(q_weight), to_ranks(k_weight), to_ranks(v_weight)], axis=2)
        qkv_mine = lax.all_to_all(qkv_parts, PLANE, split_axis=0, concat_axis=0, tiled=True).reshape(D // Z, 3 * cols)
        query_mine, pair_mine = qkv_mine[:, :cols], qkv_mine[:, cols:]
        pack = jnp.broadcast_to(pack, (R * Z, pack.shape[0]))
        pack = lax.all_to_all(pack, ALL, split_axis=0, concat_axis=0, tiled=True)
    vectors = [pack[:, i * rows_dev : (i + 1) * rows_dev].reshape(-1) for i in range(len(small))]
    gain_one, bias_one, bias_q, bias_v, bias_o, gain_two, bias_two, bias_down = vectors
    pack = pack.reshape(B, Z, X, -1)[..., len(small) * rows_dev :]
    up_dev = fc1_bias.shape[0]
    bias_up = lax.dynamic_index_in_dim(
        pack[..., :up_dev].transpose(0, 2, 1, 3).reshape(R, Z * up_dev), rank, 0, keepdims=False
    )
    group_lengths = pack[:, 0, 0, up_dev : up_dev + count].astype(jnp.int32)
    ends = jnp.sum(jnp.where(upto, group_lengths[:, :, None], 0), axis=1)
    places = at_z * span + jnp.arange(span, dtype=jnp.int32)
    starts = jnp.max(jnp.where(ends[:, None, :] <= places[None, :, None], ends[:, None, :], 0), axis=2)
    starts = starts - (at_z - 1) * span

    def feature_rows(mine):
        full = lax.all_gather(mine, "z", axis=0, tiled=True)
        return full.reshape(Z, B, X, rows_dev, -1).transpose(1, 0, 2, 3, 4).reshape(D, -1)

    weight_kv = feature_rows(pair_mine)
    bias_kv = jnp.concatenate([jnp.zeros((cols,), single), mine(bias_v)])
    bias_one, query_mine, weight_o = lax.optimization_barrier((bias_one, query_mine, weight_o))
    normed_low = layer_norm(local, gain_one, bias_one).astype(bfloat)

    def gather_plane(rows, cid, name):
        if fast:
            return plane_gather(rows, (), [], None, cid, name)[0]
        return lax.all_gather(rows, PLANE, axis=0, tiled=True)

    def gather_plane_dot(rows, weight, shift, out_type, turned, cid, name):
        if fast:
            return gather_dot(rows, weight, shift, out_type, turned, cid, name)
        rows = lax.all_gather(rows, PLANE, axis=0, tiled=True)
        return rows, ((dot_nt if turned else dot)(rows, weight) + shift).astype(out_type)

    def reduce_plane(left, weight, turned, cid, name):
        if fast:
            return dot_reduce([left], [weight], turned, cid, name)
        terms = (dot_nt if turned else dot)(left, weight).astype(bfloat)
        return lax.psum_scatter(terms, PLANE, scatter_dimension=0, tiled=True).astype(single)

    normed_all = gather_plane(normed_low, 0, "gather_normed")
    units = fc1_bias.shape[0] // 2
    halves = [jnp.concatenate([fc1_weight.T[i : i + units], fc2_weight[i : i + units]]) for i in (0, units)]

    def gather_units(mine):
        return lax.all_gather(mine, "z", axis=0, tiled=True).reshape(Z, 2, units, D)

    normed_all, weight_kv, unit_one = lax.optimization_barrier((normed_all, weight_kv, halves[0]))
    weight_q = feature_rows(query_mine)
    unit_one = gather_units(unit_one)
    key_value = (dot(normed_all, weight_kv) + bias_kv).astype(bfloat)
    up = [(i, i + 1) for i in range(Z - 1)]
    down = [(i + 1, i) for i in range(Z - 1)]
    cotangent = out_grad[0].astype(single) * (group_tok / active_total)
    branch_grad = (active * cotangent).astype(bfloat)
    down_b_grad = column_sums(branch_grad)
    key_value, branch_grad = lax.optimization_barrier((key_value, branch_grad))
    before = lax.ppermute(key_value, "z", up)
    branch_all = gather_plane(branch_grad, 7, "gather_branch")
    branch_all, late_normed = lax.optimization_barrier((branch_all, normed_all))
    query = (dot(late_normed, weight_q) + mine(bias_q)).astype(bfloat)
    before, query = lax.optimization_barrier((before, query))
    starts = starts.reshape(B * span, 1)
    context = attention_forward(starts, query, key_value, before, B)
    context, unit_two = lax.optimization_barrier((context, halves[1]))
    unit_two = gather_units(unit_two)

    attended = reduce_plane(context, weight_o, False, 1, "attended") + bias_o
    middle = local + active * attended
    normed_two = layer_norm(middle, gain_two, bias_two).astype(bfloat)
    bias_up = bias_up.reshape(Z, 2, units)
    bias_up = [bias_up[:, i].reshape(1, Z * units) for i in range(2)]

    def sum_halves(left, right, turned, cid, name):
        if fast:
            return dot_reduce(left, right, turned, cid, name)
        terms = sum((dot_nt if turned else dot)(a, w) for a, w in zip(left, right)).astype(bfloat)
        return lax.psum_scatter(terms, PLANE, scatter_dimension=0, tiled=True).astype(single)

    def sum_z(grads):
        return lax.psum_scatter(grads.reshape(Z * 2 * units, D), "z", scatter_dimension=0, tiled=True)

    if fast:
        branch_rows = branch_all.reshape(R, tok, D)
        two_all, hidden_one, pre_one, bias_one_up, grads = first_units(normed_two, branch_rows, unit_one, bias_up[0], 2)
        shard_one = sum_z(grads)
        hidden_two, bias_two_up, normed_two_grad, grads = last_units(
            two_all, branch_rows, pre_one, unit_one, unit_two, bias_up[1], 3
        )
        shard_two = sum_z(grads)
        up_b_halves = [bias_one_up[0], bias_two_up[0]]
    else:
        two_all = gather_plane(normed_two, 2, "gather_two")

        def half_units(weights, bias):
            weight_up, weight_down = [weights[:, i].reshape(Z * units, D) for i in (0, 1)]
            hidden, gelu_pull = jax.vjp(partial(jax.nn.gelu, approximate=True), dot_nt(two_all, weight_up) + bias)
            hidden = hidden.astype(bfloat)
            pre_grad = gelu_pull(dot_nt(branch_all, weight_down))[0].astype(bfloat)
            grads = dot_tn(pre_grad, two_all), dot_tn(hidden, branch_all)
            grads = jnp.stack([g.astype(bfloat).reshape(Z, units, D) for g in grads], axis=1)
            return hidden, pre_grad, sum_z(grads), weight_up, weight_down

        hidden_one, pre_one, shard_one, up_one, down_one = half_units(unit_one, bias_up[0])
        hidden_two, pre_two, shard_two, up_two, down_two = half_units(unit_two, bias_up[1])
        up_b_halves = [column_sums(pre_one), column_sums(pre_two)]
        normed_two_grad = sum_halves([pre_one, pre_two], [up_one, up_two], False, 3, "up_grad")
    up_b_grad = jnp.stack([half.reshape(Z, units) for half in up_b_halves], axis=1).reshape(-1)

    middle_part, gain_two_grad, bias_two_grad = norm_backward(middle, normed_two_grad, gain_two)
    middle_grad = cotangent + middle_part
    attended_grad = (active * middle_grad).astype(bfloat)
    out_b_grad = column_sums(attended_grad)
    attended_all, context_grad = gather_plane_dot(
        attended_grad, weight_o, jnp.zeros((1, cols), single), bfloat, True, 5, "attended_grad"
    )
    context_grad, shard_one = lax.optimization_barrier((context_grad, shard_one))
    out_w_grad = dot_tn(context, attended_all)
    query_grad, edge, pair = attention_backward(starts, query, key_value, before, context_grad, B)
    hidden_one, edge, pair, query_grad = lax.optimization_barrier((hidden_one, edge, pair, query_grad))
    after = lax.ppermute(edge, "z", down)
    query_w_grad = dot_tn(normed_all, query_grad).astype(bfloat)
    hidden_one, query_w_grad, out_w_grad = lax.optimization_barrier((hidden_one, query_w_grad, out_w_grad))
    downs = [unit_one, unit_two] if fast else [down_one, down_two]
    branch = sum_halves([hidden_one, hidden_two], downs, False, 4, "down")
    branch, after, shard_two = lax.optimization_barrier((branch, after, shard_two))
    outputs = middle + active * (branch + bias_down)
    pair_grad = (pair + after.astype(single)).astype(bfloat)
    pair_w_grad = dot_tn(normed_all, pair_grad).astype(bfloat)
    pair_grad, pair_w_grad = lax.optimization_barrier((pair_grad, pair_w_grad))
    normed_grad = sum_halves([query_grad, pair_grad], [weight_q, weight_kv], True, 6, "qkv_grad")
    query_b_grad = column_sums(query_grad)
    value_b_grad = column_sums(pair_grad[:, cols:])
    input_part, gain_one_grad, bias_one_grad = norm_backward(local, normed_grad, gain_one)
    input_grad = middle_grad + input_part

    def sum_to_owners(vectors, axes, parts):
        split = jnp.concatenate([v.reshape(parts, -1) for v in vectors], axis=1)
        summed = jnp.sum(lax.all_to_all(split, axes, split_axis=0, concat_axis=0, tiled=True), axis=0)
        widths = [v.shape[0] // parts for v in vectors]
        return [summed[sum(widths[:i]) : sum(widths[: i + 1])] for i in range(len(widths))]

    qkv_w_grad = jnp.concatenate([query_w_grad, pair_w_grad], axis=1)
    qkv_w_grad = qkv_w_grad.reshape(B, Z, X, rows_dev, 3 * cols).transpose(1, 0, 2, 3, 4).reshape(D, 3 * cols)
    qkv_w_grad = lax.psum_scatter(qkv_w_grad, "z", scatter_dimension=0, tiled=True).reshape(R, rows_dev, 3 * cols)
    device_sums = [gain_one_grad, bias_one_grad, out_b_grad, gain_two_grad, bias_two_grad, down_b_grad]
    if fast:
        rank_sums = jnp.concatenate([v.reshape(Z, -1) for v in (query_b_grad, value_b_grad, up_b_grad)], axis=1)
        here = (jnp.arange(R) == rank).reshape(B, 1, X, 1)
        rank_sums = jnp.where(here, rank_sums[None, :, None, :], 0.0).reshape(R * Z, -1)
        rows = jnp.concatenate([v.reshape(R * Z, -1) for v in device_sums] + [rank_sums], axis=1)
        q_w_shard, k_w_shard, v_w_shard, summed = settle(qkv_w_grad, rows, 9)
        sums = [summed[0, i * rows_dev : (i + 1) * rows_dev] for i in range(len(device_sums) + 2)]
        q_b_shard, v_b_shard = sums[len(device_sums) :]
        up_b_shard = summed[0, (len(device_sums) + 2) * rows_dev :]
    else:
        qkv_w_grad = lax.all_to_all(qkv_w_grad, PLANE, split_axis=0, concat_axis=0, tiled=True)
        q_w_shard, k_w_shard, v_w_shard = [
            from_ranks(qkv_w_grad[..., i : i + cols]).astype(single) for i in range(0, 3 * cols, cols)
        ]
        sums = sum_to_owners(device_sums, ALL, R * Z)
        [up_b_shard] = sum_to_owners([up_b_grad], "z", Z)
    if whole_heads:
        out_w_shard = lax.psum_scatter(out_w_grad.astype(bfloat), "z", scatter_dimension=0, tiled=True).astype(single)
        if not fast:
            q_b_shard, v_b_shard = sum_to_owners([query_b_grad, value_b_grad], "z", Z)
    else:

        def placed(rows):
            full = jnp.zeros((D,) + rows.shape[1:], rows.dtype)
            full = lax.dynamic_update_slice_in_dim(full, rows, rank * cols, 0)
            return lax.psum_scatter(full, ALL, scatter_dimension=0, tiled=True).astype(single)

        out_w_shard = placed(out_w_grad.astype(bfloat))
        q_b_shard = placed(query_b_grad)
        v_b_shard = placed(value_b_grad)
    return (
        outputs.astype(bfloat)[None],
        input_grad.astype(bfloat)[None],
        sums[0],
        sums[1],
        q_w_shard,
        q_b_shard,
        k_w_shard,
        v_w_shard,
        v_b_shard,
        out_w_shard,
        sums[2],
        sums[3],
        sums[4],
        jnp.concatenate([shard_one[:units], shard_two[:units]]).T.astype(single),
        up_b_shard,
        jnp.concatenate([shard_one[units:], shard_two[units:]]).astype(single),
        sums[5],
    )


def solution(mesh):
    groups, parts = mesh.shape["batch"], mesh.shape["seq"]
    inner = Mesh(mesh.devices.reshape(groups, SPANS, parts // SPANS), ("b", "z", "x"))
    token = P("b", ("z", "x"), None)
    vector = P(ALL)
    rows = P(ALL, None)
    columns = P(None, ALL)
    return jax.shard_map(
        on_device,
        mesh=inner,
        in_specs=(
            token,
            P("b", None),
            P("b", None),
            P(),
            token,
            vector,
            vector,
            rows,
            vector,
            rows,
            rows,
            vector,
            rows,
            vector,
            vector,
            vector,
            columns,
            vector,
            rows,
            vector,
        ),
        out_specs=(
            token,
            token,
            vector,
            vector,
            rows,
            vector,
            rows,
            rows,
            vector,
            rows,
            vector,
            vector,
            vector,
            columns,
            vector,
            rows,
            vector,
        ),
        check_vma=False,
    )
```

```python
import functools
from functools import partial

import jax
import jax.numpy as jnp
from jax import lax
from jax.experimental import pallas as pl
from jax.experimental.pallas import tpu as pltpu
from jax.sharding import Mesh
from jax.sharding import PartitionSpec as P

HEAD_DIM = 64
SPANS = 4

bfloat = jnp.bfloat16
single = jnp.float32

PLANE = ("b", "x")
ALL = ("b", "z", "x")
MESH = pl.DeviceIdType.MESH
TILE = 512

def plane_place():
    b, z, x = lax.axis_index("b"), lax.axis_index("z"), lax.axis_index("x")
    sib_b = b + 1 - 2 * lax.rem(b, 2)
    far_b = lax.rem(b + 2, 4)
    far_sib_b = lax.rem(sib_b + 2, 4)
    ids = {"s": (sib_b, z, x), "x": (b, z, 1 - x), "y": (far_b, z, x)}
    ranks = {
        "o": b * 2 + x,
        "s": sib_b * 2 + x,
        "x": b * 2 + 1 - x,
        "xs": sib_b * 2 + 1 - x,
        "y": far_b * 2 + x,
        "ys": far_sib_b * 2 + x,
        "d": far_b * 2 + 1 - x,
        "ds": far_sib_b * 2 + 1 - x,
    }
    return ids, ranks

def greet(ids):
    barrier = pltpu.get_barrier_semaphore()
    for device in ids.values():
        pl.semaphore_signal(barrier, inc=1, device_id=device, device_id_type=MESH)
    pl.semaphore_wait(barrier, len(ids))

def tiles(lo, hi, body):
    def step(i, _):
        body(pl.ds(pl.multiple_of(i * TILE, TILE), TILE))
        return 0
    lax.fori_loop(lo // TILE, hi // TILE, step, 0)

def gather_kernel(body_of, n_in, n_out, x_ref, *refs):
    ins = refs[:n_in]; all_ref = refs[n_in]; outs = refs[n_in + 1 : n_in + 1 + n_out]
    held, send, recv, keep = refs[n_in + 1 + n_out :]
    ids, at = plane_place()
    half = x_ref.shape[0] // 2
    parts = (pl.ds(0, half), pl.ds(half, half))
    greet(ids)
    count = [0]
    started = []
    def ship(src, dst, to):
        n = count[0]; count[0] += 1
        c = pltpu.make_async_remote_copy(src_ref=src, dst_ref=dst, send_sem=send.at[n], recv_sem=recv.at[n], device_id=ids[to], device_id_type=MESH)
        c.start(); started.append(c)
        return c
    own = at["o"]
    x0 = ship(x_ref.at[parts[0]], held.at[own, parts[0]], "x")
    y1 = ship(x_ref.at[parts[1]], held.at[own, parts[1]], "y")
    x1 = ship(x_ref.at[parts[1]], held.at[own, parts[1]], "x")
    y0 = ship(x_ref.at[parts[0]], held.at[own, parts[0]], "y")
    s0 = ship(x_ref, held.at[own], "s")
    kept = []
    def done(rank, src):
        c = pltpu.make_async_copy(src, all_ref.at[rank], keep.at[len(kept)])
        c.start(); kept.append(c)
        if body_of is not None:
            body_of(rank, src, ins, outs)
    done(own, x_ref)
    s0.wait_recv()
    done(at["s"], held.at[at["s"]])
    x0.wait_recv()
    ry = ship(held.at[at["x"], parts[0]], held.at[at["x"], parts[0]], "y")
    y1.wait_recv()
    rx = ship(held.at[at["y"], parts[1]], held.at[at["y"], parts[1]], "x")
    x1.wait_recv()
    sx = ship(held.at[at["x"]], held.at[at["x"]], "s")
    y0.wait_recv()
    sy = ship(held.at[at["y"]], held.at[at["y"]], "s")
    done(at["x"], held.at[at["x"]])
    done(at["y"], held.at[at["y"]])
    sx.wait_recv()
    done(at["xs"], held.at[at["xs"]])
    sy.wait_recv()
    done(at["ys"], held.at[at["ys"]])
    ry.wait_recv(); rx.wait_recv()
    sd = ship(held.at[at["d"]], held.at[at["d"]], "s")
    done(at["d"], held.at[at["d"]])
    sd.wait_recv()
    done(at["ds"], held.at[at["ds"]])
    for c in started: c.wait_send()
    for c in kept: c.wait()

def vmem(n): return [pl.BlockSpec(memory_space=pltpu.VMEM)] * n

def plane_gather(x, ins, out_types, body_of, cid, name, ranks=8):
    tok, D = x.shape
    res = pl.pallas_call(
        functools.partial(gather_kernel, body_of, len(ins), len(out_types)),
        out_shape=[jax.ShapeDtypeStruct((ranks, tok, D), x.dtype), *out_types],
        in_specs=vmem(1 + len(ins)),
        out_specs=[pl.BlockSpec(memory_space=pl.ANY)] + vmem(len(out_types)),
        scratch_shapes=[pltpu.VMEM((ranks, tok, D), x.dtype), pltpu.SemaphoreType.DMA((10,)), pltpu.SemaphoreType.DMA((10,)), pltpu.SemaphoreType.DMA((8,))],
        compiler_params=pltpu.CompilerParams(collective_id=cid, has_side_effects=True, vmem_limit_bytes=60 << 20),
        cost_estimate=pl.CostEstimate(flops=1 << 30, bytes_accessed=128 << 20, transcendentals=0),
        name=name,
    )(x, *ins)
    return res[0].reshape(ranks * tok, D), *res[1:]

def gather_dot(x, w, bias, out_dtype, turned, cid, name):
    ranks, tok, D = 8, *x.shape
    N = w.shape[0] if turned else w.shape[1]
    tile = min(N, 512) if N % 512 == 0 else 256
    def body(rank, src, ins, outs):
        w_ref, b_ref = ins
        def step(i, _):
            cols = pl.ds(pl.multiple_of(i * tile, tile), tile)
            if turned:
                y = lax.dot_general(src[...], w_ref[cols, :], (((1,), (1,)), ((), ())), preferred_element_type=single)
            else:
                y = jnp.dot(src[...], w_ref[:, cols], preferred_element_type=single)
            outs[0][rank, :, cols] = (y + b_ref[:, cols]).astype(out_dtype)
            return 0
        lax.fori_loop(0, N // tile, step, 0)
    all_, y = plane_gather(x, (w, bias), [jax.ShapeDtypeStruct((ranks, tok, N), out_dtype)], body, cid, name)
    return all_, y.reshape(ranks * tok, N)

def reduce_kernel(turned, pairs, *refs):
    left, right = refs[:pairs], refs[pairs : 2 * pairs]
    out_ref, sib_out, sib_in, stage, landed, send, recv = refs[2 * pairs :]
    ids, at = plane_place()
    D = out_ref.shape[1]
    mid = D // 2
    greet(ids)
    count = [0]; started = []
    def ship(src, dst, to):
        n = count[0]; count[0] += 1
        c = pltpu.make_async_remote_copy(src_ref=src, dst_ref=dst, send_sem=send.at[n], recv_sem=recv.at[n], device_id=ids[to], device_id_type=MESH)
        c.start(); started.append(c)
        return c
    def term(rank, cols):
        if turned:
            return sum(dot_nt(a[rank], w[cols, :]) for a, w in zip(left, right))
        rows = [w[:, 1, :, cols].reshape(-1, TILE) if len(w.shape) == 4 else w[:, cols] for w in right]
        return sum(dot(a[rank], w) for a, w in zip(left, rows))
    order = ("d", "x", "y", "o")
    twin = {"d": "ds", "x": "xs", "y": "ys", "o": "s"}
    sib = []
    def to_sibling():
        j = len(sib)
        def fill(cols):
            sib_out[j, :, cols] = term(at[twin[order[j]]], cols).astype(bfloat)
        tiles(0, D, fill)
        sib.append(ship(sib_out.at[j], sib_in.at[j], "s"))
    def pair(j, cols):
        return term(at[order[j]], cols) + sib_in[j, :, cols].astype(single)
    def local(h, cols):
        return pl.ds(pl.multiple_of(cols.start - h * mid, TILE), TILE)
    def put(j, h, extra=None):
        def fill(cols):
            value = pair(j, cols)
            if extra is not None:
                value = value + landed[extra, :, local(h, cols)].astype(single)
            stage[j, h, :, local(h, cols)] = value.astype(bfloat)
        tiles(h * mid, (h + 1) * mid, fill)
    to_sibling()
    to_sibling()
    sib[0].wait_recv()
    put(0, 0)
    d_a = ship(stage.at[0, 0], landed.at[0], "x")
    put(0, 1)
    d_b = ship(stage.at[0, 1], landed.at[1], "y")
    to_sibling()
    sib[1].wait_recv()
    put(1, 0)
    x_a = ship(stage.at[1, 0], landed.at[2], "x")
    sib[2].wait_recv()
    put(2, 1)
    y_b = ship(stage.at[2, 1], landed.at[3], "y")
    to_sibling()
    sib[3].wait_recv()
    def first(cols):
        out_ref[:, cols] = pair(3, cols)
    tiles(0, D, first)
    d_b.wait_recv()
    put(1, 1, extra=1)
    x_b = ship(stage.at[1, 1], landed.at[5], "x")
    d_a.wait_recv()
    put(2, 0, extra=0)
    y_a = ship(stage.at[2, 0], landed.at[4], "y")
    x_a.wait_recv(); y_b.wait_recv(); x_b.wait_recv(); y_a.wait_recv()
    for h, (n, m) in enumerate(((2, 4), (3, 5))):
        def add(cols, h=h, n=n, m=m):
            c = local(h, cols)
            out_ref[:, cols] = out_ref[:, cols] + landed[n, :, c].astype(single) + landed[m, :, c].astype(single)
        tiles(h * mid, (h + 1) * mid, add)
    for c in started: c.wait_send()

def dot_reduce(left, right, turned, cid, name):
    ranks = 8
    D = right[0].shape[0] if turned else right[0].shape[-1]
    tok = left[0].size // left[0].shape[-1] // ranks
    return pl.pallas_call(
        functools.partial(reduce_kernel, turned, len(left)),
        out_shape=jax.ShapeDtypeStruct((tok, D), single),
        in_specs=vmem(2 * len(left)), out_specs=vmem(1)[0],
        scratch_shapes=[pltpu.VMEM((4, tok, D), bfloat), pltpu.VMEM((4, tok, D), bfloat), pltpu.VMEM((3, 2, tok, D // 2), bfloat), pltpu.VMEM((6, tok, D // 2), bfloat),
            pltpu.SemaphoreType.DMA((10,)), pltpu.SemaphoreType.DMA((10,))],
        compiler_params=pltpu.CompilerParams(collective_id=cid, has_side_effects=True, vmem_limit_bytes=60 << 20),
        cost_estimate=pl.CostEstimate(flops=1 << 30, bytes_accessed=128 << 20, transcendentals=0),
        name=name,
    )(*[a.reshape(ranks, tok, -1) for a in left], *right)


def dot(left, right):
    return jnp.dot(left, right, preferred_element_type=single)


def dot_tn(left, right):
    return lax.dot_general(left, right, (((0,), (0,)), ((), ())), preferred_element_type=single)


def dot_nt(left, right):
    return lax.dot_general(left, right, (((1,), (1,)), ((), ())), preferred_element_type=single)


def layer_norm(values, gain_vec, shift_vec):
    center = jnp.mean(values, axis=-1, keepdims=True)
    centered = values - center
    spread = jnp.mean(centered * centered, axis=-1, keepdims=True)
    return centered * lax.rsqrt(spread + 1e-05) * gain_vec + shift_vec


def column_sums(matrix):
    return jnp.sum(matrix.astype(single), axis=0)


def shipper(send, recv, ids):
    started = []

    def ship(src, dst, to):
        n = len(started)
        copy = pltpu.make_async_remote_copy(
            src_ref=src, dst_ref=dst, send_sem=send.at[n], recv_sem=recv.at[n], device_id=ids[to], device_id_type=MESH
        )
        copy.start()
        started.append(copy)
        return copy

    return ship, started


TWIN = {"o": "s", "x": "xs", "y": "ys", "d": "ds"}


def unit_rows(w_ref, i):
    parts, _, units, D = w_ref.shape
    return w_ref[:, i].reshape(parts * units, D)


def hidden_units(src, branch, w_ref, b_ref, hid_ref, pg_ref, pb_ref, rank):
    pre = dot_nt(src[...], unit_rows(w_ref, 0)) + b_ref[...]
    square = pre * pre
    bend = jnp.tanh(0.7978845608028654 * (pre + 0.044715 * (pre * square)))
    rise = 0.5 * (1.0 + bend)
    hid_ref[rank] = (pre * rise).astype(bfloat)
    slope = rise + (0.5 * 0.7978845608028654) * pre * (1.0 - bend * bend) * (1.0 + 3 * 0.044715 * square)
    grad = (dot_nt(branch[...], unit_rows(w_ref, 1)) * slope).astype(bfloat)
    pg_ref[rank] = grad
    pb_ref[...] += jnp.sum(grad.astype(single), axis=0, keepdims=True)


def first_units_kernel(
    x_ref, bg_ref, w_ref, b_ref, all_ref, hid_ref, pg_ref, pb_ref, grad_ref,
    held, bg, total, send, recv, keep, load,
):
    ids, at = plane_place()
    tok = x_ref.shape[0]
    half = tok // 2
    parts = (pl.ds(0, half), pl.ds(half, half))
    own = at["o"]
    loads = {}
    for n, name in enumerate(at):
        loads[name] = pltpu.make_async_copy(bg_ref.at[at[name]], bg.at[at[name]], load.at[n])
        loads[name].start()
    greet(ids)
    ship, started = shipper(send, recv, ids)
    x0 = ship(x_ref.at[parts[0]], held.at[own, parts[0]], "x")
    y1 = ship(x_ref.at[parts[1]], held.at[own, parts[1]], "y")
    x1 = ship(x_ref.at[parts[1]], held.at[own, parts[1]], "x")
    y0 = ship(x_ref.at[parts[0]], held.at[own, parts[0]], "y")
    s0 = ship(x_ref, held.at[own], "s")
    pb_ref[...] = jnp.zeros_like(pb_ref)
    kept = []

    def units(name):
        rank = at[name]
        src = x_ref if name == "o" else held.at[rank]
        copy = pltpu.make_async_copy(src, all_ref.at[rank], keep.at[len(kept)])
        copy.start()
        kept.append(copy)
        loads[name].wait()
        hidden_units(src, bg.at[rank], w_ref, b_ref, hid_ref, pg_ref, pb_ref, rank)

    def weigh(name, last=False):
        units_at = grad_ref.shape[2]
        per = 256 // units_at

        def rows(i, _):
            here = pl.ds(pl.multiple_of(i * 256, 256), 256)
            owners = pl.ds(i * per, per)
            for j, left in enumerate((pg_ref, hid_ref)):
                term = 0
                for n in (name, TWIN[name]):
                    right = bg[at[n]] if j else (x_ref[...] if n == "o" else held[at[n]])
                    term = term + dot_tn(left[at[n], :, here], right)
                term = term.reshape(per, units_at, -1)
                if name == "o":
                    total[owners, j] = term
                elif last:
                    grad_ref[owners, j] = (total[owners, j] + term).astype(bfloat)
                else:
                    total[owners, j] += term
            return 0

        lax.fori_loop(0, hid_ref.shape[2] // 256, rows, 0)

    units("o")
    s0.wait_recv()
    units("s")
    x0.wait_recv()
    ry = ship(held.at[at["x"], parts[0]], held.at[at["x"], parts[0]], "y")
    y1.wait_recv()
    rx = ship(held.at[at["y"], parts[1]], held.at[at["y"], parts[1]], "x")
    weigh("o")
    x1.wait_recv()
    sx = ship(held.at[at["x"]], held.at[at["x"]], "s")
    y0.wait_recv()
    sy = ship(held.at[at["y"]], held.at[at["y"]], "s")
    units("x")
    sx.wait_recv()
    units("xs")
    units("y")
    sy.wait_recv()
    units("ys")
    weigh("x")
    ry.wait_recv()
    rx.wait_recv()
    sd = ship(held.at[at["d"]], held.at[at["d"]], "s")
    weigh("y")
    units("d")
    sd.wait_recv()
    units("ds")
    weigh("d", last=True)
    for copy in started:
        copy.wait_send()
    for copy in kept:
        copy.wait()


def last_units_kernel(
    all_ref, bg_ref, pg1_ref, w1_ref, w_ref, b_ref, hid_ref, pb_ref, r_ref, grad_ref,
    held, bg, pg_ref, sib_out, sib_in, stage, landed, send, recv, load, load_b,
):
    ids, at = plane_place()
    ranks, tok, D = held.shape
    mid = D // 2
    names = ("ds", "d", "xs", "x", "ys", "y", "s", "o")
    loads = {}
    for n, name in enumerate(names):
        loads[name] = [
            pltpu.make_async_copy(all_ref.at[at[name]], held.at[at[name]], load.at[n]),
            pltpu.make_async_copy(bg_ref.at[at[name]], bg.at[at[name]], load_b.at[n]),
        ]
        for copy in loads[name]:
            copy.start()
    greet(ids)
    ship, started = shipper(send, recv, ids)
    pb_ref[...] = jnp.zeros_like(pb_ref)

    def units(name):
        for copy in loads[name]:
            copy.wait()
        rank = at[name]
        hidden_units(held.at[rank], bg.at[rank], w_ref, b_ref, hid_ref, pg_ref, pb_ref, rank)

    def term(name, cols):
        rank = at[name]
        first, second = [w[:, 0, :, cols].reshape(-1, TILE) for w in (w1_ref, w_ref)]
        return dot(pg1_ref[rank], first) + dot(pg_ref[rank], second)

    order = ("d", "x", "y", "o")

    def to_sibling(j):
        def fill(cols):
            sib_out[j, :, cols] = term(TWIN[order[j]], cols).astype(bfloat)

        tiles(0, D, fill)
        return ship(sib_out.at[j], sib_in.at[j], "s")

    def pair(j, cols):
        return term(order[j], cols) + sib_in[j, :, cols].astype(single)

    def local(h, cols):
        return pl.ds(pl.multiple_of(cols.start - h * mid, TILE), TILE)

    def put(j, h, extra=None):
        def fill(cols):
            value = pair(j, cols)
            if extra is not None:
                value = value + landed[extra, :, local(h, cols)].astype(single)
            stage[j, h, :, local(h, cols)] = value.astype(bfloat)

        tiles(h * mid, (h + 1) * mid, fill)

    units("ds")
    d_sib = to_sibling(0)
    units("d")
    d_sib.wait_recv()
    put(0, 0)
    d_a = ship(stage.at[0, 0], landed.at[0], "x")
    put(0, 1)
    d_b = ship(stage.at[0, 1], landed.at[1], "y")
    units("xs")
    x_sib = to_sibling(1)
    units("x")
    x_sib.wait_recv()
    put(1, 0)
    x_a = ship(stage.at[1, 0], landed.at[2], "x")
    units("ys")
    y_sib = to_sibling(2)
    units("y")
    y_sib.wait_recv()
    put(2, 1)
    y_b = ship(stage.at[2, 1], landed.at[3], "y")
    d_b.wait_recv()
    put(1, 1, extra=1)
    x_b = ship(stage.at[1, 1], landed.at[5], "x")
    d_a.wait_recv()
    put(2, 0, extra=0)
    y_a = ship(stage.at[2, 0], landed.at[4], "y")
    units("s")
    own_sib = to_sibling(3)
    units("o")
    own_sib.wait_recv()

    def first(cols):
        r_ref[:, cols] = pair(3, cols)

    tiles(0, D, first)

    units_at = grad_ref.shape[2]
    per = 256 // units_at
    tokens = ranks * tok

    def grads(i, _):
        here = pl.ds(pl.multiple_of(i * 256, 256), 256)
        owners = pl.ds(i * per, per)
        for j, (left, right) in enumerate(((pg_ref, held), (hid_ref, bg))):
            value = dot_tn(left[:, :, here].reshape(tokens, 256), right[...].reshape(tokens, D))
            grad_ref[owners, j] = value.astype(bfloat).reshape(per, units_at, D)
        return 0

    lax.fori_loop(0, hid_ref.shape[2] // 256, grads, 0)
    for copy in (x_a, y_b, x_b, y_a):
        copy.wait_recv()
    for h, (n, m) in enumerate(((2, 4), (3, 5))):

        def add(cols, h=h, n=n, m=m):
            c = local(h, cols)
            r_ref[:, cols] = r_ref[:, cols] + landed[n, :, c].astype(single) + landed[m, :, c].astype(single)

        tiles(h * mid, (h + 1) * mid, add)
    for copy in started:
        copy.wait_send()


def first_units(x, bg, w, bias, cid):
    ranks = 8
    tok, D = x.shape
    F = bias.shape[1]
    anywhere = pl.BlockSpec(memory_space=pl.ANY)
    inside = pl.BlockSpec(memory_space=pltpu.VMEM)
    return pl.pallas_call(
        first_units_kernel,
        out_shape=[
            jax.ShapeDtypeStruct((ranks, tok, D), bfloat),
            jax.ShapeDtypeStruct((ranks, tok, F), bfloat),
            jax.ShapeDtypeStruct((ranks, tok, F), bfloat),
            jax.ShapeDtypeStruct((1, F), single),
            jax.ShapeDtypeStruct(w.shape, bfloat),
        ],
        in_specs=[inside, anywhere, inside, inside],
        out_specs=[anywhere, inside, inside, inside, inside],
        scratch_shapes=[
            pltpu.VMEM((ranks, tok, D), bfloat),
            pltpu.VMEM((ranks, tok, D), bfloat),
            pltpu.VMEM(w.shape, single),
            pltpu.SemaphoreType.DMA((10,)),
            pltpu.SemaphoreType.DMA((10,)),
            pltpu.SemaphoreType.DMA((8,)),
            pltpu.SemaphoreType.DMA((8,)),
        ],
        compiler_params=pltpu.CompilerParams(collective_id=cid, has_side_effects=True, vmem_limit_bytes=62 << 20),
        cost_estimate=pl.CostEstimate(flops=1 << 30, bytes_accessed=160 << 20, transcendentals=0),
        name="first_units",
    )(x, bg, w, bias)


def last_units(rows, bg, pg, w1, w, bias, cid):
    ranks, tok, D = rows.shape
    F = bias.shape[1]
    anywhere = pl.BlockSpec(memory_space=pl.ANY)
    inside = pl.BlockSpec(memory_space=pltpu.VMEM)
    return pl.pallas_call(
        last_units_kernel,
        out_shape=[
            jax.ShapeDtypeStruct((ranks, tok, F), bfloat),
            jax.ShapeDtypeStruct((1, F), single),
            jax.ShapeDtypeStruct((tok, D), single),
            jax.ShapeDtypeStruct(w.shape, bfloat),
        ],
        in_specs=[anywhere, anywhere, inside, inside, inside, inside],
        out_specs=[inside] * 4,
        scratch_shapes=[
            pltpu.VMEM((ranks, tok, D), bfloat),
            pltpu.VMEM((ranks, tok, D), bfloat),
            pltpu.VMEM((ranks, tok, F), bfloat),
            pltpu.VMEM((4, tok, D), bfloat),
            pltpu.VMEM((4, tok, D), bfloat),
            pltpu.VMEM((3, 2, tok, D // 2), bfloat),
            pltpu.VMEM((6, tok, D // 2), bfloat),
            pltpu.SemaphoreType.DMA((10,)),
            pltpu.SemaphoreType.DMA((10,)),
            pltpu.SemaphoreType.DMA((8,)),
            pltpu.SemaphoreType.DMA((8,)),
        ],
        compiler_params=pltpu.CompilerParams(collective_id=cid, has_side_effects=True, vmem_limit_bytes=62 << 20),
        cost_estimate=pl.CostEstimate(flops=1 << 30, bytes_accessed=160 << 20, transcendentals=0),
        name="last_units",
    )(rows, bg, pg, w1, w, bias)


def everyone(width):
    b, z, x = lax.axis_index("b"), lax.axis_index("z"), lax.axis_index("x")
    rank, me = b * 2 + x, (b * 4 + z) * 2 + x

    def in_plane(i):
        other = lax.rem(rank + i, 8)
        return other, (other // 2, z, lax.rem(other, 2))

    def anywhere(i):
        other = lax.rem(me + i, width)
        return other, (other // 8, lax.rem(other // 2, 4), lax.rem(other, 2))

    return rank, me, in_plane, anywhere


def exchange(blocks, landed, rows, gathered, same_row, sems):
    plane_send, plane_recv, all_send, all_recv = sems
    width = gathered.shape[0]
    rank, me, in_plane, anywhere = everyone(width)
    barrier = pltpu.get_barrier_semaphore()

    def each(count, body):
        def step(i, _):
            body(i)
            return 0

        lax.fori_loop(1, count, step, 0)

    each(width, lambda i: pl.semaphore_signal(barrier, inc=1, device_id=anywhere(i)[1], device_id_type=MESH))
    pl.semaphore_wait(barrier, width - 1)

    def block(i):
        other, device = in_plane(i)
        return pltpu.make_async_remote_copy(
            src_ref=blocks.at[other], dst_ref=landed.at[rank], send_sem=plane_send.at[i], recv_sem=plane_recv.at[i],
            device_id=device, device_id_type=MESH,
        )

    def row(i):
        other, device = anywhere(i)
        return pltpu.make_async_remote_copy(
            src_ref=rows.at[0] if same_row else rows.at[other], dst_ref=gathered.at[me],
            send_sem=all_send.at[i], recv_sem=all_recv.at[i], device_id=device, device_id_type=MESH,
        )

    each(8, lambda i: block(i).start())
    each(width, lambda i: row(i).start())
    landed[rank] = blocks[rank]
    gathered[me] = rows[0] if same_row else rows[me]
    each(width, lambda i: row(i).wait())
    each(8, lambda i: block(i).wait())


def head_at(rank, i):
    return (rank // 2 * 4 + i) * 2 + rank % 2


def spread_kernel(q_ref, k_ref, v_ref, pack_ref, q_out, kv_out, pack_out, blocks, landed, gathered, *sems):
    cols = q_out.shape[2]
    for rank in range(8):
        for part, ref in enumerate((q_ref, k_ref, v_ref)):
            heads = [ref[:, head_at(rank, i) * HEAD_DIM : (head_at(rank, i) + 1) * HEAD_DIM] for i in range(4)]
            blocks[rank, :, part * cols : (part + 1) * cols] = jnp.concatenate(heads, axis=1)
    exchange(blocks, landed, pack_ref, gathered, True, sems)
    q_out[...] = landed[:, :, :cols]
    kv_out[...] = landed[:, :, cols:]
    pack_out[...] = gathered[...]


def settle_kernel(w_ref, rows_ref, q_out, k_out, v_out, sums_ref, landed, gathered, *sems):
    cols = w_ref.shape[2] // 3
    exchange(w_ref, landed, rows_ref, gathered, False, sems)
    for part, out in enumerate((q_out, k_out, v_out)):
        for pair in range(out.shape[1] // 128):
            sides = []
            for head in (2 * pair, 2 * pair + 1):
                rank, i = head // 8 * 2 + head % 2, head // 2 % 4
                at = part * cols + i * HEAD_DIM
                sides.append(landed[rank, :, at : at + HEAD_DIM])
            out[:, pair * 128 : (pair + 1) * 128] = jnp.concatenate(sides, axis=1).astype(single)
    sums_ref[...] = jnp.sum(gathered[...], axis=0)


def exchange_call(kernel, out_shape, args, blocks, landed, gathered, cid, name):
    inside = pl.BlockSpec(memory_space=pltpu.VMEM)
    width = gathered[0]
    return pl.pallas_call(
        kernel,
        out_shape=out_shape,
        in_specs=[inside] * len(args),
        out_specs=[inside] * len(out_shape),
        scratch_shapes=blocks
        + [
            pltpu.VMEM(landed, bfloat),
            pltpu.VMEM(gathered, single),
            pltpu.SemaphoreType.DMA((8,)),
            pltpu.SemaphoreType.DMA((8,)),
            pltpu.SemaphoreType.DMA((width,)),
            pltpu.SemaphoreType.DMA((width,)),
        ],
        compiler_params=pltpu.CompilerParams(collective_id=cid, has_side_effects=True, vmem_limit_bytes=32 << 20),
        cost_estimate=pl.CostEstimate(flops=1 << 20, bytes_accessed=32 << 20, transcendentals=0),
        name=name,
    )(*args)


def spread(q, k, v, pack, devices, cid):
    rows, D = q.shape
    cols = D // 8
    return exchange_call(
        spread_kernel,
        [
            jax.ShapeDtypeStruct((8, rows, cols), bfloat),
            jax.ShapeDtypeStruct((8, rows, 2 * cols), bfloat),
            jax.ShapeDtypeStruct((devices, 1, pack.shape[0]), single),
        ],
        (q, k, v, pack[None, None]),
        [pltpu.VMEM((8, rows, 3 * cols), bfloat)],
        (8, rows, 3 * cols),
        (devices, 1, pack.shape[0]),
        cid,
        "spread",
    )


def settle(weights, rows, cid):
    _, tall, wide = weights.shape
    D = wide // 3 * 8
    return exchange_call(
        settle_kernel,
        [jax.ShapeDtypeStruct((tall, D), single)] * 3 + [jax.ShapeDtypeStruct((1, rows.shape[1]), single)],
        (weights, rows[:, None]),
        [],
        weights.shape,
        (rows.shape[0], 1, rows.shape[1]),
        cid,
        "settle",
    )


def windows(span):
    block = span // 2
    return [(i * block, i * block + block + span) for i in range(2)]

def key_window(before, own, lo, hi, span):
    return jnp.concatenate([before[lo:span], own[0 : hi - span]], axis=0)

def hidden_bias(start_ref, i, block, lo, hi, span):
    rows = span + i * block + lax.broadcasted_iota(jnp.int32, (block, hi - lo), 0)
    keys = lo + lax.broadcasted_iota(jnp.int32, (block, hi - lo), 1)
    start = start_ref[i * block : (i + 1) * block, :]
    return jnp.where((keys >= start) & (keys <= rows), 0.0, -1e30).astype(single)

def attend_kernel(start_ref, q_ref, k_ref, v_ref, kb_ref, vb_ref, out_ref):
    span, cols = q_ref.shape
    block = span // 2
    lane = lax.broadcasted_iota(jnp.int32, (block, cols), 1) // HEAD_DIM
    for i, (lo, hi) in enumerate(windows(span)):
        rows = pl.ds(i * block, block)
        bias = hidden_bias(start_ref, i, block, lo, hi, span)
        keys = key_window(kb_ref, k_ref, lo, hi, span)
        vals = key_window(vb_ref, v_ref, lo, hi, span)
        query = q_ref[rows, :] * jnp.asarray(HEAD_DIM ** (-0.5), bfloat)
        def head(h, total):
            mine = lane == h
            scores = dot_nt(jnp.where(mine, query, 0), keys) + bias
            weights = jnp.exp(scores - jnp.max(scores, axis=1, keepdims=True))
            part = jnp.dot(weights.astype(bfloat), vals, preferred_element_type=single)
            part = part * (1.0 / jnp.sum(weights, axis=1, keepdims=True))
            return jnp.where(mine, part, total)
        total = lax.fori_loop(0, cols // HEAD_DIM, head, jnp.zeros((block, cols), single), unroll=True)
        out_ref[rows, :] = total.astype(bfloat)

def attend_back_kernel(start_ref, q_ref, k_ref, v_ref, kb_ref, vb_ref, do_ref, dq_ref, edge_ref, pair_ref, dk, dv):
    span, cols = q_ref.shape
    block = span // 2
    scale = HEAD_DIM ** (-0.5)
    dk[...] = jnp.zeros_like(dk)
    dv[...] = jnp.zeros_like(dv)
    lane = lax.broadcasted_iota(jnp.int32, (block, cols), 1) // HEAD_DIM
    for i, (lo, hi) in enumerate(windows(span)):
        rows = pl.ds(i * block, block)
        bias = hidden_bias(start_ref, i, block, lo, hi, span)
        keys = key_window(kb_ref, k_ref, lo, hi, span)
        vals = key_window(vb_ref, v_ref, lo, hi, span)
        query = q_ref[rows, :] * jnp.asarray(scale, bfloat)
        grad = do_ref[rows, :]
        def head(h, total):
            mine = lane == h
            query_h = jnp.where(mine, query, 0)
            grad_h = jnp.where(mine, grad, 0)
            scores = dot_nt(query_h, keys) + bias
            weights = jnp.exp(scores - jnp.max(scores, axis=1, keepdims=True))
            probs = weights * (1.0 / jnp.sum(weights, axis=1, keepdims=True))
            prob_grad = dot_nt(grad_h, vals)
            row_dot = jnp.sum(probs * prob_grad, axis=1, keepdims=True)
            score_grad = (probs * (prob_grad - row_dot)).astype(bfloat)
            dv[lo:hi, :] += dot_tn(probs.astype(bfloat), grad_h)
            dk[lo:hi, :] += dot_tn(score_grad, query_h)
            part = jnp.dot(score_grad, keys, preferred_element_type=single)
            return jnp.where(mine, part, total)
        total = lax.fori_loop(0, cols // HEAD_DIM, head, jnp.zeros((block, cols), single), unroll=True)
        dq_ref[rows, :] = (total * scale).astype(bfloat)
    edge_ref[:, :cols] = dk[:span, :].astype(bfloat)
    edge_ref[:, cols:] = dv[:span, :].astype(bfloat)
    pair_ref[:, :cols] = dk[span:, :]
    pair_ref[:, cols:] = dv[span:, :]

def attention_specs(span, cols):
    def at(j):
        return pl.BlockSpec((span, cols), lambda g: (g, j))
    return [pl.BlockSpec((span, 1), lambda g: (g, 0)), at(0), at(0), at(1), at(0), at(1)]

def attend(starts, query, key_value, before, groups):
    span, cols = query.shape[0] // groups, query.shape[1]
    return pl.pallas_call(
        attend_kernel,
        grid=(groups,),
        out_shape=jax.ShapeDtypeStruct((groups * span, cols), bfloat),
        in_specs=attention_specs(span, cols),
        out_specs=pl.BlockSpec((span, cols), lambda g: (g, 0)),
        compiler_params=pltpu.CompilerParams(vmem_limit_bytes=60 << 20),
        name="attend",
    )(starts, query, key_value, key_value, before, before)

def attend_back(starts, query, key_value, before, grad, groups):
    span, cols = query.shape[0] // groups, query.shape[1]
    rows = groups * span
    return pl.pallas_call(
        attend_back_kernel,
        grid=(groups,),
        out_shape=[jax.ShapeDtypeStruct((rows, cols), bfloat), jax.ShapeDtypeStruct((rows, 2 * cols), bfloat), jax.ShapeDtypeStruct((rows, 2 * cols), single)],
        in_specs=attention_specs(span, cols) + [pl.BlockSpec((span, cols), lambda g: (g, 0))],
        out_specs=[pl.BlockSpec((span, cols), lambda g: (g, 0))] + [pl.BlockSpec((span, 2 * cols), lambda g: (g, 0))] * 2,
        scratch_shapes=[pltpu.VMEM((2 * span, cols), single)] * 2,
        compiler_params=pltpu.CompilerParams(vmem_limit_bytes=60 << 20),
        name="attend_back",
    )(starts, query, key_value, key_value, before, before, grad)


def attention_heads(starts, query, key_value, before, groups):
    span, cols = query.shape[0] // groups, query.shape[1]
    both = jnp.concatenate([before.reshape(groups, span, -1), key_value.reshape(groups, span, -1)], axis=1)
    key_two, value_two = [both[..., i * cols : (i + 1) * cols].reshape(groups, 2 * span, -1, HEAD_DIM) for i in (0, 1)]
    query = query.reshape(groups, span, -1, HEAD_DIM)
    keys = jnp.arange(2 * span)[None, None, :]
    rows = span + jnp.arange(span)[None, :, None]
    allowed = (keys >= starts.reshape(groups, span, 1)) & (keys <= rows)
    scores = jnp.einsum("gqhd,gkhd->ghqk", query, key_two, preferred_element_type=single) * HEAD_DIM ** (-0.5)
    scores = jnp.where(allowed[:, None], scores, -1e30)
    weights = jnp.exp(scores - jnp.max(scores, axis=-1, keepdims=True))
    return query, key_two, value_two, weights / jnp.sum(weights, axis=-1, keepdims=True)


def attention_forward(starts, query, key_value, before, groups):
    if query.shape[1] % 128 == 0:
        return attend(starts, query, key_value, before, groups)
    _, _, value_two, probs = attention_heads(starts, query, key_value, before, groups)
    context = jnp.einsum("ghqk,gkhd->gqhd", probs.astype(bfloat), value_two, preferred_element_type=single)
    return context.astype(bfloat).reshape(query.shape)


def attention_backward(starts, query, key_value, before, grad, groups):
    if query.shape[1] % 128 == 0:
        return attend_back(starts, query, key_value, before, grad, groups)
    rows = query.shape[0]
    query, key_two, value_two, probs = attention_heads(starts, query, key_value, before, groups)
    span = query.shape[1]
    grad = grad.reshape(query.shape)
    prob_grad = jnp.einsum("gqhd,gkhd->ghqk", grad, value_two, preferred_element_type=single)
    row_dot = jnp.sum(probs * prob_grad, axis=-1, keepdims=True)
    score_grad = (probs * (prob_grad - row_dot)).astype(bfloat)
    query_grad = jnp.einsum("ghqk,gkhd->gqhd", score_grad, key_two, preferred_element_type=single) * HEAD_DIM ** (-0.5)
    key_grad = jnp.einsum("ghqk,gqhd->gkhd", score_grad, query, preferred_element_type=single) * HEAD_DIM ** (-0.5)
    value_grad = jnp.einsum("ghqk,gqhd->gkhd", probs.astype(bfloat), grad, preferred_element_type=single)
    pair = jnp.concatenate([t.reshape(groups, 2 * span, -1) for t in (key_grad, value_grad)], axis=2)
    edge, pair = [t.reshape(rows, -1) for t in (pair[:, :span].astype(bfloat), pair[:, span:])]
    return query_grad.astype(bfloat).reshape(rows, -1), edge, pair


def norm_backward(values, out_grad, gain_vec):
    center = jnp.mean(values, axis=-1, keepdims=True)
    centered = values - center
    rs = lax.rsqrt(jnp.mean(centered * centered, axis=-1, keepdims=True) + 1e-05)
    xhat = centered * rs
    g = out_grad * gain_vec
    part = rs * (g - jnp.mean(g, axis=-1, keepdims=True) - xhat * jnp.mean(g * xhat, axis=-1, keepdims=True))
    return part, jnp.sum(out_grad * xhat, axis=0), jnp.sum(out_grad, axis=0)


def on_device(
    inputs,
    exit_layers,
    lengths,
    layer_index,
    out_grad,
    ln1_gain,
    ln1_bias,
    q_weight,
    q_bias,
    k_weight,
    v_weight,
    v_bias,
    o_weight,
    o_bias,
    ln2_gain,
    ln2_bias,
    fc1_weight,
    fc1_bias,
    fc2_weight,
    fc2_bias,
):
    B, Z, X = lax.axis_size("b"), lax.axis_size("z"), lax.axis_size("x")
    R = B * X
    local = inputs[0].astype(single)
    tok, D = local.shape
    span = X * tok
    group_tok = Z * span
    at_z, at_x = lax.axis_index("z"), lax.axis_index("x")
    rank = lax.axis_index("b") * X + at_x
    rows_dev = q_weight.shape[0]
    cols = D // R
    heads = cols // HEAD_DIM
    whole_heads = rows_dev % HEAD_DIM == 0
    fast = (B, Z, X, rows_dev) == (4, 4, 2, HEAD_DIM)

    group_active = (exit_layers[0] > layer_index[0]).astype(single)
    active_total = jnp.sum(group_active)
    active = lax.dynamic_slice_in_dim(group_active, at_z * span + at_x * tok, tok, 0)[:, None]

    count = lengths.shape[1]
    upto = jnp.arange(count)[:, None] <= jnp.arange(count)[None, :]
    def to_ranks(matrix):
        lead = matrix.shape[:-1]
        if whole_heads:
            matrix = matrix.reshape(*lead, B, Z, X, rows_dev)
            k = len(lead)
            return matrix.transpose(k, k + 2, *range(k), k + 1, k + 3).reshape(R, *lead, cols)
        return jnp.moveaxis(matrix.reshape(*lead, R, cols), -2, 0)

    def from_ranks(parts):
        if whole_heads:
            parts = parts.reshape(B, X, -1, Z, rows_dev)
            return parts.transpose(2, 0, 3, 1, 4).reshape(-1, D)
        return parts.transpose(1, 0, 2).reshape(-1, D)

    def mine(vector):
        return lax.dynamic_index_in_dim(to_ranks(vector), rank, 0, keepdims=False)

    if whole_heads:
        weight_o = lax.all_gather(o_weight, "z", axis=0, tiled=True)
    else:
        weight_o = lax.dynamic_slice_in_dim(lax.all_gather(o_weight, ALL, axis=0, tiled=True), rank * cols, cols, 0)
    small = [ln1_gain, ln1_bias, q_bias, v_bias, o_bias, ln2_gain, ln2_bias, fc2_bias]
    pack = jnp.concatenate([v.astype(single) for v in (*small, fc1_bias, lengths[0])])
    pack = jnp.concatenate([pack, jnp.zeros((-pack.shape[0] % 128,), single)])
    if fast:
        query_mine, pair_mine, pack = spread(q_weight, k_weight, v_weight, pack, R * Z, 8)
        query_mine, pair_mine, pack = query_mine.reshape(-1, cols), pair_mine.reshape(-1, 2 * cols), pack[:, 0]
    else:
        qkv_parts = jnp.concatenate([to_ranks(q_weight), to_ranks(k_weight), to_ranks(v_weight)], axis=2)
        qkv_mine = lax.all_to_all(qkv_parts, PLANE, split_axis=0, concat_axis=0, tiled=True).reshape(D // Z, 3 * cols)
        query_mine, pair_mine = qkv_mine[:, :cols], qkv_mine[:, cols:]
        pack = jnp.broadcast_to(pack, (R * Z, pack.shape[0]))
        pack = lax.all_to_all(pack, ALL, split_axis=0, concat_axis=0, tiled=True)
    vectors = [pack[:, i * rows_dev : (i + 1) * rows_dev].reshape(-1) for i in range(len(small))]
    gain_one, bias_one, bias_q, bias_v, bias_o, gain_two, bias_two, bias_down = vectors
    pack = pack.reshape(B, Z, X, -1)[..., len(small) * rows_dev :]
    up_dev = fc1_bias.shape[0]
    bias_up = lax.dynamic_index_in_dim(
        pack[..., :up_dev].transpose(0, 2, 1, 3).reshape(R, Z * up_dev), rank, 0, keepdims=False
    )
    group_lengths = pack[:, 0, 0, up_dev : up_dev + count].astype(jnp.int32)
    ends = jnp.sum(jnp.where(upto, group_lengths[:, :, None], 0), axis=1)
    places = at_z * span + jnp.arange(span, dtype=jnp.int32)
    starts = jnp.max(jnp.where(ends[:, None, :] <= places[None, :, None], ends[:, None, :], 0), axis=2)
    starts = starts - (at_z - 1) * span

    def feature_rows(mine):
        full = lax.all_gather(mine, "z", axis=0, tiled=True)
        return full.reshape(Z, B, X, rows_dev, -1).transpose(1, 0, 2, 3, 4).reshape(D, -1)

    weight_kv = feature_rows(pair_mine)
    bias_kv = jnp.concatenate([jnp.zeros((cols,), single), mine(bias_v)])
    bias_one, query_mine, weight_o = lax.optimization_barrier((bias_one, query_mine, weight_o))
    normed_low = layer_norm(local, gain_one, bias_one).astype(bfloat)

    def gather_plane(rows, cid, name):
        if fast:
            return plane_gather(rows, (), [], None, cid, name)[0]
        return lax.all_gather(rows, PLANE, axis=0, tiled=True)

    def gather_plane_dot(rows, weight, shift, out_type, turned, cid, name):
        if fast:
            return gather_dot(rows, weight, shift, out_type, turned, cid, name)
        rows = lax.all_gather(rows, PLANE, axis=0, tiled=True)
        return rows, ((dot_nt if turned else dot)(rows, weight) + shift).astype(out_type)

    def reduce_plane(left, weight, turned, cid, name):
        if fast:
            return dot_reduce([left], [weight], turned, cid, name)
        terms = (dot_nt if turned else dot)(left, weight).astype(bfloat)
        return lax.psum_scatter(terms, PLANE, scatter_dimension=0, tiled=True).astype(single)

    normed_all = gather_plane(normed_low, 0, "gather_normed")
    units = fc1_bias.shape[0] // 2
    halves = [jnp.concatenate([fc1_weight.T[i : i + units], fc2_weight[i : i + units]]) for i in (0, units)]

    def gather_units(mine):
        return lax.all_gather(mine, "z", axis=0, tiled=True).reshape(Z, 2, units, D)

    normed_all, weight_kv, unit_one = lax.optimization_barrier((normed_all, weight_kv, halves[0]))
    weight_q = feature_rows(query_mine)
    unit_one = gather_units(unit_one)
    key_value = (dot(normed_all, weight_kv) + bias_kv).astype(bfloat)
    up = [(i, i + 1) for i in range(Z - 1)]
    down = [(i + 1, i) for i in range(Z - 1)]
    cotangent = out_grad[0].astype(single) * (group_tok / active_total)
    branch_grad = (active * cotangent).astype(bfloat)
    down_b_grad = column_sums(branch_grad)
    key_value, branch_grad = lax.optimization_barrier((key_value, branch_grad))
    before = lax.ppermute(key_value, "z", up)
    branch_all = gather_plane(branch_grad, 7, "gather_branch")
    branch_all, late_normed = lax.optimization_barrier((branch_all, normed_all))
    query = (dot(late_normed, weight_q) + mine(bias_q)).astype(bfloat)
    before, query = lax.optimization_barrier((before, query))
    starts = starts.reshape(B * span, 1)
    context = attention_forward(starts, query, key_value, before, B)
    context, unit_two = lax.optimization_barrier((context, halves[1]))
    unit_two = gather_units(unit_two)

    attended = reduce_plane(context, weight_o, False, 1, "attended") + bias_o
    middle = local + active * attended
    normed_two = layer_norm(middle, gain_two, bias_two).astype(bfloat)
    bias_up = bias_up.reshape(Z, 2, units)
    bias_up = [bias_up[:, i].reshape(1, Z * units) for i in range(2)]

    def sum_halves(left, right, turned, cid, name):
        if fast:
            return dot_reduce(left, right, turned, cid, name)
        terms = sum((dot_nt if turned else dot)(a, w) for a, w in zip(left, right)).astype(bfloat)
        return lax.psum_scatter(terms, PLANE, scatter_dimension=0, tiled=True).astype(single)

    def sum_z(grads):
        return lax.psum_scatter(grads.reshape(Z * 2 * units, D), "z", scatter_dimension=0, tiled=True)

    if fast:
        branch_rows = branch_all.reshape(R, tok, D)
        two_all, hidden_one, pre_one, bias_one_up, grads = first_units(normed_two, branch_rows, unit_one, bias_up[0], 2)
        shard_one = sum_z(grads)
        hidden_two, bias_two_up, normed_two_grad, grads = last_units(
            two_all, branch_rows, pre_one, unit_one, unit_two, bias_up[1], 3
        )
        shard_two = sum_z(grads)
        up_b_halves = [bias_one_up[0], bias_two_up[0]]
    else:
        two_all = gather_plane(normed_two, 2, "gather_two")

        def half_units(weights, bias):
            weight_up, weight_down = [weights[:, i].reshape(Z * units, D) for i in (0, 1)]
            hidden, gelu_pull = jax.vjp(partial(jax.nn.gelu, approximate=True), dot_nt(two_all, weight_up) + bias)
            hidden = hidden.astype(bfloat)
            pre_grad = gelu_pull(dot_nt(branch_all, weight_down))[0].astype(bfloat)
            grads = dot_tn(pre_grad, two_all), dot_tn(hidden, branch_all)
            grads = jnp.stack([g.astype(bfloat).reshape(Z, units, D) for g in grads], axis=1)
            return hidden, pre_grad, sum_z(grads), weight_up, weight_down

        hidden_one, pre_one, shard_one, up_one, down_one = half_units(unit_one, bias_up[0])
        hidden_two, pre_two, shard_two, up_two, down_two = half_units(unit_two, bias_up[1])
        up_b_halves = [column_sums(pre_one), column_sums(pre_two)]
        normed_two_grad = sum_halves([pre_one, pre_two], [up_one, up_two], False, 3, "up_grad")
    up_b_grad = jnp.stack([half.reshape(Z, units) for half in up_b_halves], axis=1).reshape(-1)

    middle_part, gain_two_grad, bias_two_grad = norm_backward(middle, normed_two_grad, gain_two)
    middle_grad = cotangent + middle_part
    attended_grad = (active * middle_grad).astype(bfloat)
    out_b_grad = column_sums(attended_grad)
    attended_all, context_grad = gather_plane_dot(
        attended_grad, weight_o, jnp.zeros((1, cols), single), bfloat, True, 5, "attended_grad"
    )
    context_grad, shard_one = lax.optimization_barrier((context_grad, shard_one))
    out_w_grad = dot_tn(context, attended_all)
    query_grad, edge, pair = attention_backward(starts, query, key_value, before, context_grad, B)
    hidden_one, edge, pair, query_grad = lax.optimization_barrier((hidden_one, edge, pair, query_grad))
    after = lax.ppermute(edge, "z", down)
    query_w_grad = dot_tn(normed_all, query_grad).astype(bfloat)
    hidden_one, query_w_grad, out_w_grad = lax.optimization_barrier((hidden_one, query_w_grad, out_w_grad))
    downs = [unit_one, unit_two] if fast else [down_one, down_two]
    branch = sum_halves([hidden_one, hidden_two], downs, False, 4, "down")
    branch, after, shard_two = lax.optimization_barrier((branch, after, shard_two))
    outputs = middle + active * (branch + bias_down)
    pair_grad = (pair + after.astype(single)).astype(bfloat)
    pair_w_grad = dot_tn(normed_all, pair_grad).astype(bfloat)
    pair_grad, pair_w_grad = lax.optimization_barrier((pair_grad, pair_w_grad))
    normed_grad = sum_halves([query_grad, pair_grad], [weight_q, weight_kv], True, 6, "qkv_grad")
    query_b_grad = column_sums(query_grad)
    value_b_grad = column_sums(pair_grad[:, cols:])
    input_part, gain_one_grad, bias_one_grad = norm_backward(local, normed_grad, gain_one)
    input_grad = middle_grad + input_part

    def sum_to_owners(vectors, axes, parts):
        split = jnp.concatenate([v.reshape(parts, -1) for v in vectors], axis=1)
        summed = jnp.sum(lax.all_to_all(split, axes, split_axis=0, concat_axis=0, tiled=True), axis=0)
        widths = [v.shape[0] // parts for v in vectors]
        return [summed[sum(widths[:i]) : sum(widths[: i + 1])] for i in range(len(widths))]

    qkv_w_grad = jnp.concatenate([query_w_grad, pair_w_grad], axis=1)
    qkv_w_grad = qkv_w_grad.reshape(B, Z, X, rows_dev, 3 * cols).transpose(1, 0, 2, 3, 4).reshape(D, 3 * cols)
    qkv_w_grad = lax.psum_scatter(qkv_w_grad, "z", scatter_dimension=0, tiled=True).reshape(R, rows_dev, 3 * cols)
    qkv_w_grad, out_w_grad = lax.optimization_barrier((qkv_w_grad, out_w_grad))
    device_sums = [gain_one_grad, bias_one_grad, out_b_grad, gain_two_grad, bias_two_grad, down_b_grad]
    if fast:
        rank_sums = jnp.concatenate([v.reshape(Z, -1) for v in (query_b_grad, value_b_grad, up_b_grad)], axis=1)
        here = (jnp.arange(R) == rank).reshape(B, 1, X, 1)
        rank_sums = jnp.where(here, rank_sums[None, :, None, :], 0.0).reshape(R * Z, -1)
        rows = jnp.concatenate([v.reshape(R * Z, -1) for v in device_sums] + [rank_sums], axis=1)
        q_w_shard, k_w_shard, v_w_shard, summed = settle(qkv_w_grad, rows, 9)
        sums = [summed[0, i * rows_dev : (i + 1) * rows_dev] for i in range(len(device_sums) + 2)]
        q_b_shard, v_b_shard = sums[len(device_sums) :]
        up_b_shard = summed[0, (len(device_sums) + 2) * rows_dev :]
    else:
        qkv_w_grad = lax.all_to_all(qkv_w_grad, PLANE, split_axis=0, concat_axis=0, tiled=True)
        q_w_shard, k_w_shard, v_w_shard = [
            from_ranks(qkv_w_grad[..., i : i + cols]).astype(single) for i in range(0, 3 * cols, cols)
        ]
        sums = sum_to_owners(device_sums, ALL, R * Z)
        [up_b_shard] = sum_to_owners([up_b_grad], "z", Z)
    if whole_heads:
        out_w_shard = lax.psum_scatter(out_w_grad.astype(bfloat), "z", scatter_dimension=0, tiled=True).astype(single)
        if not fast:
            q_b_shard, v_b_shard = sum_to_owners([query_b_grad, value_b_grad], "z", Z)
    else:

        def placed(rows):
            full = jnp.zeros((D,) + rows.shape[1:], rows.dtype)
            full = lax.dynamic_update_slice_in_dim(full, rows, rank * cols, 0)
            return lax.psum_scatter(full, ALL, scatter_dimension=0, tiled=True).astype(single)

        out_w_shard = placed(out_w_grad.astype(bfloat))
        q_b_shard = placed(query_b_grad)
        v_b_shard = placed(value_b_grad)
    return (
        outputs.astype(bfloat)[None],
        input_grad.astype(bfloat)[None],
        sums[0],
        sums[1],
        q_w_shard,
        q_b_shard,
        k_w_shard,
        v_w_shard,
        v_b_shard,
        out_w_shard,
        sums[2],
        sums[3],
        sums[4],
        jnp.concatenate([shard_one[:units], shard_two[:units]]).T.astype(single),
        up_b_shard,
        jnp.concatenate([shard_one[units:], shard_two[units:]]).astype(single),
        sums[5],
    )


def solution(mesh):
    groups, parts = mesh.shape["batch"], mesh.shape["seq"]
    inner = Mesh(mesh.devices.reshape(groups, SPANS, parts // SPANS), ("b", "z", "x"))
    token = P("b", ("z", "x"), None)
    vector = P(ALL)
    rows = P(ALL, None)
    columns = P(None, ALL)
    return jax.shard_map(
        on_device,
        mesh=inner,
        in_specs=(
            token,
            P("b", None),
            P("b", None),
            P(),
            token,
            vector,
            vector,
            rows,
            vector,
            rows,
            rows,
            vector,
            rows,
            vector,
            vector,
            vector,
            columns,
            vector,
            rows,
            vector,
        ),
        out_specs=(
            token,
            token,
            vector,
            vector,
            rows,
            vector,
            rows,
            rows,
            vector,
            rows,
            vector,
            vector,
            vector,
            columns,
            vector,
            rows,
            vector,
        ),
        check_vma=False,
    )
```

```python
import functools
from functools import partial

import jax
import jax.numpy as jnp
from jax import lax
from jax.experimental import pallas as pl
from jax.experimental.pallas import tpu as pltpu
from jax.sharding import Mesh
from jax.sharding import PartitionSpec as P

HEAD_DIM = 64
SPANS = 4

bfloat = jnp.bfloat16
single = jnp.float32

PLANE = ("b", "x")
ALL = ("b", "z", "x")
MESH = pl.DeviceIdType.MESH
TILE = 512

def plane_place():
    b, z, x = lax.axis_index("b"), lax.axis_index("z"), lax.axis_index("x")
    sib_b = b + 1 - 2 * lax.rem(b, 2)
    far_b = lax.rem(b + 2, 4)
    far_sib_b = lax.rem(sib_b + 2, 4)
    ids = {"s": (sib_b, z, x), "x": (b, z, 1 - x), "y": (far_b, z, x)}
    ranks = {
        "o": b * 2 + x,
        "s": sib_b * 2 + x,
        "x": b * 2 + 1 - x,
        "xs": sib_b * 2 + 1 - x,
        "y": far_b * 2 + x,
        "ys": far_sib_b * 2 + x,
        "d": far_b * 2 + 1 - x,
        "ds": far_sib_b * 2 + 1 - x,
    }
    return ids, ranks

def greet(ids):
    barrier = pltpu.get_barrier_semaphore()
    for device in ids.values():
        pl.semaphore_signal(barrier, inc=1, device_id=device, device_id_type=MESH)
    pl.semaphore_wait(barrier, len(ids))

def tiles(lo, hi, body):
    def step(i, _):
        body(pl.ds(pl.multiple_of(i * TILE, TILE), TILE))
        return 0
    lax.fori_loop(lo // TILE, hi // TILE, step, 0)

def gather_kernel(body_of, beside, n_in, n_out, x_ref, *refs):
    ins = refs[:n_in]; all_ref = refs[n_in]; outs = refs[n_in + 1 : n_in + 1 + n_out]
    held, send, recv, keep, *more = refs[n_in + 1 + n_out :]
    work = None if beside is None else beside(ins, outs, more)
    ids, at = plane_place()
    half = x_ref.shape[0] // 2
    parts = (pl.ds(0, half), pl.ds(half, half))
    greet(ids)
    count = [0]
    started = []
    def ship(src, dst, to):
        n = count[0]; count[0] += 1
        c = pltpu.make_async_remote_copy(src_ref=src, dst_ref=dst, send_sem=send.at[n], recv_sem=recv.at[n], device_id=ids[to], device_id_type=MESH)
        c.start(); started.append(c)
        return c
    own = at["o"]
    x0 = ship(x_ref.at[parts[0]], held.at[own, parts[0]], "x")
    y1 = ship(x_ref.at[parts[1]], held.at[own, parts[1]], "y")
    x1 = ship(x_ref.at[parts[1]], held.at[own, parts[1]], "x")
    y0 = ship(x_ref.at[parts[0]], held.at[own, parts[0]], "y")
    s0 = ship(x_ref, held.at[own], "s")
    kept = []
    def done(rank, src):
        c = pltpu.make_async_copy(src, all_ref.at[rank], keep.at[len(kept)])
        c.start(); kept.append(c)
        if body_of is not None:
            body_of(rank, src, ins, outs)
    done(own, x_ref)
    s0.wait_recv()
    done(at["s"], held.at[at["s"]])
    x0.wait_recv()
    ry = ship(held.at[at["x"], parts[0]], held.at[at["x"], parts[0]], "y")
    y1.wait_recv()
    rx = ship(held.at[at["y"], parts[1]], held.at[at["y"], parts[1]], "x")
    if work is not None:
        work()
    x1.wait_recv()
    sx = ship(held.at[at["x"]], held.at[at["x"]], "s")
    y0.wait_recv()
    sy = ship(held.at[at["y"]], held.at[at["y"]], "s")
    done(at["x"], held.at[at["x"]])
    done(at["y"], held.at[at["y"]])
    sx.wait_recv()
    done(at["xs"], held.at[at["xs"]])
    sy.wait_recv()
    done(at["ys"], held.at[at["ys"]])
    ry.wait_recv(); rx.wait_recv()
    sd = ship(held.at[at["d"]], held.at[at["d"]], "s")
    done(at["d"], held.at[at["d"]])
    sd.wait_recv()
    done(at["ds"], held.at[at["ds"]])
    for c in started: c.wait_send()
    for c in kept: c.wait()

def vmem(n): return [pl.BlockSpec(memory_space=pltpu.VMEM)] * n

def plane_gather(x, ins, out_types, body_of, cid, name, ranks=8, beside=None, far=(), more=()):
    tok, D = x.shape
    res = pl.pallas_call(
        functools.partial(gather_kernel, body_of, beside, len(ins) + len(far), len(out_types)),
        out_shape=[jax.ShapeDtypeStruct((ranks, tok, D), x.dtype), *out_types],
        in_specs=vmem(1 + len(ins)) + [pl.BlockSpec(memory_space=pl.ANY)] * len(far),
        out_specs=[pl.BlockSpec(memory_space=pl.ANY)] + vmem(len(out_types)),
        scratch_shapes=[pltpu.VMEM((ranks, tok, D), x.dtype), pltpu.SemaphoreType.DMA((10,)), pltpu.SemaphoreType.DMA((10,)), pltpu.SemaphoreType.DMA((8,)), *more],
        compiler_params=pltpu.CompilerParams(collective_id=cid, has_side_effects=True, vmem_limit_bytes=60 << 20),
        cost_estimate=pl.CostEstimate(flops=1 << 30, bytes_accessed=128 << 20, transcendentals=0),
        name=name,
    )(x, *ins, *far)
    return res[0].reshape(ranks * tok, D), *res[1:]

def gather_dot(x, w, bias, out_dtype, turned, cid, name, extra_out=(), **beside):
    ranks, tok, D = 8, *x.shape
    N = w.shape[0] if turned else w.shape[1]
    tile = min(N, 512) if N % 512 == 0 else 256
    def body(rank, src, ins, outs):
        w_ref, b_ref = ins[:2]
        def step(i, _):
            cols = pl.ds(pl.multiple_of(i * tile, tile), tile)
            if turned:
                y = lax.dot_general(src[...], w_ref[cols, :], (((1,), (1,)), ((), ())), preferred_element_type=single)
            else:
                y = jnp.dot(src[...], w_ref[:, cols], preferred_element_type=single)
            outs[0][rank, :, cols] = (y + b_ref[:, cols]).astype(out_dtype)
            return 0
        lax.fori_loop(0, N // tile, step, 0)
    types = [jax.ShapeDtypeStruct((ranks, tok, N), out_dtype), *extra_out]
    all_, y, *rest = plane_gather(x, (w, bias), types, body, cid, name, **beside)
    return all_, y.reshape(ranks * tok, N), *rest

def reduce_kernel(turned, pairs, *refs):
    left, right = refs[:pairs], refs[pairs : 2 * pairs]
    out_ref, sib_out, sib_in, stage, landed, send, recv = refs[2 * pairs :]
    ids, at = plane_place()
    D = out_ref.shape[1]
    mid = D // 2
    greet(ids)
    count = [0]; started = []
    def ship(src, dst, to):
        n = count[0]; count[0] += 1
        c = pltpu.make_async_remote_copy(src_ref=src, dst_ref=dst, send_sem=send.at[n], recv_sem=recv.at[n], device_id=ids[to], device_id_type=MESH)
        c.start(); started.append(c)
        return c
    def term(rank, cols):
        if turned:
            return sum(dot_nt(a[rank], w[cols, :]) for a, w in zip(left, right))
        rows = [w[:, 1, :, cols].reshape(-1, TILE) if len(w.shape) == 4 else w[:, cols] for w in right]
        return sum(dot(a[rank], w) for a, w in zip(left, rows))
    order = ("d", "x", "y", "o")
    twin = {"d": "ds", "x": "xs", "y": "ys", "o": "s"}
    sib = {}
    def to_sibling(j, h):
        def fill(cols):
            sib_out[j, h, :, local(h, cols)] = term(at[twin[order[j]]], cols).astype(bfloat)
        tiles(h * mid, (h + 1) * mid, fill)
        sib[j, h] = ship(sib_out.at[j, h], sib_in.at[j, h], "s")
    def local(h, cols):
        return pl.ds(pl.multiple_of(cols.start - h * mid, TILE), TILE)
    def pair(j, h, cols):
        return term(at[order[j]], cols) + sib_in[j, h, :, local(h, cols)].astype(single)
    def put(j, h, extra=None):
        sib[j, h].wait_recv()
        def fill(cols):
            value = pair(j, h, cols)
            if extra is not None:
                value = value + landed[extra, :, local(h, cols)].astype(single)
            stage[j, h, :, local(h, cols)] = value.astype(bfloat)
        tiles(h * mid, (h + 1) * mid, fill)
    to_sibling(0, 0)
    to_sibling(0, 1)
    put(0, 0)
    d_a = ship(stage.at[0, 0], landed.at[0], "x")
    put(0, 1)
    d_b = ship(stage.at[0, 1], landed.at[1], "y")
    to_sibling(1, 0)
    to_sibling(2, 1)
    put(1, 0)
    x_a = ship(stage.at[1, 0], landed.at[2], "x")
    put(2, 1)
    y_b = ship(stage.at[2, 1], landed.at[3], "y")
    for j, h in ((1, 1), (2, 0), (3, 0), (3, 1)):
        to_sibling(j, h)
    d_b.wait_recv()
    put(1, 1, extra=1)
    x_b = ship(stage.at[1, 1], landed.at[5], "x")
    d_a.wait_recv()
    put(2, 0, extra=0)
    y_a = ship(stage.at[2, 0], landed.at[4], "y")
    for h in range(2):
        sib[3, h].wait_recv()
        def first(cols, h=h):
            out_ref[:, cols] = pair(3, h, cols)
        tiles(h * mid, (h + 1) * mid, first)
    x_a.wait_recv(); y_b.wait_recv(); x_b.wait_recv(); y_a.wait_recv()
    for h, (n, m) in enumerate(((2, 4), (3, 5))):
        def add(cols, h=h, n=n, m=m):
            c = local(h, cols)
            out_ref[:, cols] = out_ref[:, cols] + landed[n, :, c].astype(single) + landed[m, :, c].astype(single)
        tiles(h * mid, (h + 1) * mid, add)
    for c in started: c.wait_send()

def dot_reduce(left, right, turned, cid, name):
    ranks = 8
    D = right[0].shape[0] if turned else right[0].shape[-1]
    tok = left[0].size // left[0].shape[-1] // ranks
    return pl.pallas_call(
        functools.partial(reduce_kernel, turned, len(left)),
        out_shape=jax.ShapeDtypeStruct((tok, D), single),
        in_specs=vmem(2 * len(left)), out_specs=vmem(1)[0],
        scratch_shapes=[pltpu.VMEM((4, 2, tok, D // 2), bfloat), pltpu.VMEM((4, 2, tok, D // 2), bfloat), pltpu.VMEM((3, 2, tok, D // 2), bfloat), pltpu.VMEM((6, tok, D // 2), bfloat),
            pltpu.SemaphoreType.DMA((14,)), pltpu.SemaphoreType.DMA((14,))],
        compiler_params=pltpu.CompilerParams(collective_id=cid, has_side_effects=True, vmem_limit_bytes=60 << 20),
        cost_estimate=pl.CostEstimate(flops=1 << 30, bytes_accessed=128 << 20, transcendentals=0),
        name=name,
    )(*[a.reshape(ranks, tok, -1) for a in left], *right)


def dot(left, right):
    return jnp.dot(left, right, preferred_element_type=single)


def dot_tn(left, right):
    return lax.dot_general(left, right, (((0,), (0,)), ((), ())), preferred_element_type=single)


def dot_nt(left, right):
    return lax.dot_general(left, right, (((1,), (1,)), ((), ())), preferred_element_type=single)


def layer_norm(values, gain_vec, shift_vec):
    center = jnp.mean(values, axis=-1, keepdims=True)
    centered = values - center
    spread = jnp.mean(centered * centered, axis=-1, keepdims=True)
    return centered * lax.rsqrt(spread + 1e-05) * gain_vec + shift_vec


def column_sums(matrix):
    return jnp.sum(matrix.astype(single), axis=0)


def shipper(send, recv, ids):
    started = []

    def ship(src, dst, to):
        n = len(started)
        copy = pltpu.make_async_remote_copy(
            src_ref=src, dst_ref=dst, send_sem=send.at[n], recv_sem=recv.at[n], device_id=ids[to], device_id_type=MESH
        )
        copy.start()
        started.append(copy)
        return copy

    return ship, started


TWIN = {"o": "s", "x": "xs", "y": "ys", "d": "ds"}


def unit_rows(w_ref, i):
    parts, _, units, D = w_ref.shape
    return w_ref[:, i].reshape(parts * units, D)


def hidden_units(src, branch, w_ref, b_ref, hid_ref, pg_ref, pb_ref, rank):
    pre = dot_nt(src[...], unit_rows(w_ref, 0)) + b_ref[...]
    square = pre * pre
    bend = jnp.tanh(0.7978845608028654 * (pre + 0.044715 * (pre * square)))
    rise = 0.5 * (1.0 + bend)
    hid_ref[rank] = (pre * rise).astype(bfloat)
    slope = rise + (0.5 * 0.7978845608028654) * pre * (1.0 - bend * bend) * (1.0 + 3 * 0.044715 * square)
    grad = (dot_nt(branch[...], unit_rows(w_ref, 1)) * slope).astype(bfloat)
    pg_ref[rank] = grad
    pb_ref[...] += jnp.sum(grad.astype(single), axis=0, keepdims=True)


def first_units_kernel(
    x_ref, bg_ref, w_ref, b_ref, all_ref, hid_ref, pg_ref, pb_ref, grad_ref,
    held, bg, total, send, recv, keep, load,
):
    ids, at = plane_place()
    tok = x_ref.shape[0]
    half = tok // 2
    parts = (pl.ds(0, half), pl.ds(half, half))
    own = at["o"]
    loads = {}
    for n, name in enumerate(at):
        loads[name] = pltpu.make_async_copy(bg_ref.at[at[name]], bg.at[at[name]], load.at[n])
        loads[name].start()
    greet(ids)
    ship, started = shipper(send, recv, ids)
    x0 = ship(x_ref.at[parts[0]], held.at[own, parts[0]], "x")
    y1 = ship(x_ref.at[parts[1]], held.at[own, parts[1]], "y")
    x1 = ship(x_ref.at[parts[1]], held.at[own, parts[1]], "x")
    y0 = ship(x_ref.at[parts[0]], held.at[own, parts[0]], "y")
    s0 = ship(x_ref, held.at[own], "s")
    pb_ref[...] = jnp.zeros_like(pb_ref)
    kept = []

    def units(name):
        rank = at[name]
        src = x_ref if name == "o" else held.at[rank]
        copy = pltpu.make_async_copy(src, all_ref.at[rank], keep.at[len(kept)])
        copy.start()
        kept.append(copy)
        loads[name].wait()
        hidden_units(src, bg.at[rank], w_ref, b_ref, hid_ref, pg_ref, pb_ref, rank)

    def weigh(name, last=False):
        units_at = grad_ref.shape[2]
        per = 256 // units_at

        def rows(i, _):
            here = pl.ds(pl.multiple_of(i * 256, 256), 256)
            owners = pl.ds(i * per, per)
            for j, left in enumerate((pg_ref, hid_ref)):
                term = 0
                for n in (name, TWIN[name]):
                    right = bg[at[n]] if j else (x_ref[...] if n == "o" else held[at[n]])
                    term = term + dot_tn(left[at[n], :, here], right)
                term = term.reshape(per, units_at, -1)
                if name == "o":
                    total[owners, j] = term
                elif last:
                    grad_ref[owners, j] = (total[owners, j] + term).astype(bfloat)
                else:
                    total[owners, j] += term
            return 0

        lax.fori_loop(0, hid_ref.shape[2] // 256, rows, 0)

    units("o")
    s0.wait_recv()
    units("s")
    x0.wait_recv()
    ry = ship(held.at[at["x"], parts[0]], held.at[at["x"], parts[0]], "y")
    y1.wait_recv()
    rx = ship(held.at[at["y"], parts[1]], held.at[at["y"], parts[1]], "x")
    weigh("o")
    x1.wait_recv()
    sx = ship(held.at[at["x"]], held.at[at["x"]], "s")
    y0.wait_recv()
    sy = ship(held.at[at["y"]], held.at[at["y"]], "s")
    units("x")
    sx.wait_recv()
    units("xs")
    units("y")
    sy.wait_recv()
    units("ys")
    weigh("x")
    ry.wait_recv()
    rx.wait_recv()
    sd = ship(held.at[at["d"]], held.at[at["d"]], "s")
    weigh("y")
    units("d")
    sd.wait_recv()
    units("ds")
    weigh("d", last=True)
    for copy in started:
        copy.wait_send()
    for copy in kept:
        copy.wait()


def last_units_kernel(
    all_ref, bg_ref, pg1_ref, w1_ref, w_ref, b_ref, hid_ref, pg_ref, pb_ref, r_ref,
    held, bg, sib_out, sib_in, stage, landed, send, recv, load, load_b,
):
    ids, at = plane_place()
    ranks, tok, D = held.shape
    mid = D // 2
    names = ("ds", "d", "xs", "x", "ys", "y", "s", "o")
    loads = {}
    for n, name in enumerate(names):
        loads[name] = [
            pltpu.make_async_copy(all_ref.at[at[name]], held.at[at[name]], load.at[n]),
            pltpu.make_async_copy(bg_ref.at[at[name]], bg.at[at[name]], load_b.at[n]),
        ]
        for copy in loads[name]:
            copy.start()
    greet(ids)
    ship, started = shipper(send, recv, ids)
    pb_ref[...] = jnp.zeros_like(pb_ref)

    def units(name):
        for copy in loads[name]:
            copy.wait()
        rank = at[name]
        hidden_units(held.at[rank], bg.at[rank], w_ref, b_ref, hid_ref, pg_ref, pb_ref, rank)

    def term(name, cols):
        rank = at[name]
        first, second = [w[:, 0, :, cols].reshape(-1, TILE) for w in (w1_ref, w_ref)]
        return dot(pg1_ref[rank], first) + dot(pg_ref[rank], second)

    order = ("d", "x", "y", "o")

    def to_sibling(j):
        def fill(cols):
            sib_out[j, :, cols] = term(TWIN[order[j]], cols).astype(bfloat)

        tiles(0, D, fill)
        return ship(sib_out.at[j], sib_in.at[j], "s")

    def pair(j, cols):
        return term(order[j], cols) + sib_in[j, :, cols].astype(single)

    def local(h, cols):
        return pl.ds(pl.multiple_of(cols.start - h * mid, TILE), TILE)

    def put(j, h, extra=None):
        def fill(cols):
            value = pair(j, cols)
            if extra is not None:
                value = value + landed[extra, :, local(h, cols)].astype(single)
            stage[j, h, :, local(h, cols)] = value.astype(bfloat)

        tiles(h * mid, (h + 1) * mid, fill)

    units("ds")
    d_sib = to_sibling(0)
    units("d")
    d_sib.wait_recv()
    put(0, 0)
    d_a = ship(stage.at[0, 0], landed.at[0], "x")
    put(0, 1)
    d_b = ship(stage.at[0, 1], landed.at[1], "y")
    units("xs")
    x_sib = to_sibling(1)
    units("x")
    x_sib.wait_recv()
    put(1, 0)
    x_a = ship(stage.at[1, 0], landed.at[2], "x")
    units("ys")
    y_sib = to_sibling(2)
    units("y")
    y_sib.wait_recv()
    put(2, 1)
    y_b = ship(stage.at[2, 1], landed.at[3], "y")
    d_b.wait_recv()
    put(1, 1, extra=1)
    x_b = ship(stage.at[1, 1], landed.at[5], "x")
    d_a.wait_recv()
    put(2, 0, extra=0)
    y_a = ship(stage.at[2, 0], landed.at[4], "y")
    units("s")
    own_sib = to_sibling(3)
    units("o")
    own_sib.wait_recv()

    def first(cols):
        r_ref[:, cols] = pair(3, cols)

    tiles(0, D, first)

    for copy in (x_a, y_b, x_b, y_a):
        copy.wait_recv()
    for h, (n, m) in enumerate(((2, 4), (3, 5))):

        def add(cols, h=h, n=n, m=m):
            c = local(h, cols)
            r_ref[:, cols] = r_ref[:, cols] + landed[n, :, c].astype(single) + landed[m, :, c].astype(single)

        tiles(h * mid, (h + 1) * mid, add)
    for copy in started:
        copy.wait_send()


def first_units(x, bg, w, bias, cid):
    ranks = 8
    tok, D = x.shape
    F = bias.shape[1]
    anywhere = pl.BlockSpec(memory_space=pl.ANY)
    inside = pl.BlockSpec(memory_space=pltpu.VMEM)
    return pl.pallas_call(
        first_units_kernel,
        out_shape=[
            jax.ShapeDtypeStruct((ranks, tok, D), bfloat),
            jax.ShapeDtypeStruct((ranks, tok, F), bfloat),
            jax.ShapeDtypeStruct((ranks, tok, F), bfloat),
            jax.ShapeDtypeStruct((1, F), single),
            jax.ShapeDtypeStruct(w.shape, bfloat),
        ],
        in_specs=[inside, anywhere, inside, inside],
        out_specs=[anywhere, inside, inside, inside, inside],
        scratch_shapes=[
            pltpu.VMEM((ranks, tok, D), bfloat),
            pltpu.VMEM((ranks, tok, D), bfloat),
            pltpu.VMEM(w.shape, single),
            pltpu.SemaphoreType.DMA((10,)),
            pltpu.SemaphoreType.DMA((10,)),
            pltpu.SemaphoreType.DMA((8,)),
            pltpu.SemaphoreType.DMA((8,)),
        ],
        compiler_params=pltpu.CompilerParams(collective_id=cid, has_side_effects=True, vmem_limit_bytes=62 << 20),
        cost_estimate=pl.CostEstimate(flops=1 << 30, bytes_accessed=160 << 20, transcendentals=0),
        name="first_units",
    )(x, bg, w, bias)


def last_units(rows, bg, pg, w1, w, bias, cid):
    ranks, tok, D = rows.shape
    F = bias.shape[1]
    anywhere = pl.BlockSpec(memory_space=pl.ANY)
    inside = pl.BlockSpec(memory_space=pltpu.VMEM)
    return pl.pallas_call(
        last_units_kernel,
        out_shape=[
            jax.ShapeDtypeStruct((ranks, tok, F), bfloat),
            jax.ShapeDtypeStruct((ranks, tok, F), bfloat),
            jax.ShapeDtypeStruct((1, F), single),
            jax.ShapeDtypeStruct((tok, D), single),
        ],
        in_specs=[anywhere, anywhere, inside, inside, inside, inside],
        out_specs=[inside] * 4,
        scratch_shapes=[
            pltpu.VMEM((ranks, tok, D), bfloat),
            pltpu.VMEM((ranks, tok, D), bfloat),
            pltpu.VMEM((4, tok, D), bfloat),
            pltpu.VMEM((4, tok, D), bfloat),
            pltpu.VMEM((3, 2, tok, D // 2), bfloat),
            pltpu.VMEM((6, tok, D // 2), bfloat),
            pltpu.SemaphoreType.DMA((10,)),
            pltpu.SemaphoreType.DMA((10,)),
            pltpu.SemaphoreType.DMA((8,)),
            pltpu.SemaphoreType.DMA((8,)),
        ],
        compiler_params=pltpu.CompilerParams(collective_id=cid, has_side_effects=True, vmem_limit_bytes=62 << 20),
        cost_estimate=pl.CostEstimate(flops=1 << 30, bytes_accessed=160 << 20, transcendentals=0),
        name="last_units",
    )(rows, bg, pg, w1, w, bias)


def attended_grads(x, w, tokens, cid):
    two, bg, hid, pg = tokens
    ranks, tok, D = two.shape
    F = hid.shape[2]
    units_at = (4, 2, F // 4, D)[2]
    per = 256 // units_at

    def beside(ins, outs, more):
        *inside, load = more
        loads = [pltpu.make_async_copy(ref, buf, load.at[n]) for n, (ref, buf) in enumerate(zip(ins[2:], inside))]
        for copy in loads:
            copy.start()

        def work():
            for copy in loads:
                copy.wait()
            two_in, bg_in, hid_in, pg_in = inside

            def step(i, _):
                here = pl.ds(pl.multiple_of(i * 256, 256), 256)
                for j, (left, right) in enumerate(((pg_in, two_in), (hid_in, bg_in))):
                    value = dot_tn(left[:, :, here].reshape(ranks * tok, 256), right[...].reshape(ranks * tok, D))
                    outs[1][pl.ds(i * per, per), j] = value.astype(bfloat).reshape(per, units_at, D)
                return 0

            lax.fori_loop(0, F // 256, step, 0)

        return work

    return gather_dot(
        x, w, jnp.zeros((1, w.shape[0]), single), bfloat, True, cid, "attended_grad",
        extra_out=[jax.ShapeDtypeStruct((4, 2, F // 4, D), bfloat)], beside=beside, far=tokens,
        more=[pltpu.VMEM(t.shape, bfloat) for t in tokens] + [pltpu.SemaphoreType.DMA((4,))],
    )


def everyone(width):
    b, z, x = lax.axis_index("b"), lax.axis_index("z"), lax.axis_index("x")
    rank, me = b * 2 + x, (b * 4 + z) * 2 + x

    def in_plane(i):
        other = lax.rem(rank + i, 8)
        return other, (other // 2, z, lax.rem(other, 2))

    def anywhere(i):
        other = lax.rem(me + i, width)
        return other, (other // 8, lax.rem(other // 2, 4), lax.rem(other, 2))

    return rank, me, in_plane, anywhere


def exchange(blocks, landed, rows, gathered, same_row, sems):
    plane_send, plane_recv, all_send, all_recv = sems
    width = gathered.shape[0]
    rank, me, in_plane, anywhere = everyone(width)
    barrier = pltpu.get_barrier_semaphore()

    def each(count, body):
        def step(i, _):
            body(i)
            return 0

        lax.fori_loop(1, count, step, 0)

    each(width, lambda i: pl.semaphore_signal(barrier, inc=1, device_id=anywhere(i)[1], device_id_type=MESH))
    pl.semaphore_wait(barrier, width - 1)

    def block(i):
        other, device = in_plane(i)
        return pltpu.make_async_remote_copy(
            src_ref=blocks.at[other], dst_ref=landed.at[rank], send_sem=plane_send.at[i], recv_sem=plane_recv.at[i],
            device_id=device, device_id_type=MESH,
        )

    def row(i):
        other, device = anywhere(i)
        return pltpu.make_async_remote_copy(
            src_ref=rows.at[0] if same_row else rows.at[other], dst_ref=gathered.at[me],
            send_sem=all_send.at[i], recv_sem=all_recv.at[i], device_id=device, device_id_type=MESH,
        )

    each(8, lambda i: block(i).start())
    each(width, lambda i: row(i).start())
    landed[rank] = blocks[rank]
    gathered[me] = rows[0] if same_row else rows[me]
    each(width, lambda i: row(i).wait())
    each(8, lambda i: block(i).wait())


def head_at(rank, i):
    return (rank // 2 * 4 + i) * 2 + rank % 2


def spread_kernel(q_ref, k_ref, v_ref, pack_ref, q_out, kv_out, pack_out, blocks, landed, gathered, *sems):
    cols = q_out.shape[2]
    for rank in range(8):
        for part, ref in enumerate((q_ref, k_ref, v_ref)):
            heads = [ref[:, head_at(rank, i) * HEAD_DIM : (head_at(rank, i) + 1) * HEAD_DIM] for i in range(4)]
            blocks[rank, :, part * cols : (part + 1) * cols] = jnp.concatenate(heads, axis=1)
    exchange(blocks, landed, pack_ref, gathered, True, sems)
    q_out[...] = landed[:, :, :cols]
    kv_out[...] = landed[:, :, cols:]
    pack_out[...] = gathered[...]


def settle_kernel(w_ref, rows_ref, q_out, k_out, v_out, sums_ref, landed, gathered, *sems):
    cols = w_ref.shape[2] // 3
    exchange(w_ref, landed, rows_ref, gathered, False, sems)
    for part, out in enumerate((q_out, k_out, v_out)):
        for pair in range(out.shape[1] // 128):
            sides = []
            for head in (2 * pair, 2 * pair + 1):
                rank, i = head // 8 * 2 + head % 2, head // 2 % 4
                at = part * cols + i * HEAD_DIM
                sides.append(landed[rank, :, at : at + HEAD_DIM])
            out[:, pair * 128 : (pair + 1) * 128] = jnp.concatenate(sides, axis=1).astype(single)
    sums_ref[...] = jnp.sum(gathered[...], axis=0)


def exchange_call(kernel, out_shape, args, blocks, landed, gathered, cid, name):
    inside = pl.BlockSpec(memory_space=pltpu.VMEM)
    width = gathered[0]
    return pl.pallas_call(
        kernel,
        out_shape=out_shape,
        in_specs=[inside] * len(args),
        out_specs=[inside] * len(out_shape),
        scratch_shapes=blocks
        + [
            pltpu.VMEM(landed, bfloat),
            pltpu.VMEM(gathered, single),
            pltpu.SemaphoreType.DMA((8,)),
            pltpu.SemaphoreType.DMA((8,)),
            pltpu.SemaphoreType.DMA((width,)),
            pltpu.SemaphoreType.DMA((width,)),
        ],
        compiler_params=pltpu.CompilerParams(collective_id=cid, has_side_effects=True, vmem_limit_bytes=32 << 20),
        cost_estimate=pl.CostEstimate(flops=1 << 20, bytes_accessed=32 << 20, transcendentals=0),
        name=name,
    )(*args)


def spread(q, k, v, pack, devices, cid):
    rows, D = q.shape
    cols = D // 8
    return exchange_call(
        spread_kernel,
        [
            jax.ShapeDtypeStruct((8, rows, cols), bfloat),
            jax.ShapeDtypeStruct((8, rows, 2 * cols), bfloat),
            jax.ShapeDtypeStruct((devices, 1, pack.shape[0]), single),
        ],
        (q, k, v, pack[None, None]),
        [pltpu.VMEM((8, rows, 3 * cols), bfloat)],
        (8, rows, 3 * cols),
        (devices, 1, pack.shape[0]),
        cid,
        "spread",
    )


def settle(weights, rows, cid):
    _, tall, wide = weights.shape
    D = wide // 3 * 8
    return exchange_call(
        settle_kernel,
        [jax.ShapeDtypeStruct((tall, D), single)] * 3 + [jax.ShapeDtypeStruct((1, rows.shape[1]), single)],
        (weights, rows[:, None]),
        [],
        weights.shape,
        (rows.shape[0], 1, rows.shape[1]),
        cid,
        "settle",
    )


def windows(span):
    block = span // 2
    return [(i * block, i * block + block + span) for i in range(2)]

def key_window(before, own, lo, hi, span):
    return jnp.concatenate([before[lo:span], own[0 : hi - span]], axis=0)

def hidden_bias(start_ref, i, block, lo, hi, span):
    rows = span + i * block + lax.broadcasted_iota(jnp.int32, (block, hi - lo), 0)
    keys = lo + lax.broadcasted_iota(jnp.int32, (block, hi - lo), 1)
    start = start_ref[i * block : (i + 1) * block, :]
    return jnp.where((keys >= start) & (keys <= rows), 0.0, -1e30).astype(single)

def attend_kernel(start_ref, q_ref, k_ref, v_ref, kb_ref, vb_ref, out_ref):
    span, cols = q_ref.shape
    block = span // 2
    lane = lax.broadcasted_iota(jnp.int32, (block, cols), 1) // HEAD_DIM
    for i, (lo, hi) in enumerate(windows(span)):
        rows = pl.ds(i * block, block)
        bias = hidden_bias(start_ref, i, block, lo, hi, span)
        keys = key_window(kb_ref, k_ref, lo, hi, span)
        vals = key_window(vb_ref, v_ref, lo, hi, span)
        query = q_ref[rows, :] * jnp.asarray(HEAD_DIM ** (-0.5), bfloat)
        def head(h, total):
            mine = lane == h
            scores = dot_nt(jnp.where(mine, query, 0), keys) + bias
            weights = jnp.exp(scores - jnp.max(scores, axis=1, keepdims=True))
            part = jnp.dot(weights.astype(bfloat), vals, preferred_element_type=single)
            part = part * (1.0 / jnp.sum(weights, axis=1, keepdims=True))
            return jnp.where(mine, part, total)
        total = lax.fori_loop(0, cols // HEAD_DIM, head, jnp.zeros((block, cols), single), unroll=True)
        out_ref[rows, :] = total.astype(bfloat)

def attend_back_kernel(start_ref, q_ref, k_ref, v_ref, kb_ref, vb_ref, do_ref, dq_ref, edge_ref, pair_ref, dk, dv):
    span, cols = q_ref.shape
    block = span // 2
    scale = HEAD_DIM ** (-0.5)
    dk[...] = jnp.zeros_like(dk)
    dv[...] = jnp.zeros_like(dv)
    lane = lax.broadcasted_iota(jnp.int32, (block, cols), 1) // HEAD_DIM
    for i, (lo, hi) in enumerate(windows(span)):
        rows = pl.ds(i * block, block)
        bias = hidden_bias(start_ref, i, block, lo, hi, span)
        keys = key_window(kb_ref, k_ref, lo, hi, span)
        vals = key_window(vb_ref, v_ref, lo, hi, span)
        query = q_ref[rows, :] * jnp.asarray(scale, bfloat)
        grad = do_ref[rows, :]
        def head(h, total):
            mine = lane == h
            query_h = jnp.where(mine, query, 0)
            grad_h = jnp.where(mine, grad, 0)
            scores = dot_nt(query_h, keys) + bias
            weights = jnp.exp(scores - jnp.max(scores, axis=1, keepdims=True))
            probs = weights * (1.0 / jnp.sum(weights, axis=1, keepdims=True))
            prob_grad = dot_nt(grad_h, vals)
            row_dot = jnp.sum(probs * prob_grad, axis=1, keepdims=True)
            score_grad = (probs * (prob_grad - row_dot)).astype(bfloat)
            dv[lo:hi, :] += dot_tn(probs.astype(bfloat), grad_h)
            dk[lo:hi, :] += dot_tn(score_grad, query_h)
            part = jnp.dot(score_grad, keys, preferred_element_type=single)
            return jnp.where(mine, part, total)
        total = lax.fori_loop(0, cols // HEAD_DIM, head, jnp.zeros((block, cols), single), unroll=True)
        dq_ref[rows, :] = (total * scale).astype(bfloat)
    edge_ref[:, :cols] = dk[:span, :].astype(bfloat)
    edge_ref[:, cols:] = dv[:span, :].astype(bfloat)
    pair_ref[:, :cols] = dk[span:, :]
    pair_ref[:, cols:] = dv[span:, :]

def attention_specs(span, cols):
    def at(j):
        return pl.BlockSpec((span, cols), lambda g: (g, j))
    return [pl.BlockSpec((span, 1), lambda g: (g, 0)), at(0), at(0), at(1), at(0), at(1)]

def attend(starts, query, key_value, before, groups):
    span, cols = query.shape[0] // groups, query.shape[1]
    return pl.pallas_call(
        attend_kernel,
        grid=(groups,),
        out_shape=jax.ShapeDtypeStruct((groups * span, cols), bfloat),
        in_specs=attention_specs(span, cols),
        out_specs=pl.BlockSpec((span, cols), lambda g: (g, 0)),
        compiler_params=pltpu.CompilerParams(vmem_limit_bytes=60 << 20),
        name="attend",
    )(starts, query, key_value, key_value, before, before)

def attend_back(starts, query, key_value, before, grad, groups):
    span, cols = query.shape[0] // groups, query.shape[1]
    rows = groups * span
    return pl.pallas_call(
        attend_back_kernel,
        grid=(groups,),
        out_shape=[jax.ShapeDtypeStruct((rows, cols), bfloat), jax.ShapeDtypeStruct((rows, 2 * cols), bfloat), jax.ShapeDtypeStruct((rows, 2 * cols), single)],
        in_specs=attention_specs(span, cols) + [pl.BlockSpec((span, cols), lambda g: (g, 0))],
        out_specs=[pl.BlockSpec((span, cols), lambda g: (g, 0))] + [pl.BlockSpec((span, 2 * cols), lambda g: (g, 0))] * 2,
        scratch_shapes=[pltpu.VMEM((2 * span, cols), single)] * 2,
        compiler_params=pltpu.CompilerParams(vmem_limit_bytes=60 << 20),
        name="attend_back",
    )(starts, query, key_value, key_value, before, before, grad)


def attention_heads(starts, query, key_value, before, groups):
    span, cols = query.shape[0] // groups, query.shape[1]
    both = jnp.concatenate([before.reshape(groups, span, -1), key_value.reshape(groups, span, -1)], axis=1)
    key_two, value_two = [both[..., i * cols : (i + 1) * cols].reshape(groups, 2 * span, -1, HEAD_DIM) for i in (0, 1)]
    query = query.reshape(groups, span, -1, HEAD_DIM)
    keys = jnp.arange(2 * span)[None, None, :]
    rows = span + jnp.arange(span)[None, :, None]
    allowed = (keys >= starts.reshape(groups, span, 1)) & (keys <= rows)
    scores = jnp.einsum("gqhd,gkhd->ghqk", query, key_two, preferred_element_type=single) * HEAD_DIM ** (-0.5)
    scores = jnp.where(allowed[:, None], scores, -1e30)
    weights = jnp.exp(scores - jnp.max(scores, axis=-1, keepdims=True))
    return query, key_two, value_two, weights / jnp.sum(weights, axis=-1, keepdims=True)


def attention_forward(starts, query, key_value, before, groups):
    if query.shape[1] % 128 == 0:
        return attend(starts, query, key_value, before, groups)
    _, _, value_two, probs = attention_heads(starts, query, key_value, before, groups)
    context = jnp.einsum("ghqk,gkhd->gqhd", probs.astype(bfloat), value_two, preferred_element_type=single)
    return context.astype(bfloat).reshape(query.shape)


def attention_backward(starts, query, key_value, before, grad, groups):
    if query.shape[1] % 128 == 0:
        return attend_back(starts, query, key_value, before, grad, groups)
    rows = query.shape[0]
    query, key_two, value_two, probs = attention_heads(starts, query, key_value, before, groups)
    span = query.shape[1]
    grad = grad.reshape(query.shape)
    prob_grad = jnp.einsum("gqhd,gkhd->ghqk", grad, value_two, preferred_element_type=single)
    row_dot = jnp.sum(probs * prob_grad, axis=-1, keepdims=True)
    score_grad = (probs * (prob_grad - row_dot)).astype(bfloat)
    query_grad = jnp.einsum("ghqk,gkhd->gqhd", score_grad, key_two, preferred_element_type=single) * HEAD_DIM ** (-0.5)
    key_grad = jnp.einsum("ghqk,gqhd->gkhd", score_grad, query, preferred_element_type=single) * HEAD_DIM ** (-0.5)
    value_grad = jnp.einsum("ghqk,gqhd->gkhd", probs.astype(bfloat), grad, preferred_element_type=single)
    pair = jnp.concatenate([t.reshape(groups, 2 * span, -1) for t in (key_grad, value_grad)], axis=2)
    edge, pair = [t.reshape(rows, -1) for t in (pair[:, :span].astype(bfloat), pair[:, span:])]
    return query_grad.astype(bfloat).reshape(rows, -1), edge, pair


def norm_backward(values, out_grad, gain_vec):
    center = jnp.mean(values, axis=-1, keepdims=True)
    centered = values - center
    rs = lax.rsqrt(jnp.mean(centered * centered, axis=-1, keepdims=True) + 1e-05)
    xhat = centered * rs
    g = out_grad * gain_vec
    part = rs * (g - jnp.mean(g, axis=-1, keepdims=True) - xhat * jnp.mean(g * xhat, axis=-1, keepdims=True))
    return part, jnp.sum(out_grad * xhat, axis=0), jnp.sum(out_grad, axis=0)


def on_device(
    inputs,
    exit_layers,
    lengths,
    layer_index,
    out_grad,
    ln1_gain,
    ln1_bias,
    q_weight,
    q_bias,
    k_weight,
    v_weight,
    v_bias,
    o_weight,
    o_bias,
    ln2_gain,
    ln2_bias,
    fc1_weight,
    fc1_bias,
    fc2_weight,
    fc2_bias,
):
    B, Z, X = lax.axis_size("b"), lax.axis_size("z"), lax.axis_size("x")
    R = B * X
    local = inputs[0].astype(single)
    tok, D = local.shape
    span = X * tok
    group_tok = Z * span
    at_z, at_x = lax.axis_index("z"), lax.axis_index("x")
    rank = lax.axis_index("b") * X + at_x
    rows_dev = q_weight.shape[0]
    cols = D // R
    heads = cols // HEAD_DIM
    whole_heads = rows_dev % HEAD_DIM == 0
    fast = (B, Z, X, rows_dev) == (4, 4, 2, HEAD_DIM)

    group_active = (exit_layers[0] > layer_index[0]).astype(single)
    active_total = jnp.sum(group_active)
    active = lax.dynamic_slice_in_dim(group_active, at_z * span + at_x * tok, tok, 0)[:, None]

    count = lengths.shape[1]
    upto = jnp.arange(count)[:, None] <= jnp.arange(count)[None, :]
    def to_ranks(matrix):
        lead = matrix.shape[:-1]
        if whole_heads:
            matrix = matrix.reshape(*lead, B, Z, X, rows_dev)
            k = len(lead)
            return matrix.transpose(k, k + 2, *range(k), k + 1, k + 3).reshape(R, *lead, cols)
        return jnp.moveaxis(matrix.reshape(*lead, R, cols), -2, 0)

    def from_ranks(parts):
        if whole_heads:
            parts = parts.reshape(B, X, -1, Z, rows_dev)
            return parts.transpose(2, 0, 3, 1, 4).reshape(-1, D)
        return parts.transpose(1, 0, 2).reshape(-1, D)

    def mine(vector):
        return lax.dynamic_index_in_dim(to_ranks(vector), rank, 0, keepdims=False)

    if whole_heads:
        weight_o = lax.all_gather(o_weight, "z", axis=0, tiled=True)
    else:
        weight_o = lax.dynamic_slice_in_dim(lax.all_gather(o_weight, ALL, axis=0, tiled=True), rank * cols, cols, 0)
    small = [ln1_gain, ln1_bias, q_bias, v_bias, o_bias, ln2_gain, ln2_bias, fc2_bias]
    pack = jnp.concatenate([v.astype(single) for v in (*small, fc1_bias, lengths[0])])
    pack = jnp.concatenate([pack, jnp.zeros((-pack.shape[0] % 128,), single)])
    if fast:
        query_mine, pair_mine, pack = spread(q_weight, k_weight, v_weight, pack, R * Z, 8)
        query_mine, pair_mine, pack = query_mine.reshape(-1, cols), pair_mine.reshape(-1, 2 * cols), pack[:, 0]
    else:
        qkv_parts = jnp.concatenate([to_ranks(q_weight), to_ranks(k_weight), to_ranks(v_weight)], axis=2)
        qkv_mine = lax.all_to_all(qkv_parts, PLANE, split_axis=0, concat_axis=0, tiled=True).reshape(D // Z, 3 * cols)
        query_mine, pair_mine = qkv_mine[:, :cols], qkv_mine[:, cols:]
        pack = jnp.broadcast_to(pack, (R * Z, pack.shape[0]))
        pack = lax.all_to_all(pack, ALL, split_axis=0, concat_axis=0, tiled=True)
    vectors = [pack[:, i * rows_dev : (i + 1) * rows_dev].reshape(-1) for i in range(len(small))]
    gain_one, bias_one, bias_q, bias_v, bias_o, gain_two, bias_two, bias_down = vectors
    pack = pack.reshape(B, Z, X, -1)[..., len(small) * rows_dev :]
    up_dev = fc1_bias.shape[0]
    bias_up = lax.dynamic_index_in_dim(
        pack[..., :up_dev].transpose(0, 2, 1, 3).reshape(R, Z * up_dev), rank, 0, keepdims=False
    )
    group_lengths = pack[:, 0, 0, up_dev : up_dev + count].astype(jnp.int32)
    ends = jnp.sum(jnp.where(upto, group_lengths[:, :, None], 0), axis=1)
    places = at_z * span + jnp.arange(span, dtype=jnp.int32)
    starts = jnp.max(jnp.where(ends[:, None, :] <= places[None, :, None], ends[:, None, :], 0), axis=2)
    starts = starts - (at_z - 1) * span

    def feature_rows(mine):
        full = lax.all_gather(mine, "z", axis=0, tiled=True)
        return full.reshape(Z, B, X, rows_dev, -1).transpose(1, 0, 2, 3, 4).reshape(D, -1)

    weight_kv = feature_rows(pair_mine)
    bias_kv = jnp.concatenate([jnp.zeros((cols,), single), mine(bias_v)])
    bias_one, query_mine, weight_o = lax.optimization_barrier((bias_one, query_mine, weight_o))
    normed_low = layer_norm(local, gain_one, bias_one).astype(bfloat)

    def gather_plane(rows, cid, name):
        if fast:
            return plane_gather(rows, (), [], None, cid, name)[0]
        return lax.all_gather(rows, PLANE, axis=0, tiled=True)

    def reduce_plane(left, weight, turned, cid, name):
        if fast:
            return dot_reduce([left], [weight], turned, cid, name)
        terms = (dot_nt if turned else dot)(left, weight).astype(bfloat)
        return lax.psum_scatter(terms, PLANE, scatter_dimension=0, tiled=True).astype(single)

    normed_all = gather_plane(normed_low, 0, "gather_normed")
    units = fc1_bias.shape[0] // 2
    halves = [jnp.concatenate([fc1_weight.T[i : i + units], fc2_weight[i : i + units]]) for i in (0, units)]

    def gather_units(mine):
        return lax.all_gather(mine, "z", axis=0, tiled=True).reshape(Z, 2, units, D)

    normed_all, weight_kv, unit_one = lax.optimization_barrier((normed_all, weight_kv, halves[0]))
    weight_q = feature_rows(query_mine)
    unit_one = gather_units(unit_one)
    key_value = (dot(normed_all, weight_kv) + bias_kv).astype(bfloat)
    up = [(i, i + 1) for i in range(Z - 1)]
    down = [(i + 1, i) for i in range(Z - 1)]
    cotangent = out_grad[0].astype(single) * (group_tok / active_total)
    branch_grad = (active * cotangent).astype(bfloat)
    down_b_grad = column_sums(branch_grad)
    key_value, branch_grad = lax.optimization_barrier((key_value, branch_grad))
    before = lax.ppermute(key_value, "z", up)
    branch_all = gather_plane(branch_grad, 7, "gather_branch")
    branch_all, late_normed = lax.optimization_barrier((branch_all, normed_all))
    query = (dot(late_normed, weight_q) + mine(bias_q)).astype(bfloat)
    before, query = lax.optimization_barrier((before, query))
    starts = starts.reshape(B * span, 1)
    context = attention_forward(starts, query, key_value, before, B)
    context, unit_two = lax.optimization_barrier((context, halves[1]))
    unit_two = gather_units(unit_two)

    attended = reduce_plane(context, weight_o, False, 1, "attended") + bias_o
    middle = local + active * attended
    normed_two = layer_norm(middle, gain_two, bias_two).astype(bfloat)
    bias_up = bias_up.reshape(Z, 2, units)
    bias_up = [bias_up[:, i].reshape(1, Z * units) for i in range(2)]

    def sum_halves(left, right, turned, cid, name):
        if fast:
            return dot_reduce(left, right, turned, cid, name)
        terms = sum((dot_nt if turned else dot)(a, w) for a, w in zip(left, right)).astype(bfloat)
        return lax.psum_scatter(terms, PLANE, scatter_dimension=0, tiled=True).astype(single)

    def sum_z(grads):
        return lax.psum_scatter(grads.reshape(Z * 2 * units, D), "z", scatter_dimension=0, tiled=True)

    if fast:
        branch_rows = branch_all.reshape(R, tok, D)
        two_all, hidden_one, pre_one, bias_one_up, grads = first_units(normed_two, branch_rows, unit_one, bias_up[0], 2)
        shard_one = sum_z(grads)
        hidden_two, pre_two, bias_two_up, normed_two_grad = last_units(
            two_all, branch_rows, pre_one, unit_one, unit_two, bias_up[1], 3
        )
        up_b_halves = [bias_one_up[0], bias_two_up[0]]
    else:
        two_all = gather_plane(normed_two, 2, "gather_two")

        def half_units(weights, bias):
            weight_up, weight_down = [weights[:, i].reshape(Z * units, D) for i in (0, 1)]
            hidden, gelu_pull = jax.vjp(partial(jax.nn.gelu, approximate=True), dot_nt(two_all, weight_up) + bias)
            hidden = hidden.astype(bfloat)
            pre_grad = gelu_pull(dot_nt(branch_all, weight_down))[0].astype(bfloat)
            grads = dot_tn(pre_grad, two_all), dot_tn(hidden, branch_all)
            grads = jnp.stack([g.astype(bfloat).reshape(Z, units, D) for g in grads], axis=1)
            return hidden, pre_grad, sum_z(grads), weight_up, weight_down

        hidden_one, pre_one, shard_one, up_one, down_one = half_units(unit_one, bias_up[0])
        hidden_two, pre_two, shard_two, up_two, down_two = half_units(unit_two, bias_up[1])
        up_b_halves = [column_sums(pre_one), column_sums(pre_two)]
        normed_two_grad = sum_halves([pre_one, pre_two], [up_one, up_two], False, 3, "up_grad")
    up_b_grad = jnp.stack([half.reshape(Z, units) for half in up_b_halves], axis=1).reshape(-1)

    middle_part, gain_two_grad, bias_two_grad = norm_backward(middle, normed_two_grad, gain_two)
    middle_grad = cotangent + middle_part
    attended_grad = (active * middle_grad).astype(bfloat)
    out_b_grad = column_sums(attended_grad)
    if fast:
        attended_all, context_grad, grads = attended_grads(
            attended_grad, weight_o, (two_all, branch_rows, hidden_two, pre_two), 5
        )
        shard_two = sum_z(grads)
    else:
        attended_all = gather_plane(attended_grad, 5, "attended_grad")
        context_grad = dot_nt(attended_all, weight_o).astype(bfloat)
    context_grad, shard_one = lax.optimization_barrier((context_grad, shard_one))
    out_w_grad = dot_tn(context, attended_all)
    query_grad, edge, pair = attention_backward(starts, query, key_value, before, context_grad, B)
    hidden_one, edge, pair, query_grad = lax.optimization_barrier((hidden_one, edge, pair, query_grad))
    after = lax.ppermute(edge, "z", down)
    query_w_grad = dot_tn(normed_all, query_grad).astype(bfloat)
    hidden_one, query_w_grad, out_w_grad = lax.optimization_barrier((hidden_one, query_w_grad, out_w_grad))
    downs = [unit_one, unit_two] if fast else [down_one, down_two]
    branch = sum_halves([hidden_one, hidden_two], downs, False, 4, "down")
    up_w_shard = jnp.concatenate([shard_one[:units], shard_two[:units]]).T.astype(single)
    down_w_shard = jnp.concatenate([shard_one[units:], shard_two[units:]]).astype(single)
    query_b_grad = column_sums(query_grad)
    branch, after, up_w_shard, down_w_shard, query_b_grad, query_w_grad = lax.optimization_barrier(
        (branch, after, up_w_shard, down_w_shard, query_b_grad, query_w_grad)
    )
    outputs = middle + active * (branch + bias_down)
    pair_grad = (pair + after.astype(single)).astype(bfloat)
    pair_w_grad = dot_tn(normed_all, pair_grad).astype(bfloat)
    pair_grad, pair_w_grad = lax.optimization_barrier((pair_grad, pair_w_grad))
    normed_grad = sum_halves([query_grad, pair_grad], [weight_q, weight_kv], True, 6, "qkv_grad")
    value_b_grad = column_sums(pair_grad[:, cols:])
    input_part, gain_one_grad, bias_one_grad = norm_backward(local, normed_grad, gain_one)
    input_grad = middle_grad + input_part

    def sum_to_owners(vectors, axes, parts):
        split = jnp.concatenate([v.reshape(parts, -1) for v in vectors], axis=1)
        summed = jnp.sum(lax.all_to_all(split, axes, split_axis=0, concat_axis=0, tiled=True), axis=0)
        widths = [v.shape[0] // parts for v in vectors]
        return [summed[sum(widths[:i]) : sum(widths[: i + 1])] for i in range(len(widths))]

    qkv_w_grad = jnp.concatenate([query_w_grad, pair_w_grad], axis=1)
    qkv_w_grad = qkv_w_grad.reshape(B, Z, X, rows_dev, 3 * cols).transpose(1, 0, 2, 3, 4).reshape(D, 3 * cols)
    qkv_w_grad = lax.psum_scatter(qkv_w_grad, "z", scatter_dimension=0, tiled=True).reshape(R, rows_dev, 3 * cols)
    qkv_w_grad, out_w_grad = lax.optimization_barrier((qkv_w_grad, out_w_grad))
    device_sums = [gain_one_grad, bias_one_grad, out_b_grad, gain_two_grad, bias_two_grad, down_b_grad]
    if fast:
        rank_sums = jnp.concatenate([v.reshape(Z, -1) for v in (query_b_grad, value_b_grad, up_b_grad)], axis=1)
        here = (jnp.arange(R) == rank).reshape(B, 1, X, 1)
        rank_sums = jnp.where(here, rank_sums[None, :, None, :], 0.0).reshape(R * Z, -1)
        rows = jnp.concatenate([v.reshape(R * Z, -1) for v in device_sums] + [rank_sums], axis=1)
        q_w_shard, k_w_shard, v_w_shard, summed = settle(qkv_w_grad, rows, 9)
        sums = [summed[0, i * rows_dev : (i + 1) * rows_dev] for i in range(len(device_sums) + 2)]
        q_b_shard, v_b_shard = sums[len(device_sums) :]
        up_b_shard = summed[0, (len(device_sums) + 2) * rows_dev :]
    else:
        qkv_w_grad = lax.all_to_all(qkv_w_grad, PLANE, split_axis=0, concat_axis=0, tiled=True)
        q_w_shard, k_w_shard, v_w_shard = [
            from_ranks(qkv_w_grad[..., i : i + cols]).astype(single) for i in range(0, 3 * cols, cols)
        ]
        sums = sum_to_owners(device_sums, ALL, R * Z)
        [up_b_shard] = sum_to_owners([up_b_grad], "z", Z)
    if whole_heads:
        out_w_shard = lax.psum_scatter(out_w_grad.astype(bfloat), "z", scatter_dimension=0, tiled=True).astype(single)
        if not fast:
            q_b_shard, v_b_shard = sum_to_owners([query_b_grad, value_b_grad], "z", Z)
    else:

        def placed(rows):
            full = jnp.zeros((D,) + rows.shape[1:], rows.dtype)
            full = lax.dynamic_update_slice_in_dim(full, rows, rank * cols, 0)
            return lax.psum_scatter(full, ALL, scatter_dimension=0, tiled=True).astype(single)

        out_w_shard = placed(out_w_grad.astype(bfloat))
        q_b_shard = placed(query_b_grad)
        v_b_shard = placed(value_b_grad)
    return (
        outputs.astype(bfloat)[None],
        input_grad.astype(bfloat)[None],
        sums[0],
        sums[1],
        q_w_shard,
        q_b_shard,
        k_w_shard,
        v_w_shard,
        v_b_shard,
        out_w_shard,
        sums[2],
        sums[3],
        sums[4],
        up_w_shard,
        up_b_shard,
        down_w_shard,
        sums[5],
    )


def solution(mesh):
    groups, parts = mesh.shape["batch"], mesh.shape["seq"]
    inner = Mesh(mesh.devices.reshape(groups, SPANS, parts // SPANS), ("b", "z", "x"))
    token = P("b", ("z", "x"), None)
    vector = P(ALL)
    rows = P(ALL, None)
    columns = P(None, ALL)
    return jax.shard_map(
        on_device,
        mesh=inner,
        in_specs=(
            token,
            P("b", None),
            P("b", None),
            P(),
            token,
            vector,
            vector,
            rows,
            vector,
            rows,
            rows,
            vector,
            rows,
            vector,
            vector,
            vector,
            columns,
            vector,
            rows,
            vector,
        ),
        out_specs=(
            token,
            token,
            vector,
            vector,
            rows,
            vector,
            rows,
            rows,
            vector,
            rows,
            vector,
            vector,
            vector,
            columns,
            vector,
            rows,
            vector,
        ),
        check_vma=False,
    )
```

```python
import functools
from functools import partial

import jax
import jax.numpy as jnp
from jax import lax
from jax.experimental import pallas as pl
from jax.experimental.pallas import tpu as pltpu
from jax.sharding import Mesh
from jax.sharding import PartitionSpec as P

HEAD_DIM = 64
SPANS = 4

bfloat = jnp.bfloat16
single = jnp.float32

PLANE = ("b", "x")
ALL = ("b", "z", "x")
MESH = pl.DeviceIdType.MESH
TILE = 512

def plane_place():
    b, z, x = lax.axis_index("b"), lax.axis_index("z"), lax.axis_index("x")
    sib_b = b + 1 - 2 * lax.rem(b, 2)
    far_b = lax.rem(b + 2, 4)
    far_sib_b = lax.rem(sib_b + 2, 4)
    ids = {"s": (sib_b, z, x), "x": (b, z, 1 - x), "y": (far_b, z, x)}
    ranks = {
        "o": b * 2 + x,
        "s": sib_b * 2 + x,
        "x": b * 2 + 1 - x,
        "xs": sib_b * 2 + 1 - x,
        "y": far_b * 2 + x,
        "ys": far_sib_b * 2 + x,
        "d": far_b * 2 + 1 - x,
        "ds": far_sib_b * 2 + 1 - x,
    }
    return ids, ranks

def greet(ids):
    barrier = pltpu.get_barrier_semaphore()
    for device in ids.values():
        pl.semaphore_signal(barrier, inc=1, device_id=device, device_id_type=MESH)
    pl.semaphore_wait(barrier, len(ids))

def tiles(lo, hi, body):
    def step(i, _):
        body(pl.ds(pl.multiple_of(i * TILE, TILE), TILE))
        return 0
    lax.fori_loop(lo // TILE, hi // TILE, step, 0)

def gather_kernel(body_of, n_in, n_out, x_ref, *refs):
    ins = refs[:n_in]; all_ref = refs[n_in]; outs = refs[n_in + 1 : n_in + 1 + n_out]
    held, send, recv, keep = refs[n_in + 1 + n_out :]
    ids, at = plane_place()
    half = x_ref.shape[0] // 2
    parts = (pl.ds(0, half), pl.ds(half, half))
    greet(ids)
    count = [0]
    started = []
    def ship(src, dst, to):
        n = count[0]; count[0] += 1
        c = pltpu.make_async_remote_copy(src_ref=src, dst_ref=dst, send_sem=send.at[n], recv_sem=recv.at[n], device_id=ids[to], device_id_type=MESH)
        c.start(); started.append(c)
        return c
    own = at["o"]
    x0 = ship(x_ref.at[parts[0]], held.at[own, parts[0]], "x")
    y1 = ship(x_ref.at[parts[1]], held.at[own, parts[1]], "y")
    x1 = ship(x_ref.at[parts[1]], held.at[own, parts[1]], "x")
    y0 = ship(x_ref.at[parts[0]], held.at[own, parts[0]], "y")
    s0 = ship(x_ref, held.at[own], "s")
    kept = []
    def done(rank, src):
        c = pltpu.make_async_copy(src, all_ref.at[rank], keep.at[len(kept)])
        c.start(); kept.append(c)
        if body_of is not None:
            body_of(rank, src, ins, outs)
    done(own, x_ref)
    s0.wait_recv()
    done(at["s"], held.at[at["s"]])
    x0.wait_recv()
    ry = ship(held.at[at["x"], parts[0]], held.at[at["x"], parts[0]], "y")
    y1.wait_recv()
    rx = ship(held.at[at["y"], parts[1]], held.at[at["y"], parts[1]], "x")
    x1.wait_recv()
    sx = ship(held.at[at["x"]], held.at[at["x"]], "s")
    y0.wait_recv()
    sy = ship(held.at[at["y"]], held.at[at["y"]], "s")
    done(at["x"], held.at[at["x"]])
    done(at["y"], held.at[at["y"]])
    sx.wait_recv()
    done(at["xs"], held.at[at["xs"]])
    sy.wait_recv()
    done(at["ys"], held.at[at["ys"]])
    ry.wait_recv(); rx.wait_recv()
    sd = ship(held.at[at["d"]], held.at[at["d"]], "s")
    done(at["d"], held.at[at["d"]])
    sd.wait_recv()
    done(at["ds"], held.at[at["ds"]])
    for c in started: c.wait_send()
    for c in kept: c.wait()

def vmem(n): return [pl.BlockSpec(memory_space=pltpu.VMEM)] * n

def plane_gather(x, ins, out_types, body_of, cid, name, ranks=8):
    tok, D = x.shape
    res = pl.pallas_call(
        functools.partial(gather_kernel, body_of, len(ins), len(out_types)),
        out_shape=[jax.ShapeDtypeStruct((ranks, tok, D), x.dtype), *out_types],
        in_specs=vmem(1 + len(ins)),
        out_specs=[pl.BlockSpec(memory_space=pl.ANY)] + vmem(len(out_types)),
        scratch_shapes=[pltpu.VMEM((ranks, tok, D), x.dtype), pltpu.SemaphoreType.DMA((10,)), pltpu.SemaphoreType.DMA((10,)), pltpu.SemaphoreType.DMA((8,))],
        compiler_params=pltpu.CompilerParams(collective_id=cid, has_side_effects=True, vmem_limit_bytes=60 << 20),
        cost_estimate=pl.CostEstimate(flops=1 << 30, bytes_accessed=128 << 20, transcendentals=0),
        name=name,
    )(x, *ins)
    return res[0].reshape(ranks * tok, D), *res[1:]

def gather_dot(x, w, bias, out_dtype, turned, cid, name):
    ranks, tok, D = 8, *x.shape
    N = w.shape[0] if turned else w.shape[1]
    tile = min(N, 512) if N % 512 == 0 else 256
    def body(rank, src, ins, outs):
        w_ref, b_ref = ins
        def step(i, _):
            cols = pl.ds(pl.multiple_of(i * tile, tile), tile)
            if turned:
                y = lax.dot_general(src[...], w_ref[cols, :], (((1,), (1,)), ((), ())), preferred_element_type=single)
            else:
                y = jnp.dot(src[...], w_ref[:, cols], preferred_element_type=single)
            outs[0][rank, :, cols] = (y + b_ref[:, cols]).astype(out_dtype)
            return 0
        lax.fori_loop(0, N // tile, step, 0)
    all_, y = plane_gather(x, (w, bias), [jax.ShapeDtypeStruct((ranks, tok, N), out_dtype)], body, cid, name)
    return all_, y.reshape(ranks * tok, N)

def reduce_kernel(turned, pairs, *refs):
    left, right = refs[:pairs], refs[pairs : 2 * pairs]
    out_ref, sib_out, sib_in, stage, landed, send, recv = refs[2 * pairs :]
    ids, at = plane_place()
    D = out_ref.shape[1]
    mid = D // 2
    greet(ids)
    count = [0]; started = []
    def ship(src, dst, to):
        n = count[0]; count[0] += 1
        c = pltpu.make_async_remote_copy(src_ref=src, dst_ref=dst, send_sem=send.at[n], recv_sem=recv.at[n], device_id=ids[to], device_id_type=MESH)
        c.start(); started.append(c)
        return c
    def term(rank, cols):
        if turned:
            return sum(dot_nt(a[rank], w[cols, :]) for a, w in zip(left, right))
        rows = [w[:, 1, :, cols].reshape(-1, TILE) if len(w.shape) == 4 else w[:, cols] for w in right]
        return sum(dot(a[rank], w) for a, w in zip(left, rows))
    order = ("d", "x", "y", "o")
    twin = {"d": "ds", "x": "xs", "y": "ys", "o": "s"}
    sib = {}
    def to_sibling(j, h):
        def fill(cols):
            sib_out[j, h, :, local(h, cols)] = term(at[twin[order[j]]], cols).astype(bfloat)
        tiles(h * mid, (h + 1) * mid, fill)
        sib[j, h] = ship(sib_out.at[j, h], sib_in.at[j, h], "s")
    def local(h, cols):
        return pl.ds(pl.multiple_of(cols.start - h * mid, TILE), TILE)
    def pair(j, h, cols):
        return term(at[order[j]], cols) + sib_in[j, h, :, local(h, cols)].astype(single)
    def put(j, h, extra=None):
        sib[j, h].wait_recv()
        def fill(cols):
            value = pair(j, h, cols)
            if extra is not None:
                value = value + landed[extra, :, local(h, cols)].astype(single)
            stage[j, h, :, local(h, cols)] = value.astype(bfloat)
        tiles(h * mid, (h + 1) * mid, fill)
    to_sibling(0, 0)
    to_sibling(0, 1)
    put(0, 0)
    d_a = ship(stage.at[0, 0], landed.at[0], "x")
    put(0, 1)
    d_b = ship(stage.at[0, 1], landed.at[1], "y")
    to_sibling(1, 0)
    to_sibling(2, 1)
    put(1, 0)
    x_a = ship(stage.at[1, 0], landed.at[2], "x")
    put(2, 1)
    y_b = ship(stage.at[2, 1], landed.at[3], "y")
    for j, h in ((1, 1), (2, 0), (3, 0), (3, 1)):
        to_sibling(j, h)
    d_b.wait_recv()
    put(1, 1, extra=1)
    x_b = ship(stage.at[1, 1], landed.at[5], "x")
    d_a.wait_recv()
    put(2, 0, extra=0)
    y_a = ship(stage.at[2, 0], landed.at[4], "y")
    for h in range(2):
        sib[3, h].wait_recv()
        def first(cols, h=h):
            out_ref[:, cols] = pair(3, h, cols)
        tiles(h * mid, (h + 1) * mid, first)
    x_a.wait_recv(); y_b.wait_recv(); x_b.wait_recv(); y_a.wait_recv()
    for h, (n, m) in enumerate(((2, 4), (3, 5))):
        def add(cols, h=h, n=n, m=m):
            c = local(h, cols)
            out_ref[:, cols] = out_ref[:, cols] + landed[n, :, c].astype(single) + landed[m, :, c].astype(single)
        tiles(h * mid, (h + 1) * mid, add)
    for c in started: c.wait_send()

def dot_reduce(left, right, turned, cid, name):
    ranks = 8
    D = right[0].shape[0] if turned else right[0].shape[-1]
    tok = left[0].size // left[0].shape[-1] // ranks
    return pl.pallas_call(
        functools.partial(reduce_kernel, turned, len(left)),
        out_shape=jax.ShapeDtypeStruct((tok, D), single),
        in_specs=vmem(2 * len(left)), out_specs=vmem(1)[0],
        scratch_shapes=[pltpu.VMEM((4, 2, tok, D // 2), bfloat), pltpu.VMEM((4, 2, tok, D // 2), bfloat), pltpu.VMEM((3, 2, tok, D // 2), bfloat), pltpu.VMEM((6, tok, D // 2), bfloat),
            pltpu.SemaphoreType.DMA((14,)), pltpu.SemaphoreType.DMA((14,))],
        compiler_params=pltpu.CompilerParams(collective_id=cid, has_side_effects=True, vmem_limit_bytes=60 << 20),
        cost_estimate=pl.CostEstimate(flops=1 << 30, bytes_accessed=128 << 20, transcendentals=0),
        name=name,
    )(*[a.reshape(ranks, tok, -1) for a in left], *right)


def dot(left, right):
    return jnp.dot(left, right, preferred_element_type=single)


def dot_tn(left, right):
    return lax.dot_general(left, right, (((0,), (0,)), ((), ())), preferred_element_type=single)


def dot_nt(left, right):
    return lax.dot_general(left, right, (((1,), (1,)), ((), ())), preferred_element_type=single)


def layer_norm(values, gain_vec, shift_vec):
    center = jnp.mean(values, axis=-1, keepdims=True)
    centered = values - center
    spread = jnp.mean(centered * centered, axis=-1, keepdims=True)
    return centered * lax.rsqrt(spread + 1e-05) * gain_vec + shift_vec


def column_sums(matrix):
    return jnp.sum(matrix.astype(single), axis=0)


def shipper(send, recv, ids):
    started = []

    def ship(src, dst, to):
        n = len(started)
        copy = pltpu.make_async_remote_copy(
            src_ref=src, dst_ref=dst, send_sem=send.at[n], recv_sem=recv.at[n], device_id=ids[to], device_id_type=MESH
        )
        copy.start()
        started.append(copy)
        return copy

    return ship, started


TWIN = {"o": "s", "x": "xs", "y": "ys", "d": "ds"}


def unit_rows(w_ref, i):
    parts, _, units, D = w_ref.shape
    return w_ref[:, i].reshape(parts * units, D)


def hidden_units(src, branch, w_ref, b_ref, hid_ref, pg_ref, pb_ref, rank):
    pre = dot_nt(src[...], unit_rows(w_ref, 0)) + b_ref[...]
    square = pre * pre
    bend = jnp.tanh(0.7978845608028654 * (pre + 0.044715 * (pre * square)))
    rise = 0.5 * (1.0 + bend)
    hid_ref[rank] = (pre * rise).astype(bfloat)
    slope = rise + (0.5 * 0.7978845608028654) * pre * (1.0 - bend * bend) * (1.0 + 3 * 0.044715 * square)
    grad = (dot_nt(branch[...], unit_rows(w_ref, 1)) * slope).astype(bfloat)
    pg_ref[rank] = grad
    pb_ref[...] += jnp.sum(grad.astype(single), axis=0, keepdims=True)


def first_units_kernel(
    x_ref, bg_ref, w_ref, b_ref, all_ref, hid_ref, pg_ref, pb_ref, grad_ref,
    held, bg, total, send, recv, keep, load,
):
    ids, at = plane_place()
    tok = x_ref.shape[0]
    half = tok // 2
    parts = (pl.ds(0, half), pl.ds(half, half))
    own = at["o"]
    loads = {}
    for n, name in enumerate(at):
        loads[name] = pltpu.make_async_copy(bg_ref.at[at[name]], bg.at[at[name]], load.at[n])
        loads[name].start()
    greet(ids)
    ship, started = shipper(send, recv, ids)
    x0 = ship(x_ref.at[parts[0]], held.at[own, parts[0]], "x")
    y1 = ship(x_ref.at[parts[1]], held.at[own, parts[1]], "y")
    x1 = ship(x_ref.at[parts[1]], held.at[own, parts[1]], "x")
    y0 = ship(x_ref.at[parts[0]], held.at[own, parts[0]], "y")
    s0 = ship(x_ref, held.at[own], "s")
    pb_ref[...] = jnp.zeros_like(pb_ref)
    kept = []

    def units(name):
        rank = at[name]
        src = x_ref if name == "o" else held.at[rank]
        copy = pltpu.make_async_copy(src, all_ref.at[rank], keep.at[len(kept)])
        copy.start()
        kept.append(copy)
        loads[name].wait()
        hidden_units(src, bg.at[rank], w_ref, b_ref, hid_ref, pg_ref, pb_ref, rank)

    def weigh(name, last=False):
        units_at = grad_ref.shape[2]
        per = 256 // units_at

        def rows(i, _):
            here = pl.ds(pl.multiple_of(i * 256, 256), 256)
            owners = pl.ds(i * per, per)
            for j, left in enumerate((pg_ref, hid_ref)):
                term = 0
                for n in (name, TWIN[name]):
                    right = bg[at[n]] if j else (x_ref[...] if n == "o" else held[at[n]])
                    term = term + dot_tn(left[at[n], :, here], right)
                term = term.reshape(per, units_at, -1)
                if name == "o":
                    total[owners, j] = term
                elif last:
                    grad_ref[owners, j] = (total[owners, j] + term).astype(bfloat)
                else:
                    total[owners, j] += term
            return 0

        lax.fori_loop(0, hid_ref.shape[2] // 256, rows, 0)

    units("o")
    s0.wait_recv()
    units("s")
    x0.wait_recv()
    ry = ship(held.at[at["x"], parts[0]], held.at[at["x"], parts[0]], "y")
    y1.wait_recv()
    rx = ship(held.at[at["y"], parts[1]], held.at[at["y"], parts[1]], "x")
    weigh("o")
    x1.wait_recv()
    sx = ship(held.at[at["x"]], held.at[at["x"]], "s")
    y0.wait_recv()
    sy = ship(held.at[at["y"]], held.at[at["y"]], "s")
    units("x")
    sx.wait_recv()
    units("xs")
    units("y")
    sy.wait_recv()
    units("ys")
    weigh("x")
    ry.wait_recv()
    rx.wait_recv()
    sd = ship(held.at[at["d"]], held.at[at["d"]], "s")
    weigh("y")
    units("d")
    sd.wait_recv()
    units("ds")
    weigh("d", last=True)
    for copy in started:
        copy.wait_send()
    for copy in kept:
        copy.wait()


def last_units_kernel(
    all_ref, bg_ref, pg1_ref, w1_ref, w_ref, b_ref, hid_ref, pb_ref, r_ref, grad_ref,
    held, bg, pg_ref, sib_out, sib_in, stage, landed, send, recv, load, load_b,
):
    ids, at = plane_place()
    ranks, tok, D = held.shape
    mid = D // 2
    names = ("ds", "d", "xs", "x", "ys", "y", "s", "o")
    loads = {}
    for n, name in enumerate(names):
        loads[name] = [
            pltpu.make_async_copy(all_ref.at[at[name]], held.at[at[name]], load.at[n]),
            pltpu.make_async_copy(bg_ref.at[at[name]], bg.at[at[name]], load_b.at[n]),
        ]
        for copy in loads[name]:
            copy.start()
    greet(ids)
    ship, started = shipper(send, recv, ids)
    pb_ref[...] = jnp.zeros_like(pb_ref)

    def units(name):
        for copy in loads[name]:
            copy.wait()
        rank = at[name]
        hidden_units(held.at[rank], bg.at[rank], w_ref, b_ref, hid_ref, pg_ref, pb_ref, rank)

    def term(name, cols):
        rank = at[name]
        first, second = [w[:, 0, :, cols].reshape(-1, TILE) for w in (w1_ref, w_ref)]
        return dot(pg1_ref[rank], first) + dot(pg_ref[rank], second)

    order = ("d", "x", "y", "o")

    def to_sibling(j):
        def fill(cols):
            sib_out[j, :, cols] = term(TWIN[order[j]], cols).astype(bfloat)

        tiles(0, D, fill)
        return ship(sib_out.at[j], sib_in.at[j], "s")

    def pair(j, cols):
        return term(order[j], cols) + sib_in[j, :, cols].astype(single)

    def local(h, cols):
        return pl.ds(pl.multiple_of(cols.start - h * mid, TILE), TILE)

    def put(j, h, extra=None):
        def fill(cols):
            value = pair(j, cols)
            if extra is not None:
                value = value + landed[extra, :, local(h, cols)].astype(single)
            stage[j, h, :, local(h, cols)] = value.astype(bfloat)

        tiles(h * mid, (h + 1) * mid, fill)

    units("ds")
    d_sib = to_sibling(0)
    units("d")
    d_sib.wait_recv()
    put(0, 0)
    d_a = ship(stage.at[0, 0], landed.at[0], "x")
    put(0, 1)
    d_b = ship(stage.at[0, 1], landed.at[1], "y")
    units("xs")
    x_sib = to_sibling(1)
    units("x")
    x_sib.wait_recv()
    put(1, 0)
    x_a = ship(stage.at[1, 0], landed.at[2], "x")
    units("ys")
    y_sib = to_sibling(2)
    units("y")
    y_sib.wait_recv()
    put(2, 1)
    y_b = ship(stage.at[2, 1], landed.at[3], "y")
    d_b.wait_recv()
    put(1, 1, extra=1)
    x_b = ship(stage.at[1, 1], landed.at[5], "x")
    d_a.wait_recv()
    put(2, 0, extra=0)
    y_a = ship(stage.at[2, 0], landed.at[4], "y")
    units("s")
    own_sib = to_sibling(3)
    units("o")
    own_sib.wait_recv()

    def first(cols):
        r_ref[:, cols] = pair(3, cols)

    tiles(0, D, first)

    units_at = grad_ref.shape[2]
    per = 256 // units_at
    tokens = ranks * tok

    def grads(i, _):
        here = pl.ds(pl.multiple_of(i * 256, 256), 256)
        owners = pl.ds(i * per, per)
        for j, (left, right) in enumerate(((pg_ref, held), (hid_ref, bg))):
            value = dot_tn(left[:, :, here].reshape(tokens, 256), right[...].reshape(tokens, D))
            grad_ref[owners, j] = value.astype(bfloat).reshape(per, units_at, D)
        return 0

    lax.fori_loop(0, hid_ref.shape[2] // 256, grads, 0)
    for copy in (x_a, y_b, x_b, y_a):
        copy.wait_recv()
    for h, (n, m) in enumerate(((2, 4), (3, 5))):

        def add(cols, h=h, n=n, m=m):
            c = local(h, cols)
            r_ref[:, cols] = r_ref[:, cols] + landed[n, :, c].astype(single) + landed[m, :, c].astype(single)

        tiles(h * mid, (h + 1) * mid, add)
    for copy in started:
        copy.wait_send()


def first_units(x, bg, w, bias, cid):
    ranks = 8
    tok, D = x.shape
    F = bias.shape[1]
    anywhere = pl.BlockSpec(memory_space=pl.ANY)
    inside = pl.BlockSpec(memory_space=pltpu.VMEM)
    return pl.pallas_call(
        first_units_kernel,
        out_shape=[
            jax.ShapeDtypeStruct((ranks, tok, D), bfloat),
            jax.ShapeDtypeStruct((ranks, tok, F), bfloat),
            jax.ShapeDtypeStruct((ranks, tok, F), bfloat),
            jax.ShapeDtypeStruct((1, F), single),
            jax.ShapeDtypeStruct(w.shape, bfloat),
        ],
        in_specs=[inside, anywhere, inside, inside],
        out_specs=[anywhere, inside, inside, inside, inside],
        scratch_shapes=[
            pltpu.VMEM((ranks, tok, D), bfloat),
            pltpu.VMEM((ranks, tok, D), bfloat),
            pltpu.VMEM(w.shape, single),
            pltpu.SemaphoreType.DMA((10,)),
            pltpu.SemaphoreType.DMA((10,)),
            pltpu.SemaphoreType.DMA((8,)),
            pltpu.SemaphoreType.DMA((8,)),
        ],
        compiler_params=pltpu.CompilerParams(collective_id=cid, has_side_effects=True, vmem_limit_bytes=62 << 20),
        cost_estimate=pl.CostEstimate(flops=1 << 30, bytes_accessed=160 << 20, transcendentals=0),
        name="first_units",
    )(x, bg, w, bias)


def last_units(rows, bg, pg, w1, w, bias, cid):
    ranks, tok, D = rows.shape
    F = bias.shape[1]
    anywhere = pl.BlockSpec(memory_space=pl.ANY)
    inside = pl.BlockSpec(memory_space=pltpu.VMEM)
    return pl.pallas_call(
        last_units_kernel,
        out_shape=[
            jax.ShapeDtypeStruct((ranks, tok, F), bfloat),
            jax.ShapeDtypeStruct((1, F), single),
            jax.ShapeDtypeStruct((tok, D), single),
            jax.ShapeDtypeStruct(w.shape, bfloat),
        ],
        in_specs=[anywhere, anywhere, inside, inside, inside, inside],
        out_specs=[inside] * 4,
        scratch_shapes=[
            pltpu.VMEM((ranks, tok, D), bfloat),
            pltpu.VMEM((ranks, tok, D), bfloat),
            pltpu.VMEM((ranks, tok, F), bfloat),
            pltpu.VMEM((4, tok, D), bfloat),
            pltpu.VMEM((4, tok, D), bfloat),
            pltpu.VMEM((3, 2, tok, D // 2), bfloat),
            pltpu.VMEM((6, tok, D // 2), bfloat),
            pltpu.SemaphoreType.DMA((10,)),
            pltpu.SemaphoreType.DMA((10,)),
            pltpu.SemaphoreType.DMA((8,)),
            pltpu.SemaphoreType.DMA((8,)),
        ],
        compiler_params=pltpu.CompilerParams(collective_id=cid, has_side_effects=True, vmem_limit_bytes=62 << 20),
        cost_estimate=pl.CostEstimate(flops=1 << 30, bytes_accessed=160 << 20, transcendentals=0),
        name="last_units",
    )(rows, bg, pg, w1, w, bias)


def everyone(width):
    b, z, x = lax.axis_index("b"), lax.axis_index("z"), lax.axis_index("x")
    rank, me = b * 2 + x, (b * 4 + z) * 2 + x

    def in_plane(i):
        other = lax.rem(rank + i, 8)
        return other, (other // 2, z, lax.rem(other, 2))

    def anywhere(i):
        other = lax.rem(me + i, width)
        return other, (other // 8, lax.rem(other // 2, 4), lax.rem(other, 2))

    return rank, me, in_plane, anywhere


def exchange(blocks, landed, rows, gathered, same_row, sems):
    plane_send, plane_recv, all_send, all_recv = sems
    width = gathered.shape[0]
    rank, me, in_plane, anywhere = everyone(width)
    barrier = pltpu.get_barrier_semaphore()

    def each(count, body):
        def step(i, _):
            body(i)
            return 0

        lax.fori_loop(1, count, step, 0)

    each(width, lambda i: pl.semaphore_signal(barrier, inc=1, device_id=anywhere(i)[1], device_id_type=MESH))
    pl.semaphore_wait(barrier, width - 1)

    def block(i):
        other, device = in_plane(i)
        return pltpu.make_async_remote_copy(
            src_ref=blocks.at[other], dst_ref=landed.at[rank], send_sem=plane_send.at[i], recv_sem=plane_recv.at[i],
            device_id=device, device_id_type=MESH,
        )

    def row(i):
        other, device = anywhere(i)
        return pltpu.make_async_remote_copy(
            src_ref=rows.at[0] if same_row else rows.at[other], dst_ref=gathered.at[me],
            send_sem=all_send.at[i], recv_sem=all_recv.at[i], device_id=device, device_id_type=MESH,
        )

    each(8, lambda i: block(i).start())
    each(width, lambda i: row(i).start())
    landed[rank] = blocks[rank]
    gathered[me] = rows[0] if same_row else rows[me]
    each(width, lambda i: row(i).wait())
    each(8, lambda i: block(i).wait())


def head_at(rank, i):
    return (rank // 2 * 4 + i) * 2 + rank % 2


def spread_kernel(q_ref, k_ref, v_ref, pack_ref, q_out, kv_out, pack_out, blocks, landed, gathered, *sems):
    cols = q_out.shape[2]
    for rank in range(8):
        for part, ref in enumerate((q_ref, k_ref, v_ref)):
            heads = [ref[:, head_at(rank, i) * HEAD_DIM : (head_at(rank, i) + 1) * HEAD_DIM] for i in range(4)]
            blocks[rank, :, part * cols : (part + 1) * cols] = jnp.concatenate(heads, axis=1)
    exchange(blocks, landed, pack_ref, gathered, True, sems)
    q_out[...] = landed[:, :, :cols]
    kv_out[...] = landed[:, :, cols:]
    pack_out[...] = gathered[...]


def settle_kernel(w_ref, rows_ref, q_out, k_out, v_out, sums_ref, landed, gathered, *sems):
    cols = w_ref.shape[2] // 3
    exchange(w_ref, landed, rows_ref, gathered, False, sems)
    for part, out in enumerate((q_out, k_out, v_out)):
        for pair in range(out.shape[1] // 128):
            sides = []
            for head in (2 * pair, 2 * pair + 1):
                rank, i = head // 8 * 2 + head % 2, head // 2 % 4
                at = part * cols + i * HEAD_DIM
                sides.append(landed[rank, :, at : at + HEAD_DIM])
            out[:, pair * 128 : (pair + 1) * 128] = jnp.concatenate(sides, axis=1).astype(single)
    sums_ref[...] = jnp.sum(gathered[...], axis=0)


def exchange_call(kernel, out_shape, args, blocks, landed, gathered, cid, name):
    inside = pl.BlockSpec(memory_space=pltpu.VMEM)
    width = gathered[0]
    return pl.pallas_call(
        kernel,
        out_shape=out_shape,
        in_specs=[inside] * len(args),
        out_specs=[inside] * len(out_shape),
        scratch_shapes=blocks
        + [
            pltpu.VMEM(landed, bfloat),
            pltpu.VMEM(gathered, single),
            pltpu.SemaphoreType.DMA((8,)),
            pltpu.SemaphoreType.DMA((8,)),
            pltpu.SemaphoreType.DMA((width,)),
            pltpu.SemaphoreType.DMA((width,)),
        ],
        compiler_params=pltpu.CompilerParams(collective_id=cid, has_side_effects=True, vmem_limit_bytes=32 << 20),
        cost_estimate=pl.CostEstimate(flops=1 << 20, bytes_accessed=32 << 20, transcendentals=0),
        name=name,
    )(*args)


def spread(q, k, v, pack, devices, cid):
    rows, D = q.shape
    cols = D // 8
    return exchange_call(
        spread_kernel,
        [
            jax.ShapeDtypeStruct((8, rows, cols), bfloat),
            jax.ShapeDtypeStruct((8, rows, 2 * cols), bfloat),
            jax.ShapeDtypeStruct((devices, 1, pack.shape[0]), single),
        ],
        (q, k, v, pack[None, None]),
        [pltpu.VMEM((8, rows, 3 * cols), bfloat)],
        (8, rows, 3 * cols),
        (devices, 1, pack.shape[0]),
        cid,
        "spread",
    )


def settle(weights, rows, cid):
    _, tall, wide = weights.shape
    D = wide // 3 * 8
    return exchange_call(
        settle_kernel,
        [jax.ShapeDtypeStruct((tall, D), single)] * 3 + [jax.ShapeDtypeStruct((1, rows.shape[1]), single)],
        (weights, rows[:, None]),
        [],
        weights.shape,
        (rows.shape[0], 1, rows.shape[1]),
        cid,
        "settle",
    )


def windows(span):
    block = span // 2
    return [(i * block, i * block + block + span) for i in range(2)]

def key_window(before, own, lo, hi, span):
    if lo >= span:
        return own[lo - span : hi - span]
    return jnp.concatenate([before[lo:span], own[0 : hi - span]], axis=0)

def hidden_bias(start_ref, i, block, lo, hi, span):
    rows = span + i * block + lax.broadcasted_iota(jnp.int32, (block, hi - lo), 0)
    keys = lo + lax.broadcasted_iota(jnp.int32, (block, hi - lo), 1)
    start = start_ref[i * block : (i + 1) * block, :]
    return jnp.where((keys >= start) & (keys <= rows), 0.0, -1e30).astype(single)

def each_window(first_ref, span, body):
    block = span // 2
    for i, (lo, hi) in enumerate(windows(span)):
        begins = first_ref[pl.program_id(0) * 2 + i]
        pl.when(begins >= lo + block)(functools.partial(body, i, lo + block, hi))
        pl.when(begins < lo + block)(functools.partial(body, i, lo, hi))


def attend_kernel(first_ref, start_ref, q_ref, k_ref, v_ref, kb_ref, vb_ref, out_ref):
    span, cols = q_ref.shape
    block = span // 2

    def body(i, lo, hi):
        lane = lax.broadcasted_iota(jnp.int32, (block, cols), 1) // HEAD_DIM
        rows = pl.ds(i * block, block)
        bias = hidden_bias(start_ref, i, block, lo, hi, span)
        keys = key_window(kb_ref, k_ref, lo, hi, span)
        vals = key_window(vb_ref, v_ref, lo, hi, span)
        query = q_ref[rows, :] * jnp.asarray(HEAD_DIM ** (-0.5), bfloat)

        def head(h, total):
            mine = lane == h
            scores = dot_nt(jnp.where(mine, query, 0), keys) + bias
            weights = jnp.exp(scores - jnp.max(scores, axis=1, keepdims=True))
            part = jnp.dot(weights.astype(bfloat), vals, preferred_element_type=single)
            part = part * (1.0 / jnp.sum(weights, axis=1, keepdims=True))
            return jnp.where(mine, part, total)

        total = lax.fori_loop(0, cols // HEAD_DIM, head, jnp.zeros((block, cols), single), unroll=True)
        out_ref[rows, :] = total.astype(bfloat)

    each_window(first_ref, span, body)


def attend_back_kernel(
    first_ref, start_ref, q_ref, k_ref, v_ref, kb_ref, vb_ref, do_ref, dq_ref, edge_ref, pair_ref, dk, dv
):
    span, cols = q_ref.shape
    block = span // 2
    scale = HEAD_DIM ** (-0.5)
    dk[...] = jnp.zeros_like(dk)
    dv[...] = jnp.zeros_like(dv)

    def body(i, lo, hi):
        lane = lax.broadcasted_iota(jnp.int32, (block, cols), 1) // HEAD_DIM
        rows = pl.ds(i * block, block)
        bias = hidden_bias(start_ref, i, block, lo, hi, span)
        keys = key_window(kb_ref, k_ref, lo, hi, span)
        vals = key_window(vb_ref, v_ref, lo, hi, span)
        query = q_ref[rows, :] * jnp.asarray(scale, bfloat)
        grad = do_ref[rows, :]

        def head(h, total):
            mine = lane == h
            query_h = jnp.where(mine, query, 0)
            grad_h = jnp.where(mine, grad, 0)
            scores = dot_nt(query_h, keys) + bias
            weights = jnp.exp(scores - jnp.max(scores, axis=1, keepdims=True))
            probs = weights * (1.0 / jnp.sum(weights, axis=1, keepdims=True))
            prob_grad = dot_nt(grad_h, vals)
            row_dot = jnp.sum(probs * prob_grad, axis=1, keepdims=True)
            score_grad = (probs * (prob_grad - row_dot)).astype(bfloat)
            dv[lo:hi, :] += dot_tn(probs.astype(bfloat), grad_h)
            dk[lo:hi, :] += dot_tn(score_grad, query_h)
            part = jnp.dot(score_grad, keys, preferred_element_type=single)
            return jnp.where(mine, part, total)

        total = lax.fori_loop(0, cols // HEAD_DIM, head, jnp.zeros((block, cols), single), unroll=True)
        dq_ref[rows, :] = (total * scale).astype(bfloat)

    each_window(first_ref, span, body)
    edge_ref[:, :cols] = dk[:span, :].astype(bfloat)
    edge_ref[:, cols:] = dv[:span, :].astype(bfloat)
    pair_ref[:, :cols] = dk[span:, :]
    pair_ref[:, cols:] = dv[span:, :]


def block_starts(starts, groups):
    return starts.reshape(groups * 2, -1)[:, 0]


def attention_specs(span, cols):
    def at(j):
        return pl.BlockSpec((span, cols), lambda g, _: (g, j))
    return [pl.BlockSpec((span, 1), lambda g, _: (g, 0)), at(0), at(0), at(1), at(0), at(1)]

def attend(starts, query, key_value, before, groups):
    span, cols = query.shape[0] // groups, query.shape[1]
    return pl.pallas_call(
        attend_kernel,
        out_shape=jax.ShapeDtypeStruct((groups * span, cols), bfloat),
        grid_spec=pltpu.PrefetchScalarGridSpec(
            num_scalar_prefetch=1,
            grid=(groups,),
            in_specs=attention_specs(span, cols),
            out_specs=pl.BlockSpec((span, cols), lambda g, _: (g, 0)),
        ),
        compiler_params=pltpu.CompilerParams(vmem_limit_bytes=60 << 20),
        name="attend",
    )(block_starts(starts, groups), starts, query, key_value, key_value, before, before)

def attend_back(starts, query, key_value, before, grad, groups):
    span, cols = query.shape[0] // groups, query.shape[1]
    rows = groups * span
    return pl.pallas_call(
        attend_back_kernel,
        out_shape=[
            jax.ShapeDtypeStruct((rows, cols), bfloat),
            jax.ShapeDtypeStruct((rows, 2 * cols), bfloat),
            jax.ShapeDtypeStruct((rows, 2 * cols), single),
        ],
        grid_spec=pltpu.PrefetchScalarGridSpec(
            num_scalar_prefetch=1,
            grid=(groups,),
            in_specs=attention_specs(span, cols) + [pl.BlockSpec((span, cols), lambda g, _: (g, 0))],
            out_specs=[pl.BlockSpec((span, cols), lambda g, _: (g, 0))]
            + [pl.BlockSpec((span, 2 * cols), lambda g, _: (g, 0))] * 2,
            scratch_shapes=[pltpu.VMEM((2 * span, cols), single)] * 2,
        ),
        compiler_params=pltpu.CompilerParams(vmem_limit_bytes=60 << 20),
        name="attend_back",
    )(block_starts(starts, groups), starts, query, key_value, key_value, before, before, grad)


def attention_heads(starts, query, key_value, before, groups):
    span, cols = query.shape[0] // groups, query.shape[1]
    both = jnp.concatenate([before.reshape(groups, span, -1), key_value.reshape(groups, span, -1)], axis=1)
    key_two, value_two = [both[..., i * cols : (i + 1) * cols].reshape(groups, 2 * span, -1, HEAD_DIM) for i in (0, 1)]
    query = query.reshape(groups, span, -1, HEAD_DIM)
    keys = jnp.arange(2 * span)[None, None, :]
    rows = span + jnp.arange(span)[None, :, None]
    allowed = (keys >= starts.reshape(groups, span, 1)) & (keys <= rows)
    scores = jnp.einsum("gqhd,gkhd->ghqk", query, key_two, preferred_element_type=single) * HEAD_DIM ** (-0.5)
    scores = jnp.where(allowed[:, None], scores, -1e30)
    weights = jnp.exp(scores - jnp.max(scores, axis=-1, keepdims=True))
    return query, key_two, value_two, weights / jnp.sum(weights, axis=-1, keepdims=True)


def attention_forward(starts, query, key_value, before, groups):
    if query.shape[1] % 128 == 0:
        return attend(starts, query, key_value, before, groups)
    _, _, value_two, probs = attention_heads(starts, query, key_value, before, groups)
    context = jnp.einsum("ghqk,gkhd->gqhd", probs.astype(bfloat), value_two, preferred_element_type=single)
    return context.astype(bfloat).reshape(query.shape)


def attention_backward(starts, query, key_value, before, grad, groups):
    if query.shape[1] % 128 == 0:
        return attend_back(starts, query, key_value, before, grad, groups)
    rows = query.shape[0]
    query, key_two, value_two, probs = attention_heads(starts, query, key_value, before, groups)
    span = query.shape[1]
    grad = grad.reshape(query.shape)
    prob_grad = jnp.einsum("gqhd,gkhd->ghqk", grad, value_two, preferred_element_type=single)
    row_dot = jnp.sum(probs * prob_grad, axis=-1, keepdims=True)
    score_grad = (probs * (prob_grad - row_dot)).astype(bfloat)
    query_grad = jnp.einsum("ghqk,gkhd->gqhd", score_grad, key_two, preferred_element_type=single) * HEAD_DIM ** (-0.5)
    key_grad = jnp.einsum("ghqk,gqhd->gkhd", score_grad, query, preferred_element_type=single) * HEAD_DIM ** (-0.5)
    value_grad = jnp.einsum("ghqk,gqhd->gkhd", probs.astype(bfloat), grad, preferred_element_type=single)
    pair = jnp.concatenate([t.reshape(groups, 2 * span, -1) for t in (key_grad, value_grad)], axis=2)
    edge, pair = [t.reshape(rows, -1) for t in (pair[:, :span].astype(bfloat), pair[:, span:])]
    return query_grad.astype(bfloat).reshape(rows, -1), edge, pair


def norm_backward(values, out_grad, gain_vec):
    center = jnp.mean(values, axis=-1, keepdims=True)
    centered = values - center
    rs = lax.rsqrt(jnp.mean(centered * centered, axis=-1, keepdims=True) + 1e-05)
    xhat = centered * rs
    g = out_grad * gain_vec
    part = rs * (g - jnp.mean(g, axis=-1, keepdims=True) - xhat * jnp.mean(g * xhat, axis=-1, keepdims=True))
    return part, jnp.sum(out_grad * xhat, axis=0), jnp.sum(out_grad, axis=0)


def on_device(
    inputs,
    exit_layers,
    lengths,
    layer_index,
    out_grad,
    ln1_gain,
    ln1_bias,
    q_weight,
    q_bias,
    k_weight,
    v_weight,
    v_bias,
    o_weight,
    o_bias,
    ln2_gain,
    ln2_bias,
    fc1_weight,
    fc1_bias,
    fc2_weight,
    fc2_bias,
):
    B, Z, X = lax.axis_size("b"), lax.axis_size("z"), lax.axis_size("x")
    R = B * X
    local = inputs[0].astype(single)
    tok, D = local.shape
    span = X * tok
    group_tok = Z * span
    at_z, at_x = lax.axis_index("z"), lax.axis_index("x")
    rank = lax.axis_index("b") * X + at_x
    rows_dev = q_weight.shape[0]
    cols = D // R
    heads = cols // HEAD_DIM
    whole_heads = rows_dev % HEAD_DIM == 0
    fast = (B, Z, X, rows_dev) == (4, 4, 2, HEAD_DIM)

    group_active = (exit_layers[0] > layer_index[0]).astype(single)
    active_total = jnp.sum(group_active)
    active = lax.dynamic_slice_in_dim(group_active, at_z * span + at_x * tok, tok, 0)[:, None]

    count = lengths.shape[1]
    upto = jnp.arange(count)[:, None] <= jnp.arange(count)[None, :]
    def to_ranks(matrix):
        lead = matrix.shape[:-1]
        if whole_heads:
            matrix = matrix.reshape(*lead, B, Z, X, rows_dev)
            k = len(lead)
            return matrix.transpose(k, k + 2, *range(k), k + 1, k + 3).reshape(R, *lead, cols)
        return jnp.moveaxis(matrix.reshape(*lead, R, cols), -2, 0)

    def from_ranks(parts):
        if whole_heads:
            parts = parts.reshape(B, X, -1, Z, rows_dev)
            return parts.transpose(2, 0, 3, 1, 4).reshape(-1, D)
        return parts.transpose(1, 0, 2).reshape(-1, D)

    def mine(vector):
        return lax.dynamic_index_in_dim(to_ranks(vector), rank, 0, keepdims=False)

    if whole_heads:
        weight_o = lax.all_gather(o_weight, "z", axis=0, tiled=True)
    else:
        weight_o = lax.dynamic_slice_in_dim(lax.all_gather(o_weight, ALL, axis=0, tiled=True), rank * cols, cols, 0)
    small = [ln1_gain, ln1_bias, q_bias, v_bias, o_bias, ln2_gain, ln2_bias, fc2_bias]
    pack = jnp.concatenate([v.astype(single) for v in (*small, fc1_bias, lengths[0])])
    pack = jnp.concatenate([pack, jnp.zeros((-pack.shape[0] % 128,), single)])
    if fast:
        query_mine, pair_mine, pack = spread(q_weight, k_weight, v_weight, pack, R * Z, 8)
        query_mine, pair_mine, pack = query_mine.reshape(-1, cols), pair_mine.reshape(-1, 2 * cols), pack[:, 0]
    else:
        qkv_parts = jnp.concatenate([to_ranks(q_weight), to_ranks(k_weight), to_ranks(v_weight)], axis=2)
        qkv_mine = lax.all_to_all(qkv_parts, PLANE, split_axis=0, concat_axis=0, tiled=True).reshape(D // Z, 3 * cols)
        query_mine, pair_mine = qkv_mine[:, :cols], qkv_mine[:, cols:]
        pack = jnp.broadcast_to(pack, (R * Z, pack.shape[0]))
        pack = lax.all_to_all(pack, ALL, split_axis=0, concat_axis=0, tiled=True)
    vectors = [pack[:, i * rows_dev : (i + 1) * rows_dev].reshape(-1) for i in range(len(small))]
    gain_one, bias_one, bias_q, bias_v, bias_o, gain_two, bias_two, bias_down = vectors
    pack = pack.reshape(B, Z, X, -1)[..., len(small) * rows_dev :]
    up_dev = fc1_bias.shape[0]
    bias_up = lax.dynamic_index_in_dim(
        pack[..., :up_dev].transpose(0, 2, 1, 3).reshape(R, Z * up_dev), rank, 0, keepdims=False
    )
    group_lengths = pack[:, 0, 0, up_dev : up_dev + count].astype(jnp.int32)
    ends = jnp.sum(jnp.where(upto, group_lengths[:, :, None], 0), axis=1)
    places = at_z * span + jnp.arange(span, dtype=jnp.int32)
    starts = jnp.max(jnp.where(ends[:, None, :] <= places[None, :, None], ends[:, None, :], 0), axis=2)
    starts = starts - (at_z - 1) * span

    def feature_rows(mine):
        full = lax.all_gather(mine, "z", axis=0, tiled=True)
        return full.reshape(Z, B, X, rows_dev, -1).transpose(1, 0, 2, 3, 4).reshape(D, -1)

    weight_kv = feature_rows(pair_mine)
    bias_kv = jnp.concatenate([jnp.zeros((cols,), single), mine(bias_v)])
    bias_one, query_mine, weight_o = lax.optimization_barrier((bias_one, query_mine, weight_o))
    normed_low = layer_norm(local, gain_one, bias_one).astype(bfloat)

    def gather_plane(rows, cid, name):
        if fast:
            return plane_gather(rows, (), [], None, cid, name)[0]
        return lax.all_gather(rows, PLANE, axis=0, tiled=True)

    def gather_plane_dot(rows, weight, shift, out_type, turned, cid, name):
        if fast:
            return gather_dot(rows, weight, shift, out_type, turned, cid, name)
        rows = lax.all_gather(rows, PLANE, axis=0, tiled=True)
        return rows, ((dot_nt if turned else dot)(rows, weight) + shift).astype(out_type)

    def reduce_plane(left, weight, turned, cid, name):
        if fast:
            return dot_reduce([left], [weight], turned, cid, name)
        terms = (dot_nt if turned else dot)(left, weight).astype(bfloat)
        return lax.psum_scatter(terms, PLANE, scatter_dimension=0, tiled=True).astype(single)

    normed_all = gather_plane(normed_low, 0, "gather_normed")
    units = fc1_bias.shape[0] // 2
    halves = [jnp.concatenate([fc1_weight.T[i : i + units], fc2_weight[i : i + units]]) for i in (0, units)]

    def gather_units(mine):
        return lax.all_gather(mine, "z", axis=0, tiled=True).reshape(Z, 2, units, D)

    normed_all, weight_kv, unit_one = lax.optimization_barrier((normed_all, weight_kv, halves[0]))
    weight_q = feature_rows(query_mine)
    unit_one = gather_units(unit_one)
    key_value = (dot(normed_all, weight_kv) + bias_kv).astype(bfloat)
    up = [(i, i + 1) for i in range(Z - 1)]
    down = [(i + 1, i) for i in range(Z - 1)]
    cotangent = out_grad[0].astype(single) * (group_tok / active_total)
    branch_grad = (active * cotangent).astype(bfloat)
    down_b_grad = column_sums(branch_grad)
    key_value, branch_grad = lax.optimization_barrier((key_value, branch_grad))
    before = lax.ppermute(key_value, "z", up)
    branch_all = gather_plane(branch_grad, 7, "gather_branch")
    branch_all, late_normed = lax.optimization_barrier((branch_all, normed_all))
    query = (dot(late_normed, weight_q) + mine(bias_q)).astype(bfloat)
    before, query = lax.optimization_barrier((before, query))
    starts = starts.reshape(B * span, 1)
    context = attention_forward(starts, query, key_value, before, B)
    context, unit_two = lax.optimization_barrier((context, halves[1]))
    unit_two = gather_units(unit_two)

    attended = reduce_plane(context, weight_o, False, 1, "attended") + bias_o
    middle = local + active * attended
    normed_two = layer_norm(middle, gain_two, bias_two).astype(bfloat)
    bias_up = bias_up.reshape(Z, 2, units)
    bias_up = [bias_up[:, i].reshape(1, Z * units) for i in range(2)]

    def sum_halves(left, right, turned, cid, name):
        if fast:
            return dot_reduce(left, right, turned, cid, name)
        terms = sum((dot_nt if turned else dot)(a, w) for a, w in zip(left, right)).astype(bfloat)
        return lax.psum_scatter(terms, PLANE, scatter_dimension=0, tiled=True).astype(single)

    def sum_z(grads):
        return lax.psum_scatter(grads.reshape(Z * 2 * units, D), "z", scatter_dimension=0, tiled=True)

    if fast:
        branch_rows = branch_all.reshape(R, tok, D)
        two_all, hidden_one, pre_one, bias_one_up, grads = first_units(normed_two, branch_rows, unit_one, bias_up[0], 2)
        shard_one = sum_z(grads)
        hidden_two, bias_two_up, normed_two_grad, grads = last_units(
            two_all, branch_rows, pre_one, unit_one, unit_two, bias_up[1], 3
        )
        shard_two = sum_z(grads)
        up_b_halves = [bias_one_up[0], bias_two_up[0]]
    else:
        two_all = gather_plane(normed_two, 2, "gather_two")

        def half_units(weights, bias):
            weight_up, weight_down = [weights[:, i].reshape(Z * units, D) for i in (0, 1)]
            hidden, gelu_pull = jax.vjp(partial(jax.nn.gelu, approximate=True), dot_nt(two_all, weight_up) + bias)
            hidden = hidden.astype(bfloat)
            pre_grad = gelu_pull(dot_nt(branch_all, weight_down))[0].astype(bfloat)
            grads = dot_tn(pre_grad, two_all), dot_tn(hidden, branch_all)
            grads = jnp.stack([g.astype(bfloat).reshape(Z, units, D) for g in grads], axis=1)
            return hidden, pre_grad, sum_z(grads), weight_up, weight_down

        hidden_one, pre_one, shard_one, up_one, down_one = half_units(unit_one, bias_up[0])
        hidden_two, pre_two, shard_two, up_two, down_two = half_units(unit_two, bias_up[1])
        up_b_halves = [column_sums(pre_one), column_sums(pre_two)]
        normed_two_grad = sum_halves([pre_one, pre_two], [up_one, up_two], False, 3, "up_grad")
    up_b_grad = jnp.stack([half.reshape(Z, units) for half in up_b_halves], axis=1).reshape(-1)

    middle_part, gain_two_grad, bias_two_grad = norm_backward(middle, normed_two_grad, gain_two)
    middle_grad = cotangent + middle_part
    attended_grad = (active * middle_grad).astype(bfloat)
    out_b_grad = column_sums(attended_grad)
    attended_all, context_grad = gather_plane_dot(
        attended_grad, weight_o, jnp.zeros((1, cols), single), bfloat, True, 5, "attended_grad"
    )
    context_grad, shard_one = lax.optimization_barrier((context_grad, shard_one))
    out_w_grad = dot_tn(context, attended_all)
    query_grad, edge, pair = attention_backward(starts, query, key_value, before, context_grad, B)
    hidden_one, edge, pair, query_grad = lax.optimization_barrier((hidden_one, edge, pair, query_grad))
    after = lax.ppermute(edge, "z", down)
    query_w_grad = dot_tn(normed_all, query_grad).astype(bfloat)
    hidden_one, query_w_grad, out_w_grad = lax.optimization_barrier((hidden_one, query_w_grad, out_w_grad))
    downs = [unit_one, unit_two] if fast else [down_one, down_two]
    branch = sum_halves([hidden_one, hidden_two], downs, False, 4, "down")
    branch, after, shard_two = lax.optimization_barrier((branch, after, shard_two))
    outputs = middle + active * (branch + bias_down)
    pair_grad = (pair + after.astype(single)).astype(bfloat)
    pair_w_grad = dot_tn(normed_all, pair_grad).astype(bfloat)
    pair_grad, pair_w_grad = lax.optimization_barrier((pair_grad, pair_w_grad))
    normed_grad = sum_halves([query_grad, pair_grad], [weight_q, weight_kv], True, 6, "qkv_grad")
    query_b_grad = column_sums(query_grad)
    value_b_grad = column_sums(pair_grad[:, cols:])
    input_part, gain_one_grad, bias_one_grad = norm_backward(local, normed_grad, gain_one)
    input_grad = middle_grad + input_part

    def sum_to_owners(vectors, axes, parts):
        split = jnp.concatenate([v.reshape(parts, -1) for v in vectors], axis=1)
        summed = jnp.sum(lax.all_to_all(split, axes, split_axis=0, concat_axis=0, tiled=True), axis=0)
        widths = [v.shape[0] // parts for v in vectors]
        return [summed[sum(widths[:i]) : sum(widths[: i + 1])] for i in range(len(widths))]

    qkv_w_grad = jnp.concatenate([query_w_grad, pair_w_grad], axis=1)
    qkv_w_grad = qkv_w_grad.reshape(B, Z, X, rows_dev, 3 * cols).transpose(1, 0, 2, 3, 4).reshape(D, 3 * cols)
    qkv_w_grad = lax.psum_scatter(qkv_w_grad, "z", scatter_dimension=0, tiled=True).reshape(R, rows_dev, 3 * cols)
    qkv_w_grad, out_w_grad = lax.optimization_barrier((qkv_w_grad, out_w_grad))
    device_sums = [gain_one_grad, bias_one_grad, out_b_grad, gain_two_grad, bias_two_grad, down_b_grad]
    if fast:
        rank_sums = jnp.concatenate([v.reshape(Z, -1) for v in (query_b_grad, value_b_grad, up_b_grad)], axis=1)
        here = (jnp.arange(R) == rank).reshape(B, 1, X, 1)
        rank_sums = jnp.where(here, rank_sums[None, :, None, :], 0.0).reshape(R * Z, -1)
        rows = jnp.concatenate([v.reshape(R * Z, -1) for v in device_sums] + [rank_sums], axis=1)
        q_w_shard, k_w_shard, v_w_shard, summed = settle(qkv_w_grad, rows, 9)
        sums = [summed[0, i * rows_dev : (i + 1) * rows_dev] for i in range(len(device_sums) + 2)]
        q_b_shard, v_b_shard = sums[len(device_sums) :]
        up_b_shard = summed[0, (len(device_sums) + 2) * rows_dev :]
    else:
        qkv_w_grad = lax.all_to_all(qkv_w_grad, PLANE, split_axis=0, concat_axis=0, tiled=True)
        q_w_shard, k_w_shard, v_w_shard = [
            from_ranks(qkv_w_grad[..., i : i + cols]).astype(single) for i in range(0, 3 * cols, cols)
        ]
        sums = sum_to_owners(device_sums, ALL, R * Z)
        [up_b_shard] = sum_to_owners([up_b_grad], "z", Z)
    if whole_heads:
        out_w_shard = lax.psum_scatter(out_w_grad.astype(bfloat), "z", scatter_dimension=0, tiled=True).astype(single)
        if not fast:
            q_b_shard, v_b_shard = sum_to_owners([query_b_grad, value_b_grad], "z", Z)
    else:

        def placed(rows):
            full = jnp.zeros((D,) + rows.shape[1:], rows.dtype)
            full = lax.dynamic_update_slice_in_dim(full, rows, rank * cols, 0)
            return lax.psum_scatter(full, ALL, scatter_dimension=0, tiled=True).astype(single)

        out_w_shard = placed(out_w_grad.astype(bfloat))
        q_b_shard = placed(query_b_grad)
        v_b_shard = placed(value_b_grad)
    return (
        outputs.astype(bfloat)[None],
        input_grad.astype(bfloat)[None],
        sums[0],
        sums[1],
        q_w_shard,
        q_b_shard,
        k_w_shard,
        v_w_shard,
        v_b_shard,
        out_w_shard,
        sums[2],
        sums[3],
        sums[4],
        jnp.concatenate([shard_one[:units], shard_two[:units]]).T.astype(single),
        up_b_shard,
        jnp.concatenate([shard_one[units:], shard_two[units:]]).astype(single),
        sums[5],
    )


def solution(mesh):
    groups, parts = mesh.shape["batch"], mesh.shape["seq"]
    inner = Mesh(mesh.devices.reshape(groups, SPANS, parts // SPANS), ("b", "z", "x"))
    token = P("b", ("z", "x"), None)
    vector = P(ALL)
    rows = P(ALL, None)
    columns = P(None, ALL)
    return jax.shard_map(
        on_device,
        mesh=inner,
        in_specs=(
            token,
            P("b", None),
            P("b", None),
            P(),
            token,
            vector,
            vector,
            rows,
            vector,
            rows,
            rows,
            vector,
            rows,
            vector,
            vector,
            vector,
            columns,
            vector,
            rows,
            vector,
        ),
        out_specs=(
            token,
            token,
            vector,
            vector,
            rows,
            vector,
            rows,
            rows,
            vector,
            rows,
            vector,
            vector,
            vector,
            columns,
            vector,
            rows,
            vector,
        ),
        check_vma=False,
    )
```

```python
import functools
from functools import partial

import jax
import jax.numpy as jnp
from jax import lax
from jax.experimental import pallas as pl
from jax.experimental.pallas import tpu as pltpu
from jax.sharding import Mesh
from jax.sharding import PartitionSpec as P

HEAD_DIM = 64
SPANS = 4

bfloat = jnp.bfloat16
single = jnp.float32

PLANE = ("b", "x")
ALL = ("b", "z", "x")
MESH = pl.DeviceIdType.MESH
TILE = 512

def plane_place():
    b, z, x = lax.axis_index("b"), lax.axis_index("z"), lax.axis_index("x")
    sib_b = b + 1 - 2 * lax.rem(b, 2)
    far_b = lax.rem(b + 2, 4)
    far_sib_b = lax.rem(sib_b + 2, 4)
    ids = {"s": (sib_b, z, x), "x": (b, z, 1 - x), "y": (far_b, z, x)}
    ranks = {
        "o": b * 2 + x,
        "s": sib_b * 2 + x,
        "x": b * 2 + 1 - x,
        "xs": sib_b * 2 + 1 - x,
        "y": far_b * 2 + x,
        "ys": far_sib_b * 2 + x,
        "d": far_b * 2 + 1 - x,
        "ds": far_sib_b * 2 + 1 - x,
    }
    return ids, ranks

def greet(ids):
    barrier = pltpu.get_barrier_semaphore()
    for device in ids.values():
        pl.semaphore_signal(barrier, inc=1, device_id=device, device_id_type=MESH)
    pl.semaphore_wait(barrier, len(ids))

def tiles(lo, hi, body):
    def step(i, _):
        body(pl.ds(pl.multiple_of(i * TILE, TILE), TILE))
        return 0
    lax.fori_loop(lo // TILE, hi // TILE, step, 0)

def gather_kernel(body_of, n_in, n_out, x_ref, *refs):
    ins = refs[:n_in]; all_ref = refs[n_in]; outs = refs[n_in + 1 : n_in + 1 + n_out]
    held, send, recv, keep = refs[n_in + 1 + n_out :]
    ids, at = plane_place()
    half = x_ref.shape[0] // 2
    parts = (pl.ds(0, half), pl.ds(half, half))
    greet(ids)
    count = [0]
    started = []
    def ship(src, dst, to):
        n = count[0]; count[0] += 1
        c = pltpu.make_async_remote_copy(src_ref=src, dst_ref=dst, send_sem=send.at[n], recv_sem=recv.at[n], device_id=ids[to], device_id_type=MESH)
        c.start(); started.append(c)
        return c
    own = at["o"]
    x0 = ship(x_ref.at[parts[0]], held.at[own, parts[0]], "x")
    y1 = ship(x_ref.at[parts[1]], held.at[own, parts[1]], "y")
    x1 = ship(x_ref.at[parts[1]], held.at[own, parts[1]], "x")
    y0 = ship(x_ref.at[parts[0]], held.at[own, parts[0]], "y")
    s0 = ship(x_ref, held.at[own], "s")
    kept = []
    def done(rank, src):
        c = pltpu.make_async_copy(src, all_ref.at[rank], keep.at[len(kept)])
        c.start(); kept.append(c)
        if body_of is not None:
            body_of(rank, src, ins, outs)
    done(own, x_ref)
    s0.wait_recv()
    done(at["s"], held.at[at["s"]])
    x0.wait_recv()
    ry = ship(held.at[at["x"], parts[0]], held.at[at["x"], parts[0]], "y")
    y1.wait_recv()
    rx = ship(held.at[at["y"], parts[1]], held.at[at["y"], parts[1]], "x")
    x1.wait_recv()
    sx = ship(held.at[at["x"]], held.at[at["x"]], "s")
    y0.wait_recv()
    sy = ship(held.at[at["y"]], held.at[at["y"]], "s")
    done(at["x"], held.at[at["x"]])
    done(at["y"], held.at[at["y"]])
    sx.wait_recv()
    done(at["xs"], held.at[at["xs"]])
    sy.wait_recv()
    done(at["ys"], held.at[at["ys"]])
    ry.wait_recv(); rx.wait_recv()
    sd = ship(held.at[at["d"]], held.at[at["d"]], "s")
    done(at["d"], held.at[at["d"]])
    sd.wait_recv()
    done(at["ds"], held.at[at["ds"]])
    for c in started: c.wait_send()
    for c in kept: c.wait()

def vmem(n): return [pl.BlockSpec(memory_space=pltpu.VMEM)] * n

def plane_gather(x, ins, out_types, body_of, cid, name, ranks=8):
    tok, D = x.shape
    res = pl.pallas_call(
        functools.partial(gather_kernel, body_of, len(ins), len(out_types)),
        out_shape=[jax.ShapeDtypeStruct((ranks, tok, D), x.dtype), *out_types],
        in_specs=vmem(1 + len(ins)),
        out_specs=[pl.BlockSpec(memory_space=pl.ANY)] + vmem(len(out_types)),
        scratch_shapes=[pltpu.VMEM((ranks, tok, D), x.dtype), pltpu.SemaphoreType.DMA((10,)), pltpu.SemaphoreType.DMA((10,)), pltpu.SemaphoreType.DMA((8,))],
        compiler_params=pltpu.CompilerParams(collective_id=cid, has_side_effects=True, vmem_limit_bytes=60 << 20),
        cost_estimate=pl.CostEstimate(flops=1 << 30, bytes_accessed=128 << 20, transcendentals=0),
        name=name,
    )(x, *ins)
    return res[0].reshape(ranks * tok, D), *res[1:]

def gather_dot(x, w, bias, out_dtype, turned, cid, name):
    ranks, tok, D = 8, *x.shape
    N = w.shape[0] if turned else w.shape[1]
    tile = min(N, 512) if N % 512 == 0 else 256
    def body(rank, src, ins, outs):
        w_ref, b_ref = ins
        def step(i, _):
            cols = pl.ds(pl.multiple_of(i * tile, tile), tile)
            if turned:
                y = lax.dot_general(src[...], w_ref[cols, :], (((1,), (1,)), ((), ())), preferred_element_type=single)
            else:
                y = jnp.dot(src[...], w_ref[:, cols], preferred_element_type=single)
            outs[0][rank, :, cols] = (y + b_ref[:, cols]).astype(out_dtype)
            return 0
        lax.fori_loop(0, N // tile, step, 0)
    all_, y = plane_gather(x, (w, bias), [jax.ShapeDtypeStruct((ranks, tok, N), out_dtype)], body, cid, name)
    return all_, y.reshape(ranks * tok, N)

def reduce_kernel(turned, pairs, *refs):
    left, right = refs[:pairs], refs[pairs : 2 * pairs]
    out_ref, sib_out, sib_in, stage, landed, send, recv = refs[2 * pairs :]
    ids, at = plane_place()
    D = out_ref.shape[1]
    mid = D // 2
    greet(ids)
    count = [0]; started = []
    def ship(src, dst, to):
        n = count[0]; count[0] += 1
        c = pltpu.make_async_remote_copy(src_ref=src, dst_ref=dst, send_sem=send.at[n], recv_sem=recv.at[n], device_id=ids[to], device_id_type=MESH)
        c.start(); started.append(c)
        return c
    def term(rank, cols):
        if turned:
            return sum(dot_nt(a[rank], w[cols, :]) for a, w in zip(left, right))
        rows = [w[:, 1, :, cols].reshape(-1, TILE) if len(w.shape) == 4 else w[:, cols] for w in right]
        return sum(dot(a[rank], w) for a, w in zip(left, rows))
    order = ("d", "x", "y", "o")
    twin = {"d": "ds", "x": "xs", "y": "ys", "o": "s"}
    sib = {}
    def to_sibling(j, h):
        def fill(cols):
            sib_out[j, h, :, local(h, cols)] = term(at[twin[order[j]]], cols).astype(bfloat)
        tiles(h * mid, (h + 1) * mid, fill)
        sib[j, h] = ship(sib_out.at[j, h], sib_in.at[j, h], "s")
    def local(h, cols):
        return pl.ds(pl.multiple_of(cols.start - h * mid, TILE), TILE)
    def pair(j, h, cols):
        return term(at[order[j]], cols) + sib_in[j, h, :, local(h, cols)].astype(single)
    def put(j, h, extra=None):
        sib[j, h].wait_recv()
        def fill(cols):
            value = pair(j, h, cols)
            if extra is not None:
                value = value + landed[extra, :, local(h, cols)].astype(single)
            stage[j, h, :, local(h, cols)] = value.astype(bfloat)
        tiles(h * mid, (h + 1) * mid, fill)
    to_sibling(0, 0)
    to_sibling(0, 1)
    put(0, 0)
    d_a = ship(stage.at[0, 0], landed.at[0], "x")
    put(0, 1)
    d_b = ship(stage.at[0, 1], landed.at[1], "y")
    to_sibling(1, 0)
    to_sibling(2, 1)
    put(1, 0)
    x_a = ship(stage.at[1, 0], landed.at[2], "x")
    put(2, 1)
    y_b = ship(stage.at[2, 1], landed.at[3], "y")
    for j, h in ((1, 1), (2, 0), (3, 0), (3, 1)):
        to_sibling(j, h)
    d_b.wait_recv()
    put(1, 1, extra=1)
    x_b = ship(stage.at[1, 1], landed.at[5], "x")
    d_a.wait_recv()
    put(2, 0, extra=0)
    y_a = ship(stage.at[2, 0], landed.at[4], "y")
    for h in range(2):
        sib[3, h].wait_recv()
        def first(cols, h=h):
            out_ref[:, cols] = pair(3, h, cols)
        tiles(h * mid, (h + 1) * mid, first)
    x_a.wait_recv(); y_b.wait_recv(); x_b.wait_recv(); y_a.wait_recv()
    for h, (n, m) in enumerate(((2, 4), (3, 5))):
        def add(cols, h=h, n=n, m=m):
            c = local(h, cols)
            out_ref[:, cols] = out_ref[:, cols] + landed[n, :, c].astype(single) + landed[m, :, c].astype(single)
        tiles(h * mid, (h + 1) * mid, add)
    for c in started: c.wait_send()

def dot_reduce(left, right, turned, cid, name):
    ranks = 8
    D = right[0].shape[0] if turned else right[0].shape[-1]
    tok = left[0].size // left[0].shape[-1] // ranks
    return pl.pallas_call(
        functools.partial(reduce_kernel, turned, len(left)),
        out_shape=jax.ShapeDtypeStruct((tok, D), single),
        in_specs=vmem(2 * len(left)), out_specs=vmem(1)[0],
        scratch_shapes=[pltpu.VMEM((4, 2, tok, D // 2), bfloat), pltpu.VMEM((4, 2, tok, D // 2), bfloat), pltpu.VMEM((3, 2, tok, D // 2), bfloat), pltpu.VMEM((6, tok, D // 2), bfloat),
            pltpu.SemaphoreType.DMA((14,)), pltpu.SemaphoreType.DMA((14,))],
        compiler_params=pltpu.CompilerParams(collective_id=cid, has_side_effects=True, vmem_limit_bytes=60 << 20),
        cost_estimate=pl.CostEstimate(flops=1 << 30, bytes_accessed=128 << 20, transcendentals=0),
        name=name,
    )(*[a.reshape(ranks, tok, -1) for a in left], *right)


def dot(left, right):
    return jnp.dot(left, right, preferred_element_type=single)


def dot_tn(left, right):
    return lax.dot_general(left, right, (((0,), (0,)), ((), ())), preferred_element_type=single)


def dot_nt(left, right):
    return lax.dot_general(left, right, (((1,), (1,)), ((), ())), preferred_element_type=single)


def layer_norm(values, gain_vec, shift_vec):
    center = jnp.mean(values, axis=-1, keepdims=True)
    centered = values - center
    spread = jnp.mean(centered * centered, axis=-1, keepdims=True)
    return centered * lax.rsqrt(spread + 1e-05) * gain_vec + shift_vec


def column_sums(matrix):
    return jnp.sum(matrix.astype(single), axis=0)


def shipper(send, recv, ids):
    started = []

    def ship(src, dst, to):
        n = len(started)
        copy = pltpu.make_async_remote_copy(
            src_ref=src, dst_ref=dst, send_sem=send.at[n], recv_sem=recv.at[n], device_id=ids[to], device_id_type=MESH
        )
        copy.start()
        started.append(copy)
        return copy

    return ship, started


TWIN = {"o": "s", "x": "xs", "y": "ys", "d": "ds"}


def unit_rows(w_ref, i):
    parts, _, units, D = w_ref.shape
    return w_ref[:, i].reshape(parts * units, D)


def hidden_units(src, branch, w_ref, b_ref, hid_ref, pg_ref, pb_ref, rank):
    pre = dot_nt(src[...], unit_rows(w_ref, 0)) + b_ref[...]
    square = pre * pre
    bend = jnp.tanh(0.7978845608028654 * (pre + 0.044715 * (pre * square)))
    rise = 0.5 * (1.0 + bend)
    hid_ref[rank] = (pre * rise).astype(bfloat)
    slope = rise + (0.5 * 0.7978845608028654) * pre * (1.0 - bend * bend) * (1.0 + 3 * 0.044715 * square)
    grad = (dot_nt(branch[...], unit_rows(w_ref, 1)) * slope).astype(bfloat)
    pg_ref[rank] = grad
    pb_ref[...] += jnp.sum(grad.astype(single), axis=0, keepdims=True)


def first_units_kernel(
    x_ref, bg_ref, w_ref, b_ref, all_ref, hid_ref, pg_ref, pb_ref, grad_ref,
    held, bg, total, send, recv, keep, load,
):
    ids, at = plane_place()
    tok = x_ref.shape[0]
    half = tok // 2
    parts = (pl.ds(0, half), pl.ds(half, half))
    own = at["o"]
    loads = {}
    for n, name in enumerate(at):
        loads[name] = pltpu.make_async_copy(bg_ref.at[at[name]], bg.at[at[name]], load.at[n])
        loads[name].start()
    greet(ids)
    ship, started = shipper(send, recv, ids)
    x0 = ship(x_ref.at[parts[0]], held.at[own, parts[0]], "x")
    y1 = ship(x_ref.at[parts[1]], held.at[own, parts[1]], "y")
    x1 = ship(x_ref.at[parts[1]], held.at[own, parts[1]], "x")
    y0 = ship(x_ref.at[parts[0]], held.at[own, parts[0]], "y")
    s0 = ship(x_ref, held.at[own], "s")
    pb_ref[...] = jnp.zeros_like(pb_ref)
    kept = []

    def units(name):
        rank = at[name]
        src = x_ref if name == "o" else held.at[rank]
        copy = pltpu.make_async_copy(src, all_ref.at[rank], keep.at[len(kept)])
        copy.start()
        kept.append(copy)
        loads[name].wait()
        hidden_units(src, bg.at[rank], w_ref, b_ref, hid_ref, pg_ref, pb_ref, rank)

    def weigh(name, last=False):
        units_at = grad_ref.shape[2]
        per = 256 // units_at

        def rows(i, _):
            here = pl.ds(pl.multiple_of(i * 256, 256), 256)
            owners = pl.ds(i * per, per)
            for j, left in enumerate((pg_ref, hid_ref)):
                term = 0
                for n in (name, TWIN[name]):
                    right = bg[at[n]] if j else (x_ref[...] if n == "o" else held[at[n]])
                    term = term + dot_tn(left[at[n], :, here], right)
                term = term.reshape(per, units_at, -1)
                if name == "o":
                    total[owners, j] = term
                elif last:
                    grad_ref[owners, j] = (total[owners, j] + term).astype(bfloat)
                else:
                    total[owners, j] += term
            return 0

        lax.fori_loop(0, hid_ref.shape[2] // 256, rows, 0)

    units("o")
    s0.wait_recv()
    units("s")
    x0.wait_recv()
    ry = ship(held.at[at["x"], parts[0]], held.at[at["x"], parts[0]], "y")
    y1.wait_recv()
    rx = ship(held.at[at["y"], parts[1]], held.at[at["y"], parts[1]], "x")
    weigh("o")
    x1.wait_recv()
    sx = ship(held.at[at["x"]], held.at[at["x"]], "s")
    y0.wait_recv()
    sy = ship(held.at[at["y"]], held.at[at["y"]], "s")
    units("x")
    sx.wait_recv()
    units("xs")
    units("y")
    sy.wait_recv()
    units("ys")
    weigh("x")
    ry.wait_recv()
    rx.wait_recv()
    sd = ship(held.at[at["d"]], held.at[at["d"]], "s")
    weigh("y")
    units("d")
    sd.wait_recv()
    units("ds")
    weigh("d", last=True)
    for copy in started:
        copy.wait_send()
    for copy in kept:
        copy.wait()


def last_units_kernel(
    all_ref, bg_ref, pg1_ref, w1_ref, w_ref, b_ref, hid_ref, pb_ref, r_ref, grad_ref,
    held, bg, pg_ref, sib_out, sib_in, stage, landed, send, recv, load, load_b,
):
    ids, at = plane_place()
    ranks, tok, D = held.shape
    mid = D // 2
    names = ("ds", "d", "xs", "x", "ys", "y", "s", "o")
    loads = {}
    for n, name in enumerate(names):
        loads[name] = [
            pltpu.make_async_copy(all_ref.at[at[name]], held.at[at[name]], load.at[n]),
            pltpu.make_async_copy(bg_ref.at[at[name]], bg.at[at[name]], load_b.at[n]),
        ]
        for copy in loads[name]:
            copy.start()
    greet(ids)
    ship, started = shipper(send, recv, ids)
    pb_ref[...] = jnp.zeros_like(pb_ref)

    def units(name):
        for copy in loads[name]:
            copy.wait()
        rank = at[name]
        hidden_units(held.at[rank], bg.at[rank], w_ref, b_ref, hid_ref, pg_ref, pb_ref, rank)

    def term(name, cols):
        rank = at[name]
        first, second = [w[:, 0, :, cols].reshape(-1, TILE) for w in (w1_ref, w_ref)]
        return dot(pg1_ref[rank], first) + dot(pg_ref[rank], second)

    order = ("d", "x", "y", "o")

    def to_sibling(j):
        def fill(cols):
            sib_out[j, :, cols] = term(TWIN[order[j]], cols).astype(bfloat)

        tiles(0, D, fill)
        return ship(sib_out.at[j], sib_in.at[j], "s")

    def pair(j, cols):
        return term(order[j], cols) + sib_in[j, :, cols].astype(single)

    def local(h, cols):
        return pl.ds(pl.multiple_of(cols.start - h * mid, TILE), TILE)

    def put(j, h, extra=None):
        def fill(cols):
            value = pair(j, cols)
            if extra is not None:
                value = value + landed[extra, :, local(h, cols)].astype(single)
            stage[j, h, :, local(h, cols)] = value.astype(bfloat)

        tiles(h * mid, (h + 1) * mid, fill)

    units("ds")
    d_sib = to_sibling(0)
    units("d")
    d_sib.wait_recv()
    put(0, 0)
    d_a = ship(stage.at[0, 0], landed.at[0], "x")
    put(0, 1)
    d_b = ship(stage.at[0, 1], landed.at[1], "y")
    units("xs")
    x_sib = to_sibling(1)
    units("x")
    x_sib.wait_recv()
    put(1, 0)
    x_a = ship(stage.at[1, 0], landed.at[2], "x")
    units("ys")
    y_sib = to_sibling(2)
    units("y")
    y_sib.wait_recv()
    put(2, 1)
    y_b = ship(stage.at[2, 1], landed.at[3], "y")
    d_b.wait_recv()
    put(1, 1, extra=1)
    x_b = ship(stage.at[1, 1], landed.at[5], "x")
    d_a.wait_recv()
    put(2, 0, extra=0)
    y_a = ship(stage.at[2, 0], landed.at[4], "y")
    units("s")
    own_sib = to_sibling(3)
    units("o")
    own_sib.wait_recv()

    def first(cols):
        r_ref[:, cols] = pair(3, cols)

    tiles(0, D, first)

    units_at = grad_ref.shape[2]
    per = 256 // units_at
    tokens = ranks * tok

    def grads(i, _):
        here = pl.ds(pl.multiple_of(i * 256, 256), 256)
        owners = pl.ds(i * per, per)
        for j, (left, right) in enumerate(((pg_ref, held), (hid_ref, bg))):
            value = dot_tn(left[:, :, here].reshape(tokens, 256), right[...].reshape(tokens, D))
            grad_ref[owners, j] = value.astype(bfloat).reshape(per, units_at, D)
        return 0

    lax.fori_loop(0, hid_ref.shape[2] // 256, grads, 0)
    for copy in (x_a, y_b, x_b, y_a):
        copy.wait_recv()
    for h, (n, m) in enumerate(((2, 4), (3, 5))):

        def add(cols, h=h, n=n, m=m):
            c = local(h, cols)
            r_ref[:, cols] = r_ref[:, cols] + landed[n, :, c].astype(single) + landed[m, :, c].astype(single)

        tiles(h * mid, (h + 1) * mid, add)
    for copy in started:
        copy.wait_send()


def first_units(x, bg, w, bias, cid):
    ranks = 8
    tok, D = x.shape
    F = bias.shape[1]
    anywhere = pl.BlockSpec(memory_space=pl.ANY)
    inside = pl.BlockSpec(memory_space=pltpu.VMEM)
    return pl.pallas_call(
        first_units_kernel,
        out_shape=[
            jax.ShapeDtypeStruct((ranks, tok, D), bfloat),
            jax.ShapeDtypeStruct((ranks, tok, F), bfloat),
            jax.ShapeDtypeStruct((ranks, tok, F), bfloat),
            jax.ShapeDtypeStruct((1, F), single),
            jax.ShapeDtypeStruct(w.shape, bfloat),
        ],
        in_specs=[inside, anywhere, inside, inside],
        out_specs=[anywhere, inside, inside, inside, inside],
        scratch_shapes=[
            pltpu.VMEM((ranks, tok, D), bfloat),
            pltpu.VMEM((ranks, tok, D), bfloat),
            pltpu.VMEM(w.shape, single),
            pltpu.SemaphoreType.DMA((10,)),
            pltpu.SemaphoreType.DMA((10,)),
            pltpu.SemaphoreType.DMA((8,)),
            pltpu.SemaphoreType.DMA((8,)),
        ],
        compiler_params=pltpu.CompilerParams(collective_id=cid, has_side_effects=True, vmem_limit_bytes=62 << 20),
        cost_estimate=pl.CostEstimate(flops=1 << 30, bytes_accessed=160 << 20, transcendentals=0),
        name="first_units",
    )(x, bg, w, bias)


def last_units(rows, bg, pg, w1, w, bias, cid):
    ranks, tok, D = rows.shape
    F = bias.shape[1]
    anywhere = pl.BlockSpec(memory_space=pl.ANY)
    inside = pl.BlockSpec(memory_space=pltpu.VMEM)
    return pl.pallas_call(
        last_units_kernel,
        out_shape=[
            jax.ShapeDtypeStruct((ranks, tok, F), bfloat),
            jax.ShapeDtypeStruct((1, F), single),
            jax.ShapeDtypeStruct((tok, D), single),
            jax.ShapeDtypeStruct(w.shape, bfloat),
        ],
        in_specs=[anywhere, anywhere, inside, inside, inside, inside],
        out_specs=[inside] * 4,
        scratch_shapes=[
            pltpu.VMEM((ranks, tok, D), bfloat),
            pltpu.VMEM((ranks, tok, D), bfloat),
            pltpu.VMEM((ranks, tok, F), bfloat),
            pltpu.VMEM((4, tok, D), bfloat),
            pltpu.VMEM((4, tok, D), bfloat),
            pltpu.VMEM((3, 2, tok, D // 2), bfloat),
            pltpu.VMEM((6, tok, D // 2), bfloat),
            pltpu.SemaphoreType.DMA((10,)),
            pltpu.SemaphoreType.DMA((10,)),
            pltpu.SemaphoreType.DMA((8,)),
            pltpu.SemaphoreType.DMA((8,)),
        ],
        compiler_params=pltpu.CompilerParams(collective_id=cid, has_side_effects=True, vmem_limit_bytes=62 << 20),
        cost_estimate=pl.CostEstimate(flops=1 << 30, bytes_accessed=160 << 20, transcendentals=0),
        name="last_units",
    )(rows, bg, pg, w1, w, bias)


def everyone(width):
    b, z, x = lax.axis_index("b"), lax.axis_index("z"), lax.axis_index("x")
    rank, me = b * 2 + x, (b * 4 + z) * 2 + x

    def in_plane(i):
        other = lax.rem(rank + i, 8)
        return other, (other // 2, z, lax.rem(other, 2))

    def anywhere(i):
        other = lax.rem(me + i, width)
        return other, (other // 8, lax.rem(other // 2, 4), lax.rem(other, 2))

    return rank, me, in_plane, anywhere


def exchange(blocks, landed, rows, gathered, same_row, sems):
    plane_send, plane_recv, all_send, all_recv = sems
    width = gathered.shape[0]
    rank, me, in_plane, anywhere = everyone(width)
    barrier = pltpu.get_barrier_semaphore()

    def each(count, body):
        def step(i, _):
            body(i)
            return 0

        lax.fori_loop(1, count, step, 0)

    each(width, lambda i: pl.semaphore_signal(barrier, inc=1, device_id=anywhere(i)[1], device_id_type=MESH))
    pl.semaphore_wait(barrier, width - 1)

    def block(i):
        other, device = in_plane(i)
        return pltpu.make_async_remote_copy(
            src_ref=blocks.at[other], dst_ref=landed.at[rank], send_sem=plane_send.at[i], recv_sem=plane_recv.at[i],
            device_id=device, device_id_type=MESH,
        )

    def row(i):
        other, device = anywhere(i)
        return pltpu.make_async_remote_copy(
            src_ref=rows.at[0] if same_row else rows.at[other], dst_ref=gathered.at[me],
            send_sem=all_send.at[i], recv_sem=all_recv.at[i], device_id=device, device_id_type=MESH,
        )

    each(8, lambda i: block(i).start())
    each(width, lambda i: row(i).start())
    landed[rank] = blocks[rank]
    gathered[me] = rows[0] if same_row else rows[me]
    each(width, lambda i: row(i).wait())
    each(8, lambda i: block(i).wait())


def head_at(rank, i):
    return (rank // 2 * 4 + i) * 2 + rank % 2


def spread_kernel(q_ref, k_ref, v_ref, pack_ref, q_out, kv_out, pack_out, blocks, landed, gathered, *sems):
    cols = q_out.shape[2]
    for rank in range(8):
        for part, ref in enumerate((q_ref, k_ref, v_ref)):
            heads = [ref[:, head_at(rank, i) * HEAD_DIM : (head_at(rank, i) + 1) * HEAD_DIM] for i in range(4)]
            blocks[rank, :, part * cols : (part + 1) * cols] = jnp.concatenate(heads, axis=1)
    exchange(blocks, landed, pack_ref, gathered, True, sems)
    q_out[...] = landed[:, :, :cols]
    kv_out[...] = landed[:, :, cols:]
    pack_out[...] = gathered[...]


def settle_kernel(w_ref, rows_ref, q_out, k_out, v_out, sums_ref, landed, gathered, *sems):
    cols = w_ref.shape[2] // 3
    exchange(w_ref, landed, rows_ref, gathered, False, sems)
    for part, out in enumerate((q_out, k_out, v_out)):
        for pair in range(out.shape[1] // 128):
            sides = []
            for head in (2 * pair, 2 * pair + 1):
                rank, i = head // 8 * 2 + head % 2, head // 2 % 4
                at = part * cols + i * HEAD_DIM
                sides.append(landed[rank, :, at : at + HEAD_DIM])
            out[:, pair * 128 : (pair + 1) * 128] = jnp.concatenate(sides, axis=1).astype(single)
    sums_ref[...] = jnp.sum(gathered[...], axis=0)


def exchange_call(kernel, out_shape, args, blocks, landed, gathered, cid, name):
    inside = pl.BlockSpec(memory_space=pltpu.VMEM)
    width = gathered[0]
    return pl.pallas_call(
        kernel,
        out_shape=out_shape,
        in_specs=[inside] * len(args),
        out_specs=[inside] * len(out_shape),
        scratch_shapes=blocks
        + [
            pltpu.VMEM(landed, bfloat),
            pltpu.VMEM(gathered, single),
            pltpu.SemaphoreType.DMA((8,)),
            pltpu.SemaphoreType.DMA((8,)),
            pltpu.SemaphoreType.DMA((width,)),
            pltpu.SemaphoreType.DMA((width,)),
        ],
        compiler_params=pltpu.CompilerParams(collective_id=cid, has_side_effects=True, vmem_limit_bytes=32 << 20),
        cost_estimate=pl.CostEstimate(flops=1 << 20, bytes_accessed=32 << 20, transcendentals=0),
        name=name,
    )(*args)


def spread(q, k, v, pack, devices, cid):
    rows, D = q.shape
    cols = D // 8
    return exchange_call(
        spread_kernel,
        [
            jax.ShapeDtypeStruct((8, rows, cols), bfloat),
            jax.ShapeDtypeStruct((8, rows, 2 * cols), bfloat),
            jax.ShapeDtypeStruct((devices, 1, pack.shape[0]), single),
        ],
        (q, k, v, pack[None, None]),
        [pltpu.VMEM((8, rows, 3 * cols), bfloat)],
        (8, rows, 3 * cols),
        (devices, 1, pack.shape[0]),
        cid,
        "spread",
    )


def settle(weights, rows, cid):
    _, tall, wide = weights.shape
    D = wide // 3 * 8
    return exchange_call(
        settle_kernel,
        [jax.ShapeDtypeStruct((tall, D), single)] * 3 + [jax.ShapeDtypeStruct((1, rows.shape[1]), single)],
        (weights, rows[:, None]),
        [],
        weights.shape,
        (rows.shape[0], 1, rows.shape[1]),
        cid,
        "settle",
    )


def windows(span):
    block = span // 2
    return [(i * block, i * block + block + span) for i in range(2)]

def key_window(before, own, lo, hi, span):
    if lo >= span:
        return own[lo - span : hi - span]
    return jnp.concatenate([before[lo:span], own[0 : hi - span]], axis=0)

def hidden_bias(start_ref, i, block, lo, hi, span):
    rows = span + i * block + lax.broadcasted_iota(jnp.int32, (block, hi - lo), 0)
    keys = lo + lax.broadcasted_iota(jnp.int32, (block, hi - lo), 1)
    start = start_ref[i * block : (i + 1) * block, :]
    return jnp.where((keys >= start) & (keys <= rows), 0.0, -1e30).astype(single)

def each_window(first_ref, span, body):
    block = span // 2
    for i, (lo, hi) in enumerate(windows(span)):
        begins = first_ref[pl.program_id(0) * 2 + i]
        pl.when(begins >= lo + block)(functools.partial(body, i, lo + block, hi))
        pl.when(begins < lo + block)(functools.partial(body, i, lo, hi))


def attend_kernel(first_ref, start_ref, q_ref, k_ref, v_ref, kb_ref, vb_ref, out_ref):
    span, cols = q_ref.shape
    block = span // 2

    def body(i, lo, hi):
        lane = lax.broadcasted_iota(jnp.int32, (block, cols), 1) // HEAD_DIM
        rows = pl.ds(i * block, block)
        bias = hidden_bias(start_ref, i, block, lo, hi, span)
        keys = key_window(kb_ref, k_ref, lo, hi, span)
        vals = key_window(vb_ref, v_ref, lo, hi, span)
        query = q_ref[rows, :] * jnp.asarray(HEAD_DIM ** (-0.5), bfloat)

        def head(h, total):
            mine = lane == h
            scores = dot_nt(jnp.where(mine, query, 0), keys) + bias
            weights = jnp.exp(scores - jnp.max(scores, axis=1, keepdims=True))
            part = jnp.dot(weights.astype(bfloat), vals, preferred_element_type=single)
            part = part * (1.0 / jnp.sum(weights, axis=1, keepdims=True))
            return jnp.where(mine, part, total)

        total = lax.fori_loop(0, cols // HEAD_DIM, head, jnp.zeros((block, cols), single), unroll=True)
        out_ref[rows, :] = total.astype(bfloat)

    each_window(first_ref, span, body)


def attend_back_kernel(
    first_ref, start_ref, q_ref, k_ref, v_ref, kb_ref, vb_ref, do_ref, dq_ref, edge_ref, pair_ref, dk, dv
):
    span, cols = q_ref.shape
    block = span // 2
    scale = HEAD_DIM ** (-0.5)
    dk[...] = jnp.zeros_like(dk)
    dv[...] = jnp.zeros_like(dv)

    def body(i, lo, hi):
        lane = lax.broadcasted_iota(jnp.int32, (block, cols), 1) // HEAD_DIM
        rows = pl.ds(i * block, block)
        bias = hidden_bias(start_ref, i, block, lo, hi, span)
        keys = key_window(kb_ref, k_ref, lo, hi, span)
        vals = key_window(vb_ref, v_ref, lo, hi, span)
        query = q_ref[rows, :] * jnp.asarray(scale, bfloat)
        grad = do_ref[rows, :]

        def head(h, total):
            mine = lane == h
            query_h = jnp.where(mine, query, 0)
            grad_h = jnp.where(mine, grad, 0)
            scores = dot_nt(query_h, keys) + bias
            weights = jnp.exp(scores - jnp.max(scores, axis=1, keepdims=True))
            probs = weights * (1.0 / jnp.sum(weights, axis=1, keepdims=True))
            prob_grad = dot_nt(grad_h, vals)
            row_dot = jnp.sum(probs * prob_grad, axis=1, keepdims=True)
            score_grad = (probs * (prob_grad - row_dot)).astype(bfloat)
            dv[lo:hi, :] += dot_tn(probs.astype(bfloat), grad_h)
            dk[lo:hi, :] += dot_tn(score_grad, query_h)
            part = jnp.dot(score_grad, keys, preferred_element_type=single)
            return jnp.where(mine, part, total)

        total = lax.fori_loop(0, cols // HEAD_DIM, head, jnp.zeros((block, cols), single), unroll=True)
        dq_ref[rows, :] = (total * scale).astype(bfloat)

    each_window(first_ref, span, body)
    edge_ref[:, :cols] = dk[:span, :].astype(bfloat)
    edge_ref[:, cols:] = dv[:span, :].astype(bfloat)
    pair_ref[:, :cols] = dk[span:, :]
    pair_ref[:, cols:] = dv[span:, :]


def pair_grads_kernel(pair_ref, after_ref, normed_ref, query_w_ref, grad_ref, weight_ref, bias_ref):
    block = pl.program_id(0)
    cols = query_w_ref.shape[1]
    rows = weight_ref.shape[3]

    @pl.when(block == 0)
    def _():
        grad = (pair_ref[...] + after_ref[...].astype(single)).astype(bfloat)
        grad_ref[...] = grad
        bias_ref[...] = jnp.sum(grad[:, cols:].astype(single), axis=0, keepdims=True)

    value = dot_tn(normed_ref[...], grad_ref[...]).astype(bfloat)
    xs = weight_ref.shape[2]
    for z in range(weight_ref.shape[0]):
        for x in range(xs):
            here = slice((z * xs + x) * rows, (z * xs + x + 1) * rows)
            weight_ref[z, 0, x, :, :cols] = query_w_ref[here, :]
            weight_ref[z, 0, x, :, cols:] = value[here, :]


def pair_grads(pair, after, normed, query_w, B, Z, X):
    tokens, wide = pair.shape
    D = normed.shape[1]
    per = D // B
    rows = per // (Z * X)
    cols = query_w.shape[1]
    return pl.pallas_call(
        pair_grads_kernel,
        grid=(B,),
        out_shape=[
            jax.ShapeDtypeStruct((tokens, wide), bfloat),
            jax.ShapeDtypeStruct((Z, B, X, rows, cols + wide), bfloat),
            jax.ShapeDtypeStruct((1, wide - cols), single),
        ],
        in_specs=[
            pl.BlockSpec((tokens, wide), lambda b: (0, 0)),
            pl.BlockSpec((tokens, wide), lambda b: (0, 0)),
            pl.BlockSpec((tokens, per), lambda b: (0, b)),
            pl.BlockSpec((per, cols), lambda b: (b, 0)),
        ],
        out_specs=[
            pl.BlockSpec((tokens, wide), lambda b: (0, 0)),
            pl.BlockSpec((Z, 1, X, rows, cols + wide), lambda b: (0, b, 0, 0, 0)),
            pl.BlockSpec((1, wide - cols), lambda b: (0, 0)),
        ],
        compiler_params=pltpu.CompilerParams(vmem_limit_bytes=48 << 20),
        name="pair_grads",
    )(pair, after, normed, query_w)


def block_starts(starts, groups):
    return starts.reshape(groups * 2, -1)[:, 0]


def attention_specs(span, cols):
    def at(j):
        return pl.BlockSpec((span, cols), lambda g, _: (g, j))
    return [pl.BlockSpec((span, 1), lambda g, _: (g, 0)), at(0), at(0), at(1), at(0), at(1)]

def attend(starts, query, key_value, before, groups):
    span, cols = query.shape[0] // groups, query.shape[1]
    return pl.pallas_call(
        attend_kernel,
        out_shape=jax.ShapeDtypeStruct((groups * span, cols), bfloat),
        grid_spec=pltpu.PrefetchScalarGridSpec(
            num_scalar_prefetch=1,
            grid=(groups,),
            in_specs=attention_specs(span, cols),
            out_specs=pl.BlockSpec((span, cols), lambda g, _: (g, 0)),
        ),
        compiler_params=pltpu.CompilerParams(vmem_limit_bytes=60 << 20),
        name="attend",
    )(block_starts(starts, groups), starts, query, key_value, key_value, before, before)

def attend_back(starts, query, key_value, before, grad, groups):
    span, cols = query.shape[0] // groups, query.shape[1]
    rows = groups * span
    return pl.pallas_call(
        attend_back_kernel,
        out_shape=[
            jax.ShapeDtypeStruct((rows, cols), bfloat),
            jax.ShapeDtypeStruct((rows, 2 * cols), bfloat),
            jax.ShapeDtypeStruct((rows, 2 * cols), single),
        ],
        grid_spec=pltpu.PrefetchScalarGridSpec(
            num_scalar_prefetch=1,
            grid=(groups,),
            in_specs=attention_specs(span, cols) + [pl.BlockSpec((span, cols), lambda g, _: (g, 0))],
            out_specs=[pl.BlockSpec((span, cols), lambda g, _: (g, 0))]
            + [pl.BlockSpec((span, 2 * cols), lambda g, _: (g, 0))] * 2,
            scratch_shapes=[pltpu.VMEM((2 * span, cols), single)] * 2,
        ),
        compiler_params=pltpu.CompilerParams(vmem_limit_bytes=60 << 20),
        name="attend_back",
    )(block_starts(starts, groups), starts, query, key_value, key_value, before, before, grad)


def attention_heads(starts, query, key_value, before, groups):
    span, cols = query.shape[0] // groups, query.shape[1]
    both = jnp.concatenate([before.reshape(groups, span, -1), key_value.reshape(groups, span, -1)], axis=1)
    key_two, value_two = [both[..., i * cols : (i + 1) * cols].reshape(groups, 2 * span, -1, HEAD_DIM) for i in (0, 1)]
    query = query.reshape(groups, span, -1, HEAD_DIM)
    keys = jnp.arange(2 * span)[None, None, :]
    rows = span + jnp.arange(span)[None, :, None]
    allowed = (keys >= starts.reshape(groups, span, 1)) & (keys <= rows)
    scores = jnp.einsum("gqhd,gkhd->ghqk", query, key_two, preferred_element_type=single) * HEAD_DIM ** (-0.5)
    scores = jnp.where(allowed[:, None], scores, -1e30)
    weights = jnp.exp(scores - jnp.max(scores, axis=-1, keepdims=True))
    return query, key_two, value_two, weights / jnp.sum(weights, axis=-1, keepdims=True)


def attention_forward(starts, query, key_value, before, groups):
    if query.shape[1] % 128 == 0:
        return attend(starts, query, key_value, before, groups)
    _, _, value_two, probs = attention_heads(starts, query, key_value, before, groups)
    context = jnp.einsum("ghqk,gkhd->gqhd", probs.astype(bfloat), value_two, preferred_element_type=single)
    return context.astype(bfloat).reshape(query.shape)


def attention_backward(starts, query, key_value, before, grad, groups):
    if query.shape[1] % 128 == 0:
        return attend_back(starts, query, key_value, before, grad, groups)
    rows = query.shape[0]
    query, key_two, value_two, probs = attention_heads(starts, query, key_value, before, groups)
    span = query.shape[1]
    grad = grad.reshape(query.shape)
    prob_grad = jnp.einsum("gqhd,gkhd->ghqk", grad, value_two, preferred_element_type=single)
    row_dot = jnp.sum(probs * prob_grad, axis=-1, keepdims=True)
    score_grad = (probs * (prob_grad - row_dot)).astype(bfloat)
    query_grad = jnp.einsum("ghqk,gkhd->gqhd", score_grad, key_two, preferred_element_type=single) * HEAD_DIM ** (-0.5)
    key_grad = jnp.einsum("ghqk,gqhd->gkhd", score_grad, query, preferred_element_type=single) * HEAD_DIM ** (-0.5)
    value_grad = jnp.einsum("ghqk,gqhd->gkhd", probs.astype(bfloat), grad, preferred_element_type=single)
    pair = jnp.concatenate([t.reshape(groups, 2 * span, -1) for t in (key_grad, value_grad)], axis=2)
    edge, pair = [t.reshape(rows, -1) for t in (pair[:, :span].astype(bfloat), pair[:, span:])]
    return query_grad.astype(bfloat).reshape(rows, -1), edge, pair


def norm_backward(values, out_grad, gain_vec):
    center = jnp.mean(values, axis=-1, keepdims=True)
    centered = values - center
    rs = lax.rsqrt(jnp.mean(centered * centered, axis=-1, keepdims=True) + 1e-05)
    xhat = centered * rs
    g = out_grad * gain_vec
    part = rs * (g - jnp.mean(g, axis=-1, keepdims=True) - xhat * jnp.mean(g * xhat, axis=-1, keepdims=True))
    return part, jnp.sum(out_grad * xhat, axis=0), jnp.sum(out_grad, axis=0)


def on_device(
    inputs,
    exit_layers,
    lengths,
    layer_index,
    out_grad,
    ln1_gain,
    ln1_bias,
    q_weight,
    q_bias,
    k_weight,
    v_weight,
    v_bias,
    o_weight,
    o_bias,
    ln2_gain,
    ln2_bias,
    fc1_weight,
    fc1_bias,
    fc2_weight,
    fc2_bias,
):
    B, Z, X = lax.axis_size("b"), lax.axis_size("z"), lax.axis_size("x")
    R = B * X
    local = inputs[0].astype(single)
    tok, D = local.shape
    span = X * tok
    group_tok = Z * span
    at_z, at_x = lax.axis_index("z"), lax.axis_index("x")
    rank = lax.axis_index("b") * X + at_x
    rows_dev = q_weight.shape[0]
    cols = D // R
    heads = cols // HEAD_DIM
    whole_heads = rows_dev % HEAD_DIM == 0
    fast = (B, Z, X, rows_dev) == (4, 4, 2, HEAD_DIM)

    group_active = (exit_layers[0] > layer_index[0]).astype(single)
    active_total = jnp.sum(group_active)
    active = lax.dynamic_slice_in_dim(group_active, at_z * span + at_x * tok, tok, 0)[:, None]

    count = lengths.shape[1]
    upto = jnp.arange(count)[:, None] <= jnp.arange(count)[None, :]
    def to_ranks(matrix):
        lead = matrix.shape[:-1]
        if whole_heads:
            matrix = matrix.reshape(*lead, B, Z, X, rows_dev)
            k = len(lead)
            return matrix.transpose(k, k + 2, *range(k), k + 1, k + 3).reshape(R, *lead, cols)
        return jnp.moveaxis(matrix.reshape(*lead, R, cols), -2, 0)

    def from_ranks(parts):
        if whole_heads:
            parts = parts.reshape(B, X, -1, Z, rows_dev)
            return parts.transpose(2, 0, 3, 1, 4).reshape(-1, D)
        return parts.transpose(1, 0, 2).reshape(-1, D)

    def mine(vector):
        return lax.dynamic_index_in_dim(to_ranks(vector), rank, 0, keepdims=False)

    if whole_heads:
        weight_o = lax.all_gather(o_weight, "z", axis=0, tiled=True)
    else:
        weight_o = lax.dynamic_slice_in_dim(lax.all_gather(o_weight, ALL, axis=0, tiled=True), rank * cols, cols, 0)
    small = [ln1_gain, ln1_bias, q_bias, v_bias, o_bias, ln2_gain, ln2_bias, fc2_bias]
    pack = jnp.concatenate([v.astype(single) for v in (*small, fc1_bias, lengths[0])])
    pack = jnp.concatenate([pack, jnp.zeros((-pack.shape[0] % 128,), single)])
    if fast:
        query_mine, pair_mine, pack = spread(q_weight, k_weight, v_weight, pack, R * Z, 8)
        query_mine, pair_mine, pack = query_mine.reshape(-1, cols), pair_mine.reshape(-1, 2 * cols), pack[:, 0]
    else:
        qkv_parts = jnp.concatenate([to_ranks(q_weight), to_ranks(k_weight), to_ranks(v_weight)], axis=2)
        qkv_mine = lax.all_to_all(qkv_parts, PLANE, split_axis=0, concat_axis=0, tiled=True).reshape(D // Z, 3 * cols)
        query_mine, pair_mine = qkv_mine[:, :cols], qkv_mine[:, cols:]
        pack = jnp.broadcast_to(pack, (R * Z, pack.shape[0]))
        pack = lax.all_to_all(pack, ALL, split_axis=0, concat_axis=0, tiled=True)
    vectors = [pack[:, i * rows_dev : (i + 1) * rows_dev].reshape(-1) for i in range(len(small))]
    gain_one, bias_one, bias_q, bias_v, bias_o, gain_two, bias_two, bias_down = vectors
    pack = pack.reshape(B, Z, X, -1)[..., len(small) * rows_dev :]
    up_dev = fc1_bias.shape[0]
    bias_up = lax.dynamic_index_in_dim(
        pack[..., :up_dev].transpose(0, 2, 1, 3).reshape(R, Z * up_dev), rank, 0, keepdims=False
    )
    group_lengths = pack[:, 0, 0, up_dev : up_dev + count].astype(jnp.int32)
    ends = jnp.sum(jnp.where(upto, group_lengths[:, :, None], 0), axis=1)
    places = at_z * span + jnp.arange(span, dtype=jnp.int32)
    starts = jnp.max(jnp.where(ends[:, None, :] <= places[None, :, None], ends[:, None, :], 0), axis=2)
    starts = starts - (at_z - 1) * span

    def feature_rows(mine):
        full = lax.all_gather(mine, "z", axis=0, tiled=True)
        return full.reshape(Z, B, X, rows_dev, -1).transpose(1, 0, 2, 3, 4).reshape(D, -1)

    weight_kv = feature_rows(pair_mine)
    bias_kv = jnp.concatenate([jnp.zeros((cols,), single), mine(bias_v)])
    bias_one, query_mine, weight_o = lax.optimization_barrier((bias_one, query_mine, weight_o))
    normed_low = layer_norm(local, gain_one, bias_one).astype(bfloat)

    def gather_plane(rows, cid, name):
        if fast:
            return plane_gather(rows, (), [], None, cid, name)[0]
        return lax.all_gather(rows, PLANE, axis=0, tiled=True)

    def gather_plane_dot(rows, weight, shift, out_type, turned, cid, name):
        if fast:
            return gather_dot(rows, weight, shift, out_type, turned, cid, name)
        rows = lax.all_gather(rows, PLANE, axis=0, tiled=True)
        return rows, ((dot_nt if turned else dot)(rows, weight) + shift).astype(out_type)

    def reduce_plane(left, weight, turned, cid, name):
        if fast:
            return dot_reduce([left], [weight], turned, cid, name)
        terms = (dot_nt if turned else dot)(left, weight).astype(bfloat)
        return lax.psum_scatter(terms, PLANE, scatter_dimension=0, tiled=True).astype(single)

    normed_all = gather_plane(normed_low, 0, "gather_normed")
    units = fc1_bias.shape[0] // 2
    halves = [jnp.concatenate([fc1_weight.T[i : i + units], fc2_weight[i : i + units]]) for i in (0, units)]

    def gather_units(mine):
        return lax.all_gather(mine, "z", axis=0, tiled=True).reshape(Z, 2, units, D)

    normed_all, weight_kv, unit_one = lax.optimization_barrier((normed_all, weight_kv, halves[0]))
    weight_q = feature_rows(query_mine)
    unit_one = gather_units(unit_one)
    key_value = (dot(normed_all, weight_kv) + bias_kv).astype(bfloat)
    up = [(i, i + 1) for i in range(Z - 1)]
    down = [(i + 1, i) for i in range(Z - 1)]
    cotangent = out_grad[0].astype(single) * (group_tok / active_total)
    branch_grad = (active * cotangent).astype(bfloat)
    down_b_grad = column_sums(branch_grad)
    key_value, branch_grad = lax.optimization_barrier((key_value, branch_grad))
    before = lax.ppermute(key_value, "z", up)
    branch_all = gather_plane(branch_grad, 7, "gather_branch")
    branch_all, late_normed = lax.optimization_barrier((branch_all, normed_all))
    query = (dot(late_normed, weight_q) + mine(bias_q)).astype(bfloat)
    before, query = lax.optimization_barrier((before, query))
    starts = starts.reshape(B * span, 1)
    context = attention_forward(starts, query, key_value, before, B)
    context, unit_two = lax.optimization_barrier((context, halves[1]))
    unit_two = gather_units(unit_two)

    attended = reduce_plane(context, weight_o, False, 1, "attended") + bias_o
    middle = local + active * attended
    normed_two = layer_norm(middle, gain_two, bias_two).astype(bfloat)
    bias_up = bias_up.reshape(Z, 2, units)
    bias_up = [bias_up[:, i].reshape(1, Z * units) for i in range(2)]

    def sum_halves(left, right, turned, cid, name):
        if fast:
            return dot_reduce(left, right, turned, cid, name)
        terms = sum((dot_nt if turned else dot)(a, w) for a, w in zip(left, right)).astype(bfloat)
        return lax.psum_scatter(terms, PLANE, scatter_dimension=0, tiled=True).astype(single)

    def sum_z(grads):
        return lax.psum_scatter(grads.reshape(Z * 2 * units, D), "z", scatter_dimension=0, tiled=True)

    if fast:
        branch_rows = branch_all.reshape(R, tok, D)
        two_all, hidden_one, pre_one, bias_one_up, grads = first_units(normed_two, branch_rows, unit_one, bias_up[0], 2)
        shard_one = sum_z(grads)
        hidden_two, bias_two_up, normed_two_grad, grads = last_units(
            two_all, branch_rows, pre_one, unit_one, unit_two, bias_up[1], 3
        )
        shard_two = sum_z(grads)
        up_b_halves = [bias_one_up[0], bias_two_up[0]]
    else:
        two_all = gather_plane(normed_two, 2, "gather_two")

        def half_units(weights, bias):
            weight_up, weight_down = [weights[:, i].reshape(Z * units, D) for i in (0, 1)]
            hidden, gelu_pull = jax.vjp(partial(jax.nn.gelu, approximate=True), dot_nt(two_all, weight_up) + bias)
            hidden = hidden.astype(bfloat)
            pre_grad = gelu_pull(dot_nt(branch_all, weight_down))[0].astype(bfloat)
            grads = dot_tn(pre_grad, two_all), dot_tn(hidden, branch_all)
            grads = jnp.stack([g.astype(bfloat).reshape(Z, units, D) for g in grads], axis=1)
            return hidden, pre_grad, sum_z(grads), weight_up, weight_down

        hidden_one, pre_one, shard_one, up_one, down_one = half_units(unit_one, bias_up[0])
        hidden_two, pre_two, shard_two, up_two, down_two = half_units(unit_two, bias_up[1])
        up_b_halves = [column_sums(pre_one), column_sums(pre_two)]
        normed_two_grad = sum_halves([pre_one, pre_two], [up_one, up_two], False, 3, "up_grad")
    up_b_grad = jnp.stack([half.reshape(Z, units) for half in up_b_halves], axis=1).reshape(-1)

    middle_part, gain_two_grad, bias_two_grad = norm_backward(middle, normed_two_grad, gain_two)
    middle_grad = cotangent + middle_part
    attended_grad = (active * middle_grad).astype(bfloat)
    out_b_grad = column_sums(attended_grad)
    attended_all, context_grad = gather_plane_dot(
        attended_grad, weight_o, jnp.zeros((1, cols), single), bfloat, True, 5, "attended_grad"
    )
    context_grad, shard_one = lax.optimization_barrier((context_grad, shard_one))
    out_w_grad = dot_tn(context, attended_all)
    query_grad, edge, pair = attention_backward(starts, query, key_value, before, context_grad, B)
    hidden_one, edge, pair, query_grad = lax.optimization_barrier((hidden_one, edge, pair, query_grad))
    after = lax.ppermute(edge, "z", down)
    query_w_grad = dot_tn(normed_all, query_grad).astype(bfloat)
    hidden_one, query_w_grad, out_w_grad = lax.optimization_barrier((hidden_one, query_w_grad, out_w_grad))
    downs = [unit_one, unit_two] if fast else [down_one, down_two]
    branch = sum_halves([hidden_one, hidden_two], downs, False, 4, "down")
    branch, after, shard_two = lax.optimization_barrier((branch, after, shard_two))
    if fast:
        pair_grad, qkv_w_grad, value_b_grad = pair_grads(pair, after, normed_all, query_w_grad, B, Z, X)
        value_b_grad = value_b_grad[0]
    else:
        pair_grad = (pair + after.astype(single)).astype(bfloat)
        pair_w_grad = dot_tn(normed_all, pair_grad).astype(bfloat)
        qkv_w_grad = jnp.concatenate([query_w_grad, pair_w_grad], axis=1)
        qkv_w_grad = qkv_w_grad.reshape(B, Z, X, rows_dev, 3 * cols).transpose(1, 0, 2, 3, 4)
        value_b_grad = column_sums(pair_grad[:, cols:])
    qkv_w_grad = qkv_w_grad.reshape(D, 3 * cols)
    qkv_w_grad = lax.psum_scatter(qkv_w_grad, "z", scatter_dimension=0, tiled=True).reshape(R, rows_dev, 3 * cols)
    normed_grad = sum_halves([query_grad, pair_grad], [weight_q, weight_kv], True, 6, "qkv_grad")
    query_b_grad = column_sums(query_grad)
    input_part, gain_one_grad, bias_one_grad = norm_backward(local, normed_grad, gain_one)

    def sum_to_owners(vectors, axes, parts):
        split = jnp.concatenate([v.reshape(parts, -1) for v in vectors], axis=1)
        summed = jnp.sum(lax.all_to_all(split, axes, split_axis=0, concat_axis=0, tiled=True), axis=0)
        widths = [v.shape[0] // parts for v in vectors]
        return [summed[sum(widths[:i]) : sum(widths[: i + 1])] for i in range(len(widths))]

    qkv_w_grad, out_w_grad = lax.optimization_barrier((qkv_w_grad, out_w_grad))
    device_sums = [gain_one_grad, bias_one_grad, out_b_grad, gain_two_grad, bias_two_grad, down_b_grad]
    if fast:
        rank_sums = jnp.concatenate([v.reshape(Z, -1) for v in (query_b_grad, value_b_grad, up_b_grad)], axis=1)
        here = (jnp.arange(R) == rank).reshape(B, 1, X, 1)
        rank_sums = jnp.where(here, rank_sums[None, :, None, :], 0.0).reshape(R * Z, -1)
        rows = jnp.concatenate([v.reshape(R * Z, -1) for v in device_sums] + [rank_sums], axis=1)
        q_w_shard, k_w_shard, v_w_shard, summed = settle(qkv_w_grad, rows, 9)
        sums = [summed[0, i * rows_dev : (i + 1) * rows_dev] for i in range(len(device_sums) + 2)]
        q_b_shard, v_b_shard = sums[len(device_sums) :]
        up_b_shard = summed[0, (len(device_sums) + 2) * rows_dev :]
    else:
        qkv_w_grad = lax.all_to_all(qkv_w_grad, PLANE, split_axis=0, concat_axis=0, tiled=True)
        q_w_shard, k_w_shard, v_w_shard = [
            from_ranks(qkv_w_grad[..., i : i + cols]).astype(single) for i in range(0, 3 * cols, cols)
        ]
        sums = sum_to_owners(device_sums, ALL, R * Z)
        [up_b_shard] = sum_to_owners([up_b_grad], "z", Z)
    if whole_heads:
        out_w_shard = lax.psum_scatter(out_w_grad.astype(bfloat), "z", scatter_dimension=0, tiled=True).astype(single)
        if not fast:
            q_b_shard, v_b_shard = sum_to_owners([query_b_grad, value_b_grad], "z", Z)
    else:

        def placed(rows):
            full = jnp.zeros((D,) + rows.shape[1:], rows.dtype)
            full = lax.dynamic_update_slice_in_dim(full, rows, rank * cols, 0)
            return lax.psum_scatter(full, ALL, scatter_dimension=0, tiled=True).astype(single)

        out_w_shard = placed(out_w_grad.astype(bfloat))
        q_b_shard = placed(query_b_grad)
        v_b_shard = placed(value_b_grad)
    outputs = middle + active * (branch + bias_down)
    input_grad = middle_grad + input_part
    return (
        outputs.astype(bfloat)[None],
        input_grad.astype(bfloat)[None],
        sums[0],
        sums[1],
        q_w_shard,
        q_b_shard,
        k_w_shard,
        v_w_shard,
        v_b_shard,
        out_w_shard,
        sums[2],
        sums[3],
        sums[4],
        jnp.concatenate([shard_one[:units], shard_two[:units]]).T.astype(single),
        up_b_shard,
        jnp.concatenate([shard_one[units:], shard_two[units:]]).astype(single),
        sums[5],
    )


def solution(mesh):
    groups, parts = mesh.shape["batch"], mesh.shape["seq"]
    inner = Mesh(mesh.devices.reshape(groups, SPANS, parts // SPANS), ("b", "z", "x"))
    token = P("b", ("z", "x"), None)
    vector = P(ALL)
    rows = P(ALL, None)
    columns = P(None, ALL)
    return jax.shard_map(
        on_device,
        mesh=inner,
        in_specs=(
            token,
            P("b", None),
            P("b", None),
            P(),
            token,
            vector,
            vector,
            rows,
            vector,
            rows,
            rows,
            vector,
            rows,
            vector,
            vector,
            vector,
            columns,
            vector,
            rows,
            vector,
        ),
        out_specs=(
            token,
            token,
            vector,
            vector,
            rows,
            vector,
            rows,
            rows,
            vector,
            rows,
            vector,
            vector,
            vector,
            columns,
            vector,
            rows,
            vector,
        ),
        check_vma=False,
    )
```

```python
import functools
from functools import partial

import jax
import jax.numpy as jnp
from jax import lax
from jax.experimental import pallas as pl
from jax.experimental.pallas import tpu as pltpu
from jax.sharding import Mesh
from jax.sharding import PartitionSpec as P

HEAD_DIM = 64
SPANS = 4

bfloat = jnp.bfloat16
single = jnp.float32

PLANE = ("b", "x")
ALL = ("b", "z", "x")
MESH = pl.DeviceIdType.MESH
TILE = 512

def plane_place():
    b, z, x = lax.axis_index("b"), lax.axis_index("z"), lax.axis_index("x")
    sib_b = b + 1 - 2 * lax.rem(b, 2)
    far_b = lax.rem(b + 2, 4)
    far_sib_b = lax.rem(sib_b + 2, 4)
    ids = {"s": (sib_b, z, x), "x": (b, z, 1 - x), "y": (far_b, z, x)}
    ranks = {
        "o": b * 2 + x,
        "s": sib_b * 2 + x,
        "x": b * 2 + 1 - x,
        "xs": sib_b * 2 + 1 - x,
        "y": far_b * 2 + x,
        "ys": far_sib_b * 2 + x,
        "d": far_b * 2 + 1 - x,
        "ds": far_sib_b * 2 + 1 - x,
    }
    return ids, ranks

def greet(ids):
    barrier = pltpu.get_barrier_semaphore()
    for device in ids.values():
        pl.semaphore_signal(barrier, inc=1, device_id=device, device_id_type=MESH)
    pl.semaphore_wait(barrier, len(ids))

def tiles(lo, hi, body):
    def step(i, _):
        body(pl.ds(pl.multiple_of(i * TILE, TILE), TILE))
        return 0
    lax.fori_loop(lo // TILE, hi // TILE, step, 0)

def gather_kernel(body_of, n_in, n_out, x_ref, *refs):
    ins = refs[:n_in]; all_ref = refs[n_in]; outs = refs[n_in + 1 : n_in + 1 + n_out]
    held, send, recv, keep = refs[n_in + 1 + n_out :]
    ids, at = plane_place()
    half = x_ref.shape[0] // 2
    parts = (pl.ds(0, half), pl.ds(half, half))
    greet(ids)
    count = [0]
    started = []
    def ship(src, dst, to):
        n = count[0]; count[0] += 1
        c = pltpu.make_async_remote_copy(src_ref=src, dst_ref=dst, send_sem=send.at[n], recv_sem=recv.at[n], device_id=ids[to], device_id_type=MESH)
        c.start(); started.append(c)
        return c
    own = at["o"]
    x0 = ship(x_ref.at[parts[0]], held.at[own, parts[0]], "x")
    y1 = ship(x_ref.at[parts[1]], held.at[own, parts[1]], "y")
    x1 = ship(x_ref.at[parts[1]], held.at[own, parts[1]], "x")
    y0 = ship(x_ref.at[parts[0]], held.at[own, parts[0]], "y")
    s0 = ship(x_ref, held.at[own], "s")
    kept = []
    def done(rank, src):
        c = pltpu.make_async_copy(src, all_ref.at[rank], keep.at[len(kept)])
        c.start(); kept.append(c)
        if body_of is not None:
            body_of(rank, src, ins, outs)
    done(own, x_ref)
    s0.wait_recv()
    done(at["s"], held.at[at["s"]])
    x0.wait_recv()
    ry = ship(held.at[at["x"], parts[0]], held.at[at["x"], parts[0]], "y")
    y1.wait_recv()
    rx = ship(held.at[at["y"], parts[1]], held.at[at["y"], parts[1]], "x")
    x1.wait_recv()
    sx = ship(held.at[at["x"]], held.at[at["x"]], "s")
    y0.wait_recv()
    sy = ship(held.at[at["y"]], held.at[at["y"]], "s")
    done(at["x"], held.at[at["x"]])
    done(at["y"], held.at[at["y"]])
    sx.wait_recv()
    done(at["xs"], held.at[at["xs"]])
    sy.wait_recv()
    done(at["ys"], held.at[at["ys"]])
    ry.wait_recv(); rx.wait_recv()
    sd = ship(held.at[at["d"]], held.at[at["d"]], "s")
    done(at["d"], held.at[at["d"]])
    sd.wait_recv()
    done(at["ds"], held.at[at["ds"]])
    for c in started: c.wait_send()
    for c in kept: c.wait()

def vmem(n): return [pl.BlockSpec(memory_space=pltpu.VMEM)] * n

def plane_gather(x, ins, out_types, body_of, cid, name, ranks=8):
    tok, D = x.shape
    res = pl.pallas_call(
        functools.partial(gather_kernel, body_of, len(ins), len(out_types)),
        out_shape=[jax.ShapeDtypeStruct((ranks, tok, D), x.dtype), *out_types],
        in_specs=vmem(1 + len(ins)),
        out_specs=[pl.BlockSpec(memory_space=pl.ANY)] + vmem(len(out_types)),
        scratch_shapes=[pltpu.VMEM((ranks, tok, D), x.dtype), pltpu.SemaphoreType.DMA((10,)), pltpu.SemaphoreType.DMA((10,)), pltpu.SemaphoreType.DMA((8,))],
        compiler_params=pltpu.CompilerParams(collective_id=cid, has_side_effects=True, vmem_limit_bytes=60 << 20),
        cost_estimate=pl.CostEstimate(flops=1 << 30, bytes_accessed=128 << 20, transcendentals=0),
        name=name,
    )(x, *ins)
    return res[0].reshape(ranks * tok, D), *res[1:]

def gather_dot(x, w, bias, out_dtype, turned, cid, name):
    ranks, tok, D = 8, *x.shape
    N = w.shape[0] if turned else w.shape[1]
    tile = min(N, 512) if N % 512 == 0 else 256
    def body(rank, src, ins, outs):
        w_ref, b_ref = ins
        def step(i, _):
            cols = pl.ds(pl.multiple_of(i * tile, tile), tile)
            if turned:
                y = lax.dot_general(src[...], w_ref[cols, :], (((1,), (1,)), ((), ())), preferred_element_type=single)
            else:
                y = jnp.dot(src[...], w_ref[:, cols], preferred_element_type=single)
            outs[0][rank, :, cols] = (y + b_ref[:, cols]).astype(out_dtype)
            return 0
        lax.fori_loop(0, N // tile, step, 0)
    all_, y = plane_gather(x, (w, bias), [jax.ShapeDtypeStruct((ranks, tok, N), out_dtype)], body, cid, name)
    return all_, y.reshape(ranks * tok, N)

def reduce_kernel(turned, pairs, *refs):
    left, right = refs[:pairs], refs[pairs : 2 * pairs]
    out_ref, sib_out, sib_in, stage, landed, send, recv = refs[2 * pairs :]
    ids, at = plane_place()
    D = out_ref.shape[1]
    mid = D // 2
    greet(ids)
    count = [0]; started = []
    def ship(src, dst, to):
        n = count[0]; count[0] += 1
        c = pltpu.make_async_remote_copy(src_ref=src, dst_ref=dst, send_sem=send.at[n], recv_sem=recv.at[n], device_id=ids[to], device_id_type=MESH)
        c.start(); started.append(c)
        return c
    def term(rank, cols):
        if turned:
            return sum(dot_nt(a[rank], w[cols, :]) for a, w in zip(left, right))
        rows = [w[:, 1, :, cols].reshape(-1, TILE) if len(w.shape) == 4 else w[:, cols] for w in right]
        return sum(dot(a[rank], w) for a, w in zip(left, rows))
    order = ("d", "x", "y", "o")
    twin = {"d": "ds", "x": "xs", "y": "ys", "o": "s"}
    sib = {}
    def to_sibling(j, h):
        def fill(cols):
            sib_out[j, h, :, local(h, cols)] = term(at[twin[order[j]]], cols).astype(bfloat)
        tiles(h * mid, (h + 1) * mid, fill)
        sib[j, h] = ship(sib_out.at[j, h], sib_in.at[j, h], "s")
    def local(h, cols):
        return pl.ds(pl.multiple_of(cols.start - h * mid, TILE), TILE)
    def pair(j, h, cols):
        return term(at[order[j]], cols) + sib_in[j, h, :, local(h, cols)].astype(single)
    def put(j, h, extra=None):
        sib[j, h].wait_recv()
        def fill(cols):
            value = pair(j, h, cols)
            if extra is not None:
                value = value + landed[extra, :, local(h, cols)].astype(single)
            stage[j, h, :, local(h, cols)] = value.astype(bfloat)
        tiles(h * mid, (h + 1) * mid, fill)
    to_sibling(0, 0)
    to_sibling(0, 1)
    put(0, 0)
    d_a = ship(stage.at[0, 0], landed.at[0], "x")
    put(0, 1)
    d_b = ship(stage.at[0, 1], landed.at[1], "y")
    to_sibling(1, 0)
    to_sibling(2, 1)
    put(1, 0)
    x_a = ship(stage.at[1, 0], landed.at[2], "x")
    put(2, 1)
    y_b = ship(stage.at[2, 1], landed.at[3], "y")
    for j, h in ((1, 1), (2, 0), (3, 0), (3, 1)):
        to_sibling(j, h)
    d_b.wait_recv()
    put(1, 1, extra=1)
    x_b = ship(stage.at[1, 1], landed.at[5], "x")
    d_a.wait_recv()
    put(2, 0, extra=0)
    y_a = ship(stage.at[2, 0], landed.at[4], "y")
    for h in range(2):
        sib[3, h].wait_recv()
        def first(cols, h=h):
            out_ref[:, cols] = pair(3, h, cols)
        tiles(h * mid, (h + 1) * mid, first)
    x_a.wait_recv(); y_b.wait_recv(); x_b.wait_recv(); y_a.wait_recv()
    for h, (n, m) in enumerate(((2, 4), (3, 5))):
        def add(cols, h=h, n=n, m=m):
            c = local(h, cols)
            out_ref[:, cols] = out_ref[:, cols] + landed[n, :, c].astype(single) + landed[m, :, c].astype(single)
        tiles(h * mid, (h + 1) * mid, add)
    for c in started: c.wait_send()

def dot_reduce(left, right, turned, cid, name):
    ranks = 8
    D = right[0].shape[0] if turned else right[0].shape[-1]
    tok = left[0].size // left[0].shape[-1] // ranks
    return pl.pallas_call(
        functools.partial(reduce_kernel, turned, len(left)),
        out_shape=jax.ShapeDtypeStruct((tok, D), single),
        in_specs=vmem(2 * len(left)), out_specs=vmem(1)[0],
        scratch_shapes=[pltpu.VMEM((4, 2, tok, D // 2), bfloat), pltpu.VMEM((4, 2, tok, D // 2), bfloat), pltpu.VMEM((3, 2, tok, D // 2), bfloat), pltpu.VMEM((6, tok, D // 2), bfloat),
            pltpu.SemaphoreType.DMA((14,)), pltpu.SemaphoreType.DMA((14,))],
        compiler_params=pltpu.CompilerParams(collective_id=cid, has_side_effects=True, vmem_limit_bytes=60 << 20),
        cost_estimate=pl.CostEstimate(flops=1 << 30, bytes_accessed=128 << 20, transcendentals=0),
        name=name,
    )(*[a.reshape(ranks, tok, -1) for a in left], *right)


def dot(left, right):
    return jnp.dot(left, right, preferred_element_type=single)


def dot_tn(left, right):
    return lax.dot_general(left, right, (((0,), (0,)), ((), ())), preferred_element_type=single)


def dot_nt(left, right):
    return lax.dot_general(left, right, (((1,), (1,)), ((), ())), preferred_element_type=single)


def layer_norm(values, gain_vec, shift_vec):
    center = jnp.mean(values, axis=-1, keepdims=True)
    centered = values - center
    spread = jnp.mean(centered * centered, axis=-1, keepdims=True)
    return centered * lax.rsqrt(spread + 1e-05) * gain_vec + shift_vec


def column_sums(matrix):
    return jnp.sum(matrix.astype(single), axis=0)


def shipper(send, recv, ids):
    started = []

    def ship(src, dst, to):
        n = len(started)
        copy = pltpu.make_async_remote_copy(
            src_ref=src, dst_ref=dst, send_sem=send.at[n], recv_sem=recv.at[n], device_id=ids[to], device_id_type=MESH
        )
        copy.start()
        started.append(copy)
        return copy

    return ship, started


TWIN = {"o": "s", "x": "xs", "y": "ys", "d": "ds"}


def unit_rows(w_ref, i):
    parts, _, units, D = w_ref.shape
    return w_ref[:, i].reshape(parts * units, D)


def hidden_units(src, branch, w_ref, b_ref, hid_ref, pg_ref, pb_ref, rank):
    pre = dot_nt(src[...], unit_rows(w_ref, 0)) + b_ref[...]
    square = pre * pre
    bend = jnp.tanh(0.7978845608028654 * (pre + 0.044715 * (pre * square)))
    rise = 0.5 * (1.0 + bend)
    hid_ref[rank] = (pre * rise).astype(bfloat)
    slope = rise + (0.5 * 0.7978845608028654) * pre * (1.0 - bend * bend) * (1.0 + 3 * 0.044715 * square)
    grad = (dot_nt(branch[...], unit_rows(w_ref, 1)) * slope).astype(bfloat)
    pg_ref[rank] = grad
    pb_ref[...] += jnp.sum(grad.astype(single), axis=0, keepdims=True)


def first_units_kernel(
    x_ref, bg_ref, w_ref, b_ref, all_ref, hid_ref, pg_ref, pb_ref, grad_ref,
    held, bg, total, send, recv, keep, load,
):
    ids, at = plane_place()
    tok = x_ref.shape[0]
    half = tok // 2
    parts = (pl.ds(0, half), pl.ds(half, half))
    own = at["o"]
    loads = {}
    for n, name in enumerate(at):
        loads[name] = pltpu.make_async_copy(bg_ref.at[at[name]], bg.at[at[name]], load.at[n])
    loads["o"].start()
    greet(ids)
    ship, started = shipper(send, recv, ids)
    x0 = ship(x_ref.at[parts[0]], held.at[own, parts[0]], "x")
    y1 = ship(x_ref.at[parts[1]], held.at[own, parts[1]], "y")
    x1 = ship(x_ref.at[parts[1]], held.at[own, parts[1]], "x")
    y0 = ship(x_ref.at[parts[0]], held.at[own, parts[0]], "y")
    s0 = ship(x_ref, held.at[own], "s")
    pb_ref[...] = jnp.zeros_like(pb_ref)
    kept = []

    def units(name):
        rank = at[name]
        src = x_ref if name == "o" else held.at[rank]
        copy = pltpu.make_async_copy(src, all_ref.at[rank], keep.at[len(kept)])
        copy.start()
        kept.append(copy)
        loads[name].wait()
        if name == "o":
            for other in loads:
                if other != "o":
                    loads[other].start()
        hidden_units(src, bg.at[rank], w_ref, b_ref, hid_ref, pg_ref, pb_ref, rank)

    def weigh(name, last=False):
        units_at = grad_ref.shape[2]
        per = 256 // units_at

        def rows(i, _):
            here = pl.ds(pl.multiple_of(i * 256, 256), 256)
            owners = pl.ds(i * per, per)
            for j, left in enumerate((pg_ref, hid_ref)):
                term = 0
                for n in (name, TWIN[name]):
                    right = bg[at[n]] if j else (x_ref[...] if n == "o" else held[at[n]])
                    term = term + dot_tn(left[at[n], :, here], right)
                term = term.reshape(per, units_at, -1)
                if name == "o":
                    total[owners, j] = term
                elif last:
                    grad_ref[owners, j] = (total[owners, j] + term).astype(bfloat)
                else:
                    total[owners, j] += term
            return 0

        lax.fori_loop(0, hid_ref.shape[2] // 256, rows, 0)

    units("o")
    s0.wait_recv()
    units("s")
    x0.wait_recv()
    ry = ship(held.at[at["x"], parts[0]], held.at[at["x"], parts[0]], "y")
    y1.wait_recv()
    rx = ship(held.at[at["y"], parts[1]], held.at[at["y"], parts[1]], "x")
    weigh("o")
    x1.wait_recv()
    sx = ship(held.at[at["x"]], held.at[at["x"]], "s")
    y0.wait_recv()
    sy = ship(held.at[at["y"]], held.at[at["y"]], "s")
    units("x")
    sx.wait_recv()
    units("xs")
    units("y")
    sy.wait_recv()
    units("ys")
    weigh("x")
    ry.wait_recv()
    rx.wait_recv()
    sd = ship(held.at[at["d"]], held.at[at["d"]], "s")
    weigh("y")
    units("d")
    sd.wait_recv()
    units("ds")
    weigh("d", last=True)
    for copy in started:
        copy.wait_send()
    for copy in kept:
        copy.wait()


def last_units_kernel(
    all_ref, bg_ref, pg1_ref, w1_ref, w_ref, b_ref, hid_ref, pb_ref, r_ref, grad_ref,
    held, bg, pg_ref, sib_out, sib_in, stage, landed, send, recv, load, load_b,
):
    ids, at = plane_place()
    ranks, tok, D = held.shape
    mid = D // 2
    names = ("ds", "d", "xs", "x", "ys", "y", "s", "o")
    loads = {}
    for n, name in enumerate(names):
        loads[name] = [
            pltpu.make_async_copy(all_ref.at[at[name]], held.at[at[name]], load.at[n]),
            pltpu.make_async_copy(bg_ref.at[at[name]], bg.at[at[name]], load_b.at[n]),
        ]
    for name in names[:2]:
        for copy in loads[name]:
            copy.start()
    greet(ids)
    ship, started = shipper(send, recv, ids)
    pb_ref[...] = jnp.zeros_like(pb_ref)

    def units(name):
        for copy in loads[name]:
            copy.wait()
        if name == names[0]:
            for other in names[2:]:
                for copy in loads[other]:
                    copy.start()
        rank = at[name]
        hidden_units(held.at[rank], bg.at[rank], w_ref, b_ref, hid_ref, pg_ref, pb_ref, rank)

    def term(name, cols):
        rank = at[name]
        first, second = [w[:, 0, :, cols].reshape(-1, TILE) for w in (w1_ref, w_ref)]
        return dot(pg1_ref[rank], first) + dot(pg_ref[rank], second)

    order = ("d", "x", "y", "o")

    def to_sibling(j):
        def fill(cols):
            sib_out[j, :, cols] = term(TWIN[order[j]], cols).astype(bfloat)

        tiles(0, D, fill)
        return ship(sib_out.at[j], sib_in.at[j], "s")

    def pair(j, cols):
        return term(order[j], cols) + sib_in[j, :, cols].astype(single)

    def local(h, cols):
        return pl.ds(pl.multiple_of(cols.start - h * mid, TILE), TILE)

    def put(j, h, extra=None):
        def fill(cols):
            value = pair(j, cols)
            if extra is not None:
                value = value + landed[extra, :, local(h, cols)].astype(single)
            stage[j, h, :, local(h, cols)] = value.astype(bfloat)

        tiles(h * mid, (h + 1) * mid, fill)

    units("ds")
    d_sib = to_sibling(0)
    units("d")
    d_sib.wait_recv()
    put(0, 0)
    d_a = ship(stage.at[0, 0], landed.at[0], "x")
    put(0, 1)
    d_b = ship(stage.at[0, 1], landed.at[1], "y")
    units("xs")
    x_sib = to_sibling(1)
    units("x")
    x_sib.wait_recv()
    put(1, 0)
    x_a = ship(stage.at[1, 0], landed.at[2], "x")
    units("ys")
    y_sib = to_sibling(2)
    units("y")
    y_sib.wait_recv()
    put(2, 1)
    y_b = ship(stage.at[2, 1], landed.at[3], "y")
    d_b.wait_recv()
    put(1, 1, extra=1)
    x_b = ship(stage.at[1, 1], landed.at[5], "x")
    d_a.wait_recv()
    put(2, 0, extra=0)
    y_a = ship(stage.at[2, 0], landed.at[4], "y")
    units("s")
    own_sib = to_sibling(3)
    units("o")
    own_sib.wait_recv()

    def first(cols):
        r_ref[:, cols] = pair(3, cols)

    tiles(0, D, first)

    units_at = grad_ref.shape[2]
    per = 256 // units_at
    tokens = ranks * tok

    def grads(i, _):
        here = pl.ds(pl.multiple_of(i * 256, 256), 256)
        owners = pl.ds(i * per, per)
        for j, (left, right) in enumerate(((pg_ref, held), (hid_ref, bg))):
            value = dot_tn(left[:, :, here].reshape(tokens, 256), right[...].reshape(tokens, D))
            grad_ref[owners, j] = value.astype(bfloat).reshape(per, units_at, D)
        return 0

    lax.fori_loop(0, hid_ref.shape[2] // 256, grads, 0)
    for copy in (x_a, y_b, x_b, y_a):
        copy.wait_recv()
    for h, (n, m) in enumerate(((2, 4), (3, 5))):

        def add(cols, h=h, n=n, m=m):
            c = local(h, cols)
            r_ref[:, cols] = r_ref[:, cols] + landed[n, :, c].astype(single) + landed[m, :, c].astype(single)

        tiles(h * mid, (h + 1) * mid, add)
    for copy in started:
        copy.wait_send()


def first_units(x, bg, w, bias, cid):
    ranks = 8
    tok, D = x.shape
    F = bias.shape[1]
    anywhere = pl.BlockSpec(memory_space=pl.ANY)
    inside = pl.BlockSpec(memory_space=pltpu.VMEM)
    return pl.pallas_call(
        first_units_kernel,
        out_shape=[
            jax.ShapeDtypeStruct((ranks, tok, D), bfloat),
            jax.ShapeDtypeStruct((ranks, tok, F), bfloat),
            jax.ShapeDtypeStruct((ranks, tok, F), bfloat),
            jax.ShapeDtypeStruct((1, F), single),
            jax.ShapeDtypeStruct(w.shape, bfloat),
        ],
        in_specs=[inside, anywhere, inside, inside],
        out_specs=[anywhere, inside, inside, inside, inside],
        scratch_shapes=[
            pltpu.VMEM((ranks, tok, D), bfloat),
            pltpu.VMEM((ranks, tok, D), bfloat),
            pltpu.VMEM(w.shape, single),
            pltpu.SemaphoreType.DMA((10,)),
            pltpu.SemaphoreType.DMA((10,)),
            pltpu.SemaphoreType.DMA((8,)),
            pltpu.SemaphoreType.DMA((8,)),
        ],
        compiler_params=pltpu.CompilerParams(collective_id=cid, has_side_effects=True, vmem_limit_bytes=62 << 20),
        cost_estimate=pl.CostEstimate(flops=1 << 30, bytes_accessed=160 << 20, transcendentals=0),
        name="first_units",
    )(x, bg, w, bias)


def last_units(rows, bg, pg, w1, w, bias, cid):
    ranks, tok, D = rows.shape
    F = bias.shape[1]
    anywhere = pl.BlockSpec(memory_space=pl.ANY)
    inside = pl.BlockSpec(memory_space=pltpu.VMEM)
    return pl.pallas_call(
        last_units_kernel,
        out_shape=[
            jax.ShapeDtypeStruct((ranks, tok, F), bfloat),
            jax.ShapeDtypeStruct((1, F), single),
            jax.ShapeDtypeStruct((tok, D), single),
            jax.ShapeDtypeStruct(w.shape, bfloat),
        ],
        in_specs=[anywhere, anywhere, inside, inside, inside, inside],
        out_specs=[inside] * 4,
        scratch_shapes=[
            pltpu.VMEM((ranks, tok, D), bfloat),
            pltpu.VMEM((ranks, tok, D), bfloat),
            pltpu.VMEM((ranks, tok, F), bfloat),
            pltpu.VMEM((4, tok, D), bfloat),
            pltpu.VMEM((4, tok, D), bfloat),
            pltpu.VMEM((3, 2, tok, D // 2), bfloat),
            pltpu.VMEM((6, tok, D // 2), bfloat),
            pltpu.SemaphoreType.DMA((10,)),
            pltpu.SemaphoreType.DMA((10,)),
            pltpu.SemaphoreType.DMA((8,)),
            pltpu.SemaphoreType.DMA((8,)),
        ],
        compiler_params=pltpu.CompilerParams(collective_id=cid, has_side_effects=True, vmem_limit_bytes=62 << 20),
        cost_estimate=pl.CostEstimate(flops=1 << 30, bytes_accessed=160 << 20, transcendentals=0),
        name="last_units",
    )(rows, bg, pg, w1, w, bias)


def everyone(width):
    b, z, x = lax.axis_index("b"), lax.axis_index("z"), lax.axis_index("x")
    rank, me = b * 2 + x, (b * 4 + z) * 2 + x

    def in_plane(i):
        other = lax.rem(rank + i, 8)
        return other, (other // 2, z, lax.rem(other, 2))

    def anywhere(i):
        other = lax.rem(me + i, width)
        return other, (other // 8, lax.rem(other // 2, 4), lax.rem(other, 2))

    return rank, me, in_plane, anywhere


def exchange(blocks, landed, rows, gathered, same_row, sems):
    plane_send, plane_recv, all_send, all_recv = sems
    width = gathered.shape[0]
    rank, me, in_plane, anywhere = everyone(width)
    barrier = pltpu.get_barrier_semaphore()

    def each(count, body):
        def step(i, _):
            body(i)
            return 0

        lax.fori_loop(1, count, step, 0)

    each(width, lambda i: pl.semaphore_signal(barrier, inc=1, device_id=anywhere(i)[1], device_id_type=MESH))
    pl.semaphore_wait(barrier, width - 1)

    def block(i):
        other, device = in_plane(i)
        return pltpu.make_async_remote_copy(
            src_ref=blocks.at[other], dst_ref=landed.at[rank], send_sem=plane_send.at[i], recv_sem=plane_recv.at[i],
            device_id=device, device_id_type=MESH,
        )

    def row(i):
        other, device = anywhere(i)
        return pltpu.make_async_remote_copy(
            src_ref=rows.at[0] if same_row else rows.at[other], dst_ref=gathered.at[me],
            send_sem=all_send.at[i], recv_sem=all_recv.at[i], device_id=device, device_id_type=MESH,
        )

    each(8, lambda i: block(i).start())
    each(width, lambda i: row(i).start())
    landed[rank] = blocks[rank]
    gathered[me] = rows[0] if same_row else rows[me]
    each(width, lambda i: row(i).wait())
    each(8, lambda i: block(i).wait())


def head_at(rank, i):
    return (rank // 2 * 4 + i) * 2 + rank % 2


def spread_kernel(q_ref, k_ref, v_ref, pack_ref, q_out, kv_out, pack_out, blocks, landed, gathered, *sems):
    cols = q_out.shape[2]
    for rank in range(8):
        for part, ref in enumerate((q_ref, k_ref, v_ref)):
            heads = [ref[:, head_at(rank, i) * HEAD_DIM : (head_at(rank, i) + 1) * HEAD_DIM] for i in range(4)]
            blocks[rank, :, part * cols : (part + 1) * cols] = jnp.concatenate(heads, axis=1)
    exchange(blocks, landed, pack_ref, gathered, True, sems)
    q_out[...] = landed[:, :, :cols]
    kv_out[...] = landed[:, :, cols:]
    pack_out[...] = gathered[...]


def settle_kernel(w_ref, rows_ref, q_out, k_out, v_out, sums_ref, landed, gathered, *sems):
    cols = w_ref.shape[2] // 3
    exchange(w_ref, landed, rows_ref, gathered, False, sems)
    for part, out in enumerate((q_out, k_out, v_out)):
        for pair in range(out.shape[1] // 128):
            sides = []
            for head in (2 * pair, 2 * pair + 1):
                rank, i = head // 8 * 2 + head % 2, head // 2 % 4
                at = part * cols + i * HEAD_DIM
                sides.append(landed[rank, :, at : at + HEAD_DIM])
            out[:, pair * 128 : (pair + 1) * 128] = jnp.concatenate(sides, axis=1)
    sums_ref[...] = jnp.sum(gathered[...], axis=0)


def exchange_call(kernel, out_shape, args, blocks, landed, gathered, cid, name):
    inside = pl.BlockSpec(memory_space=pltpu.VMEM)
    width = gathered[0]
    return pl.pallas_call(
        kernel,
        out_shape=out_shape,
        in_specs=[inside] * len(args),
        out_specs=[inside] * len(out_shape),
        scratch_shapes=blocks
        + [
            pltpu.VMEM(landed, bfloat),
            pltpu.VMEM(gathered, single),
            pltpu.SemaphoreType.DMA((8,)),
            pltpu.SemaphoreType.DMA((8,)),
            pltpu.SemaphoreType.DMA((width,)),
            pltpu.SemaphoreType.DMA((width,)),
        ],
        compiler_params=pltpu.CompilerParams(collective_id=cid, has_side_effects=True, vmem_limit_bytes=32 << 20),
        cost_estimate=pl.CostEstimate(flops=1 << 20, bytes_accessed=32 << 20, transcendentals=0),
        name=name,
    )(*args)


def spread(q, k, v, pack, devices, cid):
    rows, D = q.shape
    cols = D // 8
    return exchange_call(
        spread_kernel,
        [
            jax.ShapeDtypeStruct((8, rows, cols), bfloat),
            jax.ShapeDtypeStruct((8, rows, 2 * cols), bfloat),
            jax.ShapeDtypeStruct((devices, 1, pack.shape[0]), single),
        ],
        (q, k, v, pack[None, None]),
        [pltpu.VMEM((8, rows, 3 * cols), bfloat)],
        (8, rows, 3 * cols),
        (devices, 1, pack.shape[0]),
        cid,
        "spread",
    )


def settle(weights, rows, cid):
    _, tall, wide = weights.shape
    D = wide // 3 * 8
    return exchange_call(
        settle_kernel,
        [jax.ShapeDtypeStruct((tall, D), bfloat)] * 3 + [jax.ShapeDtypeStruct((1, rows.shape[1]), single)],
        (weights, rows[:, None]),
        [],
        weights.shape,
        (rows.shape[0], 1, rows.shape[1]),
        cid,
        "settle",
    )


def windows(span):
    block = span // 2
    return [(i * block, i * block + block + span) for i in range(2)]

def key_window(before, own, lo, hi, span):
    if lo >= span:
        return own[lo - span : hi - span]
    return jnp.concatenate([before[lo:span], own[0 : hi - span]], axis=0)

def hidden_bias(start_ref, i, block, lo, hi, span):
    rows = span + i * block + lax.broadcasted_iota(jnp.int32, (block, hi - lo), 0)
    keys = lo + lax.broadcasted_iota(jnp.int32, (block, hi - lo), 1)
    start = start_ref[i * block : (i + 1) * block, :]
    return jnp.where((keys >= start) & (keys <= rows), 0.0, -1e30).astype(single)

def each_window(first_ref, span, body):
    block = span // 2
    for i, (lo, hi) in enumerate(windows(span)):
        begins = first_ref[pl.program_id(0) * 2 + i]
        pl.when(begins >= lo + block)(functools.partial(body, i, lo + block, hi))
        pl.when(begins < lo + block)(functools.partial(body, i, lo, hi))


def attend_kernel(first_ref, start_ref, q_ref, k_ref, v_ref, kb_ref, vb_ref, out_ref):
    span, cols = q_ref.shape
    block = span // 2

    def body(i, lo, hi):
        lane = lax.broadcasted_iota(jnp.int32, (block, cols), 1) // HEAD_DIM
        rows = pl.ds(i * block, block)
        bias = hidden_bias(start_ref, i, block, lo, hi, span)
        keys = key_window(kb_ref, k_ref, lo, hi, span)
        vals = key_window(vb_ref, v_ref, lo, hi, span)
        query = q_ref[rows, :] * jnp.asarray(HEAD_DIM ** (-0.5), bfloat)

        def head(h, total):
            mine = lane == h
            scores = dot_nt(jnp.where(mine, query, 0), keys) + bias
            weights = jnp.exp(scores - jnp.max(scores, axis=1, keepdims=True))
            part = jnp.dot(weights.astype(bfloat), vals, preferred_element_type=single)
            part = part * (1.0 / jnp.sum(weights, axis=1, keepdims=True))
            return jnp.where(mine, part, total)

        total = lax.fori_loop(0, cols // HEAD_DIM, head, jnp.zeros((block, cols), single), unroll=True)
        out_ref[rows, :] = total.astype(bfloat)

    each_window(first_ref, span, body)


def attend_back_kernel(
    first_ref, start_ref, q_ref, k_ref, v_ref, kb_ref, vb_ref, do_ref, dq_ref, edge_ref, pair_ref, dk, dv
):
    span, cols = q_ref.shape
    block = span // 2
    scale = HEAD_DIM ** (-0.5)
    dk[...] = jnp.zeros_like(dk)
    dv[...] = jnp.zeros_like(dv)

    def body(i, lo, hi):
        lane = lax.broadcasted_iota(jnp.int32, (block, cols), 1) // HEAD_DIM
        rows = pl.ds(i * block, block)
        bias = hidden_bias(start_ref, i, block, lo, hi, span)
        keys = key_window(kb_ref, k_ref, lo, hi, span)
        vals = key_window(vb_ref, v_ref, lo, hi, span)
        query = q_ref[rows, :] * jnp.asarray(scale, bfloat)
        grad = do_ref[rows, :]

        def head(h, total):
            mine = lane == h
            query_h = jnp.where(mine, query, 0)
            grad_h = jnp.where(mine, grad, 0)
            scores = dot_nt(query_h, keys) + bias
            weights = jnp.exp(scores - jnp.max(scores, axis=1, keepdims=True))
            probs = weights * (1.0 / jnp.sum(weights, axis=1, keepdims=True))
            prob_grad = dot_nt(grad_h, vals)
            row_dot = jnp.sum(probs * prob_grad, axis=1, keepdims=True)
            score_grad = (probs * (prob_grad - row_dot)).astype(bfloat)
            dv[lo:hi, :] += dot_tn(probs.astype(bfloat), grad_h)
            dk[lo:hi, :] += dot_tn(score_grad, query_h)
            part = jnp.dot(score_grad, keys, preferred_element_type=single)
            return jnp.where(mine, part, total)

        total = lax.fori_loop(0, cols // HEAD_DIM, head, jnp.zeros((block, cols), single), unroll=True)
        dq_ref[rows, :] = (total * scale).astype(bfloat)

    each_window(first_ref, span, body)
    edge_ref[:, :cols] = dk[:span, :].astype(bfloat)
    edge_ref[:, cols:] = dv[:span, :].astype(bfloat)
    pair_ref[:, :cols] = dk[span:, :]
    pair_ref[:, cols:] = dv[span:, :]


def pair_grads_kernel(pair_ref, after_ref, normed_ref, query_w_ref, grad_ref, weight_ref, bias_ref):
    block = pl.program_id(0)
    cols = query_w_ref.shape[1]
    rows = weight_ref.shape[3]

    @pl.when(block == 0)
    def _():
        grad = (pair_ref[...] + after_ref[...].astype(single)).astype(bfloat)
        grad_ref[...] = grad
        bias_ref[...] = jnp.sum(grad[:, cols:].astype(single), axis=0, keepdims=True)

    value = dot_tn(normed_ref[...], grad_ref[...]).astype(bfloat)
    xs = weight_ref.shape[2]
    for z in range(weight_ref.shape[0]):
        for x in range(xs):
            here = slice((z * xs + x) * rows, (z * xs + x + 1) * rows)
            weight_ref[z, 0, x, :, :cols] = query_w_ref[here, :]
            weight_ref[z, 0, x, :, cols:] = value[here, :]


def pair_grads(pair, after, normed, query_w, B, Z, X):
    tokens, wide = pair.shape
    D = normed.shape[1]
    per = D // B
    rows = per // (Z * X)
    cols = query_w.shape[1]
    return pl.pallas_call(
        pair_grads_kernel,
        grid=(B,),
        out_shape=[
            jax.ShapeDtypeStruct((tokens, wide), bfloat),
            jax.ShapeDtypeStruct((Z, B, X, rows, cols + wide), bfloat),
            jax.ShapeDtypeStruct((1, wide - cols), single),
        ],
        in_specs=[
            pl.BlockSpec((tokens, wide), lambda b: (0, 0)),
            pl.BlockSpec((tokens, wide), lambda b: (0, 0)),
            pl.BlockSpec((tokens, per), lambda b: (0, b)),
            pl.BlockSpec((per, cols), lambda b: (b, 0)),
        ],
        out_specs=[
            pl.BlockSpec((tokens, wide), lambda b: (0, 0)),
            pl.BlockSpec((Z, 1, X, rows, cols + wide), lambda b: (0, b, 0, 0, 0)),
            pl.BlockSpec((1, wide - cols), lambda b: (0, 0)),
        ],
        compiler_params=pltpu.CompilerParams(vmem_limit_bytes=48 << 20),
        name="pair_grads",
    )(pair, after, normed, query_w)


def block_starts(starts, groups):
    return starts.reshape(groups * 2, -1)[:, 0]


def attention_specs(span, cols):
    def at(j):
        return pl.BlockSpec((span, cols), lambda g, _: (g, j))
    return [pl.BlockSpec((span, 1), lambda g, _: (g, 0)), at(0), at(0), at(1), at(0), at(1)]

def attend(starts, query, key_value, before, groups):
    span, cols = query.shape[0] // groups, query.shape[1]
    return pl.pallas_call(
        attend_kernel,
        out_shape=jax.ShapeDtypeStruct((groups * span, cols), bfloat),
        grid_spec=pltpu.PrefetchScalarGridSpec(
            num_scalar_prefetch=1,
            grid=(groups,),
            in_specs=attention_specs(span, cols),
            out_specs=pl.BlockSpec((span, cols), lambda g, _: (g, 0)),
        ),
        compiler_params=pltpu.CompilerParams(vmem_limit_bytes=60 << 20),
        name="attend",
    )(block_starts(starts, groups), starts, query, key_value, key_value, before, before)

def attend_back(starts, query, key_value, before, grad, groups):
    span, cols = query.shape[0] // groups, query.shape[1]
    rows = groups * span
    return pl.pallas_call(
        attend_back_kernel,
        out_shape=[
            jax.ShapeDtypeStruct((rows, cols), bfloat),
            jax.ShapeDtypeStruct((rows, 2 * cols), bfloat),
            jax.ShapeDtypeStruct((rows, 2 * cols), single),
        ],
        grid_spec=pltpu.PrefetchScalarGridSpec(
            num_scalar_prefetch=1,
            grid=(groups,),
            in_specs=attention_specs(span, cols) + [pl.BlockSpec((span, cols), lambda g, _: (g, 0))],
            out_specs=[pl.BlockSpec((span, cols), lambda g, _: (g, 0))]
            + [pl.BlockSpec((span, 2 * cols), lambda g, _: (g, 0))] * 2,
            scratch_shapes=[pltpu.VMEM((2 * span, cols), single)] * 2,
        ),
        compiler_params=pltpu.CompilerParams(vmem_limit_bytes=60 << 20),
        name="attend_back",
    )(block_starts(starts, groups), starts, query, key_value, key_value, before, before, grad)


def attention_heads(starts, query, key_value, before, groups):
    span, cols = query.shape[0] // groups, query.shape[1]
    both = jnp.concatenate([before.reshape(groups, span, -1), key_value.reshape(groups, span, -1)], axis=1)
    key_two, value_two = [both[..., i * cols : (i + 1) * cols].reshape(groups, 2 * span, -1, HEAD_DIM) for i in (0, 1)]
    query = query.reshape(groups, span, -1, HEAD_DIM)
    keys = jnp.arange(2 * span)[None, None, :]
    rows = span + jnp.arange(span)[None, :, None]
    allowed = (keys >= starts.reshape(groups, span, 1)) & (keys <= rows)
    scores = jnp.einsum("gqhd,gkhd->ghqk", query, key_two, preferred_element_type=single) * HEAD_DIM ** (-0.5)
    scores = jnp.where(allowed[:, None], scores, -1e30)
    weights = jnp.exp(scores - jnp.max(scores, axis=-1, keepdims=True))
    return query, key_two, value_two, weights / jnp.sum(weights, axis=-1, keepdims=True)


def attention_forward(starts, query, key_value, before, groups):
    if query.shape[1] % 128 == 0:
        return attend(starts, query, key_value, before, groups)
    _, _, value_two, probs = attention_heads(starts, query, key_value, before, groups)
    context = jnp.einsum("ghqk,gkhd->gqhd", probs.astype(bfloat), value_two, preferred_element_type=single)
    return context.astype(bfloat).reshape(query.shape)


def attention_backward(starts, query, key_value, before, grad, groups):
    if query.shape[1] % 128 == 0:
        return attend_back(starts, query, key_value, before, grad, groups)
    rows = query.shape[0]
    query, key_two, value_two, probs = attention_heads(starts, query, key_value, before, groups)
    span = query.shape[1]
    grad = grad.reshape(query.shape)
    prob_grad = jnp.einsum("gqhd,gkhd->ghqk", grad, value_two, preferred_element_type=single)
    row_dot = jnp.sum(probs * prob_grad, axis=-1, keepdims=True)
    score_grad = (probs * (prob_grad - row_dot)).astype(bfloat)
    query_grad = jnp.einsum("ghqk,gkhd->gqhd", score_grad, key_two, preferred_element_type=single) * HEAD_DIM ** (-0.5)
    key_grad = jnp.einsum("ghqk,gqhd->gkhd", score_grad, query, preferred_element_type=single) * HEAD_DIM ** (-0.5)
    value_grad = jnp.einsum("ghqk,gqhd->gkhd", probs.astype(bfloat), grad, preferred_element_type=single)
    pair = jnp.concatenate([t.reshape(groups, 2 * span, -1) for t in (key_grad, value_grad)], axis=2)
    edge, pair = [t.reshape(rows, -1) for t in (pair[:, :span].astype(bfloat), pair[:, span:])]
    return query_grad.astype(bfloat).reshape(rows, -1), edge, pair


def norm_backward(values, out_grad, gain_vec):
    center = jnp.mean(values, axis=-1, keepdims=True)
    centered = values - center
    rs = lax.rsqrt(jnp.mean(centered * centered, axis=-1, keepdims=True) + 1e-05)
    xhat = centered * rs
    g = out_grad * gain_vec
    part = rs * (g - jnp.mean(g, axis=-1, keepdims=True) - xhat * jnp.mean(g * xhat, axis=-1, keepdims=True))
    return part, jnp.sum(out_grad * xhat, axis=0), jnp.sum(out_grad, axis=0)


def on_device(
    inputs,
    exit_layers,
    lengths,
    layer_index,
    out_grad,
    ln1_gain,
    ln1_bias,
    q_weight,
    q_bias,
    k_weight,
    v_weight,
    v_bias,
    o_weight,
    o_bias,
    ln2_gain,
    ln2_bias,
    fc1_weight,
    fc1_bias,
    fc2_weight,
    fc2_bias,
):
    B, Z, X = lax.axis_size("b"), lax.axis_size("z"), lax.axis_size("x")
    R = B * X
    local = inputs[0].astype(single)
    tok, D = local.shape
    span = X * tok
    group_tok = Z * span
    at_z, at_x = lax.axis_index("z"), lax.axis_index("x")
    rank = lax.axis_index("b") * X + at_x
    rows_dev = q_weight.shape[0]
    cols = D // R
    heads = cols // HEAD_DIM
    whole_heads = rows_dev % HEAD_DIM == 0
    fast = (B, Z, X, rows_dev) == (4, 4, 2, HEAD_DIM)

    group_active = (exit_layers[0] > layer_index[0]).astype(single)
    active_total = jnp.sum(group_active)
    active = lax.dynamic_slice_in_dim(group_active, at_z * span + at_x * tok, tok, 0)[:, None]

    count = lengths.shape[1]
    upto = jnp.arange(count)[:, None] <= jnp.arange(count)[None, :]
    def to_ranks(matrix):
        lead = matrix.shape[:-1]
        if whole_heads:
            matrix = matrix.reshape(*lead, B, Z, X, rows_dev)
            k = len(lead)
            return matrix.transpose(k, k + 2, *range(k), k + 1, k + 3).reshape(R, *lead, cols)
        return jnp.moveaxis(matrix.reshape(*lead, R, cols), -2, 0)

    def from_ranks(parts):
        if whole_heads:
            parts = parts.reshape(B, X, -1, Z, rows_dev)
            return parts.transpose(2, 0, 3, 1, 4).reshape(-1, D)
        return parts.transpose(1, 0, 2).reshape(-1, D)

    def mine(vector):
        return lax.dynamic_index_in_dim(to_ranks(vector), rank, 0, keepdims=False)

    if whole_heads:
        weight_o = lax.all_gather(o_weight, "z", axis=0, tiled=True)
    else:
        weight_o = lax.dynamic_slice_in_dim(lax.all_gather(o_weight, ALL, axis=0, tiled=True), rank * cols, cols, 0)
    small = [ln1_gain, ln1_bias, q_bias, v_bias, o_bias, ln2_gain, ln2_bias, fc2_bias]
    pack = jnp.concatenate([v.astype(single) for v in (*small, fc1_bias, lengths[0])])
    pack = jnp.concatenate([pack, jnp.zeros((-pack.shape[0] % 128,), single)])
    if fast:
        query_mine, pair_mine, pack = spread(q_weight, k_weight, v_weight, pack, R * Z, 8)
        query_mine, pair_mine, pack = query_mine.reshape(-1, cols), pair_mine.reshape(-1, 2 * cols), pack[:, 0]
    else:
        qkv_parts = jnp.concatenate([to_ranks(q_weight), to_ranks(k_weight), to_ranks(v_weight)], axis=2)
        qkv_mine = lax.all_to_all(qkv_parts, PLANE, split_axis=0, concat_axis=0, tiled=True).reshape(D // Z, 3 * cols)
        query_mine, pair_mine = qkv_mine[:, :cols], qkv_mine[:, cols:]
        pack = jnp.broadcast_to(pack, (R * Z, pack.shape[0]))
        pack = lax.all_to_all(pack, ALL, split_axis=0, concat_axis=0, tiled=True)
    vectors = [pack[:, i * rows_dev : (i + 1) * rows_dev].reshape(-1) for i in range(len(small))]
    gain_one, bias_one, bias_q, bias_v, bias_o, gain_two, bias_two, bias_down = vectors
    pack = pack.reshape(B, Z, X, -1)[..., len(small) * rows_dev :]
    up_dev = fc1_bias.shape[0]
    bias_up = lax.dynamic_index_in_dim(
        pack[..., :up_dev].transpose(0, 2, 1, 3).reshape(R, Z * up_dev), rank, 0, keepdims=False
    )
    group_lengths = pack[:, 0, 0, up_dev : up_dev + count].astype(jnp.int32)
    ends = jnp.sum(jnp.where(upto, group_lengths[:, :, None], 0), axis=1)
    places = at_z * span + jnp.arange(span, dtype=jnp.int32)
    starts = jnp.max(jnp.where(ends[:, None, :] <= places[None, :, None], ends[:, None, :], 0), axis=2)
    starts = starts - (at_z - 1) * span

    def feature_rows(mine):
        full = lax.all_gather(mine, "z", axis=0, tiled=True)
        return full.reshape(Z, B, X, rows_dev, -1).transpose(1, 0, 2, 3, 4).reshape(D, -1)

    weight_kv = feature_rows(pair_mine)
    bias_kv = jnp.concatenate([jnp.zeros((cols,), single), mine(bias_v)])
    bias_one, query_mine, weight_o = lax.optimization_barrier((bias_one, query_mine, weight_o))
    normed_low = layer_norm(local, gain_one, bias_one).astype(bfloat)

    def gather_plane(rows, cid, name):
        if fast:
            return plane_gather(rows, (), [], None, cid, name)[0]
        return lax.all_gather(rows, PLANE, axis=0, tiled=True)

    def gather_plane_dot(rows, weight, shift, out_type, turned, cid, name):
        if fast:
            return gather_dot(rows, weight, shift, out_type, turned, cid, name)
        rows = lax.all_gather(rows, PLANE, axis=0, tiled=True)
        return rows, ((dot_nt if turned else dot)(rows, weight) + shift).astype(out_type)

    def reduce_plane(left, weight, turned, cid, name):
        if fast:
            return dot_reduce([left], [weight], turned, cid, name)
        terms = (dot_nt if turned else dot)(left, weight).astype(bfloat)
        return lax.psum_scatter(terms, PLANE, scatter_dimension=0, tiled=True).astype(single)

    normed_all = gather_plane(normed_low, 0, "gather_normed")
    units = fc1_bias.shape[0] // 2
    halves = [jnp.concatenate([fc1_weight.T[i : i + units], fc2_weight[i : i + units]]) for i in (0, units)]

    def gather_units(mine):
        return lax.all_gather(mine, "z", axis=0, tiled=True).reshape(Z, 2, units, D)

    normed_all, weight_kv, unit_one = lax.optimization_barrier((normed_all, weight_kv, halves[0]))
    weight_q = feature_rows(query_mine)
    unit_one = gather_units(unit_one)
    key_value = (dot(normed_all, weight_kv) + bias_kv).astype(bfloat)
    up = [(i, i + 1) for i in range(Z - 1)]
    down = [(i + 1, i) for i in range(Z - 1)]
    cotangent = out_grad[0].astype(single) * (group_tok / active_total)
    branch_grad = (active * cotangent).astype(bfloat)
    down_b_grad = column_sums(branch_grad)
    key_value, branch_grad = lax.optimization_barrier((key_value, branch_grad))
    before = lax.ppermute(key_value, "z", up)
    branch_all = gather_plane(branch_grad, 7, "gather_branch")
    branch_all, late_normed = lax.optimization_barrier((branch_all, normed_all))
    query = (dot(late_normed, weight_q) + mine(bias_q)).astype(bfloat)
    before, query = lax.optimization_barrier((before, query))
    starts = starts.reshape(B * span, 1)
    context = attention_forward(starts, query, key_value, before, B)
    context, unit_two = lax.optimization_barrier((context, halves[1]))
    unit_two = gather_units(unit_two)

    attended = reduce_plane(context, weight_o, False, 1, "attended") + bias_o
    middle = local + active * attended
    normed_two = layer_norm(middle, gain_two, bias_two).astype(bfloat)
    bias_up = bias_up.reshape(Z, 2, units)
    bias_up = [bias_up[:, i].reshape(1, Z * units) for i in range(2)]

    def sum_halves(left, right, turned, cid, name):
        if fast:
            return dot_reduce(left, right, turned, cid, name)
        terms = sum((dot_nt if turned else dot)(a, w) for a, w in zip(left, right)).astype(bfloat)
        return lax.psum_scatter(terms, PLANE, scatter_dimension=0, tiled=True).astype(single)

    def sum_z(grads):
        return lax.psum_scatter(grads.reshape(Z * 2 * units, D), "z", scatter_dimension=0, tiled=True)

    if fast:
        branch_rows = branch_all.reshape(R, tok, D)
        two_all, hidden_one, pre_one, bias_one_up, grads = first_units(normed_two, branch_rows, unit_one, bias_up[0], 2)
        shard_one = sum_z(grads)
        hidden_two, bias_two_up, normed_two_grad, grads = last_units(
            two_all, branch_rows, pre_one, unit_one, unit_two, bias_up[1], 3
        )
        shard_two = sum_z(grads)
        up_b_halves = [bias_one_up[0], bias_two_up[0]]
    else:
        two_all = gather_plane(normed_two, 2, "gather_two")

        def half_units(weights, bias):
            weight_up, weight_down = [weights[:, i].reshape(Z * units, D) for i in (0, 1)]
            hidden, gelu_pull = jax.vjp(partial(jax.nn.gelu, approximate=True), dot_nt(two_all, weight_up) + bias)
            hidden = hidden.astype(bfloat)
            pre_grad = gelu_pull(dot_nt(branch_all, weight_down))[0].astype(bfloat)
            grads = dot_tn(pre_grad, two_all), dot_tn(hidden, branch_all)
            grads = jnp.stack([g.astype(bfloat).reshape(Z, units, D) for g in grads], axis=1)
            return hidden, pre_grad, sum_z(grads), weight_up, weight_down

        hidden_one, pre_one, shard_one, up_one, down_one = half_units(unit_one, bias_up[0])
        hidden_two, pre_two, shard_two, up_two, down_two = half_units(unit_two, bias_up[1])
        up_b_halves = [column_sums(pre_one), column_sums(pre_two)]
        normed_two_grad = sum_halves([pre_one, pre_two], [up_one, up_two], False, 3, "up_grad")
    up_b_grad = jnp.stack([half.reshape(Z, units) for half in up_b_halves], axis=1).reshape(-1)

    middle_part, gain_two_grad, bias_two_grad = norm_backward(middle, normed_two_grad, gain_two)
    middle_grad = cotangent + middle_part
    attended_grad = (active * middle_grad).astype(bfloat)
    out_b_grad = column_sums(attended_grad)
    attended_all, context_grad = gather_plane_dot(
        attended_grad, weight_o, jnp.zeros((1, cols), single), bfloat, True, 5, "attended_grad"
    )
    context_grad, shard_one = lax.optimization_barrier((context_grad, shard_one))
    out_w_grad = dot_tn(context, attended_all)
    query_grad, edge, pair = attention_backward(starts, query, key_value, before, context_grad, B)
    hidden_one, edge, pair, query_grad = lax.optimization_barrier((hidden_one, edge, pair, query_grad))
    after = lax.ppermute(edge, "z", down)
    query_w_grad = dot_tn(normed_all, query_grad).astype(bfloat)
    hidden_one, query_w_grad, out_w_grad = lax.optimization_barrier((hidden_one, query_w_grad, out_w_grad))
    downs = [unit_one, unit_two] if fast else [down_one, down_two]
    branch = sum_halves([hidden_one, hidden_two], downs, False, 4, "down")
    branch, after, shard_two = lax.optimization_barrier((branch, after, shard_two))
    if fast:
        pair_grad, qkv_w_grad, value_b_grad = pair_grads(pair, after, normed_all, query_w_grad, B, Z, X)
        value_b_grad = value_b_grad[0]
    else:
        pair_grad = (pair + after.astype(single)).astype(bfloat)
        pair_w_grad = dot_tn(normed_all, pair_grad).astype(bfloat)
        qkv_w_grad = jnp.concatenate([query_w_grad, pair_w_grad], axis=1)
        qkv_w_grad = qkv_w_grad.reshape(B, Z, X, rows_dev, 3 * cols).transpose(1, 0, 2, 3, 4)
        value_b_grad = column_sums(pair_grad[:, cols:])
    qkv_w_grad = qkv_w_grad.reshape(D, 3 * cols)
    qkv_w_grad = lax.psum_scatter(qkv_w_grad, "z", scatter_dimension=0, tiled=True).reshape(R, rows_dev, 3 * cols)
    normed_grad = sum_halves([query_grad, pair_grad], [weight_q, weight_kv], True, 6, "qkv_grad")
    query_b_grad = column_sums(query_grad)
    input_part, gain_one_grad, bias_one_grad = norm_backward(local, normed_grad, gain_one)

    def sum_to_owners(vectors, axes, parts):
        split = jnp.concatenate([v.reshape(parts, -1) for v in vectors], axis=1)
        summed = jnp.sum(lax.all_to_all(split, axes, split_axis=0, concat_axis=0, tiled=True), axis=0)
        widths = [v.shape[0] // parts for v in vectors]
        return [summed[sum(widths[:i]) : sum(widths[: i + 1])] for i in range(len(widths))]

    qkv_w_grad, out_w_grad = lax.optimization_barrier((qkv_w_grad, out_w_grad))
    device_sums = [gain_one_grad, bias_one_grad, out_b_grad, gain_two_grad, bias_two_grad, down_b_grad]
    if fast:
        rank_sums = jnp.concatenate([v.reshape(Z, -1) for v in (query_b_grad, value_b_grad, up_b_grad)], axis=1)
        here = (jnp.arange(R) == rank).reshape(B, 1, X, 1)
        rank_sums = jnp.where(here, rank_sums[None, :, None, :], 0.0).reshape(R * Z, -1)
        rows = jnp.concatenate([v.reshape(R * Z, -1) for v in device_sums] + [rank_sums], axis=1)
        q_w_shard, k_w_shard, v_w_shard, summed = settle(qkv_w_grad, rows, 9)
        q_w_shard, k_w_shard, v_w_shard = [t.astype(single) for t in (q_w_shard, k_w_shard, v_w_shard)]
        sums = [summed[0, i * rows_dev : (i + 1) * rows_dev] for i in range(len(device_sums) + 2)]
        q_b_shard, v_b_shard = sums[len(device_sums) :]
        up_b_shard = summed[0, (len(device_sums) + 2) * rows_dev :]
    else:
        qkv_w_grad = lax.all_to_all(qkv_w_grad, PLANE, split_axis=0, concat_axis=0, tiled=True)
        q_w_shard, k_w_shard, v_w_shard = [
            from_ranks(qkv_w_grad[..., i : i + cols]).astype(single) for i in range(0, 3 * cols, cols)
        ]
        sums = sum_to_owners(device_sums, ALL, R * Z)
        [up_b_shard] = sum_to_owners([up_b_grad], "z", Z)
    if whole_heads:
        out_w_shard = lax.psum_scatter(out_w_grad.astype(bfloat), "z", scatter_dimension=0, tiled=True).astype(single)
        if not fast:
            q_b_shard, v_b_shard = sum_to_owners([query_b_grad, value_b_grad], "z", Z)
    else:

        def placed(rows):
            full = jnp.zeros((D,) + rows.shape[1:], rows.dtype)
            full = lax.dynamic_update_slice_in_dim(full, rows, rank * cols, 0)
            return lax.psum_scatter(full, ALL, scatter_dimension=0, tiled=True).astype(single)

        out_w_shard = placed(out_w_grad.astype(bfloat))
        q_b_shard = placed(query_b_grad)
        v_b_shard = placed(value_b_grad)
    outputs = middle + active * (branch + bias_down)
    input_grad = middle_grad + input_part
    return (
        outputs.astype(bfloat)[None],
        input_grad.astype(bfloat)[None],
        sums[0],
        sums[1],
        q_w_shard,
        q_b_shard,
        k_w_shard,
        v_w_shard,
        v_b_shard,
        out_w_shard,
        sums[2],
        sums[3],
        sums[4],
        jnp.concatenate([shard_one[:units], shard_two[:units]]).T.astype(single),
        up_b_shard,
        jnp.concatenate([shard_one[units:], shard_two[units:]]).astype(single),
        sums[5],
    )


def solution(mesh):
    groups, parts = mesh.shape["batch"], mesh.shape["seq"]
    inner = Mesh(mesh.devices.reshape(groups, SPANS, parts // SPANS), ("b", "z", "x"))
    token = P("b", ("z", "x"), None)
    vector = P(ALL)
    rows = P(ALL, None)
    columns = P(None, ALL)
    return jax.shard_map(
        on_device,
        mesh=inner,
        in_specs=(
            token,
            P("b", None),
            P("b", None),
            P(),
            token,
            vector,
            vector,
            rows,
            vector,
            rows,
            rows,
            vector,
            rows,
            vector,
            vector,
            vector,
            columns,
            vector,
            rows,
            vector,
        ),
        out_specs=(
            token,
            token,
            vector,
            vector,
            rows,
            vector,
            rows,
            rows,
            vector,
            rows,
            vector,
            vector,
            vector,
            columns,
            vector,
            rows,
            vector,
        ),
        check_vma=False,
    )
```

```python
import functools
from functools import partial

import jax
import jax.numpy as jnp
from jax import lax
from jax.experimental import pallas as pl
from jax.experimental.pallas import tpu as pltpu
from jax.sharding import Mesh
from jax.sharding import PartitionSpec as P

HEAD_DIM = 64
SPANS = 4

bfloat = jnp.bfloat16
single = jnp.float32

PLANE = ("b", "x")
ALL = ("b", "z", "x")
MESH = pl.DeviceIdType.MESH
TILE = 512

def plane_place():
    b, z, x = lax.axis_index("b"), lax.axis_index("z"), lax.axis_index("x")
    sib_b = b + 1 - 2 * lax.rem(b, 2)
    far_b = lax.rem(b + 2, 4)
    far_sib_b = lax.rem(sib_b + 2, 4)
    ids = {"s": (sib_b, z, x), "x": (b, z, 1 - x), "y": (far_b, z, x)}
    ranks = {
        "o": b * 2 + x,
        "s": sib_b * 2 + x,
        "x": b * 2 + 1 - x,
        "xs": sib_b * 2 + 1 - x,
        "y": far_b * 2 + x,
        "ys": far_sib_b * 2 + x,
        "d": far_b * 2 + 1 - x,
        "ds": far_sib_b * 2 + 1 - x,
    }
    return ids, ranks

def greet(ids):
    barrier = pltpu.get_barrier_semaphore()
    for device in ids.values():
        pl.semaphore_signal(barrier, inc=1, device_id=device, device_id_type=MESH)
    pl.semaphore_wait(barrier, len(ids))

def tiles(lo, hi, body):
    def step(i, _):
        body(pl.ds(pl.multiple_of(i * TILE, TILE), TILE))
        return 0
    lax.fori_loop(lo // TILE, hi // TILE, step, 0)

def gather_kernel(body_of, n_in, n_out, x_ref, *refs):
    ins = refs[:n_in]; all_ref = refs[n_in]; outs = refs[n_in + 1 : n_in + 1 + n_out]
    held, send, recv, keep = refs[n_in + 1 + n_out :]
    ids, at = plane_place()
    half = x_ref.shape[0] // 2
    parts = (pl.ds(0, half), pl.ds(half, half))
    greet(ids)
    count = [0]
    started = []
    def ship(src, dst, to):
        n = count[0]; count[0] += 1
        c = pltpu.make_async_remote_copy(src_ref=src, dst_ref=dst, send_sem=send.at[n], recv_sem=recv.at[n], device_id=ids[to], device_id_type=MESH)
        c.start(); started.append(c)
        return c
    own = at["o"]
    x0 = ship(x_ref.at[parts[0]], held.at[own, parts[0]], "x")
    y1 = ship(x_ref.at[parts[1]], held.at[own, parts[1]], "y")
    x1 = ship(x_ref.at[parts[1]], held.at[own, parts[1]], "x")
    y0 = ship(x_ref.at[parts[0]], held.at[own, parts[0]], "y")
    s0 = ship(x_ref, held.at[own], "s")
    kept = []
    def done(rank, src):
        c = pltpu.make_async_copy(src, all_ref.at[rank], keep.at[len(kept)])
        c.start(); kept.append(c)
        if body_of is not None:
            body_of(rank, src, ins, outs)
    done(own, x_ref)
    s0.wait_recv()
    done(at["s"], held.at[at["s"]])
    x0.wait_recv()
    ry = ship(held.at[at["x"], parts[0]], held.at[at["x"], parts[0]], "y")
    y1.wait_recv()
    rx = ship(held.at[at["y"], parts[1]], held.at[at["y"], parts[1]], "x")
    x1.wait_recv()
    sx = ship(held.at[at["x"]], held.at[at["x"]], "s")
    y0.wait_recv()
    sy = ship(held.at[at["y"]], held.at[at["y"]], "s")
    done(at["x"], held.at[at["x"]])
    done(at["y"], held.at[at["y"]])
    sx.wait_recv()
    done(at["xs"], held.at[at["xs"]])
    sy.wait_recv()
    done(at["ys"], held.at[at["ys"]])
    ry.wait_recv(); rx.wait_recv()
    sd = ship(held.at[at["d"]], held.at[at["d"]], "s")
    done(at["d"], held.at[at["d"]])
    sd.wait_recv()
    done(at["ds"], held.at[at["ds"]])
    for c in started: c.wait_send()
    for c in kept: c.wait()

def vmem(n): return [pl.BlockSpec(memory_space=pltpu.VMEM)] * n

def plane_gather(x, ins, out_types, body_of, cid, name, ranks=8):
    tok, D = x.shape
    res = pl.pallas_call(
        functools.partial(gather_kernel, body_of, len(ins), len(out_types)),
        out_shape=[jax.ShapeDtypeStruct((ranks, tok, D), x.dtype), *out_types],
        in_specs=vmem(1 + len(ins)),
        out_specs=[pl.BlockSpec(memory_space=pl.ANY)] + vmem(len(out_types)),
        scratch_shapes=[pltpu.VMEM((ranks, tok, D), x.dtype), pltpu.SemaphoreType.DMA((10,)), pltpu.SemaphoreType.DMA((10,)), pltpu.SemaphoreType.DMA((8,))],
        compiler_params=pltpu.CompilerParams(collective_id=cid, has_side_effects=True, vmem_limit_bytes=60 << 20),
        cost_estimate=pl.CostEstimate(flops=1 << 30, bytes_accessed=128 << 20, transcendentals=0),
        name=name,
    )(x, *ins)
    return res[0].reshape(ranks * tok, D), *res[1:]

def gather_dot(x, w, bias, out_dtype, turned, cid, name):
    ranks, tok, D = 8, *x.shape
    N = w.shape[0] if turned else w.shape[1]
    tile = min(N, 512) if N % 512 == 0 else 256
    def body(rank, src, ins, outs):
        w_ref, b_ref = ins
        def step(i, _):
            cols = pl.ds(pl.multiple_of(i * tile, tile), tile)
            if turned:
                y = lax.dot_general(src[...], w_ref[cols, :], (((1,), (1,)), ((), ())), preferred_element_type=single)
            else:
                y = jnp.dot(src[...], w_ref[:, cols], preferred_element_type=single)
            outs[0][rank, :, cols] = (y + b_ref[:, cols]).astype(out_dtype)
            return 0
        lax.fori_loop(0, N // tile, step, 0)
    all_, y = plane_gather(x, (w, bias), [jax.ShapeDtypeStruct((ranks, tok, N), out_dtype)], body, cid, name)
    return all_, y.reshape(ranks * tok, N)

def reduce_kernel(turned, pairs, *refs):
    left, right = refs[:pairs], refs[pairs : 2 * pairs]
    out_ref, sib_out, sib_in, stage, landed, send, recv = refs[2 * pairs :]
    ids, at = plane_place()
    D = out_ref.shape[1]
    mid = D // 2
    greet(ids)
    count = [0]; started = []
    def ship(src, dst, to):
        n = count[0]; count[0] += 1
        c = pltpu.make_async_remote_copy(src_ref=src, dst_ref=dst, send_sem=send.at[n], recv_sem=recv.at[n], device_id=ids[to], device_id_type=MESH)
        c.start(); started.append(c)
        return c
    def term(rank, cols):
        if turned:
            return sum(dot_nt(a[rank], w[cols, :]) for a, w in zip(left, right))
        rows = [w[:, 1, :, cols].reshape(-1, TILE) if len(w.shape) == 4 else w[:, cols] for w in right]
        return sum(dot(a[rank], w) for a, w in zip(left, rows))
    order = ("d", "x", "y", "o")
    twin = {"d": "ds", "x": "xs", "y": "ys", "o": "s"}
    sib = {}
    def to_sibling(j, h):
        def fill(cols):
            sib_out[j, h, :, local(h, cols)] = term(at[twin[order[j]]], cols).astype(bfloat)
        tiles(h * mid, (h + 1) * mid, fill)
        sib[j, h] = ship(sib_out.at[j, h], sib_in.at[j, h], "s")
    def local(h, cols):
        return pl.ds(pl.multiple_of(cols.start - h * mid, TILE), TILE)
    def pair(j, h, cols):
        return term(at[order[j]], cols) + sib_in[j, h, :, local(h, cols)].astype(single)
    def put(j, h, extra=None):
        sib[j, h].wait_recv()
        def fill(cols):
            value = pair(j, h, cols)
            if extra is not None:
                value = value + landed[extra, :, local(h, cols)].astype(single)
            stage[j, h, :, local(h, cols)] = value.astype(bfloat)
        tiles(h * mid, (h + 1) * mid, fill)
    to_sibling(0, 0)
    to_sibling(0, 1)
    put(0, 0)
    d_a = ship(stage.at[0, 0], landed.at[0], "x")
    put(0, 1)
    d_b = ship(stage.at[0, 1], landed.at[1], "y")
    to_sibling(1, 0)
    to_sibling(2, 1)
    put(1, 0)
    x_a = ship(stage.at[1, 0], landed.at[2], "x")
    put(2, 1)
    y_b = ship(stage.at[2, 1], landed.at[3], "y")
    for j, h in ((1, 1), (2, 0), (3, 0), (3, 1)):
        to_sibling(j, h)
    d_b.wait_recv()
    put(1, 1, extra=1)
    x_b = ship(stage.at[1, 1], landed.at[5], "x")
    d_a.wait_recv()
    put(2, 0, extra=0)
    y_a = ship(stage.at[2, 0], landed.at[4], "y")
    for h in range(2):
        sib[3, h].wait_recv()
        def first(cols, h=h):
            out_ref[:, cols] = pair(3, h, cols)
        tiles(h * mid, (h + 1) * mid, first)
    x_a.wait_recv(); y_b.wait_recv(); x_b.wait_recv(); y_a.wait_recv()
    for h, (n, m) in enumerate(((2, 4), (3, 5))):
        def add(cols, h=h, n=n, m=m):
            c = local(h, cols)
            out_ref[:, cols] = out_ref[:, cols] + landed[n, :, c].astype(single) + landed[m, :, c].astype(single)
        tiles(h * mid, (h + 1) * mid, add)
    for c in started: c.wait_send()

def dot_reduce(left, right, turned, cid, name):
    ranks = 8
    D = right[0].shape[0] if turned else right[0].shape[-1]
    tok = left[0].size // left[0].shape[-1] // ranks
    return pl.pallas_call(
        functools.partial(reduce_kernel, turned, len(left)),
        out_shape=jax.ShapeDtypeStruct((tok, D), single),
        in_specs=vmem(2 * len(left)), out_specs=vmem(1)[0],
        scratch_shapes=[pltpu.VMEM((4, 2, tok, D // 2), bfloat), pltpu.VMEM((4, 2, tok, D // 2), bfloat), pltpu.VMEM((3, 2, tok, D // 2), bfloat), pltpu.VMEM((6, tok, D // 2), bfloat),
            pltpu.SemaphoreType.DMA((14,)), pltpu.SemaphoreType.DMA((14,))],
        compiler_params=pltpu.CompilerParams(collective_id=cid, has_side_effects=True, vmem_limit_bytes=60 << 20),
        cost_estimate=pl.CostEstimate(flops=1 << 30, bytes_accessed=128 << 20, transcendentals=0),
        name=name,
    )(*[a.reshape(ranks, tok, -1) for a in left], *right)


def dot(left, right):
    return jnp.dot(left, right, preferred_element_type=single)


def dot_tn(left, right):
    return lax.dot_general(left, right, (((0,), (0,)), ((), ())), preferred_element_type=single)


def dot_nt(left, right):
    return lax.dot_general(left, right, (((1,), (1,)), ((), ())), preferred_element_type=single)


def layer_norm(values, gain_vec, shift_vec):
    center = jnp.mean(values, axis=-1, keepdims=True)
    centered = values - center
    spread = jnp.mean(centered * centered, axis=-1, keepdims=True)
    return centered * lax.rsqrt(spread + 1e-05) * gain_vec + shift_vec


def column_sums(matrix):
    return jnp.sum(matrix.astype(single), axis=0)


def shipper(send, recv, ids):
    started = []

    def ship(src, dst, to):
        n = len(started)
        copy = pltpu.make_async_remote_copy(
            src_ref=src, dst_ref=dst, send_sem=send.at[n], recv_sem=recv.at[n], device_id=ids[to], device_id_type=MESH
        )
        copy.start()
        started.append(copy)
        return copy

    return ship, started


TWIN = {"o": "s", "x": "xs", "y": "ys", "d": "ds"}


def unit_rows(w_ref, i):
    parts, _, units, D = w_ref.shape
    return w_ref[:, i].reshape(parts * units, D)


def hidden_units(src, branch, w_ref, b_ref, hid_ref, pg_ref, pb_ref, rank):
    pre = dot_nt(src[...], unit_rows(w_ref, 0)) + b_ref[...]
    square = pre * pre
    bend = jnp.tanh(0.7978845608028654 * (pre + 0.044715 * (pre * square)))
    rise = 0.5 * (1.0 + bend)
    hid_ref[rank] = (pre * rise).astype(bfloat)
    slope = rise + (0.5 * 0.7978845608028654) * pre * (1.0 - bend * bend) * (1.0 + 3 * 0.044715 * square)
    grad = (dot_nt(branch[...], unit_rows(w_ref, 1)) * slope).astype(bfloat)
    pg_ref[rank] = grad
    pb_ref[...] += jnp.sum(grad.astype(single), axis=0, keepdims=True)


def first_units_kernel(
    x_ref, bg_ref, w_ref, b_ref, all_ref, hid_ref, pg_ref, pb_ref, grad_ref,
    held, bg, total, send, recv, keep, load,
):
    ids, at = plane_place()
    tok = x_ref.shape[0]
    half = tok // 2
    parts = (pl.ds(0, half), pl.ds(half, half))
    own = at["o"]
    loads = {}
    for n, name in enumerate(at):
        loads[name] = pltpu.make_async_copy(bg_ref.at[at[name]], bg.at[at[name]], load.at[n])
    loads["o"].start()
    greet(ids)
    ship, started = shipper(send, recv, ids)
    x0 = ship(x_ref.at[parts[0]], held.at[own, parts[0]], "x")
    y1 = ship(x_ref.at[parts[1]], held.at[own, parts[1]], "y")
    x1 = ship(x_ref.at[parts[1]], held.at[own, parts[1]], "x")
    y0 = ship(x_ref.at[parts[0]], held.at[own, parts[0]], "y")
    s0 = ship(x_ref, held.at[own], "s")
    pb_ref[...] = jnp.zeros_like(pb_ref)
    kept = []

    def units(name):
        rank = at[name]
        src = x_ref if name == "o" else held.at[rank]
        copy = pltpu.make_async_copy(src, all_ref.at[rank], keep.at[len(kept)])
        copy.start()
        kept.append(copy)
        loads[name].wait()
        if name == "o":
            for other in loads:
                if other != "o":
                    loads[other].start()
        hidden_units(src, bg.at[rank], w_ref, b_ref, hid_ref, pg_ref, pb_ref, rank)

    def weigh(name, last=False):
        units_at = grad_ref.shape[2]
        per = 256 // units_at

        def rows(i, _):
            here = pl.ds(pl.multiple_of(i * 256, 256), 256)
            owners = pl.ds(i * per, per)
            for j, left in enumerate((pg_ref, hid_ref)):
                term = 0
                for n in (name, TWIN[name]):
                    right = bg[at[n]] if j else (x_ref[...] if n == "o" else held[at[n]])
                    term = term + dot_tn(left[at[n], :, here], right)
                term = term.reshape(per, units_at, -1)
                if name == "o":
                    total[owners, j] = term
                elif last:
                    grad_ref[owners, j] = (total[owners, j] + term).astype(bfloat)
                else:
                    total[owners, j] += term
            return 0

        lax.fori_loop(0, hid_ref.shape[2] // 256, rows, 0)

    units("o")
    s0.wait_recv()
    units("s")
    x0.wait_recv()
    ry = ship(held.at[at["x"], parts[0]], held.at[at["x"], parts[0]], "y")
    y1.wait_recv()
    rx = ship(held.at[at["y"], parts[1]], held.at[at["y"], parts[1]], "x")
    weigh("o")
    x1.wait_recv()
    sx = ship(held.at[at["x"]], held.at[at["x"]], "s")
    y0.wait_recv()
    sy = ship(held.at[at["y"]], held.at[at["y"]], "s")
    units("x")
    sx.wait_recv()
    units("xs")
    units("y")
    sy.wait_recv()
    units("ys")
    weigh("x")
    ry.wait_recv()
    rx.wait_recv()
    sd = ship(held.at[at["d"]], held.at[at["d"]], "s")
    weigh("y")
    units("d")
    sd.wait_recv()
    units("ds")
    weigh("d", last=True)
    for copy in started:
        copy.wait_send()
    for copy in kept:
        copy.wait()


def last_units_kernel(
    all_ref, bg_ref, pg1_ref, w1_ref, w_ref, b_ref, hid_ref, pb_ref, r_ref, grad_ref,
    held, bg, pg_ref, sib_out, sib_in, stage, landed, send, recv, load, load_b,
):
    ids, at = plane_place()
    ranks, tok, D = held.shape
    mid = D // 2
    names = ("ds", "d", "xs", "x", "ys", "y", "s", "o")
    loads = {}
    for n, name in enumerate(names):
        loads[name] = [
            pltpu.make_async_copy(all_ref.at[at[name]], held.at[at[name]], load.at[n]),
            pltpu.make_async_copy(bg_ref.at[at[name]], bg.at[at[name]], load_b.at[n]),
        ]
    for name in names[:2]:
        for copy in loads[name]:
            copy.start()
    greet(ids)
    ship, started = shipper(send, recv, ids)
    pb_ref[...] = jnp.zeros_like(pb_ref)

    def units(name):
        for copy in loads[name]:
            copy.wait()
        if name == names[0]:
            for other in names[2:]:
                for copy in loads[other]:
                    copy.start()
        rank = at[name]
        hidden_units(held.at[rank], bg.at[rank], w_ref, b_ref, hid_ref, pg_ref, pb_ref, rank)

    def term(name, cols):
        rank = at[name]
        first, second = [w[:, 0, :, cols].reshape(-1, TILE) for w in (w1_ref, w_ref)]
        return dot(pg1_ref[rank], first) + dot(pg_ref[rank], second)

    order = ("d", "x", "y", "o")

    def to_sibling(j):
        def fill(cols):
            sib_out[j, :, cols] = term(TWIN[order[j]], cols).astype(bfloat)

        tiles(0, D, fill)
        return ship(sib_out.at[j], sib_in.at[j], "s")

    def pair(j, cols):
        return term(order[j], cols) + sib_in[j, :, cols].astype(single)

    def local(h, cols):
        return pl.ds(pl.multiple_of(cols.start - h * mid, TILE), TILE)

    def put(j, h, extra=None):
        def fill(cols):
            value = pair(j, cols)
            if extra is not None:
                value = value + landed[extra, :, local(h, cols)].astype(single)
            stage[j, h, :, local(h, cols)] = value.astype(bfloat)

        tiles(h * mid, (h + 1) * mid, fill)

    units("ds")
    d_sib = to_sibling(0)
    units("d")
    d_sib.wait_recv()
    put(0, 0)
    d_a = ship(stage.at[0, 0], landed.at[0], "x")
    put(0, 1)
    d_b = ship(stage.at[0, 1], landed.at[1], "y")
    units("xs")
    x_sib = to_sibling(1)
    units("x")
    x_sib.wait_recv()
    put(1, 0)
    x_a = ship(stage.at[1, 0], landed.at[2], "x")
    units("ys")
    y_sib = to_sibling(2)
    units("y")
    y_sib.wait_recv()
    put(2, 1)
    y_b = ship(stage.at[2, 1], landed.at[3], "y")
    d_b.wait_recv()
    put(1, 1, extra=1)
    x_b = ship(stage.at[1, 1], landed.at[5], "x")
    d_a.wait_recv()
    put(2, 0, extra=0)
    y_a = ship(stage.at[2, 0], landed.at[4], "y")
    units("s")
    own_sib = to_sibling(3)
    units("o")
    own_sib.wait_recv()

    def first(cols):
        r_ref[:, cols] = pair(3, cols)

    tiles(0, D, first)

    units_at = grad_ref.shape[2]
    per = 256 // units_at
    tokens = ranks * tok

    def grads(i, _):
        here = pl.ds(pl.multiple_of(i * 256, 256), 256)
        owners = pl.ds(i * per, per)
        for j, (left, right) in enumerate(((pg_ref, held), (hid_ref, bg))):
            value = dot_tn(left[:, :, here].reshape(tokens, 256), right[...].reshape(tokens, D))
            grad_ref[owners, j] = value.astype(bfloat).reshape(per, units_at, D)
        return 0

    lax.fori_loop(0, hid_ref.shape[2] // 256, grads, 0)
    for copy in (x_a, y_b, x_b, y_a):
        copy.wait_recv()
    for h, (n, m) in enumerate(((2, 4), (3, 5))):

        def add(cols, h=h, n=n, m=m):
            c = local(h, cols)
            r_ref[:, cols] = r_ref[:, cols] + landed[n, :, c].astype(single) + landed[m, :, c].astype(single)

        tiles(h * mid, (h + 1) * mid, add)
    for copy in started:
        copy.wait_send()


def first_units(x, bg, w, bias, cid):
    ranks = 8
    tok, D = x.shape
    F = bias.shape[1]
    anywhere = pl.BlockSpec(memory_space=pl.ANY)
    inside = pl.BlockSpec(memory_space=pltpu.VMEM)
    return pl.pallas_call(
        first_units_kernel,
        out_shape=[
            jax.ShapeDtypeStruct((ranks, tok, D), bfloat),
            jax.ShapeDtypeStruct((ranks, tok, F), bfloat),
            jax.ShapeDtypeStruct((ranks, tok, F), bfloat),
            jax.ShapeDtypeStruct((1, F), single),
            jax.ShapeDtypeStruct(w.shape, bfloat),
        ],
        in_specs=[inside, anywhere, inside, inside],
        out_specs=[anywhere, inside, inside, inside, inside],
        scratch_shapes=[
            pltpu.VMEM((ranks, tok, D), bfloat),
            pltpu.VMEM((ranks, tok, D), bfloat),
            pltpu.VMEM(w.shape, single),
            pltpu.SemaphoreType.DMA((10,)),
            pltpu.SemaphoreType.DMA((10,)),
            pltpu.SemaphoreType.DMA((8,)),
            pltpu.SemaphoreType.DMA((8,)),
        ],
        compiler_params=pltpu.CompilerParams(collective_id=cid, has_side_effects=True, vmem_limit_bytes=62 << 20),
        cost_estimate=pl.CostEstimate(flops=1 << 30, bytes_accessed=160 << 20, transcendentals=0),
        name="first_units",
    )(x, bg, w, bias)


def last_units(rows, bg, pg, w1, w, bias, cid):
    ranks, tok, D = rows.shape
    F = bias.shape[1]
    anywhere = pl.BlockSpec(memory_space=pl.ANY)
    inside = pl.BlockSpec(memory_space=pltpu.VMEM)
    return pl.pallas_call(
        last_units_kernel,
        out_shape=[
            jax.ShapeDtypeStruct((ranks, tok, F), bfloat),
            jax.ShapeDtypeStruct((1, F), single),
            jax.ShapeDtypeStruct((tok, D), single),
            jax.ShapeDtypeStruct(w.shape, bfloat),
        ],
        in_specs=[anywhere, anywhere, inside, inside, inside, inside],
        out_specs=[inside] * 4,
        scratch_shapes=[
            pltpu.VMEM((ranks, tok, D), bfloat),
            pltpu.VMEM((ranks, tok, D), bfloat),
            pltpu.VMEM((ranks, tok, F), bfloat),
            pltpu.VMEM((4, tok, D), bfloat),
            pltpu.VMEM((4, tok, D), bfloat),
            pltpu.VMEM((3, 2, tok, D // 2), bfloat),
            pltpu.VMEM((6, tok, D // 2), bfloat),
            pltpu.SemaphoreType.DMA((10,)),
            pltpu.SemaphoreType.DMA((10,)),
            pltpu.SemaphoreType.DMA((8,)),
            pltpu.SemaphoreType.DMA((8,)),
        ],
        compiler_params=pltpu.CompilerParams(collective_id=cid, has_side_effects=True, vmem_limit_bytes=62 << 20),
        cost_estimate=pl.CostEstimate(flops=1 << 30, bytes_accessed=160 << 20, transcendentals=0),
        name="last_units",
    )(rows, bg, pg, w1, w, bias)


def everyone(width):
    b, z, x = lax.axis_index("b"), lax.axis_index("z"), lax.axis_index("x")
    rank, me = b * 2 + x, (b * 4 + z) * 2 + x

    def in_plane(i):
        other = lax.rem(rank + i, 8)
        return other, (other // 2, z, lax.rem(other, 2))

    def anywhere(i):
        other = lax.rem(me + i, width)
        return other, (other // 8, lax.rem(other // 2, 4), lax.rem(other, 2))

    return rank, me, in_plane, anywhere


def exchange(blocks, landed, rows, gathered, same_row, sems):
    plane_send, plane_recv, all_send, all_recv = sems
    width = gathered.shape[0]
    rank, me, in_plane, anywhere = everyone(width)
    barrier = pltpu.get_barrier_semaphore()

    def each(count, body):
        def step(i, _):
            body(i)
            return 0

        lax.fori_loop(1, count, step, 0)

    each(width, lambda i: pl.semaphore_signal(barrier, inc=1, device_id=anywhere(i)[1], device_id_type=MESH))
    pl.semaphore_wait(barrier, width - 1)

    def block(i):
        other, device = in_plane(i)
        return pltpu.make_async_remote_copy(
            src_ref=blocks.at[other], dst_ref=landed.at[rank], send_sem=plane_send.at[i], recv_sem=plane_recv.at[i],
            device_id=device, device_id_type=MESH,
        )

    def row(i):
        other, device = anywhere(i)
        return pltpu.make_async_remote_copy(
            src_ref=rows.at[0] if same_row else rows.at[other], dst_ref=gathered.at[me],
            send_sem=all_send.at[i], recv_sem=all_recv.at[i], device_id=device, device_id_type=MESH,
        )

    each(8, lambda i: block(i).start())
    each(width, lambda i: row(i).start())
    landed[rank] = blocks[rank]
    gathered[me] = rows[0] if same_row else rows[me]
    each(width, lambda i: row(i).wait())
    each(8, lambda i: block(i).wait())


def head_at(rank, i):
    return (rank // 2 * 4 + i) * 2 + rank % 2


def spread_kernel(q_ref, k_ref, v_ref, pack_ref, q_out, kv_out, pack_out, blocks, landed, gathered, *sems):
    cols = q_out.shape[2]
    for rank in range(8):
        for part, ref in enumerate((q_ref, k_ref, v_ref)):
            heads = [ref[:, head_at(rank, i) * HEAD_DIM : (head_at(rank, i) + 1) * HEAD_DIM] for i in range(4)]
            blocks[rank, :, part * cols : (part + 1) * cols] = jnp.concatenate(heads, axis=1)
    exchange(blocks, landed, pack_ref, gathered, True, sems)
    q_out[...] = landed[:, :, :cols]
    kv_out[...] = landed[:, :, cols:]
    pack_out[...] = gathered[...]


def settle_kernel(w_ref, rows_ref, q_out, k_out, v_out, sums_ref, landed, gathered, *sems):
    cols = w_ref.shape[2] // 3
    exchange(w_ref, landed, rows_ref, gathered, False, sems)
    for part, out in enumerate((q_out, k_out, v_out)):
        for pair in range(out.shape[1] // 128):
            sides = []
            for head in (2 * pair, 2 * pair + 1):
                rank, i = head // 8 * 2 + head % 2, head // 2 % 4
                at = part * cols + i * HEAD_DIM
                sides.append(landed[rank, :, at : at + HEAD_DIM])
            out[:, pair * 128 : (pair + 1) * 128] = jnp.concatenate(sides, axis=1)
    sums_ref[...] = jnp.sum(gathered[...], axis=0)


def exchange_call(kernel, out_shape, args, blocks, landed, gathered, cid, name):
    inside = pl.BlockSpec(memory_space=pltpu.VMEM)
    width = gathered[0]
    return pl.pallas_call(
        kernel,
        out_shape=out_shape,
        in_specs=[inside] * len(args),
        out_specs=[inside] * len(out_shape),
        scratch_shapes=blocks
        + [
            pltpu.VMEM(landed, bfloat),
            pltpu.VMEM(gathered, single),
            pltpu.SemaphoreType.DMA((8,)),
            pltpu.SemaphoreType.DMA((8,)),
            pltpu.SemaphoreType.DMA((width,)),
            pltpu.SemaphoreType.DMA((width,)),
        ],
        compiler_params=pltpu.CompilerParams(collective_id=cid, has_side_effects=True, vmem_limit_bytes=32 << 20),
        cost_estimate=pl.CostEstimate(flops=1 << 20, bytes_accessed=32 << 20, transcendentals=0),
        name=name,
    )(*args)


def spread(q, k, v, pack, devices, cid):
    rows, D = q.shape
    cols = D // 8
    return exchange_call(
        spread_kernel,
        [
            jax.ShapeDtypeStruct((8, rows, cols), bfloat),
            jax.ShapeDtypeStruct((8, rows, 2 * cols), bfloat),
            jax.ShapeDtypeStruct((devices, 1, pack.shape[0]), single),
        ],
        (q, k, v, pack[None, None]),
        [pltpu.VMEM((8, rows, 3 * cols), bfloat)],
        (8, rows, 3 * cols),
        (devices, 1, pack.shape[0]),
        cid,
        "spread",
    )


def settle(weights, rows, cid):
    _, tall, wide = weights.shape
    D = wide // 3 * 8
    return exchange_call(
        settle_kernel,
        [jax.ShapeDtypeStruct((tall, D), bfloat)] * 3 + [jax.ShapeDtypeStruct((1, rows.shape[1]), single)],
        (weights, rows[:, None]),
        [],
        weights.shape,
        (rows.shape[0], 1, rows.shape[1]),
        cid,
        "settle",
    )


def windows(span):
    block = span // 2
    return [(i * block, i * block + block + span) for i in range(2)]

def key_window(before, own, lo, hi, span):
    if lo >= span:
        return own[lo - span : hi - span]
    return jnp.concatenate([before[lo:span], own[0 : hi - span]], axis=0)

def hidden_bias(start_ref, i, block, lo, hi, span):
    rows = span + i * block + lax.broadcasted_iota(jnp.int32, (block, hi - lo), 0)
    keys = lo + lax.broadcasted_iota(jnp.int32, (block, hi - lo), 1)
    start = start_ref[i * block : (i + 1) * block, :]
    return jnp.where((keys >= start) & (keys <= rows), 0.0, -1e30).astype(single)

def each_window(first_ref, span, body):
    block = span // 2
    for i, (lo, hi) in enumerate(windows(span)):
        begins = first_ref[pl.program_id(0) * 2 + i]
        pl.when(begins >= lo + block)(functools.partial(body, i, lo + block, hi))
        pl.when(begins < lo + block)(functools.partial(body, i, lo, hi))


def attend_kernel(first_ref, start_ref, q_ref, k_ref, v_ref, kb_ref, vb_ref, out_ref):
    span, cols = q_ref.shape
    block = span // 2

    def body(i, lo, hi):
        lane = lax.broadcasted_iota(jnp.int32, (block, cols), 1) // HEAD_DIM
        rows = pl.ds(i * block, block)
        bias = hidden_bias(start_ref, i, block, lo, hi, span)
        keys = key_window(kb_ref, k_ref, lo, hi, span)
        vals = key_window(vb_ref, v_ref, lo, hi, span)
        query = q_ref[rows, :] * jnp.asarray(HEAD_DIM ** (-0.5), bfloat)

        def head(h, total):
            mine = lane == h
            scores = dot_nt(jnp.where(mine, query, 0), keys) + bias
            weights = jnp.exp(scores - jnp.max(scores, axis=1, keepdims=True))
            part = jnp.dot(weights.astype(bfloat), vals, preferred_element_type=single)
            part = part * (1.0 / jnp.sum(weights, axis=1, keepdims=True))
            return jnp.where(mine, part, total)

        total = lax.fori_loop(0, cols // HEAD_DIM, head, jnp.zeros((block, cols), single), unroll=True)
        out_ref[rows, :] = total.astype(bfloat)

    each_window(first_ref, span, body)


def attend_back_kernel(
    first_ref, start_ref, q_ref, k_ref, v_ref, kb_ref, vb_ref, do_ref, dq_ref, edge_ref, pair_ref, dk, dv
):
    span, cols = q_ref.shape
    block = span // 2
    scale = HEAD_DIM ** (-0.5)
    dk[...] = jnp.zeros_like(dk)
    dv[...] = jnp.zeros_like(dv)

    def body(i, lo, hi):
        lane = lax.broadcasted_iota(jnp.int32, (block, cols), 1) // HEAD_DIM
        rows = pl.ds(i * block, block)
        bias = hidden_bias(start_ref, i, block, lo, hi, span)
        keys = key_window(kb_ref, k_ref, lo, hi, span)
        vals = key_window(vb_ref, v_ref, lo, hi, span)
        query = q_ref[rows, :] * jnp.asarray(scale, bfloat)
        grad = do_ref[rows, :]

        def head(h, total):
            mine = lane == h
            query_h = jnp.where(mine, query, 0)
            grad_h = jnp.where(mine, grad, 0)
            scores = dot_nt(query_h, keys) + bias
            weights = jnp.exp(scores - jnp.max(scores, axis=1, keepdims=True))
            probs = weights * (1.0 / jnp.sum(weights, axis=1, keepdims=True))
            prob_grad = dot_nt(grad_h, vals)
            row_dot = jnp.sum(probs * prob_grad, axis=1, keepdims=True)
            score_grad = (probs * (prob_grad - row_dot)).astype(bfloat)
            dv[lo:hi, :] += dot_tn(probs.astype(bfloat), grad_h)
            dk[lo:hi, :] += dot_tn(score_grad, query_h)
            part = jnp.dot(score_grad, keys, preferred_element_type=single)
            return jnp.where(mine, part, total)

        total = lax.fori_loop(0, cols // HEAD_DIM, head, jnp.zeros((block, cols), single), unroll=True)
        dq_ref[rows, :] = (total * scale).astype(bfloat)

    each_window(first_ref, span, body)
    edge_ref[:, :cols] = dk[:span, :].astype(bfloat)
    edge_ref[:, cols:] = dv[:span, :].astype(bfloat)
    pair_ref[:, :cols] = dk[span:, :]
    pair_ref[:, cols:] = dv[span:, :]


def pair_grads_kernel(pair_ref, after_ref, normed_ref, query_w_ref, grad_ref, weight_ref, bias_ref):
    block = pl.program_id(0)
    cols = query_w_ref.shape[1]
    rows = weight_ref.shape[3]

    @pl.when(block == 0)
    def _():
        grad = (pair_ref[...] + after_ref[...].astype(single)).astype(bfloat)
        grad_ref[...] = grad
        bias_ref[...] = jnp.sum(grad[:, cols:].astype(single), axis=0, keepdims=True)

    value = dot_tn(normed_ref[...], grad_ref[...]).astype(bfloat)
    xs = weight_ref.shape[2]
    for z in range(weight_ref.shape[0]):
        for x in range(xs):
            here = slice((z * xs + x) * rows, (z * xs + x + 1) * rows)
            weight_ref[z, 0, x, :, :cols] = query_w_ref[here, :]
            weight_ref[z, 0, x, :, cols:] = value[here, :]


def pair_grads(pair, after, normed, query_w, B, Z, X):
    tokens, wide = pair.shape
    D = normed.shape[1]
    per = D // B
    rows = per // (Z * X)
    cols = query_w.shape[1]
    return pl.pallas_call(
        pair_grads_kernel,
        grid=(B,),
        out_shape=[
            jax.ShapeDtypeStruct((tokens, wide), bfloat),
            jax.ShapeDtypeStruct((Z, B, X, rows, cols + wide), bfloat),
            jax.ShapeDtypeStruct((1, wide - cols), single),
        ],
        in_specs=[
            pl.BlockSpec((tokens, wide), lambda b: (0, 0)),
            pl.BlockSpec((tokens, wide), lambda b: (0, 0)),
            pl.BlockSpec((tokens, per), lambda b: (0, b)),
            pl.BlockSpec((per, cols), lambda b: (b, 0)),
        ],
        out_specs=[
            pl.BlockSpec((tokens, wide), lambda b: (0, 0)),
            pl.BlockSpec((Z, 1, X, rows, cols + wide), lambda b: (0, b, 0, 0, 0)),
            pl.BlockSpec((1, wide - cols), lambda b: (0, 0)),
        ],
        compiler_params=pltpu.CompilerParams(vmem_limit_bytes=48 << 20),
        name="pair_grads",
    )(pair, after, normed, query_w)


def block_starts(starts, groups):
    return starts.reshape(groups * 2, -1)[:, 0]


def attention_specs(span, cols):
    def at(j):
        return pl.BlockSpec((span, cols), lambda g, _: (g, j))
    return [pl.BlockSpec((span, 1), lambda g, _: (g, 0)), at(0), at(0), at(1), at(0), at(1)]

def attend(starts, query, key_value, before, groups):
    span, cols = query.shape[0] // groups, query.shape[1]
    return pl.pallas_call(
        attend_kernel,
        out_shape=jax.ShapeDtypeStruct((groups * span, cols), bfloat),
        grid_spec=pltpu.PrefetchScalarGridSpec(
            num_scalar_prefetch=1,
            grid=(groups,),
            in_specs=attention_specs(span, cols),
            out_specs=pl.BlockSpec((span, cols), lambda g, _: (g, 0)),
        ),
        compiler_params=pltpu.CompilerParams(vmem_limit_bytes=60 << 20),
        name="attend",
    )(block_starts(starts, groups), starts, query, key_value, key_value, before, before)

def attend_back(starts, query, key_value, before, grad, groups):
    span, cols = query.shape[0] // groups, query.shape[1]
    rows = groups * span
    return pl.pallas_call(
        attend_back_kernel,
        out_shape=[
            jax.ShapeDtypeStruct((rows, cols), bfloat),
            jax.ShapeDtypeStruct((rows, 2 * cols), bfloat),
            jax.ShapeDtypeStruct((rows, 2 * cols), single),
        ],
        grid_spec=pltpu.PrefetchScalarGridSpec(
            num_scalar_prefetch=1,
            grid=(groups,),
            in_specs=attention_specs(span, cols) + [pl.BlockSpec((span, cols), lambda g, _: (g, 0))],
            out_specs=[pl.BlockSpec((span, cols), lambda g, _: (g, 0))]
            + [pl.BlockSpec((span, 2 * cols), lambda g, _: (g, 0))] * 2,
            scratch_shapes=[pltpu.VMEM((2 * span, cols), single)] * 2,
        ),
        compiler_params=pltpu.CompilerParams(vmem_limit_bytes=60 << 20),
        name="attend_back",
    )(block_starts(starts, groups), starts, query, key_value, key_value, before, before, grad)


def attention_heads(starts, query, key_value, before, groups):
    span, cols = query.shape[0] // groups, query.shape[1]
    both = jnp.concatenate([before.reshape(groups, span, -1), key_value.reshape(groups, span, -1)], axis=1)
    key_two, value_two = [both[..., i * cols : (i + 1) * cols].reshape(groups, 2 * span, -1, HEAD_DIM) for i in (0, 1)]
    query = query.reshape(groups, span, -1, HEAD_DIM)
    keys = jnp.arange(2 * span)[None, None, :]
    rows = span + jnp.arange(span)[None, :, None]
    allowed = (keys >= starts.reshape(groups, span, 1)) & (keys <= rows)
    scores = jnp.einsum("gqhd,gkhd->ghqk", query, key_two, preferred_element_type=single) * HEAD_DIM ** (-0.5)
    scores = jnp.where(allowed[:, None], scores, -1e30)
    weights = jnp.exp(scores - jnp.max(scores, axis=-1, keepdims=True))
    return query, key_two, value_two, weights / jnp.sum(weights, axis=-1, keepdims=True)


def attention_forward(starts, query, key_value, before, groups):
    if query.shape[1] % 128 == 0:
        return attend(starts, query, key_value, before, groups)
    _, _, value_two, probs = attention_heads(starts, query, key_value, before, groups)
    context = jnp.einsum("ghqk,gkhd->gqhd", probs.astype(bfloat), value_two, preferred_element_type=single)
    return context.astype(bfloat).reshape(query.shape)


def attention_backward(starts, query, key_value, before, grad, groups):
    if query.shape[1] % 128 == 0:
        return attend_back(starts, query, key_value, before, grad, groups)
    rows = query.shape[0]
    query, key_two, value_two, probs = attention_heads(starts, query, key_value, before, groups)
    span = query.shape[1]
    grad = grad.reshape(query.shape)
    prob_grad = jnp.einsum("gqhd,gkhd->ghqk", grad, value_two, preferred_element_type=single)
    row_dot = jnp.sum(probs * prob_grad, axis=-1, keepdims=True)
    score_grad = (probs * (prob_grad - row_dot)).astype(bfloat)
    query_grad = jnp.einsum("ghqk,gkhd->gqhd", score_grad, key_two, preferred_element_type=single) * HEAD_DIM ** (-0.5)
    key_grad = jnp.einsum("ghqk,gqhd->gkhd", score_grad, query, preferred_element_type=single) * HEAD_DIM ** (-0.5)
    value_grad = jnp.einsum("ghqk,gqhd->gkhd", probs.astype(bfloat), grad, preferred_element_type=single)
    pair = jnp.concatenate([t.reshape(groups, 2 * span, -1) for t in (key_grad, value_grad)], axis=2)
    edge, pair = [t.reshape(rows, -1) for t in (pair[:, :span].astype(bfloat), pair[:, span:])]
    return query_grad.astype(bfloat).reshape(rows, -1), edge, pair


def norm_backward(values, out_grad, gain_vec):
    center = jnp.mean(values, axis=-1, keepdims=True)
    centered = values - center
    rs = lax.rsqrt(jnp.mean(centered * centered, axis=-1, keepdims=True) + 1e-05)
    xhat = centered * rs
    g = out_grad * gain_vec
    part = rs * (g - jnp.mean(g, axis=-1, keepdims=True) - xhat * jnp.mean(g * xhat, axis=-1, keepdims=True))
    return part, jnp.sum(out_grad * xhat, axis=0), jnp.sum(out_grad, axis=0)


def on_device(
    inputs,
    exit_layers,
    lengths,
    layer_index,
    out_grad,
    ln1_gain,
    ln1_bias,
    q_weight,
    q_bias,
    k_weight,
    v_weight,
    v_bias,
    o_weight,
    o_bias,
    ln2_gain,
    ln2_bias,
    fc1_weight,
    fc1_bias,
    fc2_weight,
    fc2_bias,
):
    B, Z, X = lax.axis_size("b"), lax.axis_size("z"), lax.axis_size("x")
    R = B * X
    local = inputs[0].astype(single)
    tok, D = local.shape
    span = X * tok
    group_tok = Z * span
    at_z, at_x = lax.axis_index("z"), lax.axis_index("x")
    rank = lax.axis_index("b") * X + at_x
    rows_dev = q_weight.shape[0]
    cols = D // R
    heads = cols // HEAD_DIM
    whole_heads = rows_dev % HEAD_DIM == 0
    fast = (B, Z, X, rows_dev) == (4, 4, 2, HEAD_DIM)

    group_active = (exit_layers[0] > layer_index[0]).astype(single)
    active_total = jnp.sum(group_active)
    active = lax.dynamic_slice_in_dim(group_active, at_z * span + at_x * tok, tok, 0)[:, None]

    count = lengths.shape[1]
    upto = jnp.arange(count)[:, None] <= jnp.arange(count)[None, :]
    def to_ranks(matrix):
        lead = matrix.shape[:-1]
        if whole_heads:
            matrix = matrix.reshape(*lead, B, Z, X, rows_dev)
            k = len(lead)
            return matrix.transpose(k, k + 2, *range(k), k + 1, k + 3).reshape(R, *lead, cols)
        return jnp.moveaxis(matrix.reshape(*lead, R, cols), -2, 0)

    def from_ranks(parts):
        if whole_heads:
            parts = parts.reshape(B, X, -1, Z, rows_dev)
            return parts.transpose(2, 0, 3, 1, 4).reshape(-1, D)
        return parts.transpose(1, 0, 2).reshape(-1, D)

    def mine(vector):
        return lax.dynamic_index_in_dim(to_ranks(vector), rank, 0, keepdims=False)

    if whole_heads:
        weight_o = lax.all_gather(o_weight, "z", axis=0, tiled=True)
    else:
        weight_o = lax.dynamic_slice_in_dim(lax.all_gather(o_weight, ALL, axis=0, tiled=True), rank * cols, cols, 0)
    small = [ln1_gain, ln1_bias, q_bias, v_bias, o_bias, ln2_gain, ln2_bias, fc2_bias]
    pack = jnp.concatenate([v.astype(single) for v in (*small, fc1_bias, lengths[0])])
    pack = jnp.concatenate([pack, jnp.zeros((-pack.shape[0] % 128,), single)])
    if fast:
        query_mine, pair_mine, pack = spread(q_weight, k_weight, v_weight, pack, R * Z, 8)
        query_mine, pair_mine, pack = query_mine.reshape(-1, cols), pair_mine.reshape(-1, 2 * cols), pack[:, 0]
    else:
        qkv_parts = jnp.concatenate([to_ranks(q_weight), to_ranks(k_weight), to_ranks(v_weight)], axis=2)
        qkv_mine = lax.all_to_all(qkv_parts, PLANE, split_axis=0, concat_axis=0, tiled=True).reshape(D // Z, 3 * cols)
        query_mine, pair_mine = qkv_mine[:, :cols], qkv_mine[:, cols:]
        pack = jnp.broadcast_to(pack, (R * Z, pack.shape[0]))
        pack = lax.all_to_all(pack, ALL, split_axis=0, concat_axis=0, tiled=True)
    vectors = [pack[:, i * rows_dev : (i + 1) * rows_dev].reshape(-1) for i in range(len(small))]
    gain_one, bias_one, bias_q, bias_v, bias_o, gain_two, bias_two, bias_down = vectors
    pack = pack.reshape(B, Z, X, -1)[..., len(small) * rows_dev :]
    up_dev = fc1_bias.shape[0]
    bias_up = lax.dynamic_index_in_dim(
        pack[..., :up_dev].transpose(0, 2, 1, 3).reshape(R, Z * up_dev), rank, 0, keepdims=False
    )
    group_lengths = pack[:, 0, 0, up_dev : up_dev + count].astype(jnp.int32)
    ends = jnp.sum(jnp.where(upto, group_lengths[:, :, None], 0), axis=1)
    places = at_z * span + jnp.arange(span, dtype=jnp.int32)
    starts = jnp.max(jnp.where(ends[:, None, :] <= places[None, :, None], ends[:, None, :], 0), axis=2)
    starts = starts - (at_z - 1) * span

    def feature_rows(mine):
        full = lax.all_gather(mine, "z", axis=0, tiled=True)
        return full.reshape(Z, B, X, rows_dev, -1).transpose(1, 0, 2, 3, 4).reshape(D, -1)

    weight_all = feature_rows(jnp.concatenate([query_mine, pair_mine], axis=1))
    bias_kv = jnp.concatenate([jnp.zeros((cols,), single), mine(bias_v)])
    bias_one, weight_o = lax.optimization_barrier((bias_one, weight_o))
    normed_low = layer_norm(local, gain_one, bias_one).astype(bfloat)

    def gather_plane(rows, cid, name):
        if fast:
            return plane_gather(rows, (), [], None, cid, name)[0]
        return lax.all_gather(rows, PLANE, axis=0, tiled=True)

    def gather_plane_dot(rows, weight, shift, out_type, turned, cid, name):
        if fast:
            return gather_dot(rows, weight, shift, out_type, turned, cid, name)
        rows = lax.all_gather(rows, PLANE, axis=0, tiled=True)
        return rows, ((dot_nt if turned else dot)(rows, weight) + shift).astype(out_type)

    def reduce_plane(left, weight, turned, cid, name):
        if fast:
            return dot_reduce([left], [weight], turned, cid, name)
        terms = (dot_nt if turned else dot)(left, weight).astype(bfloat)
        return lax.psum_scatter(terms, PLANE, scatter_dimension=0, tiled=True).astype(single)

    normed_all = gather_plane(normed_low, 0, "gather_normed")
    units = fc1_bias.shape[0] // 2
    halves = [jnp.concatenate([fc1_weight.T[i : i + units], fc2_weight[i : i + units]]) for i in (0, units)]

    def gather_units(mine):
        return lax.all_gather(mine, "z", axis=0, tiled=True).reshape(Z, 2, units, D)

    normed_all, weight_all, unit_one = lax.optimization_barrier((normed_all, weight_all, halves[0]))
    weight_q, weight_kv = weight_all[:, :cols], weight_all[:, cols:]
    unit_one = gather_units(unit_one)
    key_value = (dot(normed_all, weight_kv) + bias_kv).astype(bfloat)
    up = [(i, i + 1) for i in range(Z - 1)]
    down = [(i + 1, i) for i in range(Z - 1)]
    cotangent = out_grad[0].astype(single) * (group_tok / active_total)
    branch_grad = (active * cotangent).astype(bfloat)
    down_b_grad = column_sums(branch_grad)
    key_value, branch_grad = lax.optimization_barrier((key_value, branch_grad))
    before = lax.ppermute(key_value, "z", up)
    branch_all = gather_plane(branch_grad, 7, "gather_branch")
    branch_all, late_normed = lax.optimization_barrier((branch_all, normed_all))
    query = (dot(late_normed, weight_q) + mine(bias_q)).astype(bfloat)
    before, query = lax.optimization_barrier((before, query))
    starts = starts.reshape(B * span, 1)
    context = attention_forward(starts, query, key_value, before, B)
    context, unit_two = lax.optimization_barrier((context, halves[1]))
    unit_two = gather_units(unit_two)

    attended = reduce_plane(context, weight_o, False, 1, "attended") + bias_o
    middle = local + active * attended
    normed_two = layer_norm(middle, gain_two, bias_two).astype(bfloat)
    bias_up = bias_up.reshape(Z, 2, units)
    bias_up = [bias_up[:, i].reshape(1, Z * units) for i in range(2)]

    def sum_halves(left, right, turned, cid, name):
        if fast:
            return dot_reduce(left, right, turned, cid, name)
        terms = sum((dot_nt if turned else dot)(a, w) for a, w in zip(left, right)).astype(bfloat)
        return lax.psum_scatter(terms, PLANE, scatter_dimension=0, tiled=True).astype(single)

    def sum_z(grads):
        return lax.psum_scatter(grads.reshape(Z * 2 * units, D), "z", scatter_dimension=0, tiled=True)

    if fast:
        branch_rows = branch_all.reshape(R, tok, D)
        two_all, hidden_one, pre_one, bias_one_up, grads = first_units(normed_two, branch_rows, unit_one, bias_up[0], 2)
        shard_one = sum_z(grads)
        hidden_two, bias_two_up, normed_two_grad, grads = last_units(
            two_all, branch_rows, pre_one, unit_one, unit_two, bias_up[1], 3
        )
        shard_two = sum_z(grads)
        up_b_halves = [bias_one_up[0], bias_two_up[0]]
    else:
        two_all = gather_plane(normed_two, 2, "gather_two")

        def half_units(weights, bias):
            weight_up, weight_down = [weights[:, i].reshape(Z * units, D) for i in (0, 1)]
            hidden, gelu_pull = jax.vjp(partial(jax.nn.gelu, approximate=True), dot_nt(two_all, weight_up) + bias)
            hidden = hidden.astype(bfloat)
            pre_grad = gelu_pull(dot_nt(branch_all, weight_down))[0].astype(bfloat)
            grads = dot_tn(pre_grad, two_all), dot_tn(hidden, branch_all)
            grads = jnp.stack([g.astype(bfloat).reshape(Z, units, D) for g in grads], axis=1)
            return hidden, pre_grad, sum_z(grads), weight_up, weight_down

        hidden_one, pre_one, shard_one, up_one, down_one = half_units(unit_one, bias_up[0])
        hidden_two, pre_two, shard_two, up_two, down_two = half_units(unit_two, bias_up[1])
        up_b_halves = [column_sums(pre_one), column_sums(pre_two)]
        normed_two_grad = sum_halves([pre_one, pre_two], [up_one, up_two], False, 3, "up_grad")
    up_b_grad = jnp.stack([half.reshape(Z, units) for half in up_b_halves], axis=1).reshape(-1)

    middle_part, gain_two_grad, bias_two_grad = norm_backward(middle, normed_two_grad, gain_two)
    middle_grad = cotangent + middle_part
    attended_grad = (active * middle_grad).astype(bfloat)
    out_b_grad = column_sums(attended_grad)
    attended_all, context_grad = gather_plane_dot(
        attended_grad, weight_o, jnp.zeros((1, cols), single), bfloat, True, 5, "attended_grad"
    )
    context_grad, shard_one = lax.optimization_barrier((context_grad, shard_one))
    out_w_grad = dot_tn(context, attended_all)
    query_grad, edge, pair = attention_backward(starts, query, key_value, before, context_grad, B)
    hidden_one, edge, pair, query_grad = lax.optimization_barrier((hidden_one, edge, pair, query_grad))
    after = lax.ppermute(edge, "z", down)
    query_w_grad = dot_tn(normed_all, query_grad).astype(bfloat)
    hidden_one, query_w_grad, out_w_grad = lax.optimization_barrier((hidden_one, query_w_grad, out_w_grad))
    downs = [unit_one, unit_two] if fast else [down_one, down_two]
    branch = sum_halves([hidden_one, hidden_two], downs, False, 4, "down")
    branch, after, shard_two = lax.optimization_barrier((branch, after, shard_two))
    if fast:
        pair_grad, qkv_w_grad, value_b_grad = pair_grads(pair, after, normed_all, query_w_grad, B, Z, X)
        value_b_grad = value_b_grad[0]
    else:
        pair_grad = (pair + after.astype(single)).astype(bfloat)
        pair_w_grad = dot_tn(normed_all, pair_grad).astype(bfloat)
        qkv_w_grad = jnp.concatenate([query_w_grad, pair_w_grad], axis=1)
        qkv_w_grad = qkv_w_grad.reshape(B, Z, X, rows_dev, 3 * cols).transpose(1, 0, 2, 3, 4)
        value_b_grad = column_sums(pair_grad[:, cols:])
    qkv_w_grad = qkv_w_grad.reshape(D, 3 * cols)
    qkv_w_grad = lax.psum_scatter(qkv_w_grad, "z", scatter_dimension=0, tiled=True).reshape(R, rows_dev, 3 * cols)
    normed_grad = sum_halves([query_grad, pair_grad], [weight_q, weight_kv], True, 6, "qkv_grad")
    query_b_grad = column_sums(query_grad)
    input_part, gain_one_grad, bias_one_grad = norm_backward(local, normed_grad, gain_one)

    def sum_to_owners(vectors, axes, parts):
        split = jnp.concatenate([v.reshape(parts, -1) for v in vectors], axis=1)
        summed = jnp.sum(lax.all_to_all(split, axes, split_axis=0, concat_axis=0, tiled=True), axis=0)
        widths = [v.shape[0] // parts for v in vectors]
        return [summed[sum(widths[:i]) : sum(widths[: i + 1])] for i in range(len(widths))]

    qkv_w_grad, out_w_grad = lax.optimization_barrier((qkv_w_grad, out_w_grad))
    device_sums = [gain_one_grad, bias_one_grad, out_b_grad, gain_two_grad, bias_two_grad, down_b_grad]
    if fast:
        rank_sums = jnp.concatenate([v.reshape(Z, -1) for v in (query_b_grad, value_b_grad, up_b_grad)], axis=1)
        here = (jnp.arange(R) == rank).reshape(B, 1, X, 1)
        rank_sums = jnp.where(here, rank_sums[None, :, None, :], 0.0).reshape(R * Z, -1)
        rows = jnp.concatenate([v.reshape(R * Z, -1) for v in device_sums] + [rank_sums], axis=1)
        q_w_shard, k_w_shard, v_w_shard, summed = settle(qkv_w_grad, rows, 9)
        q_w_shard, k_w_shard, v_w_shard = [t.astype(single) for t in (q_w_shard, k_w_shard, v_w_shard)]
        sums = [summed[0, i * rows_dev : (i + 1) * rows_dev] for i in range(len(device_sums) + 2)]
        q_b_shard, v_b_shard = sums[len(device_sums) :]
        up_b_shard = summed[0, (len(device_sums) + 2) * rows_dev :]
    else:
        qkv_w_grad = lax.all_to_all(qkv_w_grad, PLANE, split_axis=0, concat_axis=0, tiled=True)
        q_w_shard, k_w_shard, v_w_shard = [
            from_ranks(qkv_w_grad[..., i : i + cols]).astype(single) for i in range(0, 3 * cols, cols)
        ]
        sums = sum_to_owners(device_sums, ALL, R * Z)
        [up_b_shard] = sum_to_owners([up_b_grad], "z", Z)
    if whole_heads:
        out_w_shard = lax.psum_scatter(out_w_grad.astype(bfloat), "z", scatter_dimension=0, tiled=True).astype(single)
        if not fast:
            q_b_shard, v_b_shard = sum_to_owners([query_b_grad, value_b_grad], "z", Z)
    else:

        def placed(rows):
            full = jnp.zeros((D,) + rows.shape[1:], rows.dtype)
            full = lax.dynamic_update_slice_in_dim(full, rows, rank * cols, 0)
            return lax.psum_scatter(full, ALL, scatter_dimension=0, tiled=True).astype(single)

        out_w_shard = placed(out_w_grad.astype(bfloat))
        q_b_shard = placed(query_b_grad)
        v_b_shard = placed(value_b_grad)
    outputs = middle + active * (branch + bias_down)
    input_grad = middle_grad + input_part
    return (
        outputs.astype(bfloat)[None],
        input_grad.astype(bfloat)[None],
        sums[0],
        sums[1],
        q_w_shard,
        q_b_shard,
        k_w_shard,
        v_w_shard,
        v_b_shard,
        out_w_shard,
        sums[2],
        sums[3],
        sums[4],
        jnp.concatenate([shard_one[:units], shard_two[:units]]).T.astype(single),
        up_b_shard,
        jnp.concatenate([shard_one[units:], shard_two[units:]]).astype(single),
        sums[5],
    )


def solution(mesh):
    groups, parts = mesh.shape["batch"], mesh.shape["seq"]
    inner = Mesh(mesh.devices.reshape(groups, SPANS, parts // SPANS), ("b", "z", "x"))
    token = P("b", ("z", "x"), None)
    vector = P(ALL)
    rows = P(ALL, None)
    columns = P(None, ALL)
    return jax.shard_map(
        on_device,
        mesh=inner,
        in_specs=(
            token,
            P("b", None),
            P("b", None),
            P(),
            token,
            vector,
            vector,
            rows,
            vector,
            rows,
            rows,
            vector,
            rows,
            vector,
            vector,
            vector,
            columns,
            vector,
            rows,
            vector,
        ),
        out_specs=(
            token,
            token,
            vector,
            vector,
            rows,
            vector,
            rows,
            rows,
            vector,
            rows,
            vector,
            vector,
            vector,
            columns,
            vector,
            rows,
            vector,
        ),
        check_vma=False,
    )
```

```python
import functools
from functools import partial

import jax
import jax.numpy as jnp
from jax import lax
from jax.experimental import pallas as pl
from jax.experimental.pallas import tpu as pltpu
from jax.sharding import Mesh
from jax.sharding import PartitionSpec as P

HEAD_DIM = 64
SPANS = 4

bfloat = jnp.bfloat16
single = jnp.float32

PLANE = ("b", "x")
ALL = ("b", "z", "x")
MESH = pl.DeviceIdType.MESH
TILE = 512

def plane_place():
    b, z, x = lax.axis_index("b"), lax.axis_index("z"), lax.axis_index("x")
    sib_b = b + 1 - 2 * lax.rem(b, 2)
    far_b = lax.rem(b + 2, 4)
    far_sib_b = lax.rem(sib_b + 2, 4)
    ids = {"s": (sib_b, z, x), "x": (b, z, 1 - x), "y": (far_b, z, x)}
    ranks = {
        "o": b * 2 + x,
        "s": sib_b * 2 + x,
        "x": b * 2 + 1 - x,
        "xs": sib_b * 2 + 1 - x,
        "y": far_b * 2 + x,
        "ys": far_sib_b * 2 + x,
        "d": far_b * 2 + 1 - x,
        "ds": far_sib_b * 2 + 1 - x,
    }
    return ids, ranks

def greet(ids):
    barrier = pltpu.get_barrier_semaphore()
    for device in ids.values():
        pl.semaphore_signal(barrier, inc=1, device_id=device, device_id_type=MESH)
    pl.semaphore_wait(barrier, len(ids))

def tiles(lo, hi, body):
    def step(i, _):
        body(pl.ds(pl.multiple_of(i * TILE, TILE), TILE))
        return 0
    lax.fori_loop(lo // TILE, hi // TILE, step, 0)

def gather_kernel(body_of, n_in, n_out, x_ref, *refs):
    ins = refs[:n_in]; all_ref = refs[n_in]; outs = refs[n_in + 1 : n_in + 1 + n_out]
    held, send, recv, keep = refs[n_in + 1 + n_out :]
    ids, at = plane_place()
    half = x_ref.shape[0] // 2
    parts = (pl.ds(0, half), pl.ds(half, half))
    greet(ids)
    count = [0]
    started = []
    def ship(src, dst, to):
        n = count[0]; count[0] += 1
        c = pltpu.make_async_remote_copy(src_ref=src, dst_ref=dst, send_sem=send.at[n], recv_sem=recv.at[n], device_id=ids[to], device_id_type=MESH)
        c.start(); started.append(c)
        return c
    own = at["o"]
    x0 = ship(x_ref.at[parts[0]], held.at[own, parts[0]], "x")
    y1 = ship(x_ref.at[parts[1]], held.at[own, parts[1]], "y")
    x1 = ship(x_ref.at[parts[1]], held.at[own, parts[1]], "x")
    y0 = ship(x_ref.at[parts[0]], held.at[own, parts[0]], "y")
    s0 = ship(x_ref, held.at[own], "s")
    kept = []
    def done(rank, src):
        c = pltpu.make_async_copy(src, all_ref.at[rank], keep.at[len(kept)])
        c.start(); kept.append(c)
        if body_of is not None:
            body_of(rank, src, ins, outs)
    done(own, x_ref)
    s0.wait_recv()
    done(at["s"], held.at[at["s"]])
    x0.wait_recv()
    ry = ship(held.at[at["x"], parts[0]], held.at[at["x"], parts[0]], "y")
    y1.wait_recv()
    rx = ship(held.at[at["y"], parts[1]], held.at[at["y"], parts[1]], "x")
    x1.wait_recv()
    sx = ship(held.at[at["x"]], held.at[at["x"]], "s")
    y0.wait_recv()
    sy = ship(held.at[at["y"]], held.at[at["y"]], "s")
    done(at["x"], held.at[at["x"]])
    done(at["y"], held.at[at["y"]])
    sx.wait_recv()
    done(at["xs"], held.at[at["xs"]])
    sy.wait_recv()
    done(at["ys"], held.at[at["ys"]])
    ry.wait_recv(); rx.wait_recv()
    sd = ship(held.at[at["d"]], held.at[at["d"]], "s")
    done(at["d"], held.at[at["d"]])
    sd.wait_recv()
    done(at["ds"], held.at[at["ds"]])
    for c in started: c.wait_send()
    for c in kept: c.wait()

def vmem(n): return [pl.BlockSpec(memory_space=pltpu.VMEM)] * n

def plane_gather(x, ins, out_types, body_of, cid, name, ranks=8):
    tok, D = x.shape
    res = pl.pallas_call(
        functools.partial(gather_kernel, body_of, len(ins), len(out_types)),
        out_shape=[jax.ShapeDtypeStruct((ranks, tok, D), x.dtype), *out_types],
        in_specs=vmem(1 + len(ins)),
        out_specs=[pl.BlockSpec(memory_space=pl.ANY)] + vmem(len(out_types)),
        scratch_shapes=[pltpu.VMEM((ranks, tok, D), x.dtype), pltpu.SemaphoreType.DMA((10,)), pltpu.SemaphoreType.DMA((10,)), pltpu.SemaphoreType.DMA((8,))],
        compiler_params=pltpu.CompilerParams(collective_id=cid, has_side_effects=True, vmem_limit_bytes=60 << 20),
        cost_estimate=pl.CostEstimate(flops=1 << 30, bytes_accessed=128 << 20, transcendentals=0),
        name=name,
    )(x, *ins)
    return res[0].reshape(ranks * tok, D), *res[1:]

def gather_dot(x, w, bias, out_dtype, turned, cid, name):
    ranks, tok, D = 8, *x.shape
    N = w.shape[0] if turned else w.shape[1]
    tile = min(N, 512) if N % 512 == 0 else 256
    def body(rank, src, ins, outs):
        w_ref, b_ref = ins
        def step(i, _):
            cols = pl.ds(pl.multiple_of(i * tile, tile), tile)
            if turned:
                y = lax.dot_general(src[...], w_ref[cols, :], (((1,), (1,)), ((), ())), preferred_element_type=single)
            else:
                y = jnp.dot(src[...], w_ref[:, cols], preferred_element_type=single)
            outs[0][rank, :, cols] = (y + b_ref[:, cols]).astype(out_dtype)
            return 0
        lax.fori_loop(0, N // tile, step, 0)
    all_, y = plane_gather(x, (w, bias), [jax.ShapeDtypeStruct((ranks, tok, N), out_dtype)], body, cid, name)
    return all_, y.reshape(ranks * tok, N)

def reduce_kernel(turned, pairs, *refs):
    left, right = refs[:pairs], refs[pairs : 2 * pairs]
    out_ref, sib_out, sib_in, stage, landed, send, recv = refs[2 * pairs :]
    ids, at = plane_place()
    D = out_ref.shape[1]
    mid = D // 2
    greet(ids)
    count = [0]; started = []
    def ship(src, dst, to):
        n = count[0]; count[0] += 1
        c = pltpu.make_async_remote_copy(src_ref=src, dst_ref=dst, send_sem=send.at[n], recv_sem=recv.at[n], device_id=ids[to], device_id_type=MESH)
        c.start(); started.append(c)
        return c
    def term(rank, cols):
        if turned:
            return sum(dot_nt(a[rank], w[cols, :]) for a, w in zip(left, right))
        rows = [w[:, 1, :, cols].reshape(-1, TILE) if len(w.shape) == 4 else w[:, cols] for w in right]
        return sum(dot(a[rank], w) for a, w in zip(left, rows))
    order = ("d", "x", "y", "o")
    twin = {"d": "ds", "x": "xs", "y": "ys", "o": "s"}
    sib = {}
    def to_sibling(j, h):
        def fill(cols):
            sib_out[j, h, :, local(h, cols)] = term(at[twin[order[j]]], cols).astype(bfloat)
        tiles(h * mid, (h + 1) * mid, fill)
        sib[j, h] = ship(sib_out.at[j, h], sib_in.at[j, h], "s")
    def local(h, cols):
        return pl.ds(pl.multiple_of(cols.start - h * mid, TILE), TILE)
    def pair(j, h, cols):
        return term(at[order[j]], cols) + sib_in[j, h, :, local(h, cols)].astype(single)
    def put(j, h, extra=None):
        sib[j, h].wait_recv()
        def fill(cols):
            value = pair(j, h, cols)
            if extra is not None:
                value = value + landed[extra, :, local(h, cols)].astype(single)
            stage[j, h, :, local(h, cols)] = value.astype(bfloat)
        tiles(h * mid, (h + 1) * mid, fill)
    to_sibling(0, 0)
    to_sibling(0, 1)
    put(0, 0)
    d_a = ship(stage.at[0, 0], landed.at[0], "x")
    put(0, 1)
    d_b = ship(stage.at[0, 1], landed.at[1], "y")
    to_sibling(1, 0)
    to_sibling(2, 1)
    put(1, 0)
    x_a = ship(stage.at[1, 0], landed.at[2], "x")
    put(2, 1)
    y_b = ship(stage.at[2, 1], landed.at[3], "y")
    for j, h in ((1, 1), (2, 0), (3, 0), (3, 1)):
        to_sibling(j, h)
    d_b.wait_recv()
    put(1, 1, extra=1)
    x_b = ship(stage.at[1, 1], landed.at[5], "x")
    d_a.wait_recv()
    put(2, 0, extra=0)
    y_a = ship(stage.at[2, 0], landed.at[4], "y")
    for h in range(2):
        sib[3, h].wait_recv()
        def first(cols, h=h):
            out_ref[:, cols] = pair(3, h, cols)
        tiles(h * mid, (h + 1) * mid, first)
    x_a.wait_recv(); y_b.wait_recv(); x_b.wait_recv(); y_a.wait_recv()
    for h, (n, m) in enumerate(((2, 4), (3, 5))):
        def add(cols, h=h, n=n, m=m):
            c = local(h, cols)
            out_ref[:, cols] = out_ref[:, cols] + landed[n, :, c].astype(single) + landed[m, :, c].astype(single)
        tiles(h * mid, (h + 1) * mid, add)
    for c in started: c.wait_send()

def dot_reduce(left, right, turned, cid, name):
    ranks = 8
    D = right[0].shape[0] if turned else right[0].shape[-1]
    tok = left[0].size // left[0].shape[-1] // ranks
    return pl.pallas_call(
        functools.partial(reduce_kernel, turned, len(left)),
        out_shape=jax.ShapeDtypeStruct((tok, D), single),
        in_specs=vmem(2 * len(left)), out_specs=vmem(1)[0],
        scratch_shapes=[pltpu.VMEM((4, 2, tok, D // 2), bfloat), pltpu.VMEM((4, 2, tok, D // 2), bfloat), pltpu.VMEM((3, 2, tok, D // 2), bfloat), pltpu.VMEM((6, tok, D // 2), bfloat),
            pltpu.SemaphoreType.DMA((14,)), pltpu.SemaphoreType.DMA((14,))],
        compiler_params=pltpu.CompilerParams(collective_id=cid, has_side_effects=True, vmem_limit_bytes=60 << 20),
        cost_estimate=pl.CostEstimate(flops=1 << 30, bytes_accessed=128 << 20, transcendentals=0),
        name=name,
    )(*[a.reshape(ranks, tok, -1) for a in left], *right)


def dot(left, right):
    return jnp.dot(left, right, preferred_element_type=single)


def dot_tn(left, right):
    return lax.dot_general(left, right, (((0,), (0,)), ((), ())), preferred_element_type=single)


def dot_nt(left, right):
    return lax.dot_general(left, right, (((1,), (1,)), ((), ())), preferred_element_type=single)


def layer_norm(values, gain_vec, shift_vec):
    center = jnp.mean(values, axis=-1, keepdims=True)
    centered = values - center
    spread = jnp.mean(centered * centered, axis=-1, keepdims=True)
    return centered * lax.rsqrt(spread + 1e-05) * gain_vec + shift_vec


def column_sums(matrix):
    return jnp.sum(matrix.astype(single), axis=0)


def shipper(send, recv, ids):
    started = []

    def ship(src, dst, to):
        n = len(started)
        copy = pltpu.make_async_remote_copy(
            src_ref=src, dst_ref=dst, send_sem=send.at[n], recv_sem=recv.at[n], device_id=ids[to], device_id_type=MESH
        )
        copy.start()
        started.append(copy)
        return copy

    return ship, started


TWIN = {"o": "s", "x": "xs", "y": "ys", "d": "ds"}


def unit_rows(w_ref, i):
    parts, _, units, D = w_ref.shape
    return w_ref[:, i].reshape(parts * units, D)


def hidden_units(src, branch, w_ref, b_ref, hid_ref, pg_ref, pb_ref, rank):
    pre = dot_nt(src[...], unit_rows(w_ref, 0)) + b_ref[...]
    square = pre * pre
    bend = jnp.tanh(0.7978845608028654 * (pre + 0.044715 * (pre * square)))
    rise = 0.5 * (1.0 + bend)
    hid_ref[rank] = (pre * rise).astype(bfloat)
    slope = rise + (0.5 * 0.7978845608028654) * pre * (1.0 - bend * bend) * (1.0 + 3 * 0.044715 * square)
    grad = (dot_nt(branch[...], unit_rows(w_ref, 1)) * slope).astype(bfloat)
    pg_ref[rank] = grad
    pb_ref[...] += jnp.sum(grad.astype(single), axis=0, keepdims=True)


def first_units_kernel(
    x_ref, bg_ref, w_ref, b_ref, all_ref, hid_ref, pg_ref, pb_ref, grad_ref,
    held, bg, total, send, recv, keep, load,
):
    ids, at = plane_place()
    tok = x_ref.shape[0]
    half = tok // 2
    parts = (pl.ds(0, half), pl.ds(half, half))
    own = at["o"]
    loads = {}
    for n, name in enumerate(at):
        loads[name] = pltpu.make_async_copy(bg_ref.at[at[name]], bg.at[at[name]], load.at[n])
    loads["o"].start()
    greet(ids)
    ship, started = shipper(send, recv, ids)
    x0 = ship(x_ref.at[parts[0]], held.at[own, parts[0]], "x")
    y1 = ship(x_ref.at[parts[1]], held.at[own, parts[1]], "y")
    x1 = ship(x_ref.at[parts[1]], held.at[own, parts[1]], "x")
    y0 = ship(x_ref.at[parts[0]], held.at[own, parts[0]], "y")
    s0 = ship(x_ref, held.at[own], "s")
    pb_ref[...] = jnp.zeros_like(pb_ref)
    kept = []

    def units(name):
        rank = at[name]
        src = x_ref if name == "o" else held.at[rank]
        copy = pltpu.make_async_copy(src, all_ref.at[rank], keep.at[len(kept)])
        copy.start()
        kept.append(copy)
        loads[name].wait()
        if name == "o":
            for other in loads:
                if other != "o":
                    loads[other].start()
        hidden_units(src, bg.at[rank], w_ref, b_ref, hid_ref, pg_ref, pb_ref, rank)

    def weigh(name, last=False):
        units_at = grad_ref.shape[2]
        per = 256 // units_at

        def rows(i, _):
            here = pl.ds(pl.multiple_of(i * 256, 256), 256)
            owners = pl.ds(i * per, per)
            for j, left in enumerate((pg_ref, hid_ref)):
                term = 0
                for n in (name, TWIN[name]):
                    right = bg[at[n]] if j else (x_ref[...] if n == "o" else held[at[n]])
                    term = term + dot_tn(left[at[n], :, here], right)
                term = term.reshape(per, units_at, -1)
                if name == "o":
                    total[owners, j] = term
                elif last:
                    grad_ref[owners, j] = (total[owners, j] + term).astype(bfloat)
                else:
                    total[owners, j] += term
            return 0

        lax.fori_loop(0, hid_ref.shape[2] // 256, rows, 0)

    units("o")
    s0.wait_recv()
    units("s")
    x0.wait_recv()
    ry = ship(held.at[at["x"], parts[0]], held.at[at["x"], parts[0]], "y")
    y1.wait_recv()
    rx = ship(held.at[at["y"], parts[1]], held.at[at["y"], parts[1]], "x")
    weigh("o")
    x1.wait_recv()
    sx = ship(held.at[at["x"]], held.at[at["x"]], "s")
    y0.wait_recv()
    sy = ship(held.at[at["y"]], held.at[at["y"]], "s")
    units("x")
    sx.wait_recv()
    units("xs")
    units("y")
    sy.wait_recv()
    units("ys")
    weigh("x")
    ry.wait_recv()
    rx.wait_recv()
    sd = ship(held.at[at["d"]], held.at[at["d"]], "s")
    weigh("y")
    units("d")
    sd.wait_recv()
    units("ds")
    weigh("d", last=True)
    for copy in started:
        copy.wait_send()
    for copy in kept:
        copy.wait()


def last_units_kernel(
    all_ref, bg_ref, pg1_ref, w1_ref, w_ref, b_ref, hid_ref, pb_ref, r_ref, grad_ref,
    held, bg, pg_ref, sib_out, sib_in, stage, landed, send, recv, load, load_b,
):
    ids, at = plane_place()
    ranks, tok, D = held.shape
    mid = D // 2
    names = ("ds", "d", "xs", "x", "ys", "y", "s", "o")
    loads = {}
    for n, name in enumerate(names):
        loads[name] = [
            pltpu.make_async_copy(all_ref.at[at[name]], held.at[at[name]], load.at[n]),
            pltpu.make_async_copy(bg_ref.at[at[name]], bg.at[at[name]], load_b.at[n]),
        ]
    for name in names[:2]:
        for copy in loads[name]:
            copy.start()
    greet(ids)
    ship, started = shipper(send, recv, ids)
    pb_ref[...] = jnp.zeros_like(pb_ref)

    def units(name):
        for copy in loads[name]:
            copy.wait()
        if name == names[0]:
            for other in names[2:]:
                for copy in loads[other]:
                    copy.start()
        rank = at[name]
        hidden_units(held.at[rank], bg.at[rank], w_ref, b_ref, hid_ref, pg_ref, pb_ref, rank)

    def term(name, cols):
        rank = at[name]
        first, second = [w[:, 0, :, cols].reshape(-1, TILE) for w in (w1_ref, w_ref)]
        return dot(pg1_ref[rank], first) + dot(pg_ref[rank], second)

    order = ("d", "x", "y", "o")

    def to_sibling(j):
        def fill(cols):
            sib_out[j, :, cols] = term(TWIN[order[j]], cols).astype(bfloat)

        tiles(0, D, fill)
        return ship(sib_out.at[j], sib_in.at[j], "s")

    def pair(j, cols):
        return term(order[j], cols) + sib_in[j, :, cols].astype(single)

    def local(h, cols):
        return pl.ds(pl.multiple_of(cols.start - h * mid, TILE), TILE)

    def put(j, h, extra=None):
        def fill(cols):
            value = pair(j, cols)
            if extra is not None:
                value = value + landed[extra, :, local(h, cols)].astype(single)
            stage[j, h, :, local(h, cols)] = value.astype(bfloat)

        tiles(h * mid, (h + 1) * mid, fill)

    units("ds")
    d_sib = to_sibling(0)
    units("d")
    d_sib.wait_recv()
    put(0, 0)
    d_a = ship(stage.at[0, 0], landed.at[0], "x")
    put(0, 1)
    d_b = ship(stage.at[0, 1], landed.at[1], "y")
    units("xs")
    x_sib = to_sibling(1)
    units("x")
    x_sib.wait_recv()
    put(1, 0)
    x_a = ship(stage.at[1, 0], landed.at[2], "x")
    units("ys")
    y_sib = to_sibling(2)
    units("y")
    y_sib.wait_recv()
    put(2, 1)
    y_b = ship(stage.at[2, 1], landed.at[3], "y")
    d_b.wait_recv()
    put(1, 1, extra=1)
    x_b = ship(stage.at[1, 1], landed.at[5], "x")
    d_a.wait_recv()
    put(2, 0, extra=0)
    y_a = ship(stage.at[2, 0], landed.at[4], "y")
    units("s")
    own_sib = to_sibling(3)
    units("o")
    own_sib.wait_recv()

    def first(cols):
        r_ref[:, cols] = pair(3, cols)

    tiles(0, D, first)

    units_at = grad_ref.shape[2]
    per = 256 // units_at
    tokens = ranks * tok

    def grads(i, _):
        here = pl.ds(pl.multiple_of(i * 256, 256), 256)
        owners = pl.ds(i * per, per)
        for j, (left, right) in enumerate(((pg_ref, held), (hid_ref, bg))):
            value = dot_tn(left[:, :, here].reshape(tokens, 256), right[...].reshape(tokens, D))
            grad_ref[owners, j] = value.astype(bfloat).reshape(per, units_at, D)
        return 0

    lax.fori_loop(0, hid_ref.shape[2] // 256, grads, 0)
    for copy in (x_a, y_b, x_b, y_a):
        copy.wait_recv()
    for h, (n, m) in enumerate(((2, 4), (3, 5))):

        def add(cols, h=h, n=n, m=m):
            c = local(h, cols)
            r_ref[:, cols] = r_ref[:, cols] + landed[n, :, c].astype(single) + landed[m, :, c].astype(single)

        tiles(h * mid, (h + 1) * mid, add)
    for copy in started:
        copy.wait_send()


def first_units(x, bg, w, bias, cid):
    ranks = 8
    tok, D = x.shape
    F = bias.shape[1]
    anywhere = pl.BlockSpec(memory_space=pl.ANY)
    inside = pl.BlockSpec(memory_space=pltpu.VMEM)
    return pl.pallas_call(
        first_units_kernel,
        out_shape=[
            jax.ShapeDtypeStruct((ranks, tok, D), bfloat),
            jax.ShapeDtypeStruct((ranks, tok, F), bfloat),
            jax.ShapeDtypeStruct((ranks, tok, F), bfloat),
            jax.ShapeDtypeStruct((1, F), single),
            jax.ShapeDtypeStruct(w.shape, bfloat),
        ],
        in_specs=[inside, anywhere, inside, inside],
        out_specs=[anywhere, inside, inside, inside, inside],
        scratch_shapes=[
            pltpu.VMEM((ranks, tok, D), bfloat),
            pltpu.VMEM((ranks, tok, D), bfloat),
            pltpu.VMEM(w.shape, single),
            pltpu.SemaphoreType.DMA((10,)),
            pltpu.SemaphoreType.DMA((10,)),
            pltpu.SemaphoreType.DMA((8,)),
            pltpu.SemaphoreType.DMA((8,)),
        ],
        compiler_params=pltpu.CompilerParams(collective_id=cid, has_side_effects=True, vmem_limit_bytes=62 << 20),
        cost_estimate=pl.CostEstimate(flops=1 << 30, bytes_accessed=160 << 20, transcendentals=0),
        name="first_units",
    )(x, bg, w, bias)


def last_units(rows, bg, pg, w1, w, bias, cid):
    ranks, tok, D = rows.shape
    F = bias.shape[1]
    anywhere = pl.BlockSpec(memory_space=pl.ANY)
    inside = pl.BlockSpec(memory_space=pltpu.VMEM)
    return pl.pallas_call(
        last_units_kernel,
        out_shape=[
            jax.ShapeDtypeStruct((ranks, tok, F), bfloat),
            jax.ShapeDtypeStruct((1, F), single),
            jax.ShapeDtypeStruct((tok, D), single),
            jax.ShapeDtypeStruct(w.shape, bfloat),
        ],
        in_specs=[anywhere, anywhere, inside, inside, inside, inside],
        out_specs=[inside] * 4,
        scratch_shapes=[
            pltpu.VMEM((ranks, tok, D), bfloat),
            pltpu.VMEM((ranks, tok, D), bfloat),
            pltpu.VMEM((ranks, tok, F), bfloat),
            pltpu.VMEM((4, tok, D), bfloat),
            pltpu.VMEM((4, tok, D), bfloat),
            pltpu.VMEM((3, 2, tok, D // 2), bfloat),
            pltpu.VMEM((6, tok, D // 2), bfloat),
            pltpu.SemaphoreType.DMA((10,)),
            pltpu.SemaphoreType.DMA((10,)),
            pltpu.SemaphoreType.DMA((8,)),
            pltpu.SemaphoreType.DMA((8,)),
        ],
        compiler_params=pltpu.CompilerParams(collective_id=cid, has_side_effects=True, vmem_limit_bytes=62 << 20),
        cost_estimate=pl.CostEstimate(flops=1 << 30, bytes_accessed=160 << 20, transcendentals=0),
        name="last_units",
    )(rows, bg, pg, w1, w, bias)


def everyone(width):
    b, z, x = lax.axis_index("b"), lax.axis_index("z"), lax.axis_index("x")
    rank, me = b * 2 + x, (b * 4 + z) * 2 + x

    def in_plane(i):
        other = lax.rem(rank + i, 8)
        return other, (other // 2, z, lax.rem(other, 2))

    def anywhere(i):
        other = lax.rem(me + i, width)
        return other, (other // 8, lax.rem(other // 2, 4), lax.rem(other, 2))

    return rank, me, in_plane, anywhere


def exchange(blocks, landed, rows, gathered, same_row, sems):
    plane_send, plane_recv, all_send, all_recv = sems
    width = gathered.shape[0]
    rank, me, in_plane, anywhere = everyone(width)
    barrier = pltpu.get_barrier_semaphore()

    def each(count, body):
        def step(i, _):
            body(i)
            return 0

        lax.fori_loop(1, count, step, 0)

    each(width, lambda i: pl.semaphore_signal(barrier, inc=1, device_id=anywhere(i)[1], device_id_type=MESH))
    pl.semaphore_wait(barrier, width - 1)

    def block(i):
        other, device = in_plane(i)
        return pltpu.make_async_remote_copy(
            src_ref=blocks.at[other], dst_ref=landed.at[rank], send_sem=plane_send.at[i], recv_sem=plane_recv.at[i],
            device_id=device, device_id_type=MESH,
        )

    def row(i):
        other, device = anywhere(i)
        return pltpu.make_async_remote_copy(
            src_ref=rows.at[0] if same_row else rows.at[other], dst_ref=gathered.at[me],
            send_sem=all_send.at[i], recv_sem=all_recv.at[i], device_id=device, device_id_type=MESH,
        )

    each(8, lambda i: block(i).start())
    each(width, lambda i: row(i).start())
    landed[rank] = blocks[rank]
    gathered[me] = rows[0] if same_row else rows[me]
    each(width, lambda i: row(i).wait())
    each(8, lambda i: block(i).wait())


def head_at(rank, i):
    return (rank // 2 * 4 + i) * 2 + rank % 2


def spread_kernel(q_ref, k_ref, v_ref, pack_ref, q_out, kv_out, pack_out, blocks, landed, gathered, *sems):
    cols = q_out.shape[2]
    for rank in range(8):
        for part, ref in enumerate((q_ref, k_ref, v_ref)):
            heads = [ref[:, head_at(rank, i) * HEAD_DIM : (head_at(rank, i) + 1) * HEAD_DIM] for i in range(4)]
            blocks[rank, :, part * cols : (part + 1) * cols] = jnp.concatenate(heads, axis=1)
    exchange(blocks, landed, pack_ref, gathered, True, sems)
    q_out[...] = landed[:, :, :cols]
    kv_out[...] = landed[:, :, cols:]
    pack_out[...] = gathered[...]


def settle_kernel(w_ref, rows_ref, q_out, k_out, v_out, sums_ref, landed, gathered, *sems):
    cols = w_ref.shape[2] // 3
    exchange(w_ref, landed, rows_ref, gathered, False, sems)
    for part, out in enumerate((q_out, k_out, v_out)):
        for pair in range(out.shape[1] // 128):
            sides = []
            for head in (2 * pair, 2 * pair + 1):
                rank, i = head // 8 * 2 + head % 2, head // 2 % 4
                at = part * cols + i * HEAD_DIM
                sides.append(landed[rank, :, at : at + HEAD_DIM])
            out[:, pair * 128 : (pair + 1) * 128] = jnp.concatenate(sides, axis=1)
    sums_ref[...] = jnp.sum(gathered[...], axis=0)


def exchange_call(kernel, out_shape, args, blocks, landed, gathered, cid, name):
    inside = pl.BlockSpec(memory_space=pltpu.VMEM)
    width = gathered[0]
    return pl.pallas_call(
        kernel,
        out_shape=out_shape,
        in_specs=[inside] * len(args),
        out_specs=[inside] * len(out_shape),
        scratch_shapes=blocks
        + [
            pltpu.VMEM(landed, bfloat),
            pltpu.VMEM(gathered, single),
            pltpu.SemaphoreType.DMA((8,)),
            pltpu.SemaphoreType.DMA((8,)),
            pltpu.SemaphoreType.DMA((width,)),
            pltpu.SemaphoreType.DMA((width,)),
        ],
        compiler_params=pltpu.CompilerParams(collective_id=cid, has_side_effects=True, vmem_limit_bytes=32 << 20),
        cost_estimate=pl.CostEstimate(flops=1 << 20, bytes_accessed=32 << 20, transcendentals=0),
        name=name,
    )(*args)


def spread(q, k, v, pack, devices, cid):
    rows, D = q.shape
    cols = D // 8
    return exchange_call(
        spread_kernel,
        [
            jax.ShapeDtypeStruct((8, rows, cols), bfloat),
            jax.ShapeDtypeStruct((8, rows, 2 * cols), bfloat),
            jax.ShapeDtypeStruct((devices, 1, pack.shape[0]), single),
        ],
        (q, k, v, pack[None, None]),
        [pltpu.VMEM((8, rows, 3 * cols), bfloat)],
        (8, rows, 3 * cols),
        (devices, 1, pack.shape[0]),
        cid,
        "spread",
    )


def settle(weights, rows, cid):
    _, tall, wide = weights.shape
    D = wide // 3 * 8
    return exchange_call(
        settle_kernel,
        [jax.ShapeDtypeStruct((tall, D), bfloat)] * 3 + [jax.ShapeDtypeStruct((1, rows.shape[1]), single)],
        (weights, rows[:, None]),
        [],
        weights.shape,
        (rows.shape[0], 1, rows.shape[1]),
        cid,
        "settle",
    )


def windows(span):
    block = span // 2
    return [(i * block, i * block + block + span) for i in range(2)]

def key_window(before, own, lo, hi, span):
    if lo >= span:
        return own[lo - span : hi - span]
    return jnp.concatenate([before[lo:span], own[0 : hi - span]], axis=0)

def hidden_bias(start_ref, i, block, lo, hi, span):
    rows = span + i * block + lax.broadcasted_iota(jnp.int32, (block, hi - lo), 0)
    keys = lo + lax.broadcasted_iota(jnp.int32, (block, hi - lo), 1)
    start = start_ref[i * block : (i + 1) * block, :]
    return jnp.where((keys >= start) & (keys <= rows), 0.0, -1e30).astype(single)

def each_window(first_ref, span, body):
    block = span // 2
    for i, (lo, hi) in enumerate(windows(span)):
        begins = first_ref[pl.program_id(0) * 2 + i]
        pl.when(begins >= lo + block)(functools.partial(body, i, lo + block, hi))
        pl.when(begins < lo + block)(functools.partial(body, i, lo, hi))


def attend_kernel(first_ref, start_ref, q_ref, k_ref, v_ref, kb_ref, vb_ref, out_ref):
    span, cols = q_ref.shape
    block = span // 2

    def body(i, lo, hi):
        lane = lax.broadcasted_iota(jnp.int32, (block, cols), 1) // HEAD_DIM
        rows = pl.ds(i * block, block)
        bias = hidden_bias(start_ref, i, block, lo, hi, span)
        keys = key_window(kb_ref, k_ref, lo, hi, span)
        vals = key_window(vb_ref, v_ref, lo, hi, span)
        query = q_ref[rows, :] * jnp.asarray(HEAD_DIM ** (-0.5), bfloat)

        def head(h, total):
            mine = lane == h
            scores = dot_nt(jnp.where(mine, query, 0), keys) + bias
            weights = jnp.exp(scores - jnp.max(scores, axis=1, keepdims=True))
            part = jnp.dot(weights.astype(bfloat), vals, preferred_element_type=single)
            part = part * (1.0 / jnp.sum(weights, axis=1, keepdims=True))
            return jnp.where(mine, part, total)

        total = lax.fori_loop(0, cols // HEAD_DIM, head, jnp.zeros((block, cols), single), unroll=True)
        out_ref[rows, :] = total.astype(bfloat)

    each_window(first_ref, span, body)


def attend_back_kernel(
    first_ref, start_ref, q_ref, k_ref, v_ref, kb_ref, vb_ref, do_ref, dq_ref, edge_ref, pair_ref, dk, dv
):
    span, cols = q_ref.shape
    block = span // 2
    scale = HEAD_DIM ** (-0.5)
    dk[...] = jnp.zeros_like(dk)
    dv[...] = jnp.zeros_like(dv)

    def body(i, lo, hi):
        lane = lax.broadcasted_iota(jnp.int32, (block, cols), 1) // HEAD_DIM
        rows = pl.ds(i * block, block)
        bias = hidden_bias(start_ref, i, block, lo, hi, span)
        keys = key_window(kb_ref, k_ref, lo, hi, span)
        vals = key_window(vb_ref, v_ref, lo, hi, span)
        query = q_ref[rows, :] * jnp.asarray(scale, bfloat)
        grad = do_ref[rows, :]

        def head(h, total):
            mine = lane == h
            query_h = jnp.where(mine, query, 0)
            grad_h = jnp.where(mine, grad, 0)
            scores = dot_nt(query_h, keys) + bias
            weights = jnp.exp(scores - jnp.max(scores, axis=1, keepdims=True))
            probs = weights * (1.0 / jnp.sum(weights, axis=1, keepdims=True))
            prob_grad = dot_nt(grad_h, vals)
            row_dot = jnp.sum(probs * prob_grad, axis=1, keepdims=True)
            score_grad = (probs * (prob_grad - row_dot)).astype(bfloat)
            dv[lo:hi, :] += dot_tn(probs.astype(bfloat), grad_h)
            dk[lo:hi, :] += dot_tn(score_grad, query_h)
            part = jnp.dot(score_grad, keys, preferred_element_type=single)
            return jnp.where(mine, part, total)

        total = lax.fori_loop(0, cols // HEAD_DIM, head, jnp.zeros((block, cols), single), unroll=True)
        dq_ref[rows, :] = (total * scale).astype(bfloat)

    each_window(first_ref, span, body)
    edge_ref[:, :cols] = dk[:span, :].astype(bfloat)
    edge_ref[:, cols:] = dv[:span, :].astype(bfloat)
    pair_ref[:, :cols] = dk[span:, :].astype(bfloat)
    pair_ref[:, cols:] = dv[span:, :].astype(bfloat)


def pair_grads_kernel(pair_ref, after_ref, normed_ref, query_w_ref, grad_ref, weight_ref, bias_ref):
    block = pl.program_id(0)
    cols = query_w_ref.shape[1]
    rows = weight_ref.shape[3]

    @pl.when(block == 0)
    def _():
        grad = (pair_ref[...].astype(single) + after_ref[...].astype(single)).astype(bfloat)
        grad_ref[...] = grad
        bias_ref[...] = jnp.sum(grad[:, cols:].astype(single), axis=0, keepdims=True)

    value = dot_tn(normed_ref[...], grad_ref[...]).astype(bfloat)
    xs = weight_ref.shape[2]
    for z in range(weight_ref.shape[0]):
        for x in range(xs):
            here = slice((z * xs + x) * rows, (z * xs + x + 1) * rows)
            weight_ref[z, 0, x, :, :cols] = query_w_ref[here, :]
            weight_ref[z, 0, x, :, cols:] = value[here, :]


def pair_grads(pair, after, normed, query_w, B, Z, X):
    tokens, wide = pair.shape
    D = normed.shape[1]
    per = D // B
    rows = per // (Z * X)
    cols = query_w.shape[1]
    return pl.pallas_call(
        pair_grads_kernel,
        grid=(B,),
        out_shape=[
            jax.ShapeDtypeStruct((tokens, wide), bfloat),
            jax.ShapeDtypeStruct((Z, B, X, rows, cols + wide), bfloat),
            jax.ShapeDtypeStruct((1, wide - cols), single),
        ],
        in_specs=[
            pl.BlockSpec((tokens, wide), lambda b: (0, 0)),
            pl.BlockSpec((tokens, wide), lambda b: (0, 0)),
            pl.BlockSpec((tokens, per), lambda b: (0, b)),
            pl.BlockSpec((per, cols), lambda b: (b, 0)),
        ],
        out_specs=[
            pl.BlockSpec((tokens, wide), lambda b: (0, 0)),
            pl.BlockSpec((Z, 1, X, rows, cols + wide), lambda b: (0, b, 0, 0, 0)),
            pl.BlockSpec((1, wide - cols), lambda b: (0, 0)),
        ],
        compiler_params=pltpu.CompilerParams(vmem_limit_bytes=48 << 20),
        name="pair_grads",
    )(pair, after, normed, query_w)


def block_starts(starts, groups):
    return starts.reshape(groups * 2, -1)[:, 0]


def attention_specs(span, cols):
    def at(j):
        return pl.BlockSpec((span, cols), lambda g, _: (g, j))
    return [pl.BlockSpec((span, 1), lambda g, _: (g, 0)), at(0), at(0), at(1), at(0), at(1)]

def attend(starts, query, key_value, before, groups):
    span, cols = query.shape[0] // groups, query.shape[1]
    return pl.pallas_call(
        attend_kernel,
        out_shape=jax.ShapeDtypeStruct((groups * span, cols), bfloat),
        grid_spec=pltpu.PrefetchScalarGridSpec(
            num_scalar_prefetch=1,
            grid=(groups,),
            in_specs=attention_specs(span, cols),
            out_specs=pl.BlockSpec((span, cols), lambda g, _: (g, 0)),
        ),
        compiler_params=pltpu.CompilerParams(vmem_limit_bytes=60 << 20),
        name="attend",
    )(block_starts(starts, groups), starts, query, key_value, key_value, before, before)

def attend_back(starts, query, key_value, before, grad, groups):
    span, cols = query.shape[0] // groups, query.shape[1]
    rows = groups * span
    return pl.pallas_call(
        attend_back_kernel,
        out_shape=[
            jax.ShapeDtypeStruct((rows, cols), bfloat),
            jax.ShapeDtypeStruct((rows, 2 * cols), bfloat),
            jax.ShapeDtypeStruct((rows, 2 * cols), bfloat),
        ],
        grid_spec=pltpu.PrefetchScalarGridSpec(
            num_scalar_prefetch=1,
            grid=(groups,),
            in_specs=attention_specs(span, cols) + [pl.BlockSpec((span, cols), lambda g, _: (g, 0))],
            out_specs=[pl.BlockSpec((span, cols), lambda g, _: (g, 0))]
            + [pl.BlockSpec((span, 2 * cols), lambda g, _: (g, 0))] * 2,
            scratch_shapes=[pltpu.VMEM((2 * span, cols), single)] * 2,
        ),
        compiler_params=pltpu.CompilerParams(vmem_limit_bytes=60 << 20),
        name="attend_back",
    )(block_starts(starts, groups), starts, query, key_value, key_value, before, before, grad)


def attention_heads(starts, query, key_value, before, groups):
    span, cols = query.shape[0] // groups, query.shape[1]
    both = jnp.concatenate([before.reshape(groups, span, -1), key_value.reshape(groups, span, -1)], axis=1)
    key_two, value_two = [both[..., i * cols : (i + 1) * cols].reshape(groups, 2 * span, -1, HEAD_DIM) for i in (0, 1)]
    query = query.reshape(groups, span, -1, HEAD_DIM)
    keys = jnp.arange(2 * span)[None, None, :]
    rows = span + jnp.arange(span)[None, :, None]
    allowed = (keys >= starts.reshape(groups, span, 1)) & (keys <= rows)
    scores = jnp.einsum("gqhd,gkhd->ghqk", query, key_two, preferred_element_type=single) * HEAD_DIM ** (-0.5)
    scores = jnp.where(allowed[:, None], scores, -1e30)
    weights = jnp.exp(scores - jnp.max(scores, axis=-1, keepdims=True))
    return query, key_two, value_two, weights / jnp.sum(weights, axis=-1, keepdims=True)


def attention_forward(starts, query, key_value, before, groups):
    if query.shape[1] % 128 == 0:
        return attend(starts, query, key_value, before, groups)
    _, _, value_two, probs = attention_heads(starts, query, key_value, before, groups)
    context = jnp.einsum("ghqk,gkhd->gqhd", probs.astype(bfloat), value_two, preferred_element_type=single)
    return context.astype(bfloat).reshape(query.shape)


def attention_backward(starts, query, key_value, before, grad, groups):
    if query.shape[1] % 128 == 0:
        return attend_back(starts, query, key_value, before, grad, groups)
    rows = query.shape[0]
    query, key_two, value_two, probs = attention_heads(starts, query, key_value, before, groups)
    span = query.shape[1]
    grad = grad.reshape(query.shape)
    prob_grad = jnp.einsum("gqhd,gkhd->ghqk", grad, value_two, preferred_element_type=single)
    row_dot = jnp.sum(probs * prob_grad, axis=-1, keepdims=True)
    score_grad = (probs * (prob_grad - row_dot)).astype(bfloat)
    query_grad = jnp.einsum("ghqk,gkhd->gqhd", score_grad, key_two, preferred_element_type=single) * HEAD_DIM ** (-0.5)
    key_grad = jnp.einsum("ghqk,gqhd->gkhd", score_grad, query, preferred_element_type=single) * HEAD_DIM ** (-0.5)
    value_grad = jnp.einsum("ghqk,gqhd->gkhd", probs.astype(bfloat), grad, preferred_element_type=single)
    pair = jnp.concatenate([t.reshape(groups, 2 * span, -1) for t in (key_grad, value_grad)], axis=2)
    edge, pair = [t.reshape(rows, -1) for t in (pair[:, :span].astype(bfloat), pair[:, span:])]
    return query_grad.astype(bfloat).reshape(rows, -1), edge, pair


def norm_backward(values, out_grad, gain_vec):
    center = jnp.mean(values, axis=-1, keepdims=True)
    centered = values - center
    rs = lax.rsqrt(jnp.mean(centered * centered, axis=-1, keepdims=True) + 1e-05)
    xhat = centered * rs
    g = out_grad * gain_vec
    part = rs * (g - jnp.mean(g, axis=-1, keepdims=True) - xhat * jnp.mean(g * xhat, axis=-1, keepdims=True))
    return part, jnp.sum(out_grad * xhat, axis=0), jnp.sum(out_grad, axis=0)


def on_device(
    inputs,
    exit_layers,
    lengths,
    layer_index,
    out_grad,
    ln1_gain,
    ln1_bias,
    q_weight,
    q_bias,
    k_weight,
    v_weight,
    v_bias,
    o_weight,
    o_bias,
    ln2_gain,
    ln2_bias,
    fc1_weight,
    fc1_bias,
    fc2_weight,
    fc2_bias,
):
    B, Z, X = lax.axis_size("b"), lax.axis_size("z"), lax.axis_size("x")
    R = B * X
    local = inputs[0].astype(single)
    tok, D = local.shape
    span = X * tok
    group_tok = Z * span
    at_z, at_x = lax.axis_index("z"), lax.axis_index("x")
    rank = lax.axis_index("b") * X + at_x
    rows_dev = q_weight.shape[0]
    cols = D // R
    heads = cols // HEAD_DIM
    whole_heads = rows_dev % HEAD_DIM == 0
    fast = (B, Z, X, rows_dev) == (4, 4, 2, HEAD_DIM)

    group_active = (exit_layers[0] > layer_index[0]).astype(single)
    active_total = jnp.sum(group_active)
    active = lax.dynamic_slice_in_dim(group_active, at_z * span + at_x * tok, tok, 0)[:, None]

    count = lengths.shape[1]
    upto = jnp.arange(count)[:, None] <= jnp.arange(count)[None, :]
    def to_ranks(matrix):
        lead = matrix.shape[:-1]
        if whole_heads:
            matrix = matrix.reshape(*lead, B, Z, X, rows_dev)
            k = len(lead)
            return matrix.transpose(k, k + 2, *range(k), k + 1, k + 3).reshape(R, *lead, cols)
        return jnp.moveaxis(matrix.reshape(*lead, R, cols), -2, 0)

    def from_ranks(parts):
        if whole_heads:
            parts = parts.reshape(B, X, -1, Z, rows_dev)
            return parts.transpose(2, 0, 3, 1, 4).reshape(-1, D)
        return parts.transpose(1, 0, 2).reshape(-1, D)

    def mine(vector):
        return lax.dynamic_index_in_dim(to_ranks(vector), rank, 0, keepdims=False)

    if whole_heads:
        weight_o = lax.all_gather(o_weight, "z", axis=0, tiled=True)
    else:
        weight_o = lax.dynamic_slice_in_dim(lax.all_gather(o_weight, ALL, axis=0, tiled=True), rank * cols, cols, 0)
    small = [ln1_gain, ln1_bias, q_bias, v_bias, o_bias, ln2_gain, ln2_bias, fc2_bias]
    pack = jnp.concatenate([v.astype(single) for v in (*small, fc1_bias, lengths[0])])
    pack = jnp.concatenate([pack, jnp.zeros((-pack.shape[0] % 128,), single)])
    if fast:
        query_mine, pair_mine, pack = spread(q_weight, k_weight, v_weight, pack, R * Z, 8)
        query_mine, pair_mine, pack = query_mine.reshape(-1, cols), pair_mine.reshape(-1, 2 * cols), pack[:, 0]
    else:
        qkv_parts = jnp.concatenate([to_ranks(q_weight), to_ranks(k_weight), to_ranks(v_weight)], axis=2)
        qkv_mine = lax.all_to_all(qkv_parts, PLANE, split_axis=0, concat_axis=0, tiled=True).reshape(D // Z, 3 * cols)
        query_mine, pair_mine = qkv_mine[:, :cols], qkv_mine[:, cols:]
        pack = jnp.broadcast_to(pack, (R * Z, pack.shape[0]))
        pack = lax.all_to_all(pack, ALL, split_axis=0, concat_axis=0, tiled=True)
    vectors = [pack[:, i * rows_dev : (i + 1) * rows_dev].reshape(-1) for i in range(len(small))]
    gain_one, bias_one, bias_q, bias_v, bias_o, gain_two, bias_two, bias_down = vectors
    pack = pack.reshape(B, Z, X, -1)[..., len(small) * rows_dev :]
    up_dev = fc1_bias.shape[0]
    bias_up = lax.dynamic_index_in_dim(
        pack[..., :up_dev].transpose(0, 2, 1, 3).reshape(R, Z * up_dev), rank, 0, keepdims=False
    )
    group_lengths = pack[:, 0, 0, up_dev : up_dev + count].astype(jnp.int32)
    ends = jnp.sum(jnp.where(upto, group_lengths[:, :, None], 0), axis=1)
    places = at_z * span + jnp.arange(span, dtype=jnp.int32)
    starts = jnp.max(jnp.where(ends[:, None, :] <= places[None, :, None], ends[:, None, :], 0), axis=2)
    starts = starts - (at_z - 1) * span

    def feature_rows(mine):
        full = lax.all_gather(mine, "z", axis=0, tiled=True)
        return full.reshape(Z, B, X, rows_dev, -1).transpose(1, 0, 2, 3, 4).reshape(D, -1)

    weight_kv = feature_rows(pair_mine)
    bias_kv = jnp.concatenate([jnp.zeros((cols,), single), mine(bias_v)])
    bias_one, query_mine, weight_o = lax.optimization_barrier((bias_one, query_mine, weight_o))
    normed_low = layer_norm(local, gain_one, bias_one).astype(bfloat)

    def gather_plane(rows, cid, name):
        if fast:
            return plane_gather(rows, (), [], None, cid, name)[0]
        return lax.all_gather(rows, PLANE, axis=0, tiled=True)

    def gather_plane_dot(rows, weight, shift, out_type, turned, cid, name):
        if fast:
            return gather_dot(rows, weight, shift, out_type, turned, cid, name)
        rows = lax.all_gather(rows, PLANE, axis=0, tiled=True)
        return rows, ((dot_nt if turned else dot)(rows, weight) + shift).astype(out_type)

    def reduce_plane(left, weight, turned, cid, name):
        if fast:
            return dot_reduce([left], [weight], turned, cid, name)
        terms = (dot_nt if turned else dot)(left, weight).astype(bfloat)
        return lax.psum_scatter(terms, PLANE, scatter_dimension=0, tiled=True).astype(single)

    normed_all = gather_plane(normed_low, 0, "gather_normed")
    units = fc1_bias.shape[0] // 2
    halves = [jnp.concatenate([fc1_weight.T[i : i + units], fc2_weight[i : i + units]]) for i in (0, units)]

    def gather_units(mine):
        return lax.all_gather(mine, "z", axis=0, tiled=True).reshape(Z, 2, units, D)

    normed_all, weight_kv, unit_one = lax.optimization_barrier((normed_all, weight_kv, halves[0]))
    weight_q = feature_rows(query_mine)
    unit_one = gather_units(unit_one)
    key_value = (dot(normed_all, weight_kv) + bias_kv).astype(bfloat)
    up = [(i, i + 1) for i in range(Z - 1)]
    down = [(i + 1, i) for i in range(Z - 1)]
    cotangent = out_grad[0].astype(single) * (group_tok / active_total)
    branch_grad = (active * cotangent).astype(bfloat)
    down_b_grad = column_sums(branch_grad)
    key_value, branch_grad = lax.optimization_barrier((key_value, branch_grad))
    before = lax.ppermute(key_value, "z", up)
    branch_all = gather_plane(branch_grad, 7, "gather_branch")
    branch_all, late_normed = lax.optimization_barrier((branch_all, normed_all))
    query = (dot(late_normed, weight_q) + mine(bias_q)).astype(bfloat)
    before, query = lax.optimization_barrier((before, query))
    starts = starts.reshape(B * span, 1)
    context = attention_forward(starts, query, key_value, before, B)
    context, unit_two = lax.optimization_barrier((context, halves[1]))
    unit_two = gather_units(unit_two)

    attended = reduce_plane(context, weight_o, False, 1, "attended") + bias_o
    middle = local + active * attended
    normed_two = layer_norm(middle, gain_two, bias_two).astype(bfloat)
    bias_up = bias_up.reshape(Z, 2, units)
    bias_up = [bias_up[:, i].reshape(1, Z * units) for i in range(2)]

    def sum_halves(left, right, turned, cid, name):
        if fast:
            return dot_reduce(left, right, turned, cid, name)
        terms = sum((dot_nt if turned else dot)(a, w) for a, w in zip(left, right)).astype(bfloat)
        return lax.psum_scatter(terms, PLANE, scatter_dimension=0, tiled=True).astype(single)

    def sum_z(grads):
        return lax.psum_scatter(grads.reshape(Z * 2 * units, D), "z", scatter_dimension=0, tiled=True)

    if fast:
        branch_rows = branch_all.reshape(R, tok, D)
        two_all, hidden_one, pre_one, bias_one_up, grads = first_units(normed_two, branch_rows, unit_one, bias_up[0], 2)
        shard_one = sum_z(grads)
        hidden_two, bias_two_up, normed_two_grad, grads = last_units(
            two_all, branch_rows, pre_one, unit_one, unit_two, bias_up[1], 3
        )
        shard_two = sum_z(grads)
        up_b_halves = [bias_one_up[0], bias_two_up[0]]
    else:
        two_all = gather_plane(normed_two, 2, "gather_two")

        def half_units(weights, bias):
            weight_up, weight_down = [weights[:, i].reshape(Z * units, D) for i in (0, 1)]
            hidden, gelu_pull = jax.vjp(partial(jax.nn.gelu, approximate=True), dot_nt(two_all, weight_up) + bias)
            hidden = hidden.astype(bfloat)
            pre_grad = gelu_pull(dot_nt(branch_all, weight_down))[0].astype(bfloat)
            grads = dot_tn(pre_grad, two_all), dot_tn(hidden, branch_all)
            grads = jnp.stack([g.astype(bfloat).reshape(Z, units, D) for g in grads], axis=1)
            return hidden, pre_grad, sum_z(grads), weight_up, weight_down

        hidden_one, pre_one, shard_one, up_one, down_one = half_units(unit_one, bias_up[0])
        hidden_two, pre_two, shard_two, up_two, down_two = half_units(unit_two, bias_up[1])
        up_b_halves = [column_sums(pre_one), column_sums(pre_two)]
        normed_two_grad = sum_halves([pre_one, pre_two], [up_one, up_two], False, 3, "up_grad")
    up_b_grad = jnp.stack([half.reshape(Z, units) for half in up_b_halves], axis=1).reshape(-1)

    middle_part, gain_two_grad, bias_two_grad = norm_backward(middle, normed_two_grad, gain_two)
    middle_grad = cotangent + middle_part
    attended_grad = (active * middle_grad).astype(bfloat)
    out_b_grad = column_sums(attended_grad)
    attended_all, context_grad = gather_plane_dot(
        attended_grad, weight_o, jnp.zeros((1, cols), single), bfloat, True, 5, "attended_grad"
    )
    context_grad, shard_one = lax.optimization_barrier((context_grad, shard_one))
    out_w_grad = dot_tn(context, attended_all)
    query_grad, edge, pair = attention_backward(starts, query, key_value, before, context_grad, B)
    hidden_one, edge, pair, query_grad = lax.optimization_barrier((hidden_one, edge, pair, query_grad))
    after = lax.ppermute(edge, "z", down)
    query_w_grad = dot_tn(normed_all, query_grad).astype(bfloat)
    hidden_one, query_w_grad, out_w_grad = lax.optimization_barrier((hidden_one, query_w_grad, out_w_grad))
    downs = [unit_one, unit_two] if fast else [down_one, down_two]
    branch = sum_halves([hidden_one, hidden_two], downs, False, 4, "down")
    branch, after, shard_two = lax.optimization_barrier((branch, after, shard_two))
    if fast:
        pair_grad, qkv_w_grad, value_b_grad = pair_grads(pair, after, normed_all, query_w_grad, B, Z, X)
        value_b_grad = value_b_grad[0]
    else:
        pair_grad = (pair + after.astype(single)).astype(bfloat)
        pair_w_grad = dot_tn(normed_all, pair_grad).astype(bfloat)
        qkv_w_grad = jnp.concatenate([query_w_grad, pair_w_grad], axis=1)
        qkv_w_grad = qkv_w_grad.reshape(B, Z, X, rows_dev, 3 * cols).transpose(1, 0, 2, 3, 4)
        value_b_grad = column_sums(pair_grad[:, cols:])
    qkv_w_grad = qkv_w_grad.reshape(D, 3 * cols)
    qkv_w_grad = lax.psum_scatter(qkv_w_grad, "z", scatter_dimension=0, tiled=True).reshape(R, rows_dev, 3 * cols)
    normed_grad = sum_halves([query_grad, pair_grad], [weight_q, weight_kv], True, 6, "qkv_grad")
    query_b_grad = column_sums(query_grad)
    input_part, gain_one_grad, bias_one_grad = norm_backward(local, normed_grad, gain_one)

    def sum_to_owners(vectors, axes, parts):
        split = jnp.concatenate([v.reshape(parts, -1) for v in vectors], axis=1)
        summed = jnp.sum(lax.all_to_all(split, axes, split_axis=0, concat_axis=0, tiled=True), axis=0)
        widths = [v.shape[0] // parts for v in vectors]
        return [summed[sum(widths[:i]) : sum(widths[: i + 1])] for i in range(len(widths))]

    qkv_w_grad, out_w_grad = lax.optimization_barrier((qkv_w_grad, out_w_grad))
    device_sums = [gain_one_grad, bias_one_grad, out_b_grad, gain_two_grad, bias_two_grad, down_b_grad]
    if fast:
        rank_sums = jnp.concatenate([v.reshape(Z, -1) for v in (query_b_grad, value_b_grad, up_b_grad)], axis=1)
        here = (jnp.arange(R) == rank).reshape(B, 1, X, 1)
        rank_sums = jnp.where(here, rank_sums[None, :, None, :], 0.0).reshape(R * Z, -1)
        rows = jnp.concatenate([v.reshape(R * Z, -1) for v in device_sums] + [rank_sums], axis=1)
        q_w_shard, k_w_shard, v_w_shard, summed = settle(qkv_w_grad, rows, 9)
        q_w_shard, k_w_shard, v_w_shard = [t.astype(single) for t in (q_w_shard, k_w_shard, v_w_shard)]
        sums = [summed[0, i * rows_dev : (i + 1) * rows_dev] for i in range(len(device_sums) + 2)]
        q_b_shard, v_b_shard = sums[len(device_sums) :]
        up_b_shard = summed[0, (len(device_sums) + 2) * rows_dev :]
    else:
        qkv_w_grad = lax.all_to_all(qkv_w_grad, PLANE, split_axis=0, concat_axis=0, tiled=True)
        q_w_shard, k_w_shard, v_w_shard = [
            from_ranks(qkv_w_grad[..., i : i + cols]).astype(single) for i in range(0, 3 * cols, cols)
        ]
        sums = sum_to_owners(device_sums, ALL, R * Z)
        [up_b_shard] = sum_to_owners([up_b_grad], "z", Z)
    if whole_heads:
        out_w_shard = lax.psum_scatter(out_w_grad.astype(bfloat), "z", scatter_dimension=0, tiled=True).astype(single)
        if not fast:
            q_b_shard, v_b_shard = sum_to_owners([query_b_grad, value_b_grad], "z", Z)
    else:

        def placed(rows):
            full = jnp.zeros((D,) + rows.shape[1:], rows.dtype)
            full = lax.dynamic_update_slice_in_dim(full, rows, rank * cols, 0)
            return lax.psum_scatter(full, ALL, scatter_dimension=0, tiled=True).astype(single)

        out_w_shard = placed(out_w_grad.astype(bfloat))
        q_b_shard = placed(query_b_grad)
        v_b_shard = placed(value_b_grad)
    outputs = middle + active * (branch + bias_down)
    input_grad = middle_grad + input_part
    return (
        outputs.astype(bfloat)[None],
        input_grad.astype(bfloat)[None],
        sums[0],
        sums[1],
        q_w_shard,
        q_b_shard,
        k_w_shard,
        v_w_shard,
        v_b_shard,
        out_w_shard,
        sums[2],
        sums[3],
        sums[4],
        jnp.concatenate([shard_one[:units], shard_two[:units]]).T.astype(single),
        up_b_shard,
        jnp.concatenate([shard_one[units:], shard_two[units:]]).astype(single),
        sums[5],
    )


def solution(mesh):
    groups, parts = mesh.shape["batch"], mesh.shape["seq"]
    inner = Mesh(mesh.devices.reshape(groups, SPANS, parts // SPANS), ("b", "z", "x"))
    token = P("b", ("z", "x"), None)
    vector = P(ALL)
    rows = P(ALL, None)
    columns = P(None, ALL)
    return jax.shard_map(
        on_device,
        mesh=inner,
        in_specs=(
            token,
            P("b", None),
            P("b", None),
            P(),
            token,
            vector,
            vector,
            rows,
            vector,
            rows,
            rows,
            vector,
            rows,
            vector,
            vector,
            vector,
            columns,
            vector,
            rows,
            vector,
        ),
        out_specs=(
            token,
            token,
            vector,
            vector,
            rows,
            vector,
            rows,
            rows,
            vector,
            rows,
            vector,
            vector,
            vector,
            columns,
            vector,
            rows,
            vector,
        ),
        check_vma=False,
    )
```
